32 devices in a mesh: grp: 2 (over x), lon: 16 (over z, y, core).
Axes of the slice: x: 2, y: 2, z: 4, core: 2. Of those that a mesh axis runs over, the one named last changes fastest.
Arguments:
- grid_latent: bfloat16 [65536, 512], P(('grp', 'lon')), parts along dimension 0, may hold values from -6 to 6
- mesh_latent: bfloat16 [8192, 512], P(('grp', 'lon')), parts along dimension 0, may hold values from -6 to 6
- edge_latent: bfloat16 [98304, 512], P(('grp', 'lon')), parts along dimension 0, may hold values from -6 to 6
- mesh_cotangent: bfloat16 [8192, 512], P(('grp', 'lon')), parts along dimension 0, may hold values from -6 to 6
- edge_src: int32 [98304], P(('grp', 'lon')), parts along dimension 0, may hold values from 0 to 767, as said below
- edge_dst: int32 [98304], P(('grp', 'lon')), parts along dimension 0, may hold values from 0 to 255
- tile_count: int32 [32], P(('grp', 'lon')), parts along dimension 0, may hold values from 1 to 12, as said below
- send_rows: int32 [32, 16, 48], P(('grp', 'lon')), parts along dimension 0, may hold values from -1 to 2047, as said below
- w_edge_in: bfloat16 [1536, 512], replicated, may hold values from -0.15625 to 0.15625
- w_edge_out: bfloat16 [512, 512], replicated, may hold values from -0.25 to 0.25
- w_node_in: bfloat16 [1024, 512], replicated, may hold values from -0.1875 to 0.1875
- w_node_out: bfloat16 [512, 512], replicated, may hold values from -0.25 to 0.25
Outputs:
- grid_grad: bfloat16 [65536, 512], P(('grp', 'lon')), parts along dimension 0
- edge_grad: bfloat16 [98304, 512], P(('grp', 'lon')), parts along dimension 0
- mesh_grad: bfloat16 [8192, 512], P(('grp', 'lon')), parts along dimension 0
- grad_edge_in: float32 [3072, 512], P(('grp', 'lon')), parts along dimension 0
- grad_edge_out: float32 [1024, 512], P(('grp', 'lon')), parts along dimension 0
- grad_node_in: float32 [2048, 512], P(('grp', 'lon')), parts along dimension 0
- grad_node_out: float32 [1024, 512], P(('grp', 'lon')), parts along dimension 0
The draws below stay inside these ranges and needn't reach their ends.
There are 2 independent parts, one for each index of `grp`. The reference program is written for one: setup_inputs(seed, part) draws one part's arguments, and reference() takes and returns one part's arrays. A program takes and returns all parts, laid end to end along the dimension named above; an argument that names none is the same for every part. Nothing has to cross between parts.
Inputs may be any that keep to these rules, and one draw needn't show every extreme that they name: send_rows[p, d, s] is a row of device p's 2048 grid rows sent to device d, or -1 for an empty slot; the live entries of each list come first and are distinct. Lists are non-empty only between sectors at most 3 apart around the loop (full at distance 2 or less), except for one receiving device that gets full lists of 48 from every device. `edge_src`: every edge reads a live slot p * 48 + s of its device's received rows. `tile_count`: some device has all 12 tiles live.
All inputs are finite; a program needn't handle non-finite values.
Results may differ from the reference program's by a relative error of at most 0.015.
Values may be sent and summed in bfloat16 or wider, within the bound.
No kernel may reach another device: no remote copies, remote signals or barrier semaphores. Data moves between devices by JAX's collectives and lax.ppermute only.
A program may use at most 192 MiB of HBM per device.

```python
import jax
import jax.numpy as jnp
from jax import lax

D = 512
G_DEV = 2048
M_DEV = 256
TILE = 256
TILES = 12
CAP = 48
E_DEV = 3072
GRID = 32768
MESH = 4096
EDGES = 49152
N_LON = 16


def counts_table(key):
    first_key, second_key = jax.random.split(key)
    sender = jnp.arange(N_LON)[:, None]
    receiver = jnp.arange(N_LON)[None, :]
    apart = jnp.minimum((sender - receiver) % N_LON, (receiver - sender) % N_LON)
    partial_counts = jax.random.randint(first_key, (N_LON, N_LON), max(CAP // 3, 1), CAP + 1)
    counts = jnp.where(apart <= 2, CAP, jnp.where(apart == 3, partial_counts, 0))
    polar_receiver = jax.random.randint(second_key, (), 0, N_LON)
    counts = jnp.where(receiver == polar_receiver, CAP, counts)
    return (counts, polar_receiver)


def draw_send_rows(key, part):
    counts, polar_receiver = counts_table(key)
    key = jax.random.fold_in(key, 11)
    list_keys = jax.random.split(key, N_LON * N_LON)
    shuffles = jax.vmap(lambda single: jax.random.permutation(single, G_DEV)[:CAP])(list_keys)
    shuffles = shuffles.reshape(N_LON, N_LON, CAP)
    slot_index = jnp.arange(CAP)
    return jnp.where(slot_index[None, None, :] < counts[:, :, None], shuffles, -1).astype(jnp.int32)


def draw_edge_src(key, part):
    counts, polar_receiver = counts_table(key)
    key = jax.random.fold_in(key, 12)
    first_key, second_key, third_key = jax.random.split(key, 3)
    position = jnp.arange(EDGES)
    device_of = position // E_DEV
    offset = jax.random.randint(first_key, (EDGES,), -3, 4)
    any_peer = jax.random.randint(third_key, (EDGES,), 0, N_LON)
    source_peer = jnp.where(device_of == polar_receiver, any_peer, (device_of + offset) % N_LON)
    limits = counts[source_peer, device_of]
    slot_index = jax.random.randint(second_key, (EDGES,), 0, limits)
    source = source_peer * CAP + slot_index
    source = jnp.where((device_of == polar_receiver) & (position % E_DEV == 0), N_LON * CAP - 1, source)
    return source.astype(jnp.int32)


def draw_tile_count(key, part):
    key = jax.random.fold_in(key, 13)
    first_key, second_key = jax.random.split(key)
    tiles_live = jax.random.randint(first_key, (N_LON,), 1, TILES + 1)
    busiest = jax.random.randint(second_key, (), 0, N_LON)
    return jnp.where(jnp.arange(N_LON) == busiest, TILES, tiles_live).astype(jnp.int32)


def place_ends(result, key, low, top_value):
    longest = result.shape.index(max(result.shape))
    spots = []
    for shift in (0, 1):
        where = [jax.random.randint(jax.random.fold_in(key, axis), (), 0, length) for axis, length in enumerate(result.shape)]
        where[longest] = (where[longest] + shift) % result.shape[longest]
        spots.append(tuple(where))
    return result.at[spots[0]].set(low).at[spots[1]].set(top_value)


def steps_of(rng, dims, shards, low, top_value):
    gain = 1.0
    for dim, shards_of in shards:
        steps = jax.random.uniform(jax.random.fold_in(jax.random.fold_in(rng, 6), dim), (shards_of,), jnp.float32, low / len(shards), top_value / len(shards))
        gain = gain * jnp.repeat(jnp.exp(steps), dims[dim] // shards_of).reshape((-1,) + (1,) * (len(dims) - 1 - dim))
    return gain


def gaussian(stream_key, dims, scale, most, cuts=(), kind=jnp.bfloat16):
    array = scale * jax.random.normal(stream_key, dims, jnp.float32)
    if cuts:
        array = array * steps_of(stream_key, dims, cuts, -0.22, 0.18)
    return jnp.clip(array, -most, most).astype(kind)


def setup_inputs(seed: int = 0, part: int = 0) -> dict:
    keys = jax.random.split(jax.random.key(seed), 13)
    own_keys = jax.random.split(jax.random.fold_in(keys[12], part), 13)
    grid_latent = gaussian(own_keys[0], (GRID, D), 1.0, 6.0, ((0, 16),))
    mesh_latent = gaussian(own_keys[1], (MESH, D), 1.0, 6.0, ((0, 16),))
    edge_latent = gaussian(own_keys[2], (EDGES, D), 1.0, 6.0, ((0, 16),))
    mesh_cotangent = gaussian(own_keys[3], (MESH, D), 1.0, 6.0, ((0, 16),))
    edge_src = draw_edge_src(jax.random.fold_in(jax.random.fold_in(keys[12], part), 71), part)
    edge_dst = place_ends(jax.random.randint(own_keys[5], (EDGES,), 0, M_DEV), jax.random.fold_in(own_keys[5], 1), 0, M_DEV - 1).astype(jnp.int32)
    tile_count = draw_tile_count(jax.random.fold_in(jax.random.fold_in(keys[12], part), 71), part)
    send_rows = draw_send_rows(jax.random.fold_in(jax.random.fold_in(keys[12], part), 71), part)
    w_edge_in = gaussian(keys[8], (3 * D, D), (3 * D) ** -0.5, 0.15625)
    w_edge_out = gaussian(keys[9], (D, D), D ** -0.5, 0.25)
    w_node_in = gaussian(keys[10], (2 * D, D), (2 * D) ** -0.5, 0.1875)
    w_node_out = gaussian(keys[11], (D, D), D ** -0.5, 0.25)
    return {"grid_latent": grid_latent, "mesh_latent": mesh_latent, "edge_latent": edge_latent, "mesh_cotangent": mesh_cotangent, "edge_src": edge_src, "edge_dst": edge_dst, "tile_count": tile_count, "send_rows": send_rows, "w_edge_in": w_edge_in, "w_edge_out": w_edge_out, "w_node_in": w_node_in, "w_node_out": w_node_out}


def layer_norm(values):
    centered = values - lax.optimization_barrier(jnp.mean(values, axis=1, keepdims=True))
    inverse = lax.rsqrt(lax.optimization_barrier(jnp.mean(centered * centered, axis=1, keepdims=True)) + 1e-05)
    return (centered * inverse, inverse)

def norm_back(normed, inverse, upstream):
    first = lax.optimization_barrier(jnp.mean(upstream, axis=1, keepdims=True))
    second = lax.optimization_barrier(jnp.mean(upstream * normed, axis=1, keepdims=True))
    return inverse * (upstream - first - normed * second)

def silu_slope(values):
    sigma = jax.nn.sigmoid(values)
    return sigma * (1.0 + values * (1.0 - sigma))

def contract_rows(left, right):
    return lax.dot_general(left, right, (((0,), (0,)), ((), ())), preferred_element_type=jnp.float32)

def contract_cols(left, right):
    return lax.dot_general(left, right, (((1,), (1,)), ((), ())), preferred_element_type=jnp.float32)

def block_grads(received, edge_latent, edge_src, edge_dst, edge_live, mesh_latent, mesh_cotangent, w_edge_in, w_edge_out, w_node_in, w_node_out):
    latent_width = edge_latent.shape[1]
    mesh_count = mesh_latent.shape[0]
    slot_count = received.shape[0]
    sender_rows = jnp.take(received, edge_src, axis=0)
    onehot = (edge_dst[:, None] == jnp.arange(mesh_count, dtype=jnp.int32)[None, :]).astype(jnp.bfloat16)
    receiver_rows = jnp.dot(onehot, mesh_latent, preferred_element_type=jnp.float32).astype(jnp.bfloat16)
    joined = jnp.concatenate([edge_latent, sender_rows, receiver_rows], axis=1)
    edge_pre = jnp.dot(joined, w_edge_in, preferred_element_type=jnp.float32)
    edge_hidden = jax.nn.silu(edge_pre).astype(jnp.bfloat16)
    edge_proj = jnp.dot(edge_hidden, w_edge_out, preferred_element_type=jnp.float32)
    edge_norm, edge_inverse = layer_norm(edge_proj)
    edge_new = ((edge_latent.astype(jnp.float32) + edge_norm) * edge_live[:, None]).astype(jnp.bfloat16)
    aggregate = contract_rows(onehot, edge_new).astype(jnp.bfloat16)
    node_in = jnp.concatenate([mesh_latent, aggregate], axis=1)
    node_pre = jnp.dot(node_in, w_node_in, preferred_element_type=jnp.float32)
    node_hidden = jax.nn.silu(node_pre).astype(jnp.bfloat16)
    node_proj = jnp.dot(node_hidden, w_node_out, preferred_element_type=jnp.float32)
    node_norm, node_inverse = layer_norm(node_proj)
    upstream = mesh_cotangent.astype(jnp.float32)
    d_node_proj = norm_back(node_norm, node_inverse, upstream).astype(jnp.bfloat16)
    grad_node_out = contract_rows(node_hidden, d_node_proj)
    d_node_pre = (contract_cols(d_node_proj, w_node_out) * silu_slope(node_pre)).astype(jnp.bfloat16)
    grad_node_in = contract_rows(node_in, d_node_pre)
    d_node_in = contract_cols(d_node_pre, w_node_in)
    d_aggregate = d_node_in[:, latent_width:].astype(jnp.bfloat16)
    d_edge_new = jnp.dot(onehot, d_aggregate, preferred_element_type=jnp.float32) * edge_live[:, None]
    d_edge_proj = norm_back(edge_norm, edge_inverse, d_edge_new).astype(jnp.bfloat16)
    grad_edge_out = contract_rows(edge_hidden, d_edge_proj)
    d_edge_pre = (contract_cols(d_edge_proj, w_edge_out) * silu_slope(edge_pre)).astype(jnp.bfloat16)
    grad_edge_in = contract_rows(joined, d_edge_pre)
    d_joined = contract_cols(d_edge_pre, w_edge_in)
    edge_grad = (d_edge_new + d_joined[:, :latent_width]).astype(jnp.bfloat16)
    d_sender = d_joined[:, latent_width:2 * latent_width].astype(jnp.bfloat16)
    d_receiver = d_joined[:, 2 * latent_width:].astype(jnp.bfloat16)
    mesh_grad = (upstream + d_node_in[:, :latent_width] + contract_rows(onehot, d_receiver)).astype(jnp.bfloat16)
    d_slots = jax.ops.segment_sum(d_sender.astype(jnp.float32), edge_src, num_segments=slot_count).astype(jnp.bfloat16)
    return (d_slots, edge_grad, mesh_grad, grad_edge_in, grad_edge_out, grad_node_in, grad_node_out)

def reference(grid_latent, mesh_latent, edge_latent, mesh_cotangent, edge_src, edge_dst, tile_count, send_rows, w_edge_in, w_edge_out, w_node_in, w_node_out):
    owner = (jnp.arange(N_LON, dtype=jnp.int32) * G_DEV)[:, None, None]
    global_rows = jnp.where(send_rows >= 0, send_rows + owner, GRID).astype(jnp.int32)
    incoming = jnp.transpose(global_rows, (1, 0, 2)).reshape(N_LON, N_LON * CAP)
    padded_grid = jnp.concatenate([grid_latent, jnp.zeros((1, D), jnp.bfloat16)], axis=0)

    def per_device(pieces):
        rows, edges, sources, targets, count, mesh_rows, cotangent = pieces
        received = jnp.take(padded_grid, rows, axis=0)
        edge_live = (jnp.arange(E_DEV, dtype=jnp.int32) < count * TILE).astype(jnp.float32)
        return block_grads(received, edges, sources, targets, edge_live, mesh_rows, cotangent, w_edge_in, w_edge_out, w_node_in, w_node_out)
    results = lax.map(per_device, (incoming, edge_latent.reshape(N_LON, E_DEV, D), edge_src.reshape(N_LON, E_DEV), edge_dst.reshape(N_LON, E_DEV), tile_count, mesh_latent.reshape(N_LON, M_DEV, D), mesh_cotangent.reshape(N_LON, M_DEV, D)))
    d_slots, edge_grad, mesh_grad, grad_edge_in, grad_edge_out, grad_node_in, grad_node_out = results
    grid_grad = jax.ops.segment_sum(d_slots.reshape(-1, D).astype(jnp.float32), incoming.reshape(-1), num_segments=GRID + 1)[:GRID].astype(jnp.bfloat16)
    return (grid_grad, edge_grad.reshape(EDGES, D), mesh_grad.reshape(MESH, D), lax.optimization_barrier(jnp.sum(grad_edge_in, axis=0)), lax.optimization_barrier(jnp.sum(grad_edge_out, axis=0)), lax.optimization_barrier(jnp.sum(grad_node_in, axis=0)), lax.optimization_barrier(jnp.sum(grad_node_out, axis=0)))
```

```python
import functools

import jax
import jax.numpy as jnp
from jax import lax
from jax.experimental import pallas as pl
from jax.experimental.pallas import tpu as pltpu
from jax.sharding import PartitionSpec as P

TILE = 256
NEAR = 3
SHIFTS = (0, 1, 2, 3, -1, -2, -3)
BF16 = jnp.bfloat16
F32 = jnp.float32
VMEM_BYTES = 56 * 1024 * 1024


def dot(left, right):
    return lax.dot_general(left, right, (((1,), (0,)), ((), ())), preferred_element_type=F32)


def contract_rows(left, right):
    return lax.dot_general(left, right, (((0,), (0,)), ((), ())), preferred_element_type=F32)


def contract_cols(left, right):
    return lax.dot_general(left, right, (((1,), (1,)), ((), ())), preferred_element_type=F32)


def layer_norm(values):
    centered = values - jnp.mean(values, axis=1, keepdims=True)
    inverse = lax.rsqrt(jnp.mean(centered * centered, axis=1, keepdims=True) + 1e-05)
    return (centered * inverse, inverse)


def norm_back(normed, inverse, upstream):
    first = jnp.mean(upstream, axis=1, keepdims=True)
    second = jnp.mean(upstream * normed, axis=1, keepdims=True)
    return inverse * (upstream - first - normed * second)


def silu_and_slope(values):
    sigma = 0.5 + 0.5 * jnp.tanh(0.5 * values)
    hidden = values * sigma
    return (hidden, sigma + hidden * (1.0 - sigma))


def as_column(row):
    count = row.shape[1]
    down = lax.broadcasted_iota(jnp.int32, (count, count), 0)
    along = lax.broadcasted_iota(jnp.int32, (count, count), 1)
    picked = jnp.where(down == along, row.astype(F32), 0.0)
    return jnp.sum(picked, axis=1, keepdims=True).astype(jnp.int32)


def hot_rows(row, width):
    column = as_column(row)
    along = lax.broadcasted_iota(jnp.int32, (row.shape[1], width), 1)
    return (column == along).astype(F32).astype(BF16)


def hot_columns(row, height):
    down = lax.broadcasted_iota(jnp.int32, (height, row.shape[1]), 0)
    return (row == down).astype(F32).astype(BF16)


def list_hots(me, rows_ref, grid_count):
    peers, cap = rows_ref.shape
    pieces = []
    for shift in SHIFTS:
        target = lax.rem(me + shift + peers, peers)
        pieces.append(hot_rows(rows_ref[pl.ds(target, 1), :], grid_count))
    peer = lax.broadcasted_iota(jnp.int32, (peers, cap), 0)
    ahead = lax.rem(peer - me + peers, peers)
    apart = jnp.minimum(ahead, peers - ahead)
    far = jnp.max(jnp.where(apart > NEAR, rows_ref[...].astype(F32), -1.0), axis=0, keepdims=True)
    pieces.append(hot_rows(far.astype(jnp.int32), grid_count))
    return jnp.concatenate(pieces, axis=0)


def gather_kernel(me_ref, rows_ref, grid_ref, *out_refs):
    cap = rows_ref.shape[1]
    hots = list_hots(me_ref[0], rows_ref, grid_ref.shape[0])
    picked = dot(hots, grid_ref[...]).astype(BF16)
    for place, out_ref in enumerate(out_refs):
        out_ref[...] = picked[place * cap : (place + 1) * cap]


def scatter_kernel(me_ref, rows_ref, *refs):
    list_refs, out_ref = refs[:-1], refs[-1]
    hots = list_hots(me_ref[0], rows_ref, out_ref.shape[0])
    values = jnp.concatenate([ref[...].astype(BF16) for ref in list_refs], axis=0)
    out_ref[...] = contract_rows(hots, values).astype(BF16)


def local_kernel(dst_ref, edge_ref, mesh_ref, w_edge_ref, w_receiver_ref, out_ref, mesh_proj):
    @pl.when(pl.program_id(0) == 0)
    def _():
        mesh_proj[...] = dot(mesh_ref[...], w_receiver_ref[...]).astype(BF16)

    onehot = hot_rows(dst_ref[0], mesh_ref.shape[0])
    out_ref[...] = (
        dot(edge_ref[...], w_edge_ref[...]) + dot(onehot, mesh_proj[...])
    ).astype(BF16)


def split_out(me, peers, send_ref, keep_ref, parts):
    upper = peers // 4
    for upper_bits in range(upper):
        for low_bits in range(4):
            owner = me ^ (4 * upper_bits + low_bits)
            target = send_ref if low_bits % 2 else keep_ref
            start = 0
            for ref, share, live in parts:
                offset = pl.multiple_of(owner * share, 16)
                piece = ref[pl.ds(offset, share), :]
                if live:
                    ahead = lax.rem(owner - me + peers, peers)
                    apart = jnp.minimum(ahead, peers - ahead)
                    piece = jnp.where(apart > NEAR, piece.astype(F32), 0.0)
                target[low_bits // 2, upper_bits, start : start + share, :] = piece.astype(BF16)
                start += share


def forward_kernel(
    peers, me_ref, count_ref, src_ref, dst_ref, local_ref, edge_ref, *refs
):
    lists = refs[:10]
    (w_sender_ref, w_out_ref, w_node_in_ref, w_node_out_ref, mesh_ref, cotangent_ref) = refs[10:16]
    (received_ref, hidden_ref, slope_ref, norm_ref, inverse_ref) = refs[16:21]
    (send_ref, keep_ref, d_aggregate_ref, d_mesh_ref) = refs[21:25]
    (slot_proj, aggregate, grad_in, grad_out) = refs[25:]
    step = pl.program_id(0)
    me = me_ref[0]
    cap = lists[0].shape[0]
    width = edge_ref.shape[1]
    upper = peers // 4

    @pl.when(step == 0)
    def _():
        aggregate[...] = jnp.zeros_like(aggregate)
        w_sender = w_sender_ref[...]

        def place(owner, rows, projected):
            offset = pl.multiple_of(owner * cap, 16)
            received_ref[pl.ds(offset, cap), :] = rows
            slot_proj[pl.ds(offset, cap), :] = projected

        far = (lists[7], lists[8], lists[9])
        for ref, low_bits in zip(far, ((0,), (2,), (1, 3))):
            rows = ref[...]
            projected = dot(rows, w_sender).astype(BF16)
            at = 0
            for low in low_bits:
                for upper_bits in range(upper):
                    owner = me ^ (4 * upper_bits + low)
                    place(owner, rows[at : at + cap], projected[at : at + cap])
                    at += cap
        rows = jnp.concatenate([ref[...] for ref in lists[:7]], axis=0)
        projected = dot(rows, w_sender).astype(BF16)
        for spot, shift in enumerate(SHIFTS):
            owner = lax.rem(me - shift + peers, peers)
            place(owner, rows[spot * cap : (spot + 1) * cap], projected[spot * cap : (spot + 1) * cap])

    @pl.when(step < count_ref[0])
    def _():
        onehot = hot_rows(src_ref[0], slot_proj.shape[0])
        pre = local_ref[...].astype(F32) + dot(onehot, slot_proj[...])
        hidden, slope = silu_and_slope(pre)
        hidden = hidden.astype(BF16)
        hidden_ref[...] = hidden
        slope_ref[...] = slope.astype(BF16)
        normed, inverse = layer_norm(dot(hidden, w_out_ref[...]))
        norm_ref[...] = normed.astype(BF16)
        inverse_ref[...] = inverse
        edge_new = (edge_ref[...].astype(F32) + normed).astype(BF16)
        aggregate[...] += dot(hot_columns(dst_ref[0], aggregate.shape[0]), edge_new)

    @pl.when(step == pl.num_programs(0) - 1)
    def _():
        mesh = mesh_ref[...]
        summed = aggregate[...].astype(BF16)
        node_pre = dot(mesh, w_node_in_ref[:width, :]) + dot(summed, w_node_in_ref[width:, :])
        hidden, slope = silu_and_slope(node_pre)
        hidden = hidden.astype(BF16)
        normed, inverse = layer_norm(dot(hidden, w_node_out_ref[...]))
        upstream = cotangent_ref[...].astype(F32)
        d_proj = norm_back(normed, inverse, upstream).astype(BF16)
        d_pre = (contract_cols(d_proj, w_node_out_ref[...]) * slope).astype(BF16)
        d_mesh_ref[...] = upstream + contract_cols(d_pre, w_node_in_ref[:width, :])
        d_aggregate_ref[...] = contract_cols(d_pre, w_node_in_ref[width:, :]).astype(BF16)
        grad_out[...] = contract_rows(hidden, d_proj)
        grad_in[:width, :] = contract_rows(mesh, d_pre)
        grad_in[width:, :] = contract_rows(summed, d_pre)
        split_out(
            me,
            peers,
            send_ref,
            keep_ref,
            ((grad_in, grad_in.shape[0] // peers, False), (grad_out, grad_out.shape[0] // peers, False)),
        )


def slots_kernel(peers, me_ref, count_ref, src_ref, dst_ref, *refs):
    (hidden_ref, slope_ref, norm_ref, inverse_ref, d_aggregate_ref) = refs[:5]
    (received_ref, w_sender_ref, w_out_ref) = refs[5:8]
    (d_pre_ref, grad_sender_ref, send_ref, keep_ref) = refs[8:12]
    near_refs = refs[12:19]
    (slot_sum, grad_out, d_slots) = refs[19:]
    step = pl.program_id(0)
    me = me_ref[0]

    @pl.when(step == 0)
    def _():
        slot_sum[...] = jnp.zeros_like(slot_sum)
        grad_out[...] = jnp.zeros_like(grad_out)

    @pl.when(step < count_ref[0])
    def _():
        onehot = hot_rows(dst_ref[0], d_aggregate_ref.shape[0])
        upstream = dot(onehot, d_aggregate_ref[...])
        d_proj = norm_back(norm_ref[...].astype(F32), inverse_ref[...], upstream).astype(BF16)
        grad_out[...] += contract_rows(hidden_ref[...], d_proj)
        d_pre = (contract_cols(d_proj, w_out_ref[...]) * slope_ref[...].astype(F32)).astype(BF16)
        d_pre_ref[...] = d_pre
        slot_sum[...] += dot(hot_columns(src_ref[0], slot_sum.shape[0]), d_pre)

    @pl.when(step == pl.num_programs(0) - 1)
    def _():
        summed = slot_sum[...].astype(BF16)
        grad_sender_ref[...] = contract_rows(received_ref[...], summed)
        d_slots[...] = contract_cols(summed, w_sender_ref[...]).astype(BF16)
        cap = near_refs[0].shape[0]
        for shift, ref in zip(SHIFTS, near_refs):
            owner = lax.rem(me - shift + peers, peers)
            ref[...] = d_slots[pl.ds(pl.multiple_of(owner * cap, 16), cap), :]
        split_out(
            me,
            peers,
            send_ref,
            keep_ref,
            ((grad_out, grad_out.shape[0] // peers, False), (d_slots, cap, True)),
        )


def edges_kernel(peers, me_ref, count_ref, dst_ref, *refs):
    (edge_ref, d_pre_ref, d_aggregate_ref, d_mesh_ref, mesh_ref, grad_sender_ref) = refs[:6]
    (w_edge_ref, w_receiver_ref) = refs[6:8]
    (edge_grad_ref, mesh_grad_ref, send_ref, keep_ref) = refs[8:12]
    (grad_in, mesh_sum) = refs[12:]
    step = pl.program_id(0)
    width = edge_ref.shape[1]

    @pl.when(step == 0)
    def _():
        grad_in[:width, :] = jnp.zeros((width, grad_in.shape[1]), F32)
        mesh_sum[...] = jnp.zeros_like(mesh_sum)

    @pl.when(step < count_ref[0])
    def _():
        d_pre = d_pre_ref[...]
        onehot = hot_rows(dst_ref[0], d_aggregate_ref.shape[0])
        upstream = dot(onehot, d_aggregate_ref[...])
        edge_grad_ref[...] = (upstream + contract_cols(d_pre, w_edge_ref[...])).astype(BF16)
        grad_in[:width, :] += contract_rows(edge_ref[...], d_pre)
        mesh_sum[...] += dot(hot_columns(dst_ref[0], mesh_sum.shape[0]), d_pre)

    @pl.when(step >= count_ref[0])
    def _():
        edge_grad_ref[...] = jnp.zeros_like(edge_grad_ref)

    @pl.when(step == pl.num_programs(0) - 1)
    def _():
        summed = mesh_sum[...].astype(BF16)
        mesh_grad_ref[...] = (d_mesh_ref[...] + contract_cols(summed, w_receiver_ref[...])).astype(BF16)
        grad_in[width : 2 * width, :] = grad_sender_ref[...]
        grad_in[2 * width :, :] = contract_rows(mesh_ref[...], summed)
        split_out(me_ref[0], peers, send_ref, keep_ref, ((grad_in, grad_in.shape[0] // peers, False),))


def by_xor(peers, bits):
    return [(peer, peer ^ bits) for peer in range(peers)]


def by_shift(peers, shift):
    return [(peer, (peer + shift) % peers) for peer in range(peers)]


def send(values, perm):
    return lax.ppermute(values, "lon", perm)


def add(left, right):
    return (left.astype(F32) + right.astype(F32)).astype(BF16)


def reduce_scatter(peers, outgoing, kept):
    arrived = send(outgoing, by_xor(peers, 1))
    next_out = add(kept[1], arrived[1])
    next_kept = add(kept[0], arrived[0])
    arrived = send(next_out, by_xor(peers, 2))
    pieces = [add(next_kept[place], arrived[place]) for place in range(peers // 4)]
    total = pieces[0].astype(F32)
    for place in range(1, peers // 4):
        total = total + send(pieces[place], by_xor(peers, 4 * place)).astype(F32)
    return total


def whole(shape):
    return pl.BlockSpec(shape, lambda *_: (0,) * len(shape))


def on_device(
    grid_latent,
    mesh_latent,
    edge_latent,
    mesh_cotangent,
    edge_src,
    edge_dst,
    tile_count,
    send_rows,
    w_edge_in,
    w_edge_out,
    w_node_in,
    w_node_out,
):
    peers = lax.axis_size("lon")
    me = lax.axis_index("lon").astype(jnp.int32).reshape(1)
    upper = peers // 4
    rows = send_rows[0]
    cap = rows.shape[1]
    slots = peers * cap
    edges, width = edge_latent.shape
    mesh_count = mesh_latent.shape[0]
    grid_count = grid_latent.shape[0]
    tiles = edges // TILE
    src = edge_src.reshape(tiles, 1, TILE)
    dst = edge_dst.reshape(tiles, 1, TILE)
    smem = pl.BlockSpec(memory_space=pltpu.SMEM)
    params = pltpu.CompilerParams(vmem_limit_bytes=VMEM_BYTES)
    one_list = jax.ShapeDtypeStruct((cap, width), BF16)
    square = (width, width)

    def tile_of(last):
        return pl.BlockSpec((TILE, last), lambda step, *_: (step, 0))

    index_tile = pl.BlockSpec((1, 1, TILE), lambda step, *_: (step, 0, 0))

    def weight(place):
        return pl.BlockSpec(square, lambda *_: (place, 0))

    def halves(share):
        shape = (2, upper, share, width)
        return [jax.ShapeDtypeStruct(shape, BF16)] * 2, [whole(shape)] * 2

    lists = pl.pallas_call(
        gather_kernel,
        in_specs=[smem, whole(rows.shape), whole(grid_latent.shape)],
        out_specs=[whole((cap, width))] * 8,
        out_shape=[one_list] * 8,
        compiler_params=params,
        name="gather_lists",
    )(me, rows, grid_latent)

    near = [lists[0]] + [
        send(lists[place], by_shift(peers, SHIFTS[place])) for place in range(1, 7)
    ]
    far_own = jnp.concatenate(
        [lists[7]] + [send(lists[7], by_xor(peers, 4 * bits)) for bits in range(1, upper)], axis=0
    )
    far_next = send(far_own, by_xor(peers, 2))
    far_core = send(jnp.concatenate([far_own, far_next], axis=0), by_xor(peers, 1))

    local = pl.pallas_call(
        local_kernel,
        grid=(tiles,),
        in_specs=[index_tile, tile_of(width), whole(mesh_latent.shape), weight(0), weight(2)],
        out_specs=tile_of(width),
        out_shape=jax.ShapeDtypeStruct((edges, width), BF16),
        scratch_shapes=[pltpu.VMEM((mesh_count, width), BF16)],
        compiler_params=params,
        cost_estimate=pl.CostEstimate(
            flops=2 * edges * width * (width + mesh_count), bytes_accessed=4 * edges * width, transcendentals=0
        ),
        name="edge_local",
    )(dst, edge_latent, mesh_latent, w_edge_in, w_edge_in)

    node_shape, node_spec = halves(w_node_in.shape[0] // peers + w_node_out.shape[0] // peers)
    (received, hidden, slope, norm, inverse, node_send, node_keep, d_aggregate, d_mesh) = pl.pallas_call(
        functools.partial(forward_kernel, peers),
        grid=(tiles,),
        in_specs=[smem, smem, index_tile, index_tile, tile_of(width), tile_of(width)]
        + [whole((cap, width))] * 7
        + [whole((upper * cap, width))] * 2
        + [whole((2 * upper * cap, width))]
        + [weight(1)]
        + [whole(w.shape) for w in (w_edge_out, w_node_in, w_node_out, mesh_latent, mesh_cotangent)],
        out_specs=[whole((slots, width))]
        + [tile_of(width)] * 3
        + [tile_of(1)]
        + node_spec
        + [whole((mesh_count, width))] * 2,
        out_shape=[jax.ShapeDtypeStruct((slots, width), BF16)]
        + [jax.ShapeDtypeStruct((edges, width), BF16)] * 3
        + [jax.ShapeDtypeStruct((edges, 1), F32)]
        + node_shape
        + [jax.ShapeDtypeStruct((mesh_count, width), BF16), jax.ShapeDtypeStruct((mesh_count, width), F32)],
        scratch_shapes=[
            pltpu.VMEM((slots, width), BF16),
            pltpu.VMEM((mesh_count, width), F32),
            pltpu.VMEM(w_node_in.shape, F32),
            pltpu.VMEM(w_node_out.shape, F32),
        ],
        compiler_params=params,
        name="forward",
    )(
        me,
        tile_count,
        src,
        dst,
        local,
        edge_latent,
        *near,
        far_own,
        far_next,
        far_core,
        w_edge_in,
        w_edge_out,
        w_node_in,
        w_node_out,
        mesh_latent,
        mesh_cotangent,
    )

    slot_shape, slot_spec = halves(w_edge_out.shape[0] // peers + cap)
    results = pl.pallas_call(
        functools.partial(slots_kernel, peers),
        grid=(tiles,),
        in_specs=[smem, smem, index_tile, index_tile]
        + [tile_of(width)] * 3
        + [tile_of(1), whole((mesh_count, width)), whole((slots, width)), weight(1), whole(square)],
        out_specs=[tile_of(width), whole(square)] + slot_spec + [whole((cap, width))] * 7,
        out_shape=[jax.ShapeDtypeStruct((edges, width), BF16), jax.ShapeDtypeStruct(square, F32)]
        + slot_shape
        + [one_list] * 7,
        scratch_shapes=[
            pltpu.VMEM((slots, width), F32),
            pltpu.VMEM(square, F32),
            pltpu.VMEM((slots, width), BF16),
        ],
        compiler_params=params,
        cost_estimate=pl.CostEstimate(
            flops=2 * edges * width * (mesh_count + 2 * width + slots),
            bytes_accessed=8 * edges * width,
            transcendentals=0,
        ),
        name="backward_slots",
    )(me, tile_count, src, dst, hidden, slope, norm, inverse, d_aggregate, received, w_edge_in, w_edge_out)
    (d_pre, grad_sender, slot_send, slot_keep), returns = results[:4], results[4:]
    returned = [returns[0]] + [
        send(returns[place], by_shift(peers, -SHIFTS[place])) for place in range(1, 7)
    ]

    edge_shape, edge_spec = halves(w_edge_in.shape[0] // peers)
    edge_grad, mesh_grad, edge_send, edge_keep = pl.pallas_call(
        functools.partial(edges_kernel, peers),
        grid=(tiles,),
        in_specs=[smem, smem, index_tile, tile_of(width), tile_of(width)]
        + [whole((mesh_count, width))] * 3
        + [whole(square), weight(0), weight(2)],
        out_specs=[tile_of(width), whole((mesh_count, width))] + edge_spec,
        out_shape=[
            jax.ShapeDtypeStruct((edges, width), BF16),
            jax.ShapeDtypeStruct((mesh_count, width), BF16),
        ]
        + edge_shape,
        scratch_shapes=[pltpu.VMEM(w_edge_in.shape, F32), pltpu.VMEM((mesh_count, width), F32)],
        compiler_params=params,
        cost_estimate=pl.CostEstimate(
            flops=2 * edges * width * (2 * mesh_count + 2 * width),
            bytes_accessed=6 * edges * width,
            transcendentals=0,
        ),
        name="backward_edges",
    )(
        me,
        tile_count,
        dst,
        edge_latent,
        d_pre,
        d_aggregate,
        d_mesh,
        mesh_latent,
        grad_sender,
        w_edge_in,
        w_edge_in,
    )

    node_total = reduce_scatter(peers, node_send, node_keep)
    slot_total = reduce_scatter(peers, slot_send, slot_keep)
    edge_total = reduce_scatter(peers, edge_send, edge_keep)
    node_rows = w_node_in.shape[0] // peers
    out_rows = w_edge_out.shape[0] // peers
    grid_grad = pl.pallas_call(
        scatter_kernel,
        in_specs=[smem, whole(rows.shape)] + [whole((cap, width))] * 8,
        out_specs=whole(grid_latent.shape),
        out_shape=jax.ShapeDtypeStruct((grid_count, width), BF16),
        compiler_params=params,
        name="scatter_lists",
    )(me, rows, *returned, slot_total[out_rows:])
    return (
        grid_grad,
        edge_grad,
        mesh_grad,
        edge_total,
        slot_total[:out_rows],
        node_total[:node_rows],
        node_total[node_rows:],
    )


def solution(mesh):
    rows = P(("grp", "lon"), None)
    flat = P(("grp", "lon"))
    return jax.shard_map(
        on_device,
        mesh=mesh,
        in_specs=(rows, rows, rows, rows, flat, flat, flat, P(("grp", "lon"), None, None)) + (P(),) * 4,
        out_specs=(rows,) * 7,
        check_vma=False,
    )
```

```python
import functools

import jax
import jax.numpy as jnp
from jax import lax
from jax.experimental import pallas as pl
from jax.experimental.pallas import tpu as pltpu
from jax.sharding import PartitionSpec as P

TILE = 256
STEP = 1024
SUB = 512
LANES = 128
NEAR = 3
SHIFTS = (0, 1, 2, 3, -1, -2, -3)
BF16 = jnp.bfloat16
F32 = jnp.float32
VMEM_BYTES = 56 * 1024 * 1024


def dot(left, right):
    return lax.dot_general(left, right, (((1,), (0,)), ((), ())), preferred_element_type=F32)


def contract_rows(left, right):
    return lax.dot_general(left, right, (((0,), (0,)), ((), ())), preferred_element_type=F32)


def contract_cols(left, right):
    return lax.dot_general(left, right, (((1,), (1,)), ((), ())), preferred_element_type=F32)


def layer_norm(values):
    centered = values - jnp.mean(values, axis=1, keepdims=True)
    inverse = lax.rsqrt(jnp.mean(centered * centered, axis=1, keepdims=True) + 1e-05)
    return (centered * inverse, inverse)


def norm_back(normed, inverse, upstream):
    first = jnp.mean(upstream, axis=1, keepdims=True)
    second = jnp.mean(upstream * normed, axis=1, keepdims=True)
    return inverse * (upstream - first - normed * second)


def silu_and_slope(values):
    sigma = 0.5 + 0.5 * jnp.tanh(0.5 * values)
    hidden = values * sigma
    return (hidden, sigma + hidden * (1.0 - sigma))


def as_column(row):
    count = row.shape[1]
    block = min(count, LANES)
    down = lax.broadcasted_iota(jnp.int32, (block, block), 0)
    along = lax.broadcasted_iota(jnp.int32, (block, block), 1)
    columns = []
    for start in range(0, count, block):
        piece = row[:, start : start + block].astype(F32)
        picked = jnp.where(down == along, piece, 0.0)
        columns.append(jnp.sum(picked, axis=1, keepdims=True))
    return jnp.concatenate(columns, axis=0).astype(jnp.int32)


def hot_rows(row, width, first=0):
    column = as_column(row) - first
    along = lax.broadcasted_iota(jnp.int32, (row.shape[1], width), 1)
    return (column == along).astype(F32).astype(BF16)


def hot_columns(row, height):
    down = lax.broadcasted_iota(jnp.int32, (height, row.shape[1]), 0)
    return (row == down).astype(F32).astype(BF16)


def live_only(row, first, count):
    place = first + lax.broadcasted_iota(jnp.int32, row.shape, 1)
    return jnp.where(place < count, row, -1)


def list_hots(me, rows_ref, grid_count, first):
    peers, cap = rows_ref.shape
    pieces = []
    for shift in SHIFTS:
        target = lax.rem(me + shift + peers, peers)
        pieces.append(hot_rows(rows_ref[pl.ds(target, 1), :], grid_count, first))
    peer = lax.broadcasted_iota(jnp.int32, (peers, cap), 0)
    ahead = lax.rem(peer - me + peers, peers)
    apart = jnp.minimum(ahead, peers - ahead)
    far = jnp.max(jnp.where(apart > NEAR, rows_ref[...].astype(F32), -1.0), axis=0, keepdims=True)
    pieces.append(hot_rows(far.astype(jnp.int32), grid_count, first))
    return jnp.concatenate(pieces, axis=0)


def gather_kernel(me_ref, rows_ref, grid_ref, *refs):
    out_refs, total = refs[:-1], refs[-1]
    cap = rows_ref.shape[1]
    step = pl.program_id(0)
    part = grid_ref.shape[0]

    @pl.when(step == 0)
    def _():
        total[...] = jnp.zeros_like(total)

    total[...] += dot(list_hots(me_ref[0], rows_ref, part, step * part), grid_ref[...])

    @pl.when(step == pl.num_programs(0) - 1)
    def _():
        for place, out_ref in enumerate(out_refs):
            out_ref[...] = total[place * cap : (place + 1) * cap, :].astype(BF16)


def scatter_kernel(skip, me_ref, rows_ref, *refs):
    list_refs, far_refs, out_ref = refs[:7], refs[7:-1], refs[-1]
    part = out_ref.shape[0]
    cap = rows_ref.shape[1]
    hots = list_hots(me_ref[0], rows_ref, part, pl.program_id(0) * part)
    far = far_refs[0][skip:, :].astype(F32)
    for ref in far_refs[1:]:
        far = far + ref[skip:, :].astype(F32)
    values = jnp.concatenate([ref[...] for ref in list_refs] + [far.astype(BF16)], axis=0)
    out_ref[...] = contract_rows(hots, values).astype(BF16)


def halves_of(ref):
    rows = ref.shape[-1] if len(ref.shape) == 3 else ref.shape[0]
    return [(start, slice(start, start + SUB)) for start in range(0, rows, SUB)]


def local_kernel(dst_ref, edge_ref, mesh_ref, w_edge_ref, w_receiver_ref, *refs):
    out_ref, mesh_proj = refs[-2:]

    @pl.when(pl.program_id(0) == 0)
    def _():
        mesh_proj[...] = dot(mesh_ref[...], w_receiver_ref[...]).astype(BF16)

    for start, part in halves_of(edge_ref):
        onehot = hot_rows(dst_ref[0, :, part], mesh_ref.shape[0])
        out_ref[part, :] = (
            dot(edge_ref[part, :], w_edge_ref[...]) + dot(onehot, mesh_proj[...])
        ).astype(BF16)


def split_out(me, peers, send_ref, keep_ref, parts):
    upper = peers // 4
    for upper_bits in range(upper):
        for low_bits in range(4):
            owner = me ^ (4 * upper_bits + low_bits)
            target = send_ref if low_bits % 2 else keep_ref
            start = 0
            for ref, share, live in parts:
                offset = pl.multiple_of(owner * share, 16)
                piece = ref[pl.ds(offset, share), :]
                if live:
                    ahead = lax.rem(owner - me + peers, peers)
                    apart = jnp.minimum(ahead, peers - ahead)
                    piece = jnp.where(apart > NEAR, piece.astype(F32), 0.0)
                target[low_bits // 2, upper_bits, start : start + share, :] = piece.astype(BF16)
                start += share


def forward_kernel(
    peers, me_ref, count_ref, src_ref, dst_ref, local_ref, edge_ref, *refs
):
    lists = refs[:10]
    (w_sender_ref, w_out_ref, w_node_in_ref, w_node_out_ref, mesh_ref, cotangent_ref) = refs[10:16]
    (received_ref, hidden_ref, slope_ref, norm_ref, inverse_ref) = refs[16:21]
    (send_ref, keep_ref, d_aggregate_ref, d_mesh_ref) = refs[21:25]
    (slot_proj, aggregate, grad_in, grad_out) = refs[25:]
    step = pl.program_id(0)
    me = me_ref[0]
    cap = lists[0].shape[0]
    width = edge_ref.shape[1]
    upper = peers // 4

    @pl.when(step == 0)
    def _():
        aggregate[...] = jnp.zeros_like(aggregate)
        w_sender = w_sender_ref[...]

        def place(owner, rows, projected):
            offset = pl.multiple_of(owner * cap, 16)
            received_ref[pl.ds(offset, cap), :] = rows
            slot_proj[pl.ds(offset, cap), :] = projected

        far = (lists[7], lists[8], lists[9])
        for ref, low_bits in zip(far, ((0,), (2,), (1, 3))):
            rows = ref[...]
            projected = dot(rows, w_sender).astype(BF16)
            at = 0
            for low in low_bits:
                for upper_bits in range(upper):
                    owner = me ^ (4 * upper_bits + low)
                    place(owner, rows[at : at + cap], projected[at : at + cap])
                    at += cap
        rows = jnp.concatenate([ref[...] for ref in lists[:7]], axis=0)
        projected = dot(rows, w_sender).astype(BF16)
        for spot, shift in enumerate(SHIFTS):
            owner = lax.rem(me - shift + peers, peers)
            place(owner, rows[spot * cap : (spot + 1) * cap], projected[spot * cap : (spot + 1) * cap])

    @pl.when(step * STEP < count_ref[0] * TILE)
    def _():
        parts = halves_of(edge_ref)
        pres = []
        for start, part in parts:
            onehot = hot_rows(src_ref[0, :, part], slot_proj.shape[0])
            pres.append(local_ref[part, :].astype(F32) + dot(onehot, slot_proj[...]))
        projs = []
        for (start, part), pre in zip(parts, pres):
            hidden, slope = silu_and_slope(pre)
            hidden = hidden.astype(BF16)
            hidden_ref[part, :] = hidden
            slope_ref[part, :] = slope.astype(BF16)
            projs.append(dot(hidden, w_out_ref[...]))
        for (start, part), proj in zip(parts, projs):
            normed, inverse = layer_norm(proj)
            norm_ref[part, :] = normed.astype(BF16)
            inverse_ref[part, :] = inverse
            edge_new = (edge_ref[part, :].astype(F32) + normed).astype(BF16)
            receivers = live_only(dst_ref[0, :, part], step * STEP + start, count_ref[0] * TILE)
            aggregate[...] += dot(hot_columns(receivers, aggregate.shape[0]), edge_new)

    @pl.when(step == pl.num_programs(0) - 1)
    def _():
        mesh = mesh_ref[...]
        summed = aggregate[...].astype(BF16)
        node_pre = dot(mesh, w_node_in_ref[:width, :]) + dot(summed, w_node_in_ref[width:, :])
        hidden, slope = silu_and_slope(node_pre)
        hidden = hidden.astype(BF16)
        normed, inverse = layer_norm(dot(hidden, w_node_out_ref[...]))
        upstream = cotangent_ref[...].astype(F32)
        d_proj = norm_back(normed, inverse, upstream).astype(BF16)
        d_pre = (contract_cols(d_proj, w_node_out_ref[...]) * slope).astype(BF16)
        d_mesh_ref[...] = upstream + contract_cols(d_pre, w_node_in_ref[:width, :])
        d_aggregate_ref[...] = contract_cols(d_pre, w_node_in_ref[width:, :]).astype(BF16)
        grad_out[...] = contract_rows(hidden, d_proj)
        grad_in[:width, :] = contract_rows(mesh, d_pre)
        grad_in[width:, :] = contract_rows(summed, d_pre)
        split_out(
            me,
            peers,
            send_ref,
            keep_ref,
            ((grad_in, grad_in.shape[0] // peers, False), (grad_out, grad_out.shape[0] // peers, False)),
        )


def slots_kernel(peers, me_ref, count_ref, src_ref, dst_ref, *refs):
    (hidden_ref, slope_ref, norm_ref, inverse_ref, d_aggregate_ref) = refs[:5]
    (received_ref, w_sender_ref, w_out_ref) = refs[5:8]
    (d_pre_ref, grad_sender_ref, send_ref, keep_ref) = refs[8:12]
    near_refs = refs[12:19]
    (slot_sum, grad_out, d_slots) = refs[19:]
    step = pl.program_id(0)
    me = me_ref[0]

    @pl.when(step == 0)
    def _():
        slot_sum[...] = jnp.zeros_like(slot_sum)
        grad_out[...] = jnp.zeros_like(grad_out)

    @pl.when(step * STEP < count_ref[0] * TILE)
    def _():
        parts = halves_of(hidden_ref)
        upstreams = []
        for start, part in parts:
            receivers = live_only(dst_ref[0, :, part], step * STEP + start, count_ref[0] * TILE)
            onehot = hot_rows(receivers, d_aggregate_ref.shape[0])
            upstreams.append(dot(onehot, d_aggregate_ref[...]))
        d_projs = []
        d_hiddens = []
        for (start, part), upstream in zip(parts, upstreams):
            d_proj = norm_back(norm_ref[part, :].astype(F32), inverse_ref[part, :], upstream).astype(BF16)
            d_projs.append(d_proj)
            d_hiddens.append(contract_cols(d_proj, w_out_ref[...]))
        for (start, part), d_proj, d_hidden in zip(parts, d_projs, d_hiddens):
            grad_out[...] += contract_rows(hidden_ref[part, :], d_proj)
            d_pre = (d_hidden * slope_ref[part, :].astype(F32)).astype(BF16)
            d_pre_ref[part, :] = d_pre
            slot_sum[...] += dot(hot_columns(src_ref[0, :, part], slot_sum.shape[0]), d_pre)

    @pl.when(step == pl.num_programs(0) - 1)
    def _():
        summed = slot_sum[...].astype(BF16)
        grad_sender_ref[...] = contract_rows(received_ref[...], summed)
        d_slots[...] = contract_cols(summed, w_sender_ref[...]).astype(BF16)
        cap = near_refs[0].shape[0]
        for shift, ref in zip(SHIFTS, near_refs):
            owner = lax.rem(me - shift + peers, peers)
            ref[...] = d_slots[pl.ds(pl.multiple_of(owner * cap, 16), cap), :]
        split_out(
            me,
            peers,
            send_ref,
            keep_ref,
            ((grad_out, grad_out.shape[0] // peers, False), (d_slots, cap, True)),
        )


def edges_kernel(peers, me_ref, count_ref, dst_ref, *refs):
    (edge_ref, d_pre_ref, d_aggregate_ref, d_mesh_ref, mesh_ref, grad_sender_ref) = refs[:6]
    (w_edge_ref, w_receiver_ref) = refs[6:8]
    (edge_grad_ref, mesh_grad_ref, send_ref, keep_ref) = refs[8:12]
    (grad_in, mesh_sum) = refs[12:]
    step = pl.program_id(0)
    width = edge_ref.shape[1]

    @pl.when(step == 0)
    def _():
        grad_in[:width, :] = jnp.zeros((width, grad_in.shape[1]), F32)
        mesh_sum[...] = jnp.zeros_like(mesh_sum)

    @pl.when(step * STEP < count_ref[0] * TILE)
    def _():
        for start, part in halves_of(edge_ref):
            d_pre = d_pre_ref[part, :]
            receivers = live_only(dst_ref[0, :, part], step * STEP + start, count_ref[0] * TILE)
            onehot = hot_rows(receivers, d_aggregate_ref.shape[0])
            upstream = dot(onehot, d_aggregate_ref[...])
            edge_grad_ref[part, :] = (upstream + contract_cols(d_pre, w_edge_ref[...])).astype(BF16)
            grad_in[:width, :] += contract_rows(edge_ref[part, :], d_pre)
            mesh_sum[...] += dot(hot_columns(receivers, mesh_sum.shape[0]), d_pre)

    @pl.when(step * STEP >= count_ref[0] * TILE)
    def _():
        edge_grad_ref[...] = jnp.zeros_like(edge_grad_ref)

    @pl.when(step == pl.num_programs(0) - 1)
    def _():
        summed = mesh_sum[...].astype(BF16)
        mesh_grad_ref[...] = (d_mesh_ref[...] + contract_cols(summed, w_receiver_ref[...])).astype(BF16)
        grad_in[width : 2 * width, :] = grad_sender_ref[...]
        grad_in[2 * width :, :] = contract_rows(mesh_ref[...], summed)
        split_out(me_ref[0], peers, send_ref, keep_ref, ((grad_in, grad_in.shape[0] // peers, False),))


def by_xor(peers, bits):
    return [(peer, peer ^ bits) for peer in range(peers)]


def by_shift(peers, shift):
    return [(peer, (peer + shift) % peers) for peer in range(peers)]


def send(values, perm):
    return lax.ppermute(values, "lon", perm)


def add(left, right):
    return (left.astype(F32) + right.astype(F32)).astype(BF16)


def core_sum(peers, outgoing, kept):
    arrived = send(outgoing, by_xor(peers, 1))
    return add(kept[1], arrived[1]), add(kept[0], arrived[0])


def next_sum(peers, outgoing, kept):
    arrived = send(outgoing, by_xor(peers, 2))
    return [add(kept[place], arrived[place]) for place in range(peers // 4)]


def last_hop(peers, pieces):
    return [pieces[0]] + [
        send(pieces[place], by_xor(peers, 4 * place)) for place in range(1, peers // 4)
    ]


def total_of(terms, start, stop):
    total = terms[0][start:stop].astype(F32)
    for term in terms[1:]:
        total = total + term[start:stop].astype(F32)
    return total


def whole(shape):
    return pl.BlockSpec(shape, lambda *_: (0,) * len(shape))


def on_device(
    grid_latent,
    mesh_latent,
    edge_latent,
    mesh_cotangent,
    edge_src,
    edge_dst,
    tile_count,
    send_rows,
    w_edge_in,
    w_edge_out,
    w_node_in,
    w_node_out,
):
    peers = lax.axis_size("lon")
    me = lax.axis_index("lon").astype(jnp.int32).reshape(1)
    upper = peers // 4
    rows = send_rows[0]
    cap = rows.shape[1]
    slots = peers * cap
    edges, width = edge_latent.shape
    mesh_count = mesh_latent.shape[0]
    grid_count = grid_latent.shape[0]
    tiles = edges // STEP
    src = edge_src.reshape(tiles, 1, STEP)
    dst = edge_dst.reshape(tiles, 1, STEP)
    smem = pl.BlockSpec(memory_space=pltpu.SMEM)
    params = pltpu.CompilerParams(vmem_limit_bytes=VMEM_BYTES)
    one_list = jax.ShapeDtypeStruct((cap, width), BF16)
    square = (width, width)

    def tile_of(last):
        return pl.BlockSpec((STEP, last), lambda step, *_: (step, 0))

    index_tile = pl.BlockSpec((1, 1, STEP), lambda step, *_: (step, 0, 0))

    def weight(place):
        return pl.BlockSpec(square, lambda *_: (place, 0))

    def halves(share):
        shape = (2, upper, share, width)
        return [jax.ShapeDtypeStruct(shape, BF16)] * 2, [whole(shape)] * 2

    grid_part = grid_count // 4
    lists = pl.pallas_call(
        gather_kernel,
        grid=(4,),
        in_specs=[smem, whole(rows.shape), pl.BlockSpec((grid_part, width), lambda step: (step, 0))],
        out_specs=[whole((cap, width))] * 8,
        out_shape=[one_list] * 8,
        scratch_shapes=[pltpu.VMEM((8 * cap, width), F32)],
        compiler_params=params,
        name="gather_lists",
    )(me, rows, grid_latent)

    def local_part(first, count, *before):
        return pl.pallas_call(
            local_kernel,
            grid=(count,),
            in_specs=[
                pl.BlockSpec((1, 1, STEP), lambda step: (first + step, 0, 0)),
                pl.BlockSpec((STEP, width), lambda step: (first + step, 0)),
                whole(mesh_latent.shape),
                weight(0),
                weight(2),
            ]
            + [pl.BlockSpec(memory_space=pl.ANY)] * len(before),
            out_specs=pl.BlockSpec((STEP, width), lambda step: (first + step, 0)),
            out_shape=jax.ShapeDtypeStruct((edges, width), BF16),
            scratch_shapes=[pltpu.VMEM((mesh_count, width), BF16)],
            input_output_aliases={5: 0} if before else {},
            compiler_params=params,
            cost_estimate=pl.CostEstimate(
                flops=2 * count * STEP * width * (width + mesh_count),
                bytes_accessed=4 * count * STEP * width,
                transcendentals=0,
            ),
            name="edge_local",
        )(receivers, edge_latent, mesh_latent, w_edge_in, w_edge_in, *before)

    hops = [send(lists[7], by_xor(peers, 4 * bits)) for bits in range(1, upper)]
    near = [lists[0]] + [
        send(lists[place], by_shift(peers, SHIFTS[place])) for place in range(1, 7)
    ]
    far_own = jnp.concatenate([lists[7]] + hops, axis=0)
    far_own, receivers = lax.optimization_barrier((far_own, dst))
    far_next = send(far_own, by_xor(peers, 2))
    local = local_part(0, tiles - 1)
    far_next, near, local = lax.optimization_barrier((far_next, near, local))
    far_core = send(jnp.concatenate([far_own, far_next], axis=0), by_xor(peers, 1))
    local = local_part(tiles - 1, 1, local)

    node_shape, node_spec = halves(w_node_in.shape[0] // peers + w_node_out.shape[0] // peers)
    (received, hidden, slope, norm, inverse, node_send, node_keep, d_aggregate, d_mesh) = pl.pallas_call(
        functools.partial(forward_kernel, peers),
        grid=(tiles,),
        in_specs=[smem, smem, index_tile, index_tile, tile_of(width), tile_of(width)]
        + [whole((cap, width))] * 7
        + [whole((upper * cap, width))] * 2
        + [whole((2 * upper * cap, width))]
        + [weight(1)]
        + [whole(w.shape) for w in (w_edge_out, w_node_in, w_node_out, mesh_latent, mesh_cotangent)],
        out_specs=[whole((slots, width))]
        + [tile_of(width)] * 3
        + [tile_of(1)]
        + node_spec
        + [whole((mesh_count, width))] * 2,
        out_shape=[jax.ShapeDtypeStruct((slots, width), BF16)]
        + [jax.ShapeDtypeStruct((edges, width), BF16)] * 3
        + [jax.ShapeDtypeStruct((edges, 1), F32)]
        + node_shape
        + [jax.ShapeDtypeStruct((mesh_count, width), BF16), jax.ShapeDtypeStruct((mesh_count, width), F32)],
        scratch_shapes=[
            pltpu.VMEM((slots, width), BF16),
            pltpu.VMEM((mesh_count, width), F32),
            pltpu.VMEM(w_node_in.shape, F32),
            pltpu.VMEM(w_node_out.shape, F32),
        ],
        compiler_params=params,
        name="forward",
    )(
        me,
        tile_count,
        src,
        dst,
        local,
        edge_latent,
        *near,
        far_own,
        far_next,
        far_core,
        w_edge_in,
        w_edge_out,
        w_node_in,
        w_node_out,
        mesh_latent,
        mesh_cotangent,
    )

    node_next, node_kept = core_sum(peers, node_send, node_keep)
    slot_shape, slot_spec = halves(w_edge_out.shape[0] // peers + cap)
    results = pl.pallas_call(
        functools.partial(slots_kernel, peers),
        grid=(tiles,),
        in_specs=[smem, smem, index_tile, index_tile]
        + [tile_of(width)] * 3
        + [tile_of(1), whole((mesh_count, width)), whole((slots, width)), weight(1), whole(square)],
        out_specs=[tile_of(width), whole(square)] + slot_spec + [whole((cap, width))] * 7,
        out_shape=[jax.ShapeDtypeStruct((edges, width), BF16), jax.ShapeDtypeStruct(square, F32)]
        + slot_shape
        + [one_list] * 7,
        scratch_shapes=[
            pltpu.VMEM((slots, width), F32),
            pltpu.VMEM(square, F32),
            pltpu.VMEM((slots, width), BF16),
        ],
        compiler_params=params,
        cost_estimate=pl.CostEstimate(
            flops=2 * edges * width * (mesh_count + 2 * width + slots),
            bytes_accessed=8 * edges * width,
            transcendentals=0,
        ),
        name="backward_slots",
    )(me, tile_count, src, dst, hidden, slope, norm, inverse, d_aggregate, received, w_edge_in, w_edge_out)
    (d_pre, grad_sender, slot_send, slot_keep), returns = results[:4], results[4:]
    (node_next, node_kept, d_pre, slot_send, slot_keep, returns) = lax.optimization_barrier(
        (node_next, node_kept, d_pre, slot_send, slot_keep, returns)
    )
    node_pieces = next_sum(peers, node_next, node_kept)
    slot_next, slot_kept = core_sum(peers, slot_send, slot_keep)
    returned = [returns[0]] + [
        send(returns[place], by_shift(peers, -SHIFTS[place])) for place in range(1, 7)
    ]

    edge_shape, edge_spec = halves(w_edge_in.shape[0] // peers)
    edge_grad, mesh_grad, edge_send, edge_keep = pl.pallas_call(
        functools.partial(edges_kernel, peers),
        grid=(tiles,),
        in_specs=[smem, smem, index_tile, tile_of(width), tile_of(width)]
        + [whole((mesh_count, width))] * 3
        + [whole(square), weight(0), weight(2)],
        out_specs=[tile_of(width), whole((mesh_count, width))] + edge_spec,
        out_shape=[
            jax.ShapeDtypeStruct((edges, width), BF16),
            jax.ShapeDtypeStruct((mesh_count, width), BF16),
        ]
        + edge_shape,
        scratch_shapes=[pltpu.VMEM(w_edge_in.shape, F32), pltpu.VMEM((mesh_count, width), F32)],
        compiler_params=params,
        cost_estimate=pl.CostEstimate(
            flops=2 * edges * width * (2 * mesh_count + 2 * width),
            bytes_accessed=6 * edges * width,
            transcendentals=0,
        ),
        name="backward_edges",
    )(
        me,
        tile_count,
        dst,
        edge_latent,
        d_pre,
        d_aggregate,
        d_mesh,
        mesh_latent,
        grad_sender,
        w_edge_in,
        w_edge_in,
    )

    (node_pieces, slot_next, slot_kept, edge_send, edge_keep) = lax.optimization_barrier(
        (node_pieces, slot_next, slot_kept, edge_send, edge_keep)
    )
    slot_pieces = next_sum(peers, slot_next, slot_kept)
    node_terms = last_hop(peers, node_pieces)
    edge_next, edge_kept = core_sum(peers, edge_send, edge_keep)
    slot_terms = last_hop(peers, slot_pieces)
    edge_pieces = next_sum(peers, edge_next, edge_kept)
    edge_terms = last_hop(peers, edge_pieces)
    node_rows = w_node_in.shape[0] // peers
    out_rows = w_edge_out.shape[0] // peers
    grid_grad = pl.pallas_call(
        functools.partial(scatter_kernel, out_rows),
        grid=(4,),
        in_specs=[smem, whole(rows.shape)]
        + [whole((cap, width))] * 7
        + [whole((out_rows + cap, width))] * upper,
        out_specs=pl.BlockSpec((grid_part, width), lambda step: (step, 0)),
        out_shape=jax.ShapeDtypeStruct((grid_count, width), BF16),
        compiler_params=params,
        name="scatter_lists",
    )(me, rows, *returned, *slot_terms)
    return (
        grid_grad,
        edge_grad,
        mesh_grad,
        total_of(edge_terms, 0, w_edge_in.shape[0] // peers),
        total_of(slot_terms, 0, out_rows),
        total_of(node_terms, 0, node_rows),
        total_of(node_terms, node_rows, node_rows + w_node_out.shape[0] // peers),
    )


def solution(mesh):
    rows = P(("grp", "lon"), None)
    flat = P(("grp", "lon"))
    return jax.shard_map(
        on_device,
        mesh=mesh,
        in_specs=(rows, rows, rows, rows, flat, flat, flat, P(("grp", "lon"), None, None)) + (P(),) * 4,
        out_specs=(rows,) * 7,
        check_vma=False,
    )
```

```python
import functools

import jax
import jax.numpy as jnp
from jax import lax
from jax.experimental import pallas as pl
from jax.experimental.pallas import tpu as pltpu
from jax.sharding import PartitionSpec as P

TILE = 256
STEP = 1024
SUB = 512
LANES = 128
NEAR = 3
BF16 = jnp.bfloat16
F32 = jnp.float32
VMEM_BYTES = 56 * 1024 * 1024


def dot(left, right):
    return lax.dot_general(left, right, (((1,), (0,)), ((), ())), preferred_element_type=F32)


def contract_rows(left, right):
    return lax.dot_general(left, right, (((0,), (0,)), ((), ())), preferred_element_type=F32)


def contract_cols(left, right):
    return lax.dot_general(left, right, (((1,), (1,)), ((), ())), preferred_element_type=F32)


def layer_norm(values):
    centered = values - jnp.mean(values, axis=1, keepdims=True)
    inverse = lax.rsqrt(jnp.mean(centered * centered, axis=1, keepdims=True) + 1e-05)
    return (centered * inverse, inverse)


def norm_back(normed, inverse, upstream):
    first = jnp.mean(upstream, axis=1, keepdims=True)
    second = jnp.mean(upstream * normed, axis=1, keepdims=True)
    return inverse * (upstream - first - normed * second)


def silu_and_slope(values):
    sigma = 0.5 + 0.5 * jnp.tanh(0.5 * values)
    hidden = values * sigma
    return (hidden, sigma + hidden * (1.0 - sigma))


def as_column(row):
    count = row.shape[1]
    block = min(count, LANES)
    down = lax.broadcasted_iota(jnp.int32, (block, block), 0)
    along = lax.broadcasted_iota(jnp.int32, (block, block), 1)
    columns = []
    for start in range(0, count, block):
        piece = row[:, start : start + block].astype(F32)
        picked = jnp.where(down == along, piece, 0.0)
        columns.append(jnp.sum(picked, axis=1, keepdims=True))
    return jnp.concatenate(columns, axis=0).astype(jnp.int32)


def hot_rows(row, width, first=0):
    column = as_column(row) - first
    along = lax.broadcasted_iota(jnp.int32, (row.shape[1], width), 1)
    return (column == along).astype(F32).astype(BF16)


def hot_columns(row, height):
    down = lax.broadcasted_iota(jnp.int32, (height, row.shape[1]), 0)
    return (row == down).astype(F32).astype(BF16)


def live_only(row, first, count):
    place = first + lax.broadcasted_iota(jnp.int32, row.shape, 1)
    return jnp.where(place < count, row, -1)


def near_peers(me, peers):
    after = lax.rem(me + 2, peers)
    before = lax.rem(me + peers - 2, peers)
    across = lax.rem(me + peers - 3 + 6 * (me & 1), peers)
    return (me, me ^ 1, after, after ^ 1, before, before ^ 1, across)


def write_near(refs, cap, lists):
    mine, other, after, before, across = refs
    mine[...] = lists[0]
    other[...] = lists[1]
    after[:cap, :] = lists[2]
    after[cap:, :] = lists[3]
    before[:cap, :] = lists[4]
    before[cap:, :] = lists[5]
    across[...] = lists[6]


def read_near(refs, cap):
    mine, other, from_before, from_after, across, core_before, core_after = refs
    return [
        mine[...],
        other[...],
        from_after[:cap, :],
        core_after[cap:, :],
        from_before[:cap, :],
        core_before[cap:, :],
        across[...],
    ]


def list_hots(me, rows_ref, grid_count, first):
    peers, cap = rows_ref.shape
    pieces = []
    for target in near_peers(me, peers):
        pieces.append(hot_rows(rows_ref[pl.ds(target, 1), :], grid_count, first))
    peer = lax.broadcasted_iota(jnp.int32, (peers, cap), 0)
    ahead = lax.rem(peer - me + peers, peers)
    apart = jnp.minimum(ahead, peers - ahead)
    far = jnp.max(jnp.where(apart > NEAR, rows_ref[...].astype(F32), -1.0), axis=0, keepdims=True)
    pieces.append(hot_rows(far.astype(jnp.int32), grid_count, first))
    return jnp.concatenate(pieces, axis=0)


def gather_kernel(me_ref, rows_ref, grid_ref, *refs):
    near_refs, far_ref, total = refs[:5], refs[5], refs[6]
    cap = rows_ref.shape[1]
    step = pl.program_id(0)
    part = grid_ref.shape[0]
    found = dot(list_hots(me_ref[0], rows_ref, part, step * part), grid_ref[...])

    @pl.when(step == 0)
    def _():
        total[...] = found

    @pl.when(step == pl.num_programs(0) - 1)
    def _():
        rows = (total[...] + found).astype(BF16)
        lists = [rows[at : at + cap] for at in range(0, 8 * cap, cap)]
        write_near(near_refs, cap, lists)
        for at in range(0, far_ref.shape[0], cap):
            far_ref[at : at + cap, :] = lists[7]


def scatter_kernel(skip, me_ref, rows_ref, *refs):
    near_refs, far_ref, out_ref = refs[:7], refs[7], refs[8]
    part = out_ref.shape[0]
    peers, cap = rows_ref.shape
    share = skip + cap
    hots = list_hots(me_ref[0], rows_ref, part, pl.program_id(0) * part)
    far = jnp.zeros((cap, out_ref.shape[1]), F32)
    for at in range(skip, far_ref.shape[0], share):
        far = far + far_ref[at : at + cap, :].astype(F32)
    values = jnp.concatenate(read_near(near_refs, cap) + [far.astype(BF16)], axis=0)
    out_ref[...] = contract_rows(hots, values).astype(BF16)


def halves_of(ref):
    rows = ref.shape[-1] if len(ref.shape) == 3 else ref.shape[0]
    return [(start, slice(start, start + SUB)) for start in range(0, rows, SUB)]


def local_kernel(dst_ref, edge_ref, mesh_ref, w_edge_ref, w_receiver_ref, *refs):
    out_ref, mesh_proj = refs[-2:]

    @pl.when(pl.program_id(0) == 0)
    def _():
        mesh_proj[...] = dot(mesh_ref[...], w_receiver_ref[...]).astype(BF16)

    for start, part in halves_of(edge_ref):
        onehot = hot_rows(dst_ref[0, :, part], mesh_ref.shape[0])
        out_ref[part, :] = (
            dot(edge_ref[part, :], w_edge_ref[...]) + dot(onehot, mesh_proj[...])
        ).astype(BF16)


def split_out(me, peers, send_ref, keep_ref, parts):
    for low in range(4):
        target = send_ref if low % 2 else keep_ref
        at = 0
        for upper in range(peers // 4):
            owner = 4 * upper + ((me & 3) ^ low)
            for ref, share, far in parts:
                piece = ref[pl.ds(pl.multiple_of(owner * share, 16), share), :]
                if far:
                    ahead = lax.rem(owner - me + peers, peers)
                    apart = jnp.minimum(ahead, peers - ahead)
                    piece = jnp.where(apart > NEAR, piece.astype(F32), 0.0)
                target[low // 2, at : at + share, :] = piece.astype(BF16)
                at += share


def forward_kernel(
    peers, me_ref, count_ref, src_ref, dst_ref, local_ref, edge_ref, *refs
):
    near_refs, far_refs = refs[:7], refs[7:11]
    (w_sender_ref, w_out_ref, w_node_in_ref, w_node_out_ref, mesh_ref, cotangent_ref) = refs[11:17]
    (received_ref, hidden_ref, slope_ref, norm_ref, inverse_ref) = refs[17:22]
    (send_ref, keep_ref, d_aggregate_ref, d_mesh_ref) = refs[22:26]
    (slot_proj, aggregate, grad_in, grad_out) = refs[26:]
    step = pl.program_id(0)
    me = me_ref[0]
    cap = near_refs[0].shape[0]
    width = edge_ref.shape[1]

    @pl.when(step == 0)
    def _():
        aggregate[...] = jnp.zeros_like(aggregate)
        w_sender = w_sender_ref[...]

        def place(owner, rows, projected):
            offset = pl.multiple_of(owner * cap, 16)
            received_ref[pl.ds(offset, cap), :] = rows
            slot_proj[pl.ds(offset, cap), :] = projected

        for low, ref in enumerate(far_refs):
            rows = ref[...]
            projected = dot(rows, w_sender).astype(BF16)
            for upper in range(peers // 4):
                span = slice(upper * cap, (upper + 1) * cap)
                place(4 * upper + ((me & 3) ^ low), rows[span], projected[span])
        rows = jnp.concatenate(read_near(near_refs, cap), axis=0)
        projected = dot(rows, w_sender).astype(BF16)
        for spot, owner in enumerate(near_peers(me, peers)):
            place(owner, rows[spot * cap : (spot + 1) * cap], projected[spot * cap : (spot + 1) * cap])

    @pl.when(step * STEP < count_ref[0] * TILE)
    def _():
        parts = halves_of(edge_ref)
        pres = []
        for start, part in parts:
            onehot = hot_rows(src_ref[0, :, part], slot_proj.shape[0])
            pres.append(local_ref[part, :].astype(F32) + dot(onehot, slot_proj[...]))
        projs = []
        for (start, part), pre in zip(parts, pres):
            hidden, slope = silu_and_slope(pre)
            hidden = hidden.astype(BF16)
            hidden_ref[part, :] = hidden
            slope_ref[part, :] = slope.astype(BF16)
            projs.append(dot(hidden, w_out_ref[...]))
        for (start, part), proj in zip(parts, projs):
            normed, inverse = layer_norm(proj)
            norm_ref[part, :] = normed.astype(BF16)
            inverse_ref[part, :] = inverse
            edge_new = (edge_ref[part, :].astype(F32) + normed).astype(BF16)
            receivers = live_only(dst_ref[0, :, part], step * STEP + start, count_ref[0] * TILE)
            aggregate[...] += dot(hot_columns(receivers, aggregate.shape[0]), edge_new)

    @pl.when(step == pl.num_programs(0) - 1)
    def _():
        mesh = mesh_ref[...]
        summed = aggregate[...].astype(BF16)
        node_pre = dot(mesh, w_node_in_ref[:width, :]) + dot(summed, w_node_in_ref[width:, :])
        hidden, slope = silu_and_slope(node_pre)
        hidden = hidden.astype(BF16)
        normed, inverse = layer_norm(dot(hidden, w_node_out_ref[...]))
        upstream = cotangent_ref[...].astype(F32)
        d_proj = norm_back(normed, inverse, upstream).astype(BF16)
        d_pre = (contract_cols(d_proj, w_node_out_ref[...]) * slope).astype(BF16)
        d_mesh_ref[...] = upstream + contract_cols(d_pre, w_node_in_ref[:width, :])
        d_aggregate_ref[...] = contract_cols(d_pre, w_node_in_ref[width:, :]).astype(BF16)
        grad_out[...] = contract_rows(hidden, d_proj)
        grad_in[:width, :] = contract_rows(mesh, d_pre)
        grad_in[width:, :] = contract_rows(summed, d_pre)
        split_out(
            me,
            peers,
            send_ref,
            keep_ref,
            ((grad_in, grad_in.shape[0] // peers, False), (grad_out, grad_out.shape[0] // peers, False)),
        )


def slots_kernel(peers, me_ref, count_ref, src_ref, dst_ref, *refs):
    (hidden_ref, slope_ref, norm_ref, inverse_ref, d_aggregate_ref) = refs[:5]
    (received_ref, w_sender_ref, w_out_ref) = refs[5:8]
    (d_pre_ref, grad_sender_ref, send_ref, keep_ref) = refs[8:12]
    near_refs = refs[12:17]
    (slot_sum, grad_out, d_slots) = refs[17:]
    step = pl.program_id(0)
    me = me_ref[0]

    @pl.when(step == 0)
    def _():
        slot_sum[...] = jnp.zeros_like(slot_sum)
        grad_out[...] = jnp.zeros_like(grad_out)

    @pl.when(step * STEP < count_ref[0] * TILE)
    def _():
        parts = halves_of(hidden_ref)
        upstreams = []
        for start, part in parts:
            receivers = live_only(dst_ref[0, :, part], step * STEP + start, count_ref[0] * TILE)
            onehot = hot_rows(receivers, d_aggregate_ref.shape[0])
            upstreams.append(dot(onehot, d_aggregate_ref[...]))
        d_projs = []
        d_hiddens = []
        for (start, part), upstream in zip(parts, upstreams):
            d_proj = norm_back(norm_ref[part, :].astype(F32), inverse_ref[part, :], upstream).astype(BF16)
            d_projs.append(d_proj)
            d_hiddens.append(contract_cols(d_proj, w_out_ref[...]))
        for (start, part), d_proj, d_hidden in zip(parts, d_projs, d_hiddens):
            grad_out[...] += contract_rows(hidden_ref[part, :], d_proj)
            d_pre = (d_hidden * slope_ref[part, :].astype(F32)).astype(BF16)
            d_pre_ref[part, :] = d_pre
            slot_sum[...] += dot(hot_columns(src_ref[0, :, part], slot_sum.shape[0]), d_pre)

    @pl.when(step == pl.num_programs(0) - 1)
    def _():
        summed = slot_sum[...].astype(BF16)
        grad_sender_ref[...] = contract_rows(received_ref[...], summed)
        d_slots[...] = contract_cols(summed, w_sender_ref[...]).astype(BF16)
        cap = near_refs[0].shape[0]
        owners = near_peers(me, peers)
        write_near(
            near_refs, cap, [d_slots[pl.ds(pl.multiple_of(owner * cap, 16), cap), :] for owner in owners]
        )
        split_out(
            me,
            peers,
            send_ref,
            keep_ref,
            ((grad_out, grad_out.shape[0] // peers, False), (d_slots, cap, True)),
        )


def edges_kernel(peers, me_ref, count_ref, dst_ref, *refs):
    (edge_ref, d_pre_ref, d_aggregate_ref, d_mesh_ref, mesh_ref, grad_sender_ref) = refs[:6]
    (w_edge_ref, w_receiver_ref) = refs[6:8]
    (edge_grad_ref, mesh_grad_ref, send_ref, keep_ref) = refs[8:12]
    (grad_in, mesh_sum) = refs[12:]
    step = pl.program_id(0)
    width = edge_ref.shape[1]

    @pl.when(step == 0)
    def _():
        grad_in[:width, :] = jnp.zeros((width, grad_in.shape[1]), F32)
        mesh_sum[...] = jnp.zeros_like(mesh_sum)

    @pl.when(step * STEP < count_ref[0] * TILE)
    def _():
        for start, part in halves_of(edge_ref):
            d_pre = d_pre_ref[part, :]
            receivers = live_only(dst_ref[0, :, part], step * STEP + start, count_ref[0] * TILE)
            onehot = hot_rows(receivers, d_aggregate_ref.shape[0])
            upstream = dot(onehot, d_aggregate_ref[...])
            edge_grad_ref[part, :] = (upstream + contract_cols(d_pre, w_edge_ref[...])).astype(BF16)
            grad_in[:width, :] += contract_rows(edge_ref[part, :], d_pre)
            mesh_sum[...] += dot(hot_columns(receivers, mesh_sum.shape[0]), d_pre)

    @pl.when(step * STEP >= count_ref[0] * TILE)
    def _():
        edge_grad_ref[...] = jnp.zeros_like(edge_grad_ref)

    @pl.when(step == pl.num_programs(0) - 1)
    def _():
        summed = mesh_sum[...].astype(BF16)
        mesh_grad_ref[...] = (d_mesh_ref[...] + contract_cols(summed, w_receiver_ref[...])).astype(BF16)
        grad_in[width : 2 * width, :] = grad_sender_ref[...]
        grad_in[2 * width :, :] = contract_rows(mesh_ref[...], summed)
        split_out(me_ref[0], peers, send_ref, keep_ref, ((grad_in, grad_in.shape[0] // peers, False),))


def send(values, perm):
    return lax.ppermute(values, "lon", perm)


def by_xor(peers, bits):
    return [(peer, peer ^ bits) for peer in range(peers)]


def by_shift(peers, shift):
    return [(peer, (peer + shift) % peers) for peer in range(peers)]


def across_chips(peers):
    return [(peer, (peer + (3 if peer % 2 else -3)) % peers) for peer in range(peers)]


def exchange_upper(peers, values):
    groups = [list(range(low, peers, 4)) for low in range(4)]
    return lax.all_to_all(
        values, "lon", split_axis=0, concat_axis=0, axis_index_groups=groups, tiled=True
    )


def exchange_near(peers, lists):
    mine, other, after, before, across = lists
    return [
        mine,
        send(other, by_xor(peers, 1)),
        send(after, by_shift(peers, 2)),
        send(before, by_shift(peers, -2)),
        send(across, across_chips(peers)),
    ]


def core_near(peers, near):
    return list(near) + [send(near[2], by_xor(peers, 1)), send(near[3], by_xor(peers, 1))]


def add(left, right):
    return (left.astype(F32) + right.astype(F32)).astype(BF16)


def core_sum(peers, outgoing, kept):
    arrived = send(outgoing, by_xor(peers, 1))
    return add(kept[1], arrived[1]), add(kept[0], arrived[0])


def next_sum(peers, outgoing, kept):
    return add(kept, send(outgoing, by_xor(peers, 2)))


def total_of(peers, terms, start, stop):
    blocks = terms.reshape(peers // 4, -1, terms.shape[1])
    return jnp.sum(blocks[:, start:stop].astype(F32), axis=0)


def whole(shape):
    return pl.BlockSpec(shape, lambda *_: (0,) * len(shape))


def on_device(
    grid_latent,
    mesh_latent,
    edge_latent,
    mesh_cotangent,
    edge_src,
    edge_dst,
    tile_count,
    send_rows,
    w_edge_in,
    w_edge_out,
    w_node_in,
    w_node_out,
):
    peers = lax.axis_size("lon")
    me = lax.axis_index("lon").astype(jnp.int32).reshape(1)
    upper = peers // 4
    rows = send_rows[0]
    cap = rows.shape[1]
    slots = peers * cap
    edges, width = edge_latent.shape
    mesh_count = mesh_latent.shape[0]
    grid_count = grid_latent.shape[0]
    tiles = edges // STEP
    src = edge_src.reshape(tiles, 1, STEP)
    dst = edge_dst.reshape(tiles, 1, STEP)
    smem = pl.BlockSpec(memory_space=pltpu.SMEM)
    params = pltpu.CompilerParams(vmem_limit_bytes=VMEM_BYTES)
    square = (width, width)

    def tile_of(last):
        return pl.BlockSpec((STEP, last), lambda step, *_: (step, 0))

    index_tile = pl.BlockSpec((1, 1, STEP), lambda step, *_: (step, 0, 0))

    def weight(place):
        return pl.BlockSpec(square, lambda *_: (place, 0))

    def halves(share):
        shape = (2, upper * share, width)
        return [jax.ShapeDtypeStruct(shape, BF16)] * 2, [whole(shape)] * 2

    grid_part = grid_count // 2
    near_rows = (cap, cap, 2 * cap, 2 * cap, cap)
    near_specs = [whole((count, width)) for count in near_rows]
    near_shapes = [jax.ShapeDtypeStruct((count, width), BF16) for count in near_rows]
    core_specs = near_specs + [whole((2 * cap, width))] * 2
    lists = pl.pallas_call(
        gather_kernel,
        grid=(2,),
        in_specs=[smem, whole(rows.shape), pl.BlockSpec((grid_part, width), lambda step: (step, 0))],
        out_specs=near_specs + [whole((upper * cap, width))],
        out_shape=near_shapes + [jax.ShapeDtypeStruct((upper * cap, width), BF16)],
        scratch_shapes=[pltpu.VMEM((8 * cap, width), F32)],
        compiler_params=params,
        name="gather_lists",
    )(me, rows, grid_latent)

    def local_part(first, count, *before):
        return pl.pallas_call(
            local_kernel,
            grid=(count,),
            in_specs=[
                pl.BlockSpec((1, 1, STEP), lambda step: (first + step, 0, 0)),
                pl.BlockSpec((STEP, width), lambda step: (first + step, 0)),
                whole(mesh_latent.shape),
                weight(0),
                weight(2),
            ]
            + [pl.BlockSpec(memory_space=pl.ANY)] * len(before),
            out_specs=pl.BlockSpec((STEP, width), lambda step: (first + step, 0)),
            out_shape=jax.ShapeDtypeStruct((edges, width), BF16),
            scratch_shapes=[pltpu.VMEM((mesh_count, width), BF16)],
            input_output_aliases={5: 0} if before else {},
            compiler_params=params,
            cost_estimate=pl.CostEstimate(
                flops=2 * count * STEP * width * (width + mesh_count),
                bytes_accessed=4 * count * STEP * width,
                transcendentals=0,
            ),
            name="edge_local",
        )(receivers, edge_latent, mesh_latent, w_edge_in, w_edge_in, *before)

    far_own = exchange_upper(peers, lists[5])
    near = exchange_near(peers, lists[:5])
    far_own, receivers = lax.optimization_barrier((far_own, dst))
    far_next = send(far_own, by_xor(peers, 2))
    far_core = send(far_own, by_xor(peers, 1))
    local = local_part(0, tiles - 1)
    far_next, far_core, near, local = lax.optimization_barrier((far_next, far_core, near, local))
    near = core_near(peers, near)
    far_both = send(far_next, by_xor(peers, 1))
    local = local_part(tiles - 1, 1, local)

    node_shape, node_spec = halves(w_node_in.shape[0] // peers + w_node_out.shape[0] // peers)
    (received, hidden, slope, norm, inverse, node_send, node_keep, d_aggregate, d_mesh) = pl.pallas_call(
        functools.partial(forward_kernel, peers),
        grid=(tiles,),
        in_specs=[smem, smem, index_tile, index_tile, tile_of(width), tile_of(width)]
        + core_specs
        + [whole((upper * cap, width))] * 4
        + [weight(1)]
        + [whole(w.shape) for w in (w_edge_out, w_node_in, w_node_out, mesh_latent, mesh_cotangent)],
        out_specs=[whole((slots, width))]
        + [tile_of(width)] * 3
        + [tile_of(1)]
        + node_spec
        + [whole((mesh_count, width))] * 2,
        out_shape=[jax.ShapeDtypeStruct((slots, width), BF16)]
        + [jax.ShapeDtypeStruct((edges, width), BF16)] * 3
        + [jax.ShapeDtypeStruct((edges, 1), F32)]
        + node_shape
        + [jax.ShapeDtypeStruct((mesh_count, width), BF16), jax.ShapeDtypeStruct((mesh_count, width), F32)],
        scratch_shapes=[
            pltpu.VMEM((slots, width), BF16),
            pltpu.VMEM((mesh_count, width), F32),
            pltpu.VMEM(w_node_in.shape, F32),
            pltpu.VMEM(w_node_out.shape, F32),
        ],
        compiler_params=params,
        name="forward",
    )(
        me,
        tile_count,
        src,
        dst,
        local,
        edge_latent,
        *near,
        far_own,
        far_core,
        far_next,
        far_both,
        w_edge_in,
        w_edge_out,
        w_node_in,
        w_node_out,
        mesh_latent,
        mesh_cotangent,
    )

    node_next, node_kept = core_sum(peers, node_send, node_keep)
    slot_shape, slot_spec = halves(w_edge_out.shape[0] // peers + cap)
    results = pl.pallas_call(
        functools.partial(slots_kernel, peers),
        grid=(tiles,),
        in_specs=[smem, smem, index_tile, index_tile]
        + [tile_of(width)] * 3
        + [tile_of(1), whole((mesh_count, width)), whole((slots, width)), weight(1), whole(square)],
        out_specs=[tile_of(width), whole(square)] + slot_spec + near_specs,
        out_shape=[jax.ShapeDtypeStruct((edges, width), BF16), jax.ShapeDtypeStruct(square, F32)]
        + slot_shape
        + near_shapes,
        scratch_shapes=[
            pltpu.VMEM((slots, width), F32),
            pltpu.VMEM(square, F32),
            pltpu.VMEM((slots, width), BF16),
        ],
        compiler_params=params,
        cost_estimate=pl.CostEstimate(
            flops=2 * edges * width * (mesh_count + 2 * width + slots),
            bytes_accessed=8 * edges * width,
            transcendentals=0,
        ),
        name="backward_slots",
    )(me, tile_count, src, dst, hidden, slope, norm, inverse, d_aggregate, received, w_edge_in, w_edge_out)
    (d_pre, grad_sender, slot_send, slot_keep), returns = results[:4], results[4:]
    (node_next, node_kept, d_pre, slot_send, slot_keep, returns) = lax.optimization_barrier(
        (node_next, node_kept, d_pre, slot_send, slot_keep, returns)
    )
    node_pieces = next_sum(peers, node_next, node_kept)
    slot_next, slot_kept = core_sum(peers, slot_send, slot_keep)
    returned = exchange_near(peers, returns)

    edge_shape, edge_spec = halves(w_edge_in.shape[0] // peers)
    edge_grad, mesh_grad, edge_send, edge_keep = pl.pallas_call(
        functools.partial(edges_kernel, peers),
        grid=(tiles,),
        in_specs=[smem, smem, index_tile, tile_of(width), tile_of(width)]
        + [whole((mesh_count, width))] * 3
        + [whole(square), weight(0), weight(2)],
        out_specs=[tile_of(width), whole((mesh_count, width))] + edge_spec,
        out_shape=[
            jax.ShapeDtypeStruct((edges, width), BF16),
            jax.ShapeDtypeStruct((mesh_count, width), BF16),
        ]
        + edge_shape,
        scratch_shapes=[pltpu.VMEM(w_edge_in.shape, F32), pltpu.VMEM((mesh_count, width), F32)],
        compiler_params=params,
        cost_estimate=pl.CostEstimate(
            flops=2 * edges * width * (2 * mesh_count + 2 * width),
            bytes_accessed=6 * edges * width,
            transcendentals=0,
        ),
        name="backward_edges",
    )(
        me,
        tile_count,
        dst,
        edge_latent,
        d_pre,
        d_aggregate,
        d_mesh,
        mesh_latent,
        grad_sender,
        w_edge_in,
        w_edge_in,
    )

    (node_pieces, slot_next, slot_kept, edge_send, edge_keep) = lax.optimization_barrier(
        (node_pieces, slot_next, slot_kept, edge_send, edge_keep)
    )
    slot_pieces = next_sum(peers, slot_next, slot_kept)
    edge_next, edge_kept = core_sum(peers, edge_send, edge_keep)
    node_terms = exchange_upper(peers, node_pieces)
    returned = core_near(peers, returned)
    edge_pieces = next_sum(peers, edge_next, edge_kept)
    slot_terms = exchange_upper(peers, slot_pieces)
    edge_terms = exchange_upper(peers, edge_pieces)
    node_rows = w_node_in.shape[0] // peers
    out_rows = w_edge_out.shape[0] // peers
    grid_grad = pl.pallas_call(
        functools.partial(scatter_kernel, out_rows),
        grid=(2,),
        in_specs=[smem, whole(rows.shape)]
        + core_specs
        + [whole((upper * (out_rows + cap), width))],
        out_specs=pl.BlockSpec((grid_part, width), lambda step: (step, 0)),
        out_shape=jax.ShapeDtypeStruct((grid_count, width), BF16),
        compiler_params=params,
        name="scatter_lists",
    )(me, rows, *returned, slot_terms)
    return (
        grid_grad,
        edge_grad,
        mesh_grad,
        total_of(peers, edge_terms, 0, w_edge_in.shape[0] // peers),
        total_of(peers, slot_terms, 0, out_rows),
        total_of(peers, node_terms, 0, node_rows),
        total_of(peers, node_terms, node_rows, node_rows + w_node_out.shape[0] // peers),
    )


def solution(mesh):
    rows = P(("grp", "lon"), None)
    flat = P(("grp", "lon"))
    return jax.shard_map(
        on_device,
        mesh=mesh,
        in_specs=(rows, rows, rows, rows, flat, flat, flat, P(("grp", "lon"), None, None)) + (P(),) * 4,
        out_specs=(rows,) * 7,
        check_vma=False,
    )
```

```python
import functools

import jax
import jax.numpy as jnp
from jax import lax
from jax.experimental import pallas as pl
from jax.experimental.pallas import tpu as pltpu
from jax.sharding import PartitionSpec as P

TILE = 256
STEP = 1024
SUB = 512
LANES = 128
NEAR = 3
BF16 = jnp.bfloat16
F32 = jnp.float32
VMEM_BYTES = 56 * 1024 * 1024


def dot(left, right):
    return lax.dot_general(left, right, (((1,), (0,)), ((), ())), preferred_element_type=F32)


def contract_rows(left, right):
    return lax.dot_general(left, right, (((0,), (0,)), ((), ())), preferred_element_type=F32)


def contract_cols(left, right):
    return lax.dot_general(left, right, (((1,), (1,)), ((), ())), preferred_element_type=F32)


def layer_norm(values):
    centered = values - jnp.mean(values, axis=1, keepdims=True)
    inverse = lax.rsqrt(jnp.mean(centered * centered, axis=1, keepdims=True) + 1e-05)
    return (centered * inverse, inverse)


def norm_back(normed, inverse, upstream):
    first = jnp.mean(upstream, axis=1, keepdims=True)
    second = jnp.mean(upstream * normed, axis=1, keepdims=True)
    return inverse * (upstream - first - normed * second)


def silu_and_slope(values):
    sigma = 0.5 + 0.5 * jnp.tanh(0.5 * values)
    hidden = values * sigma
    return (hidden, sigma + hidden * (1.0 - sigma))


def as_column(row):
    count = row.shape[1]
    block = min(count, LANES)
    down = lax.broadcasted_iota(jnp.int32, (block, block), 0)
    along = lax.broadcasted_iota(jnp.int32, (block, block), 1)
    columns = []
    for start in range(0, count, block):
        piece = row[:, start : start + block].astype(F32)
        picked = jnp.where(down == along, piece, 0.0)
        columns.append(jnp.sum(picked, axis=1, keepdims=True))
    return jnp.concatenate(columns, axis=0).astype(jnp.int32)


def hot_rows(row, width, first=0):
    column = as_column(row) - first
    along = lax.broadcasted_iota(jnp.int32, (row.shape[1], width), 1)
    return (column == along).astype(F32).astype(BF16)


def hot_columns(row, height):
    down = lax.broadcasted_iota(jnp.int32, (height, row.shape[1]), 0)
    return (row == down).astype(F32).astype(BF16)


def live_only(row, first, count):
    place = first + lax.broadcasted_iota(jnp.int32, row.shape, 1)
    return jnp.where(place < count, row, -1)


def near_peers(me, peers):
    after = lax.rem(me + 2, peers)
    before = lax.rem(me + peers - 2, peers)
    across = lax.rem(me + peers - 3 + 6 * (me & 1), peers)
    return (me, me ^ 1, after, after ^ 1, before, before ^ 1, across)


def write_near(refs, cap, lists):
    mine, other, after, before, across = refs
    mine[...] = lists[0]
    other[...] = lists[1]
    after[:cap, :] = lists[2]
    after[cap:, :] = lists[3]
    before[:cap, :] = lists[4]
    before[cap:, :] = lists[5]
    across[...] = lists[6]


def read_near(refs, cap):
    mine, other, from_before, from_after, across, core_before, core_after = refs
    return [
        mine[...],
        other[...],
        from_after[:cap, :],
        core_after[cap:, :],
        from_before[:cap, :],
        core_before[cap:, :],
        across[...],
    ]


def list_hots(me, rows_ref, grid_count, first):
    peers, cap = rows_ref.shape
    pieces = []
    for target in near_peers(me, peers):
        pieces.append(hot_rows(rows_ref[pl.ds(target, 1), :], grid_count, first))
    peer = lax.broadcasted_iota(jnp.int32, (peers, cap), 0)
    ahead = lax.rem(peer - me + peers, peers)
    apart = jnp.minimum(ahead, peers - ahead)
    far = jnp.max(jnp.where(apart > NEAR, rows_ref[...].astype(F32), -1.0), axis=0, keepdims=True)
    pieces.append(hot_rows(far.astype(jnp.int32), grid_count, first))
    return jnp.concatenate(pieces, axis=0)


def gather_kernel(me_ref, rows_ref, grid_ref, *refs):
    near_refs, far_ref, total = refs[:5], refs[5], refs[6]
    cap = rows_ref.shape[1]
    step = pl.program_id(0)
    part = grid_ref.shape[0]
    found = dot(list_hots(me_ref[0], rows_ref, part, step * part), grid_ref[...])

    @pl.when(step == 0)
    def _():
        total[...] = found

    @pl.when(step == pl.num_programs(0) - 1)
    def _():
        rows = (total[...] + found).astype(BF16)
        lists = [rows[at : at + cap] for at in range(0, 8 * cap, cap)]
        write_near(near_refs, cap, lists)
        far_ref[...] = lists[7]


def scatter_kernel(skip, me_ref, rows_ref, *refs):
    near_refs, far_refs, out_ref = refs[:7], refs[7:-1], refs[-1]
    part = out_ref.shape[0]
    cap = rows_ref.shape[1]
    hots = list_hots(me_ref[0], rows_ref, part, pl.program_id(0) * part)
    far = far_refs[0][skip:, :].astype(F32)
    for ref in far_refs[1:]:
        far = far + ref[skip:, :].astype(F32)
    values = jnp.concatenate(read_near(near_refs, cap) + [far.astype(BF16)], axis=0)
    out_ref[...] = contract_rows(hots, values).astype(BF16)


def halves_of(ref):
    rows = ref.shape[-1] if len(ref.shape) == 3 else ref.shape[0]
    return [(start, slice(start, start + SUB)) for start in range(0, rows, SUB)]


def local_kernel(dst_ref, edge_ref, mesh_ref, w_edge_ref, w_receiver_ref, *refs):
    out_ref, mesh_proj = refs[-2:]

    @pl.when(pl.program_id(0) == 0)
    def _():
        mesh_proj[...] = dot(mesh_ref[...], w_receiver_ref[...]).astype(BF16)

    for start, part in halves_of(edge_ref):
        onehot = hot_rows(dst_ref[0, :, part], mesh_ref.shape[0])
        out_ref[part, :] = (
            dot(edge_ref[part, :], w_edge_ref[...]) + dot(onehot, mesh_proj[...])
        ).astype(BF16)


def split_out(me, peers, send_ref, keep_ref, parts):
    for low in range(4):
        target = send_ref if low % 2 else keep_ref
        at = 0
        for upper in range(peers // 4):
            owner = me ^ (4 * upper + low)
            for ref, share, far in parts:
                piece = ref[pl.ds(pl.multiple_of(owner * share, 16), share), :]
                if far:
                    ahead = lax.rem(owner - me + peers, peers)
                    apart = jnp.minimum(ahead, peers - ahead)
                    piece = jnp.where(apart > NEAR, piece.astype(F32), 0.0)
                target[low // 2, at : at + share, :] = piece.astype(BF16)
                at += share


def forward_kernel(
    peers, me_ref, count_ref, src_ref, dst_ref, local_ref, edge_ref, *refs
):
    near_refs, far_refs = refs[:7], refs[7:11]
    (w_sender_ref, w_out_ref, w_node_in_ref, w_node_out_ref, mesh_ref, cotangent_ref) = refs[11:17]
    (received_ref, hidden_ref, slope_ref, norm_ref, inverse_ref) = refs[17:22]
    (send_ref, keep_ref, d_aggregate_ref, d_mesh_ref) = refs[22:26]
    (slot_proj, aggregate, grad_in, grad_out) = refs[26:]
    step = pl.program_id(0)
    me = me_ref[0]
    cap = near_refs[0].shape[0]
    width = edge_ref.shape[1]

    @pl.when(step == 0)
    def _():
        aggregate[...] = jnp.zeros_like(aggregate)
        w_sender = w_sender_ref[...]

        def place(owner, rows, projected):
            offset = pl.multiple_of(owner * cap, 16)
            received_ref[pl.ds(offset, cap), :] = rows
            slot_proj[pl.ds(offset, cap), :] = projected

        for low, ref in enumerate(far_refs):
            rows = ref[...]
            projected = dot(rows, w_sender).astype(BF16)
            for upper in range(peers // 4):
                span = slice(upper * cap, (upper + 1) * cap)
                place(me ^ (4 * upper + low), rows[span], projected[span])
        rows = jnp.concatenate(read_near(near_refs, cap), axis=0)
        projected = dot(rows, w_sender).astype(BF16)
        for spot, owner in enumerate(near_peers(me, peers)):
            place(owner, rows[spot * cap : (spot + 1) * cap], projected[spot * cap : (spot + 1) * cap])

    @pl.when(step * STEP < count_ref[0] * TILE)
    def _():
        parts = halves_of(edge_ref)
        pres = []
        for start, part in parts:
            onehot = hot_rows(src_ref[0, :, part], slot_proj.shape[0])
            pres.append(local_ref[part, :].astype(F32) + dot(onehot, slot_proj[...]))
        projs = []
        for (start, part), pre in zip(parts, pres):
            hidden, slope = silu_and_slope(pre)
            hidden = hidden.astype(BF16)
            hidden_ref[part, :] = hidden
            slope_ref[part, :] = slope.astype(BF16)
            projs.append(dot(hidden, w_out_ref[...]))
        for (start, part), proj in zip(parts, projs):
            normed, inverse = layer_norm(proj)
            norm_ref[part, :] = normed.astype(BF16)
            inverse_ref[part, :] = inverse
            edge_new = (edge_ref[part, :].astype(F32) + normed).astype(BF16)
            receivers = live_only(dst_ref[0, :, part], step * STEP + start, count_ref[0] * TILE)
            aggregate[...] += dot(hot_columns(receivers, aggregate.shape[0]), edge_new)

    @pl.when(step == pl.num_programs(0) - 1)
    def _():
        mesh = mesh_ref[...]
        summed = aggregate[...].astype(BF16)
        node_pre = dot(mesh, w_node_in_ref[:width, :]) + dot(summed, w_node_in_ref[width:, :])
        hidden, slope = silu_and_slope(node_pre)
        hidden = hidden.astype(BF16)
        normed, inverse = layer_norm(dot(hidden, w_node_out_ref[...]))
        upstream = cotangent_ref[...].astype(F32)
        d_proj = norm_back(normed, inverse, upstream).astype(BF16)
        d_pre = (contract_cols(d_proj, w_node_out_ref[...]) * slope).astype(BF16)
        d_mesh_ref[...] = upstream + contract_cols(d_pre, w_node_in_ref[:width, :])
        d_aggregate_ref[...] = contract_cols(d_pre, w_node_in_ref[width:, :]).astype(BF16)
        grad_out[...] = contract_rows(hidden, d_proj)
        grad_in[:width, :] = contract_rows(mesh, d_pre)
        grad_in[width:, :] = contract_rows(summed, d_pre)
        split_out(
            me,
            peers,
            send_ref,
            keep_ref,
            ((grad_in, grad_in.shape[0] // peers, False), (grad_out, grad_out.shape[0] // peers, False)),
        )


def out_kernel(me_ref, count_ref, dst_ref, *refs):
    (hidden_ref, norm_ref, inverse_ref, d_aggregate_ref, d_proj_ref, grad_ref) = refs
    step = pl.program_id(0)

    @pl.when(step == 0)
    def _():
        grad_ref[...] = jnp.zeros_like(grad_ref)

    @pl.when(step * STEP < count_ref[0] * TILE)
    def _():
        parts = halves_of(hidden_ref)
        upstreams = []
        for start, part in parts:
            receivers = live_only(dst_ref[0, :, part], step * STEP + start, count_ref[0] * TILE)
            onehot = hot_rows(receivers, d_aggregate_ref.shape[0])
            upstreams.append(dot(onehot, d_aggregate_ref[...]))
        for (start, part), upstream in zip(parts, upstreams):
            d_proj = norm_back(norm_ref[part, :].astype(F32), inverse_ref[part, :], upstream).astype(BF16)
            d_proj_ref[part, :] = d_proj
            grad_ref[...] += contract_rows(hidden_ref[part, :], d_proj)


def slots_kernel(peers, me_ref, count_ref, src_ref, *refs):
    (d_proj_ref, slope_ref, received_ref, w_sender_ref, w_out_ref, grad_out_ref) = refs[:6]
    (d_pre_ref, grad_sender_ref, send_ref, keep_ref) = refs[6:10]
    near_refs = refs[10:15]
    (slot_sum, d_slots) = refs[15:]
    step = pl.program_id(0)
    me = me_ref[0]

    @pl.when(step == 0)
    def _():
        slot_sum[...] = jnp.zeros_like(slot_sum)

    @pl.when(step * STEP < count_ref[0] * TILE)
    def _():
        parts = halves_of(d_proj_ref)
        d_hiddens = [contract_cols(d_proj_ref[part, :], w_out_ref[...]) for start, part in parts]
        for (start, part), d_hidden in zip(parts, d_hiddens):
            d_pre = (d_hidden * slope_ref[part, :].astype(F32)).astype(BF16)
            d_pre_ref[part, :] = d_pre
            senders = live_only(src_ref[0, :, part], step * STEP + start, count_ref[0] * TILE)
            slot_sum[...] += dot(hot_columns(senders, slot_sum.shape[0]), d_pre)

    @pl.when(step == pl.num_programs(0) - 1)
    def _():
        summed = slot_sum[...].astype(BF16)
        grad_sender_ref[...] = contract_rows(received_ref[...], summed)
        d_slots[...] = contract_cols(summed, w_sender_ref[...]).astype(BF16)
        cap = near_refs[0].shape[0]
        owners = near_peers(me, peers)
        write_near(
            near_refs, cap, [d_slots[pl.ds(pl.multiple_of(owner * cap, 16), cap), :] for owner in owners]
        )
        split_out(
            me,
            peers,
            send_ref,
            keep_ref,
            ((grad_out_ref, grad_out_ref.shape[0] // peers, False), (d_slots, cap, True)),
        )


def edges_kernel(peers, me_ref, count_ref, dst_ref, *refs):
    (edge_ref, d_pre_ref, d_aggregate_ref, d_mesh_ref, mesh_ref, grad_sender_ref) = refs[:6]
    (w_edge_ref, w_receiver_ref) = refs[6:8]
    (edge_grad_ref, mesh_grad_ref, send_ref, keep_ref) = refs[8:12]
    (grad_in, mesh_sum) = refs[12:]
    step = pl.program_id(0)
    width = edge_ref.shape[1]

    @pl.when(step == 0)
    def _():
        grad_in[:width, :] = jnp.zeros((width, grad_in.shape[1]), F32)
        mesh_sum[...] = jnp.zeros_like(mesh_sum)

    @pl.when(step * STEP < count_ref[0] * TILE)
    def _():
        for start, part in halves_of(edge_ref):
            d_pre = d_pre_ref[part, :]
            receivers = live_only(dst_ref[0, :, part], step * STEP + start, count_ref[0] * TILE)
            onehot = hot_rows(receivers, d_aggregate_ref.shape[0])
            upstream = dot(onehot, d_aggregate_ref[...])
            edge_grad_ref[part, :] = (upstream + contract_cols(d_pre, w_edge_ref[...])).astype(BF16)
            grad_in[:width, :] += contract_rows(edge_ref[part, :], d_pre)
            mesh_sum[...] += dot(hot_columns(receivers, mesh_sum.shape[0]), d_pre)

    @pl.when(step * STEP >= count_ref[0] * TILE)
    def _():
        edge_grad_ref[...] = jnp.zeros_like(edge_grad_ref)

    @pl.when(step == pl.num_programs(0) - 1)
    def _():
        summed = mesh_sum[...].astype(BF16)
        mesh_grad_ref[...] = (d_mesh_ref[...] + contract_cols(summed, w_receiver_ref[...])).astype(BF16)
        grad_in[width : 2 * width, :] = grad_sender_ref[...]
        grad_in[2 * width :, :] = contract_rows(mesh_ref[...], summed)
        split_out(me_ref[0], peers, send_ref, keep_ref, ((grad_in, grad_in.shape[0] // peers, False),))


def send(values, perm):
    return lax.ppermute(values, "lon", perm)


def by_xor(peers, bits):
    return [(peer, peer ^ bits) for peer in range(peers)]


def by_shift(peers, shift):
    return [(peer, (peer + shift) % peers) for peer in range(peers)]


def across_chips(peers):
    return [(peer, (peer + (3 if peer % 2 else -3)) % peers) for peer in range(peers)]


def exchange_near(peers, lists):
    mine, other, after, before, across = lists
    return [
        mine,
        other,
        send(after, by_shift(peers, 2)),
        send(before, by_shift(peers, -2)),
        send(across, across_chips(peers)),
    ]


def core_near(peers, near):
    mine, other, after, before, across = near
    swap = by_xor(peers, 1)
    return [mine, send(other, swap), after, before, across, send(after, swap), send(before, swap)]


def add(left, right):
    return (left.astype(F32) + right.astype(F32)).astype(BF16)


def core_sum(peers, outgoing, kept):
    arrived = send(outgoing, by_xor(peers, 1))
    return add(kept[1], arrived[1]), add(kept[0], arrived[0])


def next_sum(peers, outgoing, kept):
    return add(kept, send(outgoing, by_xor(peers, 2)))


def last_terms(peers, pieces):
    count = peers // 4
    share = pieces.shape[0] // count
    terms = [pieces[:share]]
    for place in range(1, count):
        piece = pieces[place * share : (place + 1) * share]
        terms.append(send(piece, by_xor(peers, 4 * place)))
    return terms


def halve_first(peers, pieces):
    count = peers // 4
    share = pieces.shape[0] // count
    blocks = pieces.reshape(count // 2, 2, share, -1)
    return blocks[:, 0].reshape(-1, pieces.shape[1]), blocks[:, 1].reshape(-1, pieces.shape[1])


def node_last(peers, pieces):
    count = peers // 8
    share = pieces.shape[0] // count
    terms = [pieces[:share]]
    for place in range(1, count):
        piece = pieces[place * share : (place + 1) * share]
        terms.append(send(piece, by_xor(peers, 8 * place)))
    return terms


def total_of(terms, start, stop):
    total = terms[0][start:stop].astype(F32)
    for term in terms[1:]:
        total = total + term[start:stop].astype(F32)
    return total


def whole(shape):
    return pl.BlockSpec(shape, lambda *_: (0,) * len(shape))


def on_device(
    grid_latent,
    mesh_latent,
    edge_latent,
    mesh_cotangent,
    edge_src,
    edge_dst,
    tile_count,
    send_rows,
    w_edge_in,
    w_edge_out,
    w_node_in,
    w_node_out,
):
    peers = lax.axis_size("lon")
    me = lax.axis_index("lon").astype(jnp.int32).reshape(1)
    upper = peers // 4
    rows = send_rows[0]
    cap = rows.shape[1]
    slots = peers * cap
    edges, width = edge_latent.shape
    mesh_count = mesh_latent.shape[0]
    grid_count = grid_latent.shape[0]
    tiles = edges // STEP
    src = edge_src.reshape(tiles, 1, STEP)
    dst = edge_dst.reshape(tiles, 1, STEP)
    smem = pl.BlockSpec(memory_space=pltpu.SMEM)
    params = pltpu.CompilerParams(vmem_limit_bytes=VMEM_BYTES)
    square = (width, width)

    def tile_of(last):
        return pl.BlockSpec((STEP, last), lambda step, *_: (step, 0))

    index_tile = pl.BlockSpec((1, 1, STEP), lambda step, *_: (step, 0, 0))

    def weight(place):
        return pl.BlockSpec(square, lambda *_: (place, 0))

    def halves(share):
        shape = (2, upper * share, width)
        return [jax.ShapeDtypeStruct(shape, BF16)] * 2, [whole(shape)] * 2

    grid_part = grid_count // 2
    near_rows = (cap, cap, 2 * cap, 2 * cap, cap)
    near_specs = [whole((count, width)) for count in near_rows]
    near_shapes = [jax.ShapeDtypeStruct((count, width), BF16) for count in near_rows]
    core_specs = near_specs + [whole((2 * cap, width))] * 2
    lists = pl.pallas_call(
        gather_kernel,
        grid=(2,),
        in_specs=[smem, whole(rows.shape), pl.BlockSpec((grid_part, width), lambda step: (step, 0))],
        out_specs=near_specs + [whole((cap, width))],
        out_shape=near_shapes + [jax.ShapeDtypeStruct((cap, width), BF16)],
        scratch_shapes=[pltpu.VMEM((8 * cap, width), F32)],
        compiler_params=params,
        name="gather_lists",
    )(me, rows, grid_latent)

    hops = [send(lists[5], by_xor(peers, 4 * place)) for place in range(1, upper)]
    near = exchange_near(peers, lists[:5])
    far_own = jnp.concatenate([lists[5]] + hops, axis=0)
    far_own, receivers = lax.optimization_barrier((far_own, dst))
    far_next = send(far_own, by_xor(peers, 2))
    far_core = send(far_own, by_xor(peers, 1))
    local = pl.pallas_call(
        local_kernel,
        grid=(tiles,),
        in_specs=[index_tile, tile_of(width), whole(mesh_latent.shape), weight(0), weight(2)],
        out_specs=tile_of(width),
        out_shape=jax.ShapeDtypeStruct((edges, width), BF16),
        scratch_shapes=[pltpu.VMEM((mesh_count, width), BF16)],
        compiler_params=params,
        cost_estimate=pl.CostEstimate(
            flops=2 * edges * width * (width + mesh_count),
            bytes_accessed=4 * edges * width,
            transcendentals=0,
        ),
        name="edge_local",
    )(receivers, edge_latent, mesh_latent, w_edge_in, w_edge_in)
    far_next, far_core, near, local = lax.optimization_barrier((far_next, far_core, near, local))
    near = core_near(peers, near)
    far_both = send(far_next, by_xor(peers, 1))

    node_shape, node_spec = halves(w_node_in.shape[0] // peers + w_node_out.shape[0] // peers)
    (received, hidden, slope, norm, inverse, node_send, node_keep, d_aggregate, d_mesh) = pl.pallas_call(
        functools.partial(forward_kernel, peers),
        grid=(tiles,),
        in_specs=[smem, smem, index_tile, index_tile, tile_of(width), tile_of(width)]
        + core_specs
        + [whole((upper * cap, width))] * 4
        + [weight(1)]
        + [whole(w.shape) for w in (w_edge_out, w_node_in, w_node_out, mesh_latent, mesh_cotangent)],
        out_specs=[whole((slots, width))]
        + [tile_of(width)] * 3
        + [tile_of(1)]
        + node_spec
        + [whole((mesh_count, width))] * 2,
        out_shape=[jax.ShapeDtypeStruct((slots, width), BF16)]
        + [jax.ShapeDtypeStruct((edges, width), BF16)] * 3
        + [jax.ShapeDtypeStruct((edges, 1), F32)]
        + node_shape
        + [jax.ShapeDtypeStruct((mesh_count, width), BF16), jax.ShapeDtypeStruct((mesh_count, width), F32)],
        scratch_shapes=[
            pltpu.VMEM((slots, width), BF16),
            pltpu.VMEM((mesh_count, width), F32),
            pltpu.VMEM(w_node_in.shape, F32),
            pltpu.VMEM(w_node_out.shape, F32),
        ],
        compiler_params=params,
        name="forward",
    )(
        me,
        tile_count,
        src,
        dst,
        local,
        edge_latent,
        *near,
        far_own,
        far_core,
        far_next,
        far_both,
        w_edge_in,
        w_edge_out,
        w_node_in,
        w_node_out,
        mesh_latent,
        mesh_cotangent,
    )

    node_next, node_kept = core_sum(peers, node_send, node_keep)
    d_proj, grad_out = pl.pallas_call(
        out_kernel,
        grid=(tiles,),
        in_specs=[smem, smem, index_tile]
        + [tile_of(width)] * 2
        + [tile_of(1), whole((mesh_count, width))],
        out_specs=[tile_of(width), whole(square)],
        out_shape=[jax.ShapeDtypeStruct((edges, width), BF16), jax.ShapeDtypeStruct(square, F32)],
        compiler_params=params,
        cost_estimate=pl.CostEstimate(
            flops=2 * edges * width * (mesh_count + width), bytes_accessed=6 * edges * width, transcendentals=0
        ),
        name="backward_out",
    )(me, tile_count, dst, hidden, norm, inverse, d_aggregate)
    node_next, node_kept, d_proj, grad_out = lax.optimization_barrier(
        (node_next, node_kept, d_proj, grad_out)
    )
    node_pieces = next_sum(peers, node_next, node_kept)

    slot_shape, slot_spec = halves(w_edge_out.shape[0] // peers + cap)
    results = pl.pallas_call(
        functools.partial(slots_kernel, peers),
        grid=(tiles,),
        in_specs=[smem, smem, index_tile]
        + [tile_of(width)] * 2
        + [whole((slots, width)), weight(1), whole(square), whole(square)],
        out_specs=[tile_of(width), whole(square)] + slot_spec + near_specs,
        out_shape=[jax.ShapeDtypeStruct((edges, width), BF16), jax.ShapeDtypeStruct(square, F32)]
        + slot_shape
        + near_shapes,
        scratch_shapes=[pltpu.VMEM((slots, width), F32), pltpu.VMEM((slots, width), BF16)],
        compiler_params=params,
        cost_estimate=pl.CostEstimate(
            flops=2 * edges * width * (width + slots), bytes_accessed=6 * edges * width, transcendentals=0
        ),
        name="backward_slots",
    )(me, tile_count, src, d_proj, slope, received, w_edge_in, w_edge_out, grad_out)
    (d_pre, grad_sender, slot_send, slot_keep), returns = results[:4], results[4:]
    (node_pieces, d_pre, slot_send, slot_keep, returns) = lax.optimization_barrier(
        (node_pieces, d_pre, slot_send, slot_keep, returns)
    )
    slot_next, slot_kept = core_sum(peers, slot_send, slot_keep)
    returned = exchange_near(peers, returns)
    node_kept, node_next = halve_first(peers, node_pieces)
    node_pieces = add(node_kept, send(node_next, by_xor(peers, 4)))

    edge_shape, edge_spec = halves(w_edge_in.shape[0] // peers)
    edge_grad, mesh_grad, edge_send, edge_keep = pl.pallas_call(
        functools.partial(edges_kernel, peers),
        grid=(tiles,),
        in_specs=[smem, smem, index_tile, tile_of(width), tile_of(width)]
        + [whole((mesh_count, width))] * 3
        + [whole(square), weight(0), weight(2)],
        out_specs=[tile_of(width), whole((mesh_count, width))] + edge_spec,
        out_shape=[
            jax.ShapeDtypeStruct((edges, width), BF16),
            jax.ShapeDtypeStruct((mesh_count, width), BF16),
        ]
        + edge_shape,
        scratch_shapes=[pltpu.VMEM(w_edge_in.shape, F32), pltpu.VMEM((mesh_count, width), F32)],
        compiler_params=params,
        cost_estimate=pl.CostEstimate(
            flops=2 * edges * width * (2 * mesh_count + 2 * width),
            bytes_accessed=6 * edges * width,
            transcendentals=0,
        ),
        name="backward_edges",
    )(
        me,
        tile_count,
        dst,
        edge_latent,
        d_pre,
        d_aggregate,
        d_mesh,
        mesh_latent,
        grad_sender,
        w_edge_in,
        w_edge_in,
    )

    (node_pieces, slot_next, slot_kept, returned, edge_send, edge_keep) = lax.optimization_barrier(
        (node_pieces, slot_next, slot_kept, returned, edge_send, edge_keep)
    )
    slot_pieces = next_sum(peers, slot_next, slot_kept)
    edge_next, edge_kept = core_sum(peers, edge_send, edge_keep)
    node_terms = node_last(peers, node_pieces)
    returned = core_near(peers, returned)
    edge_pieces = next_sum(peers, edge_next, edge_kept)
    slot_terms = last_terms(peers, slot_pieces)
    edge_terms = last_terms(peers, edge_pieces)
    node_rows = w_node_in.shape[0] // peers
    out_rows = w_edge_out.shape[0] // peers
    grid_grad = pl.pallas_call(
        functools.partial(scatter_kernel, out_rows),
        grid=(2,),
        in_specs=[smem, whole(rows.shape)]
        + core_specs
        + [whole((out_rows + cap, width))] * upper,
        out_specs=pl.BlockSpec((grid_part, width), lambda step: (step, 0)),
        out_shape=jax.ShapeDtypeStruct((grid_count, width), BF16),
        compiler_params=params,
        name="scatter_lists",
    )(me, rows, *returned, *slot_terms)
    return (
        grid_grad,
        edge_grad,
        mesh_grad,
        total_of(edge_terms, 0, w_edge_in.shape[0] // peers),
        total_of(slot_terms, 0, out_rows),
        total_of(node_terms, 0, node_rows),
        total_of(node_terms, node_rows, node_rows + w_node_out.shape[0] // peers),
    )


def solution(mesh):
    rows = P(("grp", "lon"), None)
    flat = P(("grp", "lon"))
    return jax.shard_map(
        on_device,
        mesh=mesh,
        in_specs=(rows, rows, rows, rows, flat, flat, flat, P(("grp", "lon"), None, None)) + (P(),) * 4,
        out_specs=(rows,) * 7,
        check_vma=False,
    )
```

```python
import functools

import jax
import jax.numpy as jnp
from jax import lax
from jax.experimental import pallas as pl
from jax.experimental.pallas import tpu as pltpu
from jax.sharding import PartitionSpec as P

TILE = 256
STEP = 1024
SUB = 512
LANES = 128
NEAR = 3
BF16 = jnp.bfloat16
F32 = jnp.float32
VMEM_BYTES = 56 * 1024 * 1024


def dot(left, right):
    return lax.dot_general(left, right, (((1,), (0,)), ((), ())), preferred_element_type=F32)


def contract_rows(left, right):
    return lax.dot_general(left, right, (((0,), (0,)), ((), ())), preferred_element_type=F32)


def contract_cols(left, right):
    return lax.dot_general(left, right, (((1,), (1,)), ((), ())), preferred_element_type=F32)


def layer_norm(values):
    centered = values - jnp.mean(values, axis=1, keepdims=True)
    inverse = lax.rsqrt(jnp.mean(centered * centered, axis=1, keepdims=True) + 1e-05)
    return (centered * inverse, inverse)


def norm_back(normed, inverse, upstream):
    first = jnp.mean(upstream, axis=1, keepdims=True)
    second = jnp.mean(upstream * normed, axis=1, keepdims=True)
    return inverse * (upstream - first - normed * second)


def silu_and_slope(values):
    sigma = 0.5 + 0.5 * jnp.tanh(0.5 * values)
    hidden = values * sigma
    return (hidden, sigma + hidden * (1.0 - sigma))


def as_column(row):
    count = row.shape[1]
    block = min(count, LANES)
    down = lax.broadcasted_iota(jnp.int32, (block, block), 0)
    along = lax.broadcasted_iota(jnp.int32, (block, block), 1)
    columns = []
    for start in range(0, count, block):
        piece = row[:, start : start + block].astype(F32)
        picked = jnp.where(down == along, piece, 0.0)
        columns.append(jnp.sum(picked, axis=1, keepdims=True))
    return jnp.concatenate(columns, axis=0)


def as_row(column):
    count = column.shape[0]
    block = min(count, LANES)
    down = lax.broadcasted_iota(jnp.int32, (block, block), 0)
    along = lax.broadcasted_iota(jnp.int32, (block, block), 1)
    rows = []
    for start in range(0, count, block):
        picked = jnp.where(down == along, column[start : start + block], 0.0)
        rows.append(jnp.sum(picked, axis=0, keepdims=True))
    return jnp.concatenate(rows, axis=1)


def hot_rows(row, width, first=0):
    column = as_column(row).astype(jnp.int32) - first
    along = lax.broadcasted_iota(jnp.int32, (row.shape[1], width), 1)
    return (column == along).astype(F32).astype(BF16)


def hot_columns(row, height):
    down = lax.broadcasted_iota(jnp.int32, (height, row.shape[1]), 0)
    return (row == down).astype(F32).astype(BF16)


def live_only(row, first, count):
    place = first + lax.broadcasted_iota(jnp.int32, row.shape, 1)
    return jnp.where(place < count, row, -1)


def near_peers(me, peers):
    after = lax.rem(me + 2, peers)
    before = lax.rem(me + peers - 2, peers)
    across = lax.rem(me + peers - 3 + 6 * (me & 1), peers)
    return (me, me ^ 1, after, after ^ 1, before, before ^ 1, across)


def write_near(refs, cap, lists):
    mine, other, after, before, across = refs
    mine[...] = lists[0]
    other[...] = lists[1]
    after[:cap, :] = lists[2]
    after[cap:, :] = lists[3]
    before[:cap, :] = lists[4]
    before[cap:, :] = lists[5]
    across[...] = lists[6]


def read_near(refs, cap):
    mine, other, from_before, from_after, across, core_before, core_after = refs
    return [
        mine[...],
        other[...],
        from_after[:cap, :],
        core_after[cap:, :],
        from_before[:cap, :],
        core_before[cap:, :],
        across[...],
    ]


def list_hots(me, rows_ref, grid_count, first):
    peers, cap = rows_ref.shape
    pieces = []
    for target in near_peers(me, peers):
        pieces.append(hot_rows(rows_ref[pl.ds(target, 1), :], grid_count, first))
    peer = lax.broadcasted_iota(jnp.int32, (peers, cap), 0)
    ahead = lax.rem(peer - me + peers, peers)
    apart = jnp.minimum(ahead, peers - ahead)
    far = jnp.max(jnp.where(apart > NEAR, rows_ref[...].astype(F32), -1.0), axis=0, keepdims=True)
    pieces.append(hot_rows(far.astype(jnp.int32), grid_count, first))
    return jnp.concatenate(pieces, axis=0)


def gather_kernel(me_ref, rows_ref, grid_ref, *refs):
    near_refs, far_ref, total = refs[:5], refs[5], refs[6]
    cap = rows_ref.shape[1]
    step = pl.program_id(0)
    part = grid_ref.shape[0]
    found = dot(list_hots(me_ref[0], rows_ref, part, step * part), grid_ref[...])

    @pl.when(step == 0)
    def _():
        total[...] = found

    @pl.when(step == pl.num_programs(0) - 1)
    def _():
        rows = (total[...] + found).astype(BF16)
        lists = [rows[at : at + cap] for at in range(0, 8 * cap, cap)]
        write_near(near_refs, cap, lists)
        far_ref[...] = lists[7]


def scatter_kernel(skip, me_ref, rows_ref, *refs):
    near_refs, far_refs, out_ref = refs[:7], refs[7:-1], refs[-1]
    part = out_ref.shape[0]
    cap = rows_ref.shape[1]
    hots = list_hots(me_ref[0], rows_ref, part, pl.program_id(0) * part)
    far = far_refs[0][skip:, :].astype(F32)
    for ref in far_refs[1:]:
        far = far + ref[skip:, :].astype(F32)
    values = jnp.concatenate(read_near(near_refs, cap) + [far.astype(BF16)], axis=0)
    out_ref[...] = contract_rows(hots, values).astype(BF16)


def halves_of(ref):
    rows = ref.shape[-1] if len(ref.shape) == 3 else ref.shape[0]
    return [(start, slice(start, start + SUB)) for start in range(0, rows, SUB)]


def local_kernel(dst_ref, edge_ref, mesh_ref, w_edge_ref, w_receiver_ref, *refs):
    out_ref, mesh_proj = refs[-2:]

    @pl.when(pl.program_id(0) == 0)
    def _():
        mesh_proj[...] = dot(mesh_ref[...], w_receiver_ref[...]).astype(BF16)

    for start, part in halves_of(edge_ref):
        onehot = hot_rows(dst_ref[0, :, part], mesh_ref.shape[0])
        out_ref[part, :] = (
            dot(edge_ref[part, :], w_edge_ref[...]) + dot(onehot, mesh_proj[...])
        ).astype(BF16)


def split_out(me, peers, first, send_ref, keep_ref, parts):
    for low in range(4):
        target = send_ref if low & first else keep_ref
        half = 1 if low & (3 - first) else 0
        at = 0
        for upper in range(peers // 4):
            owner = me ^ (4 * upper + low)
            for ref, share, far in parts:
                piece = ref[pl.ds(pl.multiple_of(owner * share, 16), share), :]
                if far:
                    ahead = lax.rem(owner - me + peers, peers)
                    apart = jnp.minimum(ahead, peers - ahead)
                    piece = jnp.where(apart > NEAR, piece.astype(F32), 0.0)
                target[half, at : at + share, :] = piece.astype(BF16)
                at += share


def forward_kernel(
    peers, me_ref, count_ref, src_ref, dst_ref, local_ref, edge_ref, *refs
):
    near_refs, far_refs = refs[:7], refs[7:11]
    (w_sender_ref, w_out_ref, w_node_in_ref, w_node_out_ref, mesh_ref, cotangent_ref) = refs[11:17]
    (received_ref, hidden_ref, slope_ref, norm_ref, inverse_ref) = refs[17:22]
    (send_ref, keep_ref, d_aggregate_ref, d_mesh_ref) = refs[22:26]
    (slot_proj, aggregate, grad_in, grad_out) = refs[26:]
    step = pl.program_id(0)
    me = me_ref[0]
    cap = near_refs[0].shape[0]
    width = edge_ref.shape[1]

    @pl.when(step == 0)
    def _():
        aggregate[...] = jnp.zeros_like(aggregate)
        w_sender = w_sender_ref[...]

        def place(owner, rows, projected):
            offset = pl.multiple_of(owner * cap, 16)
            received_ref[pl.ds(offset, cap), :] = rows
            slot_proj[pl.ds(offset, cap), :] = projected

        for low, ref in enumerate(far_refs):
            rows = ref[...]
            projected = dot(rows, w_sender).astype(BF16)
            for upper in range(peers // 4):
                span = slice(upper * cap, (upper + 1) * cap)
                place(me ^ (4 * upper + low), rows[span], projected[span])
        rows = jnp.concatenate(read_near(near_refs, cap), axis=0)
        projected = dot(rows, w_sender).astype(BF16)
        for spot, owner in enumerate(near_peers(me, peers)):
            place(owner, rows[spot * cap : (spot + 1) * cap], projected[spot * cap : (spot + 1) * cap])

    @pl.when(step * STEP < count_ref[0] * TILE)
    def _():
        parts = halves_of(edge_ref)
        pres = []
        for start, part in parts:
            onehot = hot_rows(src_ref[0, :, part], slot_proj.shape[0])
            pres.append(local_ref[part, :].astype(F32) + dot(onehot, slot_proj[...]))
        projs = []
        for (start, part), pre in zip(parts, pres):
            hidden, slope = silu_and_slope(pre)
            hidden = hidden.astype(BF16)
            hidden_ref[part, :] = hidden
            slope_ref[part, :] = slope.astype(BF16)
            projs.append(dot(hidden, w_out_ref[...]))
        for (start, part), proj in zip(parts, projs):
            normed, inverse = layer_norm(proj)
            norm_ref[part, :] = normed.astype(BF16)
            inverse_ref[0, :, part] = as_row(inverse)
            edge_new = (edge_ref[part, :].astype(F32) + normed).astype(BF16)
            receivers = live_only(dst_ref[0, :, part], step * STEP + start, count_ref[0] * TILE)
            aggregate[...] += dot(hot_columns(receivers, aggregate.shape[0]), edge_new)

    @pl.when(step == pl.num_programs(0) - 1)
    def _():
        mesh = mesh_ref[...]
        summed = aggregate[...].astype(BF16)
        node_pre = dot(mesh, w_node_in_ref[:width, :]) + dot(summed, w_node_in_ref[width:, :])
        hidden, slope = silu_and_slope(node_pre)
        hidden = hidden.astype(BF16)
        normed, inverse = layer_norm(dot(hidden, w_node_out_ref[...]))
        upstream = cotangent_ref[...].astype(F32)
        d_proj = norm_back(normed, inverse, upstream).astype(BF16)
        d_pre = (contract_cols(d_proj, w_node_out_ref[...]) * slope).astype(BF16)
        d_mesh_ref[...] = upstream + contract_cols(d_pre, w_node_in_ref[:width, :])
        d_aggregate_ref[...] = contract_cols(d_pre, w_node_in_ref[width:, :]).astype(BF16)
        grad_out[...] = contract_rows(hidden, d_proj)
        grad_in[:width, :] = contract_rows(mesh, d_pre)
        grad_in[width:, :] = contract_rows(summed, d_pre)
        split_out(
            me,
            peers,
            2,
            send_ref,
            keep_ref,
            ((grad_in, grad_in.shape[0] // peers, False), (grad_out, grad_out.shape[0] // peers, False)),
        )


def backward_kernel(peers, me_ref, count_ref, src_ref, dst_ref, inverse_ref, *refs):
    (hidden_ref, slope_ref, norm_ref, edge_ref) = refs[:4]
    (d_aggregate_ref, received_ref, mesh_ref, d_mesh_ref) = refs[4:8]
    (w_sender_ref, w_receiver_ref, w_out_ref) = refs[8:11]
    (d_pre_ref, mesh_grad_ref, slot_send_ref, slot_keep_ref, edge_send_ref, edge_keep_ref) = refs[11:17]
    near_refs = refs[17:22]
    (end_sum, grad_in, grad_out, d_slots) = refs[22:]
    step = pl.program_id(0)
    me = me_ref[0]
    slots, width = received_ref.shape
    mesh_count = mesh_ref.shape[0]

    @pl.when(step == 0)
    def _():
        end_sum[...] = jnp.zeros_like(end_sum)
        grad_in[:width, :] = jnp.zeros((width, width), F32)
        grad_out[...] = jnp.zeros_like(grad_out)

    @pl.when(step * STEP < count_ref[0] * TILE)
    def _():
        parts = halves_of(hidden_ref)
        upstreams = []
        columns = []
        for start, part in parts:
            first = step * STEP + start
            live = count_ref[0] * TILE
            receivers = live_only(dst_ref[0, :, part], first, live)
            upstreams.append(dot(hot_rows(receivers, mesh_count), d_aggregate_ref[...]))
            senders = live_only(src_ref[0, :, part], first, live)
            columns.append(
                jnp.concatenate([hot_columns(senders, slots), hot_columns(receivers, mesh_count)], axis=0)
            )
        d_projs = []
        d_hiddens = []
        for (start, part), upstream in zip(parts, upstreams):
            inverse = as_column(inverse_ref[0, :, part])
            d_proj = norm_back(norm_ref[part, :].astype(F32), inverse, upstream).astype(BF16)
            d_projs.append(d_proj)
            d_hiddens.append(contract_cols(d_proj, w_out_ref[...]))
        for (start, part), d_proj, d_hidden, column in zip(parts, d_projs, d_hiddens, columns):
            grad_out[...] += contract_rows(hidden_ref[part, :], d_proj)
            d_pre = (d_hidden * slope_ref[part, :].astype(F32)).astype(BF16)
            d_pre_ref[part, :] = d_pre
            end_sum[...] += dot(column, d_pre)
            grad_in[:width, :] += contract_rows(edge_ref[part, :], d_pre)

    @pl.when(step == pl.num_programs(0) - 1)
    def _():
        summed = end_sum[:slots, :].astype(BF16)
        mesh_summed = end_sum[slots:, :].astype(BF16)
        d_slots[...] = contract_cols(summed, w_sender_ref[...]).astype(BF16)
        grad_in[width : 2 * width, :] = contract_rows(received_ref[...], summed)
        grad_in[2 * width :, :] = contract_rows(mesh_ref[...], mesh_summed)
        mesh_grad_ref[...] = (d_mesh_ref[...] + contract_cols(mesh_summed, w_receiver_ref[...])).astype(BF16)
        cap = near_refs[0].shape[0]
        owners = near_peers(me, peers)
        write_near(
            near_refs, cap, [d_slots[pl.ds(pl.multiple_of(owner * cap, 16), cap), :] for owner in owners]
        )
        out_share = grad_out.shape[0] // peers
        split_out(
            me, peers, 1, slot_send_ref, slot_keep_ref, ((grad_out, out_share, False), (d_slots, cap, True))
        )
        split_out(
            me, peers, 1, edge_send_ref, edge_keep_ref, ((grad_in, grad_in.shape[0] // peers, False),)
        )


def edges_kernel(count_ref, dst_ref, d_pre_ref, d_aggregate_ref, w_edge_ref, edge_grad_ref):
    step = pl.program_id(0)

    @pl.when(step * STEP < count_ref[0] * TILE)
    def _():
        for start, part in halves_of(d_pre_ref):
            receivers = live_only(dst_ref[0, :, part], step * STEP + start, count_ref[0] * TILE)
            upstream = dot(hot_rows(receivers, d_aggregate_ref.shape[0]), d_aggregate_ref[...])
            edge_grad_ref[part, :] = (upstream + contract_cols(d_pre_ref[part, :], w_edge_ref[...])).astype(BF16)

    @pl.when(step * STEP >= count_ref[0] * TILE)
    def _():
        edge_grad_ref[...] = jnp.zeros_like(edge_grad_ref)


def send(values, perm):
    return lax.ppermute(values, "lon", perm)


def by_xor(peers, bits):
    return [(peer, peer ^ bits) for peer in range(peers)]


def by_shift(peers, shift):
    return [(peer, (peer + shift) % peers) for peer in range(peers)]


def across_chips(peers):
    return [(peer, (peer + (3 if peer % 2 else -3)) % peers) for peer in range(peers)]


def exchange_near(peers, lists):
    mine, other, after, before, across = lists
    return [
        mine,
        other,
        send(after, by_shift(peers, 2)),
        send(before, by_shift(peers, -2)),
        send(across, across_chips(peers)),
    ]


def core_near(peers, near):
    mine, other, after, before, across = near
    swap = by_xor(peers, 1)
    return [mine, send(other, swap), after, before, across, send(after, swap), send(before, swap)]


def add(left, right):
    return (left.astype(F32) + right.astype(F32)).astype(BF16)


def first_sum(peers, bit, outgoing, kept):
    arrived = send(outgoing, by_xor(peers, bit))
    return add(kept[1], arrived[1]), add(kept[0], arrived[0])


def next_sum(peers, bit, outgoing, kept):
    return add(kept, send(outgoing, by_xor(peers, bit)))


def last_terms(peers, pieces):
    count = peers // 4
    share = pieces.shape[0] // count
    terms = [pieces[:share]]
    for place in range(1, count):
        piece = pieces[place * share : (place + 1) * share]
        terms.append(send(piece, by_xor(peers, 4 * place)))
    return terms


def halve_first(peers, pieces):
    count = peers // 4
    share = pieces.shape[0] // count
    blocks = pieces.reshape(count // 2, 2, share, -1)
    return blocks[:, 0].reshape(-1, pieces.shape[1]), blocks[:, 1].reshape(-1, pieces.shape[1])


def node_last(peers, pieces):
    count = peers // 8
    share = pieces.shape[0] // count
    terms = [pieces[:share]]
    for place in range(1, count):
        piece = pieces[place * share : (place + 1) * share]
        terms.append(send(piece, by_xor(peers, 8 * place)))
    return terms


def total_of(terms, start, stop):
    total = terms[0][start:stop].astype(F32)
    for term in terms[1:]:
        total = total + term[start:stop].astype(F32)
    return total


def whole(shape):
    return pl.BlockSpec(shape, lambda *_: (0,) * len(shape))


def on_device(
    grid_latent,
    mesh_latent,
    edge_latent,
    mesh_cotangent,
    edge_src,
    edge_dst,
    tile_count,
    send_rows,
    w_edge_in,
    w_edge_out,
    w_node_in,
    w_node_out,
):
    peers = lax.axis_size("lon")
    me = lax.axis_index("lon").astype(jnp.int32).reshape(1)
    upper = peers // 4
    rows = send_rows[0]
    cap = rows.shape[1]
    slots = peers * cap
    edges, width = edge_latent.shape
    mesh_count = mesh_latent.shape[0]
    grid_count = grid_latent.shape[0]
    tiles = edges // STEP
    src = edge_src.reshape(tiles, 1, STEP)
    dst = edge_dst.reshape(tiles, 1, STEP)
    smem = pl.BlockSpec(memory_space=pltpu.SMEM)
    params = pltpu.CompilerParams(vmem_limit_bytes=VMEM_BYTES)
    square = (width, width)

    def tile_of(last):
        return pl.BlockSpec((STEP, last), lambda step, *_: (step, 0))

    index_tile = pl.BlockSpec((1, 1, STEP), lambda step, *_: (step, 0, 0))

    def weight(place):
        return pl.BlockSpec(square, lambda *_: (place, 0))

    def halves(share):
        shape = (2, upper * share, width)
        return [jax.ShapeDtypeStruct(shape, BF16)] * 2, [whole(shape)] * 2

    grid_part = grid_count // 2
    near_rows = (cap, cap, 2 * cap, 2 * cap, cap)
    near_specs = [whole((count, width)) for count in near_rows]
    near_shapes = [jax.ShapeDtypeStruct((count, width), BF16) for count in near_rows]
    core_specs = near_specs + [whole((2 * cap, width))] * 2
    lists = pl.pallas_call(
        gather_kernel,
        grid=(2,),
        in_specs=[smem, whole(rows.shape), pl.BlockSpec((grid_part, width), lambda step: (step, 0))],
        out_specs=near_specs + [whole((cap, width))],
        out_shape=near_shapes + [jax.ShapeDtypeStruct((cap, width), BF16)],
        scratch_shapes=[pltpu.VMEM((8 * cap, width), F32)],
        compiler_params=params,
        name="gather_lists",
    )(me, rows, grid_latent)

    hops = [send(lists[5], by_xor(peers, 4 * place)) for place in range(1, upper)]
    near = exchange_near(peers, lists[:5])
    far_own = jnp.concatenate([lists[5]] + hops, axis=0)
    far_own, receivers = lax.optimization_barrier((far_own, dst))
    far_next = send(far_own, by_xor(peers, 2))
    far_core = send(far_own, by_xor(peers, 1))
    local = pl.pallas_call(
        local_kernel,
        grid=(tiles,),
        in_specs=[index_tile, tile_of(width), whole(mesh_latent.shape), weight(0), weight(2)],
        out_specs=tile_of(width),
        out_shape=jax.ShapeDtypeStruct((edges, width), BF16),
        scratch_shapes=[pltpu.VMEM((mesh_count, width), BF16)],
        compiler_params=params,
        cost_estimate=pl.CostEstimate(
            flops=2 * edges * width * (width + mesh_count),
            bytes_accessed=4 * edges * width,
            transcendentals=0,
        ),
        name="edge_local",
    )(receivers, edge_latent, mesh_latent, w_edge_in, w_edge_in)
    far_next, far_core, near, local = lax.optimization_barrier((far_next, far_core, near, local))
    near = core_near(peers, near)
    far_both = send(far_next, by_xor(peers, 1))

    node_shape, node_spec = halves(w_node_in.shape[0] // peers + w_node_out.shape[0] // peers)
    (received, hidden, slope, norm, inverse, node_send, node_keep, d_aggregate, d_mesh) = pl.pallas_call(
        functools.partial(forward_kernel, peers),
        grid=(tiles,),
        in_specs=[smem, smem, index_tile, index_tile, tile_of(width), tile_of(width)]
        + core_specs
        + [whole((upper * cap, width))] * 4
        + [weight(1)]
        + [whole(w.shape) for w in (w_edge_out, w_node_in, w_node_out, mesh_latent, mesh_cotangent)],
        out_specs=[whole((slots, width))]
        + [tile_of(width)] * 3
        + [index_tile]
        + node_spec
        + [whole((mesh_count, width))] * 2,
        out_shape=[jax.ShapeDtypeStruct((slots, width), BF16)]
        + [jax.ShapeDtypeStruct((edges, width), BF16)] * 3
        + [jax.ShapeDtypeStruct((tiles, 1, STEP), F32)]
        + node_shape
        + [jax.ShapeDtypeStruct((mesh_count, width), BF16), jax.ShapeDtypeStruct((mesh_count, width), F32)],
        scratch_shapes=[
            pltpu.VMEM((slots, width), BF16),
            pltpu.VMEM((mesh_count, width), F32),
            pltpu.VMEM(w_node_in.shape, F32),
            pltpu.VMEM(w_node_out.shape, F32),
        ],
        compiler_params=params,
        name="forward",
    )(
        me,
        tile_count,
        src,
        dst,
        local,
        edge_latent,
        *near,
        far_own,
        far_core,
        far_next,
        far_both,
        w_edge_in,
        w_edge_out,
        w_node_in,
        w_node_out,
        mesh_latent,
        mesh_cotangent,
    )

    node_next, node_kept = first_sum(peers, 2, node_send, node_keep)
    slot_shape, slot_spec = halves(w_edge_out.shape[0] // peers + cap)
    edge_shape, edge_spec = halves(w_edge_in.shape[0] // peers)
    results = pl.pallas_call(
        functools.partial(backward_kernel, peers),
        grid=(tiles,),
        in_specs=[smem, smem, index_tile, index_tile, index_tile]
        + [tile_of(width)] * 4
        + [whole((mesh_count, width)), whole((slots, width))]
        + [whole((mesh_count, width))] * 2
        + [weight(1), weight(2), whole(square)],
        out_specs=[tile_of(width), whole((mesh_count, width))] + slot_spec + edge_spec + near_specs,
        out_shape=[
            jax.ShapeDtypeStruct((edges, width), BF16),
            jax.ShapeDtypeStruct((mesh_count, width), BF16),
        ]
        + slot_shape
        + edge_shape
        + near_shapes,
        scratch_shapes=[
            pltpu.VMEM((slots + mesh_count, width), F32),
            pltpu.VMEM(w_edge_in.shape, F32),
            pltpu.VMEM(square, F32),
            pltpu.VMEM((slots, width), BF16),
        ],
        compiler_params=params,
        cost_estimate=pl.CostEstimate(
            flops=2 * edges * width * (2 * mesh_count + 3 * width + slots),
            bytes_accessed=10 * edges * width,
            transcendentals=0,
        ),
        name="backward",
    )(
        me,
        tile_count,
        src,
        dst,
        inverse,
        hidden,
        slope,
        norm,
        edge_latent,
        d_aggregate,
        received,
        mesh_latent,
        d_mesh,
        w_edge_in,
        w_edge_in,
        w_edge_out,
    )
    (d_pre, mesh_grad, slot_send, slot_keep, edge_send, edge_keep), returns = results[:6], results[6:]
    (node_next, node_kept, d_pre, slot_send, slot_keep, edge_send, edge_keep, returns) = lax.optimization_barrier(
        (node_next, node_kept, d_pre, slot_send, slot_keep, edge_send, edge_keep, returns)
    )
    slot_next, slot_kept = first_sum(peers, 1, slot_send, slot_keep)
    edge_next, edge_kept = first_sum(peers, 1, edge_send, edge_keep)
    node_pieces = next_sum(peers, 1, node_next, node_kept)
    returned = exchange_near(peers, returns)
    (slot_next, slot_kept, edge_next, edge_kept, node_pieces, returned, d_pre) = lax.optimization_barrier(
        (slot_next, slot_kept, edge_next, edge_kept, node_pieces, returned, d_pre)
    )
    slot_pieces = next_sum(peers, 2, slot_next, slot_kept)
    edge_pieces = next_sum(peers, 2, edge_next, edge_kept)
    node_kept, node_next = halve_first(peers, node_pieces)
    node_pieces = add(node_kept, send(node_next, by_xor(peers, 4)))
    edge_grad = pl.pallas_call(
        edges_kernel,
        grid=(tiles,),
        in_specs=[smem, index_tile, tile_of(width), whole((mesh_count, width)), weight(0)],
        out_specs=tile_of(width),
        out_shape=jax.ShapeDtypeStruct((edges, width), BF16),
        compiler_params=params,
        cost_estimate=pl.CostEstimate(
            flops=2 * edges * width * (mesh_count + width), bytes_accessed=4 * edges * width, transcendentals=0
        ),
        name="edge_grad",
    )(tile_count, dst, d_pre, d_aggregate, w_edge_in)
    node_pieces, slot_pieces, edge_grad = lax.optimization_barrier((node_pieces, slot_pieces, edge_grad))
    returned = core_near(peers, returned)
    slot_terms = last_terms(peers, slot_pieces)
    node_terms = node_last(peers, node_pieces)
    edge_terms = last_terms(peers, edge_pieces)
    node_terms, edge_terms[0] = lax.optimization_barrier((node_terms, edge_terms[0]))
    node_rows = w_node_in.shape[0] // peers
    out_rows = w_edge_out.shape[0] // peers
    grid_grad = pl.pallas_call(
        functools.partial(scatter_kernel, out_rows),
        grid=(2,),
        in_specs=[smem, whole(rows.shape)]
        + core_specs
        + [whole((out_rows + cap, width))] * upper,
        out_specs=pl.BlockSpec((grid_part, width), lambda step: (step, 0)),
        out_shape=jax.ShapeDtypeStruct((grid_count, width), BF16),
        compiler_params=params,
        name="scatter_lists",
    )(me, rows, *returned, *slot_terms)
    return (
        grid_grad,
        edge_grad,
        mesh_grad,
        total_of(edge_terms, 0, w_edge_in.shape[0] // peers),
        total_of(slot_terms, 0, out_rows),
        total_of(node_terms, 0, node_rows),
        total_of(node_terms, node_rows, node_rows + w_node_out.shape[0] // peers),
    )


def solution(mesh):
    rows = P(("grp", "lon"), None)
    flat = P(("grp", "lon"))
    return jax.shard_map(
        on_device,
        mesh=mesh,
        in_specs=(rows, rows, rows, rows, flat, flat, flat, P(("grp", "lon"), None, None)) + (P(),) * 4,
        out_specs=(rows,) * 7,
        check_vma=False,
    )
```

```python
import functools

import jax
import jax.numpy as jnp
from jax import lax
from jax.experimental import pallas as pl
from jax.experimental.pallas import tpu as pltpu
from jax.sharding import PartitionSpec as P

TILE = 256
STEP = 1024
SUB = 512
LANES = 128
NEAR = 3
BF16 = jnp.bfloat16
F32 = jnp.float32
VMEM_BYTES = 56 * 1024 * 1024


def dot(left, right):
    return lax.dot_general(left, right, (((1,), (0,)), ((), ())), preferred_element_type=F32)


def contract_rows(left, right):
    return lax.dot_general(left, right, (((0,), (0,)), ((), ())), preferred_element_type=F32)


def contract_cols(left, right):
    return lax.dot_general(left, right, (((1,), (1,)), ((), ())), preferred_element_type=F32)


def layer_norm(values):
    centered = values - jnp.mean(values, axis=1, keepdims=True)
    inverse = lax.rsqrt(jnp.mean(centered * centered, axis=1, keepdims=True) + 1e-05)
    return (centered * inverse, inverse)


def norm_back(normed, inverse, upstream):
    first = jnp.mean(upstream, axis=1, keepdims=True)
    second = jnp.mean(upstream * normed, axis=1, keepdims=True)
    return inverse * (upstream - first - normed * second)


def silu_and_slope(values):
    sigma = 0.5 + 0.5 * jnp.tanh(0.5 * values)
    hidden = values * sigma
    return (hidden, sigma + hidden * (1.0 - sigma))


def as_column(row):
    count = row.shape[1]
    block = min(count, LANES)
    down = lax.broadcasted_iota(jnp.int32, (block, block), 0)
    along = lax.broadcasted_iota(jnp.int32, (block, block), 1)
    columns = []
    for start in range(0, count, block):
        piece = row[:, start : start + block].astype(F32)
        picked = jnp.where(down == along, piece, 0.0)
        columns.append(jnp.sum(picked, axis=1, keepdims=True))
    return jnp.concatenate(columns, axis=0)


def as_row(column):
    count = column.shape[0]
    block = min(count, LANES)
    down = lax.broadcasted_iota(jnp.int32, (block, block), 0)
    along = lax.broadcasted_iota(jnp.int32, (block, block), 1)
    rows = []
    for start in range(0, count, block):
        picked = jnp.where(down == along, column[start : start + block], 0.0)
        rows.append(jnp.sum(picked, axis=0, keepdims=True))
    return jnp.concatenate(rows, axis=1)


def hot_rows(row, width, first=0):
    column = as_column(row).astype(jnp.int32) - first
    along = lax.broadcasted_iota(jnp.int32, (row.shape[1], width), 1)
    return (column == along).astype(F32).astype(BF16)


def hot_columns(row, height):
    down = lax.broadcasted_iota(jnp.int32, (height, row.shape[1]), 0)
    return (row == down).astype(F32).astype(BF16)


def live_only(row, first, count):
    place = first + lax.broadcasted_iota(jnp.int32, row.shape, 1)
    return jnp.where(place < count, row, -1)


def near_peers(me, peers):
    after = lax.rem(me + 2, peers)
    before = lax.rem(me + peers - 2, peers)
    across = lax.rem(me + peers - 3 + 6 * (me & 1), peers)
    return (me, me ^ 1, after, after ^ 1, before, before ^ 1, across)


def write_near(refs, cap, lists):
    mine, other, after, before, across = refs
    mine[...] = lists[0]
    other[...] = lists[1]
    after[:cap, :] = lists[2]
    after[cap:, :] = lists[3]
    before[:cap, :] = lists[4]
    before[cap:, :] = lists[5]
    across[...] = lists[6]


def read_near(refs, cap):
    mine, other, from_before, from_after, across, core_before, core_after = refs
    return [
        mine[...],
        other[...],
        from_after[:cap, :],
        core_after[cap:, :],
        from_before[:cap, :],
        core_before[cap:, :],
        across[...],
    ]


def write_back(refs, cap, lists):
    mine, swapped, after, before, across = refs
    mine[...] = lists[0]
    for place, index in enumerate((1, 3, 5)):
        swapped[place * cap : (place + 1) * cap, :] = lists[index]
    after[...] = lists[2]
    before[...] = lists[4]
    across[...] = lists[6]


def read_back(refs, cap):
    mine, swapped, from_before, from_after, across = refs
    return [
        mine[...],
        swapped[:cap, :],
        from_after[:cap, :],
        from_after[cap:, :],
        from_before[:cap, :],
        from_before[cap:, :],
        across[...],
    ]


def list_hots(me, rows_ref, grid_count, first):
    peers, cap = rows_ref.shape
    pieces = []
    for target in near_peers(me, peers):
        pieces.append(hot_rows(rows_ref[pl.ds(target, 1), :], grid_count, first))
    peer = lax.broadcasted_iota(jnp.int32, (peers, cap), 0)
    ahead = lax.rem(peer - me + peers, peers)
    apart = jnp.minimum(ahead, peers - ahead)
    far = jnp.max(jnp.where(apart > NEAR, rows_ref[...].astype(F32), -1.0), axis=0, keepdims=True)
    pieces.append(hot_rows(far.astype(jnp.int32), grid_count, first))
    return jnp.concatenate(pieces, axis=0)


def gather_kernel(me_ref, rows_ref, grid_ref, *refs):
    near_refs, far_ref, total = refs[:5], refs[5], refs[6]
    cap = rows_ref.shape[1]
    step = pl.program_id(0)
    part = grid_ref.shape[0]
    found = dot(list_hots(me_ref[0], rows_ref, part, step * part), grid_ref[...])

    @pl.when(step == 0)
    def _():
        total[...] = found

    @pl.when(step == pl.num_programs(0) - 1)
    def _():
        rows = (total[...] + found).astype(BF16)
        lists = [rows[at : at + cap] for at in range(0, 8 * cap, cap)]
        write_near(near_refs, cap, lists)
        far_ref[...] = lists[7]


def scatter_kernel(skip, me_ref, rows_ref, *refs):
    near_refs, far_refs, out_ref = refs[:5], refs[5:-1], refs[-1]
    part = out_ref.shape[0]
    cap = rows_ref.shape[1]
    hots = list_hots(me_ref[0], rows_ref, part, pl.program_id(0) * part)
    far = far_refs[0][skip:, :].astype(F32)
    for ref in far_refs[1:]:
        far = far + ref[skip:, :].astype(F32)
    values = jnp.concatenate(read_back(near_refs, cap) + [far.astype(BF16)], axis=0)
    out_ref[...] = contract_rows(hots, values).astype(BF16)


def halves_of(ref):
    rows = ref.shape[-1] if len(ref.shape) == 3 else ref.shape[0]
    return [(start, slice(start, start + SUB)) for start in range(0, rows, SUB)]


def local_kernel(dst_ref, edge_ref, mesh_ref, w_edge_ref, w_receiver_ref, out_ref, weights):
    width = edge_ref.shape[1]

    @pl.when(pl.program_id(0) == 0)
    def _():
        weights[:width, :] = w_edge_ref[...]
        weights[width:, :] = dot(mesh_ref[...], w_receiver_ref[...]).astype(BF16)

    for start, part in halves_of(edge_ref):
        onehot = hot_rows(dst_ref[0, :, part], mesh_ref.shape[0])
        joined = jnp.concatenate([edge_ref[part, :], onehot], axis=1)
        out_ref[part, :] = dot(joined, weights[...]).astype(BF16)


def split_out(me, peers, first, send_ref, keep_ref, parts):
    for low in range(4):
        target = send_ref if low & first else keep_ref
        half = 1 if low & (3 - first) else 0
        at = 0
        for upper in range(peers // 4):
            owner = me ^ (4 * upper + low)
            for ref, share, far in parts:
                piece = ref[pl.ds(pl.multiple_of(owner * share, 16), share), :]
                if far:
                    ahead = lax.rem(owner - me + peers, peers)
                    apart = jnp.minimum(ahead, peers - ahead)
                    piece = jnp.where(apart > NEAR, piece.astype(F32), 0.0)
                target[half, at : at + share, :] = piece.astype(BF16)
                at += share


def forward_kernel(
    peers, me_ref, count_ref, src_ref, dst_ref, local_ref, edge_ref, *refs
):
    near_refs, far_refs = refs[:7], refs[7:11]
    (w_sender_ref, w_out_ref, w_node_in_ref, w_node_out_ref, mesh_ref, cotangent_ref) = refs[11:17]
    (received_ref, hidden_ref, slope_ref, norm_ref, inverse_ref) = refs[17:22]
    (send_ref, keep_ref, d_aggregate_ref, d_mesh_ref) = refs[22:26]
    (slot_proj, aggregate, grad_in, grad_out) = refs[26:]
    step = pl.program_id(0)
    me = me_ref[0]
    cap = near_refs[0].shape[0]
    width = edge_ref.shape[1]

    @pl.when(step == 0)
    def _():
        aggregate[...] = jnp.zeros_like(aggregate)
        w_sender = w_sender_ref[...]

        def place(owner, rows, projected):
            offset = pl.multiple_of(owner * cap, 16)
            received_ref[pl.ds(offset, cap), :] = rows
            slot_proj[pl.ds(offset, cap), :] = projected

        for low, ref in enumerate(far_refs):
            rows = ref[...]
            projected = dot(rows, w_sender).astype(BF16)
            for upper in range(peers // 4):
                span = slice(upper * cap, (upper + 1) * cap)
                place(me ^ (4 * upper + low), rows[span], projected[span])
        rows = jnp.concatenate(read_near(near_refs, cap), axis=0)
        projected = dot(rows, w_sender).astype(BF16)
        for spot, owner in enumerate(near_peers(me, peers)):
            place(owner, rows[spot * cap : (spot + 1) * cap], projected[spot * cap : (spot + 1) * cap])

    @pl.when(step * STEP < count_ref[0] * TILE)
    def _():
        parts = halves_of(edge_ref)
        pres = []
        for start, part in parts:
            onehot = hot_rows(src_ref[0, :, part], slot_proj.shape[0])
            pres.append(local_ref[part, :].astype(F32) + dot(onehot, slot_proj[...]))
        projs = []
        for (start, part), pre in zip(parts, pres):
            hidden, slope = silu_and_slope(pre)
            hidden = hidden.astype(BF16)
            hidden_ref[part, :] = hidden
            slope_ref[part, :] = slope.astype(BF16)
            projs.append(dot(hidden, w_out_ref[...]))
        for (start, part), proj in zip(parts, projs):
            normed, inverse = layer_norm(proj)
            norm_ref[part, :] = normed.astype(BF16)
            inverse_ref[0, :, part] = as_row(inverse)
            edge_new = (edge_ref[part, :].astype(F32) + normed).astype(BF16)
            receivers = live_only(dst_ref[0, :, part], step * STEP + start, count_ref[0] * TILE)
            aggregate[...] += dot(hot_columns(receivers, aggregate.shape[0]), edge_new)

    @pl.when(step == pl.num_programs(0) - 1)
    def _():
        mesh = mesh_ref[...]
        summed = aggregate[...].astype(BF16)
        node_pre = dot(mesh, w_node_in_ref[:width, :]) + dot(summed, w_node_in_ref[width:, :])
        hidden, slope = silu_and_slope(node_pre)
        hidden = hidden.astype(BF16)
        normed, inverse = layer_norm(dot(hidden, w_node_out_ref[...]))
        upstream = cotangent_ref[...].astype(F32)
        d_proj = norm_back(normed, inverse, upstream).astype(BF16)
        d_pre = (contract_cols(d_proj, w_node_out_ref[...]) * slope).astype(BF16)
        d_mesh_ref[...] = upstream + contract_cols(d_pre, w_node_in_ref[:width, :])
        d_aggregate_ref[...] = contract_cols(d_pre, w_node_in_ref[width:, :]).astype(BF16)
        grad_out[...] = contract_rows(hidden, d_proj)
        grad_in[:width, :] = contract_rows(mesh, d_pre)
        grad_in[width:, :] = contract_rows(summed, d_pre)
        split_out(
            me,
            peers,
            2,
            send_ref,
            keep_ref,
            ((grad_in, grad_in.shape[0] // peers, False), (grad_out, grad_out.shape[0] // peers, False)),
        )


def backward_kernel(peers, me_ref, count_ref, src_ref, dst_ref, inverse_ref, *refs):
    (hidden_ref, slope_ref, norm_ref, edge_ref) = refs[:4]
    (d_aggregate_ref, received_ref, mesh_ref, d_mesh_ref) = refs[4:8]
    (w_sender_ref, w_receiver_ref, w_out_ref) = refs[8:11]
    (d_pre_ref, mesh_grad_ref, slot_send_ref, slot_keep_ref, edge_send_ref, edge_keep_ref) = refs[11:17]
    near_refs = refs[17:22]
    (end_sum, grad_in, grad_out, d_slots) = refs[22:]
    step = pl.program_id(0)
    me = me_ref[0]
    slots, width = received_ref.shape
    mesh_count = mesh_ref.shape[0]

    @pl.when(step == 0)
    def _():
        end_sum[...] = jnp.zeros_like(end_sum)
        grad_in[:width, :] = jnp.zeros((width, width), F32)
        grad_out[...] = jnp.zeros_like(grad_out)

    @pl.when(step * STEP < count_ref[0] * TILE)
    def _():
        parts = halves_of(hidden_ref)
        upstreams = []
        columns = []
        for start, part in parts:
            first = step * STEP + start
            live = count_ref[0] * TILE
            receivers = live_only(dst_ref[0, :, part], first, live)
            upstreams.append(dot(hot_rows(receivers, mesh_count), d_aggregate_ref[...]))
            senders = live_only(src_ref[0, :, part], first, live)
            columns.append(
                jnp.concatenate([hot_columns(senders, slots), hot_columns(receivers, mesh_count)], axis=0)
            )
        d_projs = []
        d_hiddens = []
        for (start, part), upstream in zip(parts, upstreams):
            inverse = as_column(inverse_ref[0, :, part])
            d_proj = norm_back(norm_ref[part, :].astype(F32), inverse, upstream).astype(BF16)
            d_projs.append(d_proj)
            d_hiddens.append(contract_cols(d_proj, w_out_ref[...]))
        for (start, part), d_proj, d_hidden, column in zip(parts, d_projs, d_hiddens, columns):
            grad_out[...] += contract_rows(hidden_ref[part, :], d_proj)
            d_pre = (d_hidden * slope_ref[part, :].astype(F32)).astype(BF16)
            d_pre_ref[part, :] = d_pre
            end_sum[...] += dot(column, d_pre)
            grad_in[:width, :] += contract_rows(edge_ref[part, :], d_pre)

    @pl.when(step == pl.num_programs(0) - 1)
    def _():
        summed = end_sum[:slots, :].astype(BF16)
        mesh_summed = end_sum[slots:, :].astype(BF16)
        d_slots[...] = contract_cols(summed, w_sender_ref[...]).astype(BF16)
        grad_in[width : 2 * width, :] = contract_rows(received_ref[...], summed)
        grad_in[2 * width :, :] = contract_rows(mesh_ref[...], mesh_summed)
        mesh_grad_ref[...] = (d_mesh_ref[...] + contract_cols(mesh_summed, w_receiver_ref[...])).astype(BF16)
        cap = near_refs[0].shape[0]
        owners = near_peers(me, peers)
        write_back(
            near_refs, cap, [d_slots[pl.ds(pl.multiple_of(owner * cap, 16), cap), :] for owner in owners]
        )
        out_share = grad_out.shape[0] // peers
        split_out(
            me, peers, 1, slot_send_ref, slot_keep_ref, ((grad_out, out_share, False), (d_slots, cap, True))
        )
        split_out(
            me, peers, 1, edge_send_ref, edge_keep_ref, ((grad_in, grad_in.shape[0] // peers, False),)
        )


def edges_kernel(count_ref, dst_ref, d_pre_ref, d_aggregate_ref, w_edge_ref, edge_grad_ref):
    step = pl.program_id(0)

    @pl.when(step * STEP < count_ref[0] * TILE)
    def _():
        for start, part in halves_of(d_pre_ref):
            receivers = live_only(dst_ref[0, :, part], step * STEP + start, count_ref[0] * TILE)
            upstream = dot(hot_rows(receivers, d_aggregate_ref.shape[0]), d_aggregate_ref[...])
            edge_grad_ref[part, :] = (upstream + contract_cols(d_pre_ref[part, :], w_edge_ref[...])).astype(BF16)

    @pl.when(step * STEP >= count_ref[0] * TILE)
    def _():
        edge_grad_ref[...] = jnp.zeros_like(edge_grad_ref)


def send(values, perm):
    return lax.ppermute(values, "lon", perm)


def by_xor(peers, bits):
    return [(peer, peer ^ bits) for peer in range(peers)]


def by_shift(peers, shift):
    return [(peer, (peer + shift) % peers) for peer in range(peers)]


def across_chips(peers):
    return [(peer, (peer + (3 if peer % 2 else -3)) % peers) for peer in range(peers)]


def exchange_near(peers, lists):
    mine, other, after, before, across = lists
    return [
        mine,
        other,
        send(after, by_shift(peers, 2)),
        send(before, by_shift(peers, -2)),
        send(across, across_chips(peers)),
    ]


def core_near(peers, near):
    mine, other, after, before, across = near
    swap = by_xor(peers, 1)
    return [mine, send(other, swap), after, before, across, send(after, swap), send(before, swap)]


def add(left, right):
    return (left.astype(F32) + right.astype(F32)).astype(BF16)


def first_sum(peers, bit, outgoing, kept):
    arrived = send(outgoing, by_xor(peers, bit))
    return add(kept[1], arrived[1]), add(kept[0], arrived[0])


def next_sum(peers, bit, outgoing, kept):
    return add(kept, send(outgoing, by_xor(peers, bit)))


def last_terms(peers, pieces):
    count = peers // 4
    share = pieces.shape[0] // count
    terms = [pieces[:share]]
    for place in range(1, count):
        piece = pieces[place * share : (place + 1) * share]
        terms.append(send(piece, by_xor(peers, 4 * place)))
    return terms


def halve_sum(peers, pieces):
    count = peers // 4
    blocks = pieces.reshape(count // 2, 2, -1, pieces.shape[1])
    kept, outgoing = [blocks[:, place].reshape(-1, pieces.shape[1]) for place in range(2)]
    return add(kept, send(outgoing, by_xor(peers, 4)))


def rest_terms(peers, pieces):
    count = peers // 8
    share = pieces.shape[0] // count
    terms = [pieces[:share]]
    for place in range(1, count):
        piece = pieces[place * share : (place + 1) * share]
        terms.append(send(piece, by_xor(peers, 8 * place)))
    return terms


def total_of(terms, start, stop):
    total = terms[0][start:stop].astype(F32)
    for term in terms[1:]:
        total = total + term[start:stop].astype(F32)
    return total


def whole(shape):
    return pl.BlockSpec(shape, lambda *_: (0,) * len(shape))


def on_device(
    grid_latent,
    mesh_latent,
    edge_latent,
    mesh_cotangent,
    edge_src,
    edge_dst,
    tile_count,
    send_rows,
    w_edge_in,
    w_edge_out,
    w_node_in,
    w_node_out,
):
    peers = lax.axis_size("lon")
    me = lax.axis_index("lon").astype(jnp.int32).reshape(1)
    upper = peers // 4
    rows = send_rows[0]
    cap = rows.shape[1]
    slots = peers * cap
    edges, width = edge_latent.shape
    mesh_count = mesh_latent.shape[0]
    grid_count = grid_latent.shape[0]
    tiles = edges // STEP
    src = edge_src.reshape(tiles, 1, STEP)
    dst = edge_dst.reshape(tiles, 1, STEP)
    smem = pl.BlockSpec(memory_space=pltpu.SMEM)
    params = pltpu.CompilerParams(vmem_limit_bytes=VMEM_BYTES)
    square = (width, width)

    def tile_of(last):
        return pl.BlockSpec((STEP, last), lambda step, *_: (step, 0))

    index_tile = pl.BlockSpec((1, 1, STEP), lambda step, *_: (step, 0, 0))

    def weight(place):
        return pl.BlockSpec(square, lambda *_: (place, 0))

    def halves(share):
        shape = (2, upper * share, width)
        return [jax.ShapeDtypeStruct(shape, BF16)] * 2, [whole(shape)] * 2

    grid_part = grid_count // 2
    near_rows = (cap, cap, 2 * cap, 2 * cap, cap)
    near_specs = [whole((count, width)) for count in near_rows]
    near_shapes = [jax.ShapeDtypeStruct((count, width), BF16) for count in near_rows]
    core_specs = near_specs + [whole((2 * cap, width))] * 2
    back_rows = (cap, 3 * cap, cap, cap, cap)
    back_specs = [whole((count, width)) for count in back_rows]
    back_shapes = [jax.ShapeDtypeStruct((count, width), BF16) for count in back_rows]
    return_specs = [whole((count, width)) for count in (cap, 3 * cap, 2 * cap, 2 * cap, cap)]
    lists = pl.pallas_call(
        gather_kernel,
        grid=(2,),
        in_specs=[smem, whole(rows.shape), pl.BlockSpec((grid_part, width), lambda step: (step, 0))],
        out_specs=near_specs + [whole((cap, width))],
        out_shape=near_shapes + [jax.ShapeDtypeStruct((cap, width), BF16)],
        scratch_shapes=[pltpu.VMEM((8 * cap, width), F32)],
        compiler_params=params,
        name="gather_lists",
    )(me, rows, grid_latent)

    hops = [send(lists[5], by_xor(peers, 4 * place)) for place in range(1, upper)]
    near = exchange_near(peers, lists[:5])
    far_own = jnp.concatenate([lists[5]] + hops, axis=0)
    far_own, receivers = lax.optimization_barrier((far_own, dst))
    far_next = send(far_own, by_xor(peers, 2))
    far_core = send(far_own, by_xor(peers, 1))
    local = pl.pallas_call(
        local_kernel,
        grid=(tiles,),
        in_specs=[index_tile, tile_of(width), whole(mesh_latent.shape), weight(0), weight(2)],
        out_specs=tile_of(width),
        out_shape=jax.ShapeDtypeStruct((edges, width), BF16),
        scratch_shapes=[pltpu.VMEM((width + mesh_count, width), BF16)],
        compiler_params=params,
        cost_estimate=pl.CostEstimate(
            flops=2 * edges * width * (width + mesh_count),
            bytes_accessed=4 * edges * width,
            transcendentals=0,
        ),
        name="edge_local",
    )(receivers, edge_latent, mesh_latent, w_edge_in, w_edge_in)
    far_next, far_core, near, local = lax.optimization_barrier((far_next, far_core, near, local))
    near = core_near(peers, near)
    far_both = send(far_next, by_xor(peers, 1))

    node_shape, node_spec = halves(w_node_in.shape[0] // peers + w_node_out.shape[0] // peers)
    (received, hidden, slope, norm, inverse, node_send, node_keep, d_aggregate, d_mesh) = pl.pallas_call(
        functools.partial(forward_kernel, peers),
        grid=(tiles,),
        in_specs=[smem, smem, index_tile, index_tile, tile_of(width), tile_of(width)]
        + core_specs
        + [whole((upper * cap, width))] * 4
        + [weight(1)]
        + [whole(w.shape) for w in (w_edge_out, w_node_in, w_node_out, mesh_latent, mesh_cotangent)],
        out_specs=[whole((slots, width))]
        + [tile_of(width)] * 3
        + [index_tile]
        + node_spec
        + [whole((mesh_count, width))] * 2,
        out_shape=[jax.ShapeDtypeStruct((slots, width), BF16)]
        + [jax.ShapeDtypeStruct((edges, width), BF16)] * 3
        + [jax.ShapeDtypeStruct((tiles, 1, STEP), F32)]
        + node_shape
        + [jax.ShapeDtypeStruct((mesh_count, width), BF16), jax.ShapeDtypeStruct((mesh_count, width), F32)],
        scratch_shapes=[
            pltpu.VMEM((slots, width), BF16),
            pltpu.VMEM((mesh_count, width), F32),
            pltpu.VMEM(w_node_in.shape, F32),
            pltpu.VMEM(w_node_out.shape, F32),
        ],
        compiler_params=params,
        name="forward",
    )(
        me,
        tile_count,
        src,
        dst,
        local,
        edge_latent,
        *near,
        far_own,
        far_core,
        far_next,
        far_both,
        w_edge_in,
        w_edge_out,
        w_node_in,
        w_node_out,
        mesh_latent,
        mesh_cotangent,
    )

    node_next, node_kept = first_sum(peers, 2, node_send, node_keep)
    slot_shape, slot_spec = halves(w_edge_out.shape[0] // peers + cap)
    edge_shape, edge_spec = halves(w_edge_in.shape[0] // peers)
    results = pl.pallas_call(
        functools.partial(backward_kernel, peers),
        grid=(tiles,),
        in_specs=[smem, smem, index_tile, index_tile, index_tile]
        + [tile_of(width)] * 4
        + [whole((mesh_count, width)), whole((slots, width))]
        + [whole((mesh_count, width))] * 2
        + [weight(1), weight(2), whole(square)],
        out_specs=[tile_of(width), whole((mesh_count, width))] + slot_spec + edge_spec + back_specs,
        out_shape=[
            jax.ShapeDtypeStruct((edges, width), BF16),
            jax.ShapeDtypeStruct((mesh_count, width), BF16),
        ]
        + slot_shape
        + edge_shape
        + back_shapes,
        scratch_shapes=[
            pltpu.VMEM((slots + mesh_count, width), F32),
            pltpu.VMEM(w_edge_in.shape, F32),
            pltpu.VMEM(square, F32),
            pltpu.VMEM((slots, width), BF16),
        ],
        compiler_params=params,
        cost_estimate=pl.CostEstimate(
            flops=2 * edges * width * (2 * mesh_count + 3 * width + slots),
            bytes_accessed=10 * edges * width,
            transcendentals=0,
        ),
        name="backward",
    )(
        me,
        tile_count,
        src,
        dst,
        inverse,
        hidden,
        slope,
        norm,
        edge_latent,
        d_aggregate,
        received,
        mesh_latent,
        d_mesh,
        w_edge_in,
        w_edge_in,
        w_edge_out,
    )
    (d_pre, mesh_grad, slot_send, slot_keep, edge_send, edge_keep), returns = results[:6], results[6:]
    (node_next, node_kept, d_pre, slot_send, slot_keep, edge_send, edge_keep, returns) = lax.optimization_barrier(
        (node_next, node_kept, d_pre, slot_send, slot_keep, edge_send, edge_keep, returns)
    )
    slot_next, slot_kept = first_sum(peers, 1, slot_send, slot_keep)
    edge_next, edge_kept = first_sum(peers, 1, edge_send, edge_keep)
    node_pieces = next_sum(peers, 1, node_next, node_kept)
    swapped = send(returns[1], by_xor(peers, 1))
    (slot_next, slot_kept, edge_next, edge_kept, swapped) = lax.optimization_barrier(
        (slot_next, slot_kept, edge_next, edge_kept, swapped)
    )
    slot_pieces = next_sum(peers, 2, slot_next, slot_kept)
    edge_pieces = next_sum(peers, 2, edge_next, edge_kept)
    to_after = jnp.concatenate([returns[2], swapped[cap : 2 * cap]], axis=0)
    to_before = jnp.concatenate([returns[3], swapped[2 * cap :]], axis=0)
    node_pieces, d_pre, to_after, to_before = lax.optimization_barrier((node_pieces, d_pre, to_after, to_before))
    node_pieces = halve_sum(peers, node_pieces)
    edge_grad = pl.pallas_call(
        edges_kernel,
        grid=(tiles,),
        in_specs=[smem, index_tile, tile_of(width), whole((mesh_count, width)), weight(0)],
        out_specs=tile_of(width),
        out_shape=jax.ShapeDtypeStruct((edges, width), BF16),
        compiler_params=params,
        cost_estimate=pl.CostEstimate(
            flops=2 * edges * width * (mesh_count + width), bytes_accessed=4 * edges * width, transcendentals=0
        ),
        name="edge_grad",
    )(tile_count, dst, d_pre, d_aggregate, w_edge_in)
    (node_pieces, slot_pieces, edge_grad, to_after, to_before, across) = lax.optimization_barrier(
        (node_pieces, slot_pieces, edge_grad, to_after, to_before, returns[4])
    )
    slot_half = halve_sum(peers, slot_pieces)
    node_terms = rest_terms(peers, node_pieces)
    near = [
        send(to_after, by_shift(peers, 2)),
        send(to_before, by_shift(peers, -2)),
        send(across, across_chips(peers)),
    ]
    slot_half, edge_pieces, near = lax.optimization_barrier((slot_half, edge_pieces, near))
    slot_terms = rest_terms(peers, slot_half)
    edge_terms = last_terms(peers, edge_pieces)
    node_terms, slot_terms = lax.optimization_barrier((node_terms, slot_terms))
    returned = [returns[0], swapped, *near]
    node_rows = w_node_in.shape[0] // peers
    out_rows = w_edge_out.shape[0] // peers
    grid_grad = pl.pallas_call(
        functools.partial(scatter_kernel, out_rows),
        grid=(2,),
        in_specs=[smem, whole(rows.shape)]
        + return_specs
        + [whole((out_rows + cap, width))] * (upper // 2),
        out_specs=pl.BlockSpec((grid_part, width), lambda step: (step, 0)),
        out_shape=jax.ShapeDtypeStruct((grid_count, width), BF16),
        compiler_params=params,
        name="scatter_lists",
    )(me, rows, *returned, *slot_terms)
    return (
        grid_grad,
        edge_grad,
        mesh_grad,
        total_of(edge_terms, 0, w_edge_in.shape[0] // peers),
        total_of(slot_terms, 0, out_rows),
        total_of(node_terms, 0, node_rows),
        total_of(node_terms, node_rows, node_rows + w_node_out.shape[0] // peers),
    )


def solution(mesh):
    rows = P(("grp", "lon"), None)
    flat = P(("grp", "lon"))
    return jax.shard_map(
        on_device,
        mesh=mesh,
        in_specs=(rows, rows, rows, rows, flat, flat, flat, P(("grp", "lon"), None, None)) + (P(),) * 4,
        out_specs=(rows,) * 7,
        check_vma=False,
    )
```

```python
import functools

import jax
import jax.numpy as jnp
from jax import lax
from jax.experimental import pallas as pl
from jax.experimental.pallas import tpu as pltpu
from jax.sharding import PartitionSpec as P

TILE = 256
STEP = 1024
SUB = 512
LANES = 128
NEAR = 3
BF16 = jnp.bfloat16
F32 = jnp.float32
VMEM_BYTES = 56 * 1024 * 1024


def dot(left, right):
    return lax.dot_general(left, right, (((1,), (0,)), ((), ())), preferred_element_type=F32)


def contract_rows(left, right):
    return lax.dot_general(left, right, (((0,), (0,)), ((), ())), preferred_element_type=F32)


def contract_cols(left, right):
    return lax.dot_general(left, right, (((1,), (1,)), ((), ())), preferred_element_type=F32)


def layer_norm(values):
    centered = values - jnp.mean(values, axis=1, keepdims=True)
    inverse = lax.rsqrt(jnp.mean(centered * centered, axis=1, keepdims=True) + 1e-05)
    return (centered * inverse, inverse)


def norm_back(normed, inverse, upstream):
    first = jnp.mean(upstream, axis=1, keepdims=True)
    second = jnp.mean(upstream * normed, axis=1, keepdims=True)
    return inverse * (upstream - first - normed * second)


def silu_and_slope(values):
    sigma = 0.5 + 0.5 * jnp.tanh(0.5 * values)
    hidden = values * sigma
    return (hidden, sigma + hidden * (1.0 - sigma))


def as_column(row):
    count = row.shape[1]
    block = min(count, LANES)
    down = lax.broadcasted_iota(jnp.int32, (block, block), 0)
    along = lax.broadcasted_iota(jnp.int32, (block, block), 1)
    columns = []
    for start in range(0, count, block):
        piece = row[:, start : start + block].astype(F32)
        picked = jnp.where(down == along, piece, 0.0)
        columns.append(jnp.sum(picked, axis=1, keepdims=True))
    return jnp.concatenate(columns, axis=0)


def as_row(column):
    count = column.shape[0]
    block = min(count, LANES)
    down = lax.broadcasted_iota(jnp.int32, (block, block), 0)
    along = lax.broadcasted_iota(jnp.int32, (block, block), 1)
    rows = []
    for start in range(0, count, block):
        picked = jnp.where(down == along, column[start : start + block], 0.0)
        rows.append(jnp.sum(picked, axis=0, keepdims=True))
    return jnp.concatenate(rows, axis=1)


def hot_rows(row, width, first=0):
    column = as_column(row).astype(jnp.int32) - first
    along = lax.broadcasted_iota(jnp.int32, (row.shape[1], width), 1)
    return (column == along).astype(F32).astype(BF16)


def hot_columns(row, height):
    down = lax.broadcasted_iota(jnp.int32, (height, row.shape[1]), 0)
    return (row == down).astype(F32).astype(BF16)


def live_only(row, first, count):
    place = first + lax.broadcasted_iota(jnp.int32, row.shape, 1)
    return jnp.where(place < count, row, -1)


def near_peers(me, peers):
    after = lax.rem(me + 2, peers)
    before = lax.rem(me + peers - 2, peers)
    across = lax.rem(me + peers - 3 + 6 * (me & 1), peers)
    return (me, me ^ 1, after, after ^ 1, before, before ^ 1, across)


def write_near(refs, cap, lists):
    mine, other, after, before, across = refs
    mine[...] = lists[0]
    other[...] = lists[1]
    after[:cap, :] = lists[2]
    after[cap:, :] = lists[3]
    before[:cap, :] = lists[4]
    before[cap:, :] = lists[5]
    across[...] = lists[6]


def read_near(refs, cap):
    mine, other, from_before, from_after, across, core_before, core_after = refs
    return [
        mine[...],
        other[...],
        from_after[:cap, :],
        core_after[cap:, :],
        from_before[:cap, :],
        core_before[cap:, :],
        across[...],
    ]


def write_back(refs, cap, lists):
    mine, swapped, after, before, across = refs
    mine[...] = lists[0]
    for place, index in enumerate((1, 3, 5)):
        swapped[place * cap : (place + 1) * cap, :] = lists[index]
    after[...] = lists[2]
    before[...] = lists[4]
    across[...] = lists[6]


def read_back(refs, cap):
    mine, swapped, from_before, from_after, across = refs
    return [
        mine[...],
        swapped[:cap, :],
        from_after[:cap, :],
        from_after[cap:, :],
        from_before[:cap, :],
        from_before[cap:, :],
        across[...],
    ]


def list_hots(me, rows_ref, grid_count, first):
    peers, cap = rows_ref.shape
    pieces = []
    for target in near_peers(me, peers):
        pieces.append(hot_rows(rows_ref[pl.ds(target, 1), :], grid_count, first))
    peer = lax.broadcasted_iota(jnp.int32, (peers, cap), 0)
    ahead = lax.rem(peer - me + peers, peers)
    apart = jnp.minimum(ahead, peers - ahead)
    far = jnp.max(jnp.where(apart > NEAR, rows_ref[...].astype(F32), -1.0), axis=0, keepdims=True)
    pieces.append(hot_rows(far.astype(jnp.int32), grid_count, first))
    return jnp.concatenate(pieces, axis=0)


def gather_kernel(me_ref, rows_ref, grid_ref, *refs):
    near_refs, far_ref, total = refs[:5], refs[5], refs[6]
    cap = rows_ref.shape[1]
    step = pl.program_id(0)
    part = grid_ref.shape[0]
    found = dot(list_hots(me_ref[0], rows_ref, part, step * part), grid_ref[...])

    @pl.when(step == 0)
    def _():
        total[...] = found

    @pl.when(step == pl.num_programs(0) - 1)
    def _():
        rows = (total[...] + found).astype(BF16)
        lists = [rows[at : at + cap] for at in range(0, 8 * cap, cap)]
        write_near(near_refs, cap, lists)
        far_ref[...] = lists[7]


def scatter_kernel(skip, me_ref, rows_ref, *refs):
    near_refs, far_refs, out_ref = refs[:5], refs[5:-1], refs[-1]
    part = out_ref.shape[0]
    cap = rows_ref.shape[1]
    hots = list_hots(me_ref[0], rows_ref, part, pl.program_id(0) * part)
    far = far_refs[0][skip:, :].astype(F32)
    for ref in far_refs[1:]:
        far = far + ref[skip:, :].astype(F32)
    values = jnp.concatenate(read_back(near_refs, cap) + [far.astype(BF16)], axis=0)
    out_ref[...] = contract_rows(hots, values).astype(BF16)


def halves_of(ref):
    rows = ref.shape[-1] if len(ref.shape) == 3 else ref.shape[0]
    return [(start, slice(start, start + SUB)) for start in range(0, rows, SUB)]


def local_kernel(dst_ref, edge_ref, mesh_ref, w_edge_ref, w_receiver_ref, out_ref, weights):
    width = edge_ref.shape[1]

    @pl.when(pl.program_id(0) == 0)
    def _():
        weights[:width, :] = w_edge_ref[...]
        weights[width:, :] = dot(mesh_ref[...], w_receiver_ref[...]).astype(BF16)

    for start, part in halves_of(edge_ref):
        onehot = hot_rows(dst_ref[0, :, part], mesh_ref.shape[0])
        joined = jnp.concatenate([edge_ref[part, :], onehot], axis=1)
        out_ref[part, :] = dot(joined, weights[...]).astype(BF16)


def split_out(me, peers, first, send_ref, keep_ref, parts):
    for low in range(4):
        target = send_ref if low & first else keep_ref
        half = 1 if low & (3 - first) else 0
        at = 0
        for upper in range(peers // 4):
            owner = me ^ (4 * upper + low)
            for ref, share, far in parts:
                piece = ref[pl.ds(pl.multiple_of(owner * share, 16), share), :]
                if far:
                    ahead = lax.rem(owner - me + peers, peers)
                    apart = jnp.minimum(ahead, peers - ahead)
                    piece = jnp.where(apart > NEAR, piece.astype(F32), 0.0)
                target[half, at : at + share, :] = piece.astype(BF16)
                at += share


def forward_kernel(
    peers, me_ref, count_ref, src_ref, dst_ref, local_ref, edge_ref, *refs
):
    near_refs, far_refs = refs[:7], refs[7:11]
    (w_sender_ref, w_out_ref, w_node_in_ref, w_node_out_ref, mesh_ref, cotangent_ref) = refs[11:17]
    (received_ref, hidden_ref, slope_ref, norm_ref, inverse_ref) = refs[17:22]
    (send_ref, keep_ref, d_aggregate_ref, d_mesh_ref) = refs[22:26]
    (slot_proj, aggregate, grad_in, grad_out) = refs[26:]
    step = pl.program_id(0)
    me = me_ref[0]
    cap = near_refs[0].shape[0]
    width = edge_ref.shape[1]

    @pl.when(step == 0)
    def _():
        aggregate[...] = jnp.zeros_like(aggregate)
        w_sender = w_sender_ref[...]

        def place(owner, rows, projected):
            offset = pl.multiple_of(owner * cap, 16)
            received_ref[pl.ds(offset, cap), :] = rows
            slot_proj[pl.ds(offset, cap), :] = projected

        for low, ref in enumerate(far_refs):
            rows = ref[...]
            projected = dot(rows, w_sender).astype(BF16)
            for upper in range(peers // 4):
                span = slice(upper * cap, (upper + 1) * cap)
                place(me ^ (4 * upper + low), rows[span], projected[span])
        rows = jnp.concatenate(read_near(near_refs, cap), axis=0)
        projected = dot(rows, w_sender).astype(BF16)
        for spot, owner in enumerate(near_peers(me, peers)):
            place(owner, rows[spot * cap : (spot + 1) * cap], projected[spot * cap : (spot + 1) * cap])

    @pl.when(step * STEP < count_ref[0] * TILE)
    def _():
        parts = halves_of(edge_ref)
        pres = []
        for start, part in parts:
            onehot = hot_rows(src_ref[0, :, part], slot_proj.shape[0])
            pres.append(local_ref[part, :].astype(F32) + dot(onehot, slot_proj[...]))
        projs = []
        for (start, part), pre in zip(parts, pres):
            hidden, slope = silu_and_slope(pre)
            hidden = hidden.astype(BF16)
            hidden_ref[part, :] = hidden
            slope_ref[part, :] = slope.astype(BF16)
            projs.append(dot(hidden, w_out_ref[...]))
        for (start, part), proj in zip(parts, projs):
            normed, inverse = layer_norm(proj)
            norm_ref[part, :] = normed.astype(BF16)
            inverse_ref[0, :, part] = as_row(inverse)
            edge_new = (edge_ref[part, :].astype(F32) + normed).astype(BF16)
            receivers = live_only(dst_ref[0, :, part], step * STEP + start, count_ref[0] * TILE)
            aggregate[...] += dot(hot_columns(receivers, aggregate.shape[0]), edge_new)

    @pl.when(step == pl.num_programs(0) - 1)
    def _():
        mesh = mesh_ref[...]
        summed = aggregate[...].astype(BF16)
        node_pre = dot(mesh, w_node_in_ref[:width, :]) + dot(summed, w_node_in_ref[width:, :])
        hidden, slope = silu_and_slope(node_pre)
        hidden = hidden.astype(BF16)
        normed, inverse = layer_norm(dot(hidden, w_node_out_ref[...]))
        upstream = cotangent_ref[...].astype(F32)
        d_proj = norm_back(normed, inverse, upstream).astype(BF16)
        d_pre = (contract_cols(d_proj, w_node_out_ref[...]) * slope).astype(BF16)
        d_mesh_ref[...] = upstream + contract_cols(d_pre, w_node_in_ref[:width, :])
        d_aggregate_ref[...] = contract_cols(d_pre, w_node_in_ref[width:, :]).astype(BF16)
        grad_out[...] = contract_rows(hidden, d_proj)
        grad_in[:width, :] = contract_rows(mesh, d_pre)
        grad_in[width:, :] = contract_rows(summed, d_pre)
        split_out(
            me,
            peers,
            2,
            send_ref,
            keep_ref,
            ((grad_in, grad_in.shape[0] // peers, False), (grad_out, grad_out.shape[0] // peers, False)),
        )


def backward_kernel(peers, me_ref, count_ref, src_ref, dst_ref, inverse_ref, *refs):
    (hidden_ref, slope_ref, norm_ref, edge_ref) = refs[:4]
    (d_aggregate_ref, received_ref, mesh_ref, d_mesh_ref) = refs[4:8]
    (w_sender_ref, w_receiver_ref, w_edge_ref, w_out_ref) = refs[8:12]
    (edge_grad_ref, mesh_grad_ref, slot_send_ref, slot_keep_ref, edge_send_ref, edge_keep_ref) = refs[12:18]
    near_refs = refs[18:23]
    (end_sum, grad_in, grad_out, d_slots) = refs[23:]
    step = pl.program_id(0)
    me = me_ref[0]
    slots, width = received_ref.shape
    mesh_count = mesh_ref.shape[0]

    @pl.when(step == 0)
    def _():
        end_sum[...] = jnp.zeros_like(end_sum)
        grad_in[:width, :] = jnp.zeros((width, width), F32)
        grad_out[...] = jnp.zeros_like(grad_out)

    @pl.when(step * STEP < count_ref[0] * TILE)
    def _():
        parts = halves_of(hidden_ref)
        upstreams = []
        columns = []
        for start, part in parts:
            first = step * STEP + start
            live = count_ref[0] * TILE
            receivers = live_only(dst_ref[0, :, part], first, live)
            upstreams.append(dot(hot_rows(receivers, mesh_count), d_aggregate_ref[...]))
            senders = live_only(src_ref[0, :, part], first, live)
            columns.append(
                jnp.concatenate([hot_columns(senders, slots), hot_columns(receivers, mesh_count)], axis=0)
            )
        d_projs = []
        d_hiddens = []
        for (start, part), upstream in zip(parts, upstreams):
            inverse = as_column(inverse_ref[0, :, part])
            d_proj = norm_back(norm_ref[part, :].astype(F32), inverse, upstream).astype(BF16)
            d_projs.append(d_proj)
            d_hiddens.append(contract_cols(d_proj, w_out_ref[...]))
        for (start, part), d_proj, d_hidden, column, upstream in zip(
            parts, d_projs, d_hiddens, columns, upstreams
        ):
            grad_out[...] += contract_rows(hidden_ref[part, :], d_proj)
            d_pre = (d_hidden * slope_ref[part, :].astype(F32)).astype(BF16)
            edge_grad_ref[part, :] = (upstream + contract_cols(d_pre, w_edge_ref[...])).astype(BF16)
            end_sum[...] += dot(column, d_pre)
            grad_in[:width, :] += contract_rows(edge_ref[part, :], d_pre)

    @pl.when(step * STEP >= count_ref[0] * TILE)
    def _():
        edge_grad_ref[...] = jnp.zeros_like(edge_grad_ref)

    @pl.when(step == pl.num_programs(0) - 1)
    def _():
        summed = end_sum[:slots, :].astype(BF16)
        mesh_summed = end_sum[slots:, :].astype(BF16)
        d_slots[...] = contract_cols(summed, w_sender_ref[...]).astype(BF16)
        grad_in[width : 2 * width, :] = contract_rows(received_ref[...], summed)
        grad_in[2 * width :, :] = contract_rows(mesh_ref[...], mesh_summed)
        mesh_grad_ref[...] = (d_mesh_ref[...] + contract_cols(mesh_summed, w_receiver_ref[...])).astype(BF16)
        cap = near_refs[0].shape[0]
        owners = near_peers(me, peers)
        write_back(
            near_refs, cap, [d_slots[pl.ds(pl.multiple_of(owner * cap, 16), cap), :] for owner in owners]
        )
        out_share = grad_out.shape[0] // peers
        split_out(
            me, peers, 1, slot_send_ref, slot_keep_ref, ((grad_out, out_share, False), (d_slots, cap, True))
        )
        split_out(
            me, peers, 1, edge_send_ref, edge_keep_ref, ((grad_in, grad_in.shape[0] // peers, False),)
        )


def send(values, perm):
    return lax.ppermute(values, "lon", perm)


def by_xor(peers, bits):
    return [(peer, peer ^ bits) for peer in range(peers)]


def by_shift(peers, shift):
    return [(peer, (peer + shift) % peers) for peer in range(peers)]


def across_chips(peers):
    return [(peer, (peer + (3 if peer % 2 else -3)) % peers) for peer in range(peers)]


def exchange_near(peers, lists):
    mine, other, after, before, across = lists
    return [
        mine,
        other,
        send(after, by_shift(peers, 2)),
        send(before, by_shift(peers, -2)),
        send(across, across_chips(peers)),
    ]


def core_near(peers, near):
    mine, other, after, before, across = near
    swap = by_xor(peers, 1)
    return [mine, send(other, swap), after, before, across, send(after, swap), send(before, swap)]


def add(left, right):
    return (left.astype(F32) + right.astype(F32)).astype(BF16)


def first_sum(peers, bit, outgoing, kept):
    arrived = send(outgoing, by_xor(peers, bit))
    return add(kept[1], arrived[1]), add(kept[0], arrived[0])


def next_sum(peers, bit, outgoing, kept):
    return add(kept, send(outgoing, by_xor(peers, bit)))


def last_terms(peers, pieces):
    count = peers // 4
    share = pieces.shape[0] // count
    terms = [pieces[:share]]
    for place in range(1, count):
        piece = pieces[place * share : (place + 1) * share]
        terms.append(send(piece, by_xor(peers, 4 * place)))
    return terms


def total_of(terms, start, stop):
    total = terms[0][start:stop].astype(F32)
    for term in terms[1:]:
        total = total + term[start:stop].astype(F32)
    return total


def whole(shape):
    return pl.BlockSpec(shape, lambda *_: (0,) * len(shape))


def on_device(
    grid_latent,
    mesh_latent,
    edge_latent,
    mesh_cotangent,
    edge_src,
    edge_dst,
    tile_count,
    send_rows,
    w_edge_in,
    w_edge_out,
    w_node_in,
    w_node_out,
):
    peers = lax.axis_size("lon")
    me = lax.axis_index("lon").astype(jnp.int32).reshape(1)
    upper = peers // 4
    rows = send_rows[0]
    cap = rows.shape[1]
    slots = peers * cap
    edges, width = edge_latent.shape
    mesh_count = mesh_latent.shape[0]
    grid_count = grid_latent.shape[0]
    tiles = edges // STEP
    src = edge_src.reshape(tiles, 1, STEP)
    dst = edge_dst.reshape(tiles, 1, STEP)
    smem = pl.BlockSpec(memory_space=pltpu.SMEM)
    params = pltpu.CompilerParams(vmem_limit_bytes=VMEM_BYTES)
    square = (width, width)

    def tile_of(last):
        return pl.BlockSpec((STEP, last), lambda step, *_: (step, 0))

    index_tile = pl.BlockSpec((1, 1, STEP), lambda step, *_: (step, 0, 0))

    def weight(place):
        return pl.BlockSpec(square, lambda *_: (place, 0))

    def halves(share):
        shape = (2, upper * share, width)
        return [jax.ShapeDtypeStruct(shape, BF16)] * 2, [whole(shape)] * 2

    grid_part = grid_count // 2
    near_rows = (cap, cap, 2 * cap, 2 * cap, cap)
    near_specs = [whole((count, width)) for count in near_rows]
    near_shapes = [jax.ShapeDtypeStruct((count, width), BF16) for count in near_rows]
    core_specs = near_specs + [whole((2 * cap, width))] * 2
    back_rows = (cap, 3 * cap, cap, cap, cap)
    back_specs = [whole((count, width)) for count in back_rows]
    back_shapes = [jax.ShapeDtypeStruct((count, width), BF16) for count in back_rows]
    return_specs = [whole((count, width)) for count in (cap, 3 * cap, 2 * cap, 2 * cap, cap)]
    lists = pl.pallas_call(
        gather_kernel,
        grid=(2,),
        in_specs=[smem, whole(rows.shape), pl.BlockSpec((grid_part, width), lambda step: (step, 0))],
        out_specs=near_specs + [whole((cap, width))],
        out_shape=near_shapes + [jax.ShapeDtypeStruct((cap, width), BF16)],
        scratch_shapes=[pltpu.VMEM((8 * cap, width), F32)],
        compiler_params=params,
        name="gather_lists",
    )(me, rows, grid_latent)

    hops = [send(lists[5], by_xor(peers, 4 * place)) for place in range(1, upper)]
    near = exchange_near(peers, lists[:5])
    far_own = jnp.concatenate([lists[5]] + hops, axis=0)
    far_own, receivers = lax.optimization_barrier((far_own, dst))
    far_next = send(far_own, by_xor(peers, 2))
    far_core = send(far_own, by_xor(peers, 1))
    local = pl.pallas_call(
        local_kernel,
        grid=(tiles,),
        in_specs=[index_tile, tile_of(width), whole(mesh_latent.shape), weight(0), weight(2)],
        out_specs=tile_of(width),
        out_shape=jax.ShapeDtypeStruct((edges, width), BF16),
        scratch_shapes=[pltpu.VMEM((width + mesh_count, width), BF16)],
        compiler_params=params,
        cost_estimate=pl.CostEstimate(
            flops=2 * edges * width * (width + mesh_count),
            bytes_accessed=4 * edges * width,
            transcendentals=0,
        ),
        name="edge_local",
    )(receivers, edge_latent, mesh_latent, w_edge_in, w_edge_in)
    far_next, far_core, near, local = lax.optimization_barrier((far_next, far_core, near, local))
    near = core_near(peers, near)
    far_both = send(far_next, by_xor(peers, 1))

    node_shape, node_spec = halves(w_node_in.shape[0] // peers + w_node_out.shape[0] // peers)
    (received, hidden, slope, norm, inverse, node_send, node_keep, d_aggregate, d_mesh) = pl.pallas_call(
        functools.partial(forward_kernel, peers),
        grid=(tiles,),
        in_specs=[smem, smem, index_tile, index_tile, tile_of(width), tile_of(width)]
        + core_specs
        + [whole((upper * cap, width))] * 4
        + [weight(1)]
        + [whole(w.shape) for w in (w_edge_out, w_node_in, w_node_out, mesh_latent, mesh_cotangent)],
        out_specs=[whole((slots, width))]
        + [tile_of(width)] * 3
        + [index_tile]
        + node_spec
        + [whole((mesh_count, width))] * 2,
        out_shape=[jax.ShapeDtypeStruct((slots, width), BF16)]
        + [jax.ShapeDtypeStruct((edges, width), BF16)] * 3
        + [jax.ShapeDtypeStruct((tiles, 1, STEP), F32)]
        + node_shape
        + [jax.ShapeDtypeStruct((mesh_count, width), BF16), jax.ShapeDtypeStruct((mesh_count, width), F32)],
        scratch_shapes=[
            pltpu.VMEM((slots, width), BF16),
            pltpu.VMEM((mesh_count, width), F32),
            pltpu.VMEM(w_node_in.shape, F32),
            pltpu.VMEM(w_node_out.shape, F32),
        ],
        compiler_params=params,
        name="forward",
    )(
        me,
        tile_count,
        src,
        dst,
        local,
        edge_latent,
        *near,
        far_own,
        far_core,
        far_next,
        far_both,
        w_edge_in,
        w_edge_out,
        w_node_in,
        w_node_out,
        mesh_latent,
        mesh_cotangent,
    )

    node_next, node_kept = first_sum(peers, 2, node_send, node_keep)
    slot_shape, slot_spec = halves(w_edge_out.shape[0] // peers + cap)
    edge_shape, edge_spec = halves(w_edge_in.shape[0] // peers)
    results = pl.pallas_call(
        functools.partial(backward_kernel, peers),
        grid=(tiles,),
        in_specs=[smem, smem, index_tile, index_tile, index_tile]
        + [tile_of(width)] * 4
        + [whole((mesh_count, width)), whole((slots, width))]
        + [whole((mesh_count, width))] * 2
        + [weight(1), weight(2), weight(0), whole(square)],
        out_specs=[tile_of(width), whole((mesh_count, width))] + slot_spec + edge_spec + back_specs,
        out_shape=[
            jax.ShapeDtypeStruct((edges, width), BF16),
            jax.ShapeDtypeStruct((mesh_count, width), BF16),
        ]
        + slot_shape
        + edge_shape
        + back_shapes,
        scratch_shapes=[
            pltpu.VMEM((slots + mesh_count, width), F32),
            pltpu.VMEM(w_edge_in.shape, F32),
            pltpu.VMEM(square, F32),
            pltpu.VMEM((slots, width), BF16),
        ],
        compiler_params=params,
        cost_estimate=pl.CostEstimate(
            flops=2 * edges * width * (2 * mesh_count + 4 * width + slots),
            bytes_accessed=10 * edges * width,
            transcendentals=0,
        ),
        name="backward",
    )(
        me,
        tile_count,
        src,
        dst,
        inverse,
        hidden,
        slope,
        norm,
        edge_latent,
        d_aggregate,
        received,
        mesh_latent,
        d_mesh,
        w_edge_in,
        w_edge_in,
        w_edge_in,
        w_edge_out,
    )
    (edge_grad, mesh_grad, slot_send, slot_keep, edge_send, edge_keep), returns = results[:6], results[6:]
    (node_next, node_kept, slot_send, slot_keep, edge_send, edge_keep, returns) = lax.optimization_barrier(
        (node_next, node_kept, slot_send, slot_keep, edge_send, edge_keep, returns)
    )
    slot_next, slot_kept = first_sum(peers, 1, slot_send, slot_keep)
    edge_next, edge_kept = first_sum(peers, 1, edge_send, edge_keep)
    node_pieces = next_sum(peers, 1, node_next, node_kept)
    swapped = send(returns[1], by_xor(peers, 1))
    slot_pieces = next_sum(peers, 2, slot_next, slot_kept)
    node_pieces, edge_next, edge_kept, swapped, slot_next = lax.optimization_barrier(
        (node_pieces, edge_next, edge_kept, swapped, slot_next)
    )
    node_terms = last_terms(peers, node_pieces)
    to_after = jnp.concatenate([returns[2], swapped[cap : 2 * cap]], axis=0)
    to_before = jnp.concatenate([returns[3], swapped[2 * cap :]], axis=0)
    near = [
        send(to_after, by_shift(peers, 2)),
        send(to_before, by_shift(peers, -2)),
        send(returns[4], across_chips(peers)),
    ]
    slot_pieces, edge_next, edge_kept = lax.optimization_barrier((slot_pieces, edge_next, edge_kept))
    edge_pieces = next_sum(peers, 2, edge_next, edge_kept)
    slot_terms = last_terms(peers, slot_pieces)
    edge_pieces, near = lax.optimization_barrier((edge_pieces, near))
    edge_terms = last_terms(peers, edge_pieces)
    node_terms, slot_terms = lax.optimization_barrier((node_terms, slot_terms))
    returned = [returns[0], swapped, *near]
    node_rows = w_node_in.shape[0] // peers
    out_rows = w_edge_out.shape[0] // peers
    grid_grad = pl.pallas_call(
        functools.partial(scatter_kernel, out_rows),
        grid=(2,),
        in_specs=[smem, whole(rows.shape)]
        + return_specs
        + [whole((out_rows + cap, width))] * upper,
        out_specs=pl.BlockSpec((grid_part, width), lambda step: (step, 0)),
        out_shape=jax.ShapeDtypeStruct((grid_count, width), BF16),
        compiler_params=params,
        name="scatter_lists",
    )(me, rows, *returned, *slot_terms)
    return (
        grid_grad,
        edge_grad,
        mesh_grad,
        total_of(edge_terms, 0, w_edge_in.shape[0] // peers),
        total_of(slot_terms, 0, out_rows),
        total_of(node_terms, 0, node_rows),
        total_of(node_terms, node_rows, node_rows + w_node_out.shape[0] // peers),
    )


def solution(mesh):
    rows = P(("grp", "lon"), None)
    flat = P(("grp", "lon"))
    return jax.shard_map(
        on_device,
        mesh=mesh,
        in_specs=(rows, rows, rows, rows, flat, flat, flat, P(("grp", "lon"), None, None)) + (P(),) * 4,
        out_specs=(rows,) * 7,
        check_vma=False,
    )
```

```python
import functools

import jax
import jax.numpy as jnp
from jax import lax
from jax.experimental import pallas as pl
from jax.experimental.pallas import tpu as pltpu
from jax.sharding import PartitionSpec as P

TILE = 256
STEP = 1024
SUB = 512
LANES = 128
NEAR = 3
BF16 = jnp.bfloat16
F32 = jnp.float32
VMEM_BYTES = 24 * 1024 * 1024


def dot(left, right):
    return lax.dot_general(left, right, (((1,), (0,)), ((), ())), preferred_element_type=F32)


def contract_rows(left, right):
    return lax.dot_general(left, right, (((0,), (0,)), ((), ())), preferred_element_type=F32)


def contract_cols(left, right):
    return lax.dot_general(left, right, (((1,), (1,)), ((), ())), preferred_element_type=F32)


def layer_norm(values):
    centered = values - jnp.mean(values, axis=1, keepdims=True)
    inverse = lax.rsqrt(jnp.mean(centered * centered, axis=1, keepdims=True) + 1e-05)
    return (centered * inverse, inverse)


def norm_back(normed, inverse, upstream):
    first = jnp.mean(upstream, axis=1, keepdims=True)
    second = jnp.mean(upstream * normed, axis=1, keepdims=True)
    return inverse * (upstream - first - normed * second)


def silu_and_slope(values):
    sigma = 0.5 + 0.5 * jnp.tanh(0.5 * values)
    hidden = values * sigma
    return (hidden, sigma + hidden * (1.0 - sigma))


def as_column(row):
    count = row.shape[1]
    block = min(count, LANES)
    down = lax.broadcasted_iota(jnp.int32, (block, block), 0)
    along = lax.broadcasted_iota(jnp.int32, (block, block), 1)
    columns = []
    for start in range(0, count, block):
        piece = row[:, start : start + block].astype(F32)
        picked = jnp.where(down == along, piece, 0.0)
        columns.append(jnp.sum(picked, axis=1, keepdims=True))
    return jnp.concatenate(columns, axis=0)


def as_row(column):
    count = column.shape[0]
    block = min(count, LANES)
    down = lax.broadcasted_iota(jnp.int32, (block, block), 0)
    along = lax.broadcasted_iota(jnp.int32, (block, block), 1)
    rows = []
    for start in range(0, count, block):
        picked = jnp.where(down == along, column[start : start + block], 0.0)
        rows.append(jnp.sum(picked, axis=0, keepdims=True))
    return jnp.concatenate(rows, axis=1)


def hot_rows(row, width, first=0):
    column = as_column(row).astype(jnp.int32) - first
    along = lax.broadcasted_iota(jnp.int32, (row.shape[1], width), 1)
    return (column == along).astype(F32).astype(BF16)


def hot_columns(row, height):
    down = lax.broadcasted_iota(jnp.int32, (height, row.shape[1]), 0)
    return (row == down).astype(F32).astype(BF16)


def live_only(row, first, count):
    place = first + lax.broadcasted_iota(jnp.int32, row.shape, 1)
    return jnp.where(place < count, row, -1)


def near_peers(me, peers):
    after = lax.rem(me + 2, peers)
    before = lax.rem(me + peers - 2, peers)
    across = lax.rem(me + peers - 3 + 6 * (me & 1), peers)
    return (me, me ^ 1, after, after ^ 1, before, before ^ 1, across)


def write_near(refs, cap, lists):
    mine, other, after, before, across = refs
    mine[...] = lists[0]
    other[...] = lists[1]
    after[:cap, :] = lists[2]
    after[cap:, :] = lists[3]
    before[:cap, :] = lists[4]
    before[cap:, :] = lists[5]
    across[...] = lists[6]


def read_near(refs, cap):
    mine, other, from_before, from_after, across, core_before, core_after = refs
    return [
        mine[...],
        other[...],
        from_after[:cap, :],
        core_after[cap:, :],
        from_before[:cap, :],
        core_before[cap:, :],
        across[...],
    ]


def write_back(refs, cap, lists):
    mine, swapped, after, before, across = refs
    mine[...] = lists[0]
    for place, index in enumerate((1, 3, 5)):
        swapped[place * cap : (place + 1) * cap, :] = lists[index]
    after[...] = lists[2]
    before[...] = lists[4]
    across[...] = lists[6]


def read_back(refs, cap):
    mine, swapped, from_before, from_after, across = refs
    return [
        mine[...],
        swapped[:cap, :],
        from_after[:cap, :],
        from_after[cap:, :],
        from_before[:cap, :],
        from_before[cap:, :],
        across[...],
    ]


def list_hots(me, rows_ref, grid_count, first):
    peers, cap = rows_ref.shape
    pieces = []
    for target in near_peers(me, peers):
        pieces.append(hot_rows(rows_ref[pl.ds(target, 1), :], grid_count, first))
    peer = lax.broadcasted_iota(jnp.int32, (peers, cap), 0)
    ahead = lax.rem(peer - me + peers, peers)
    apart = jnp.minimum(ahead, peers - ahead)
    far = jnp.max(jnp.where(apart > NEAR, rows_ref[...].astype(F32), -1.0), axis=0, keepdims=True)
    pieces.append(hot_rows(far.astype(jnp.int32), grid_count, first))
    return jnp.concatenate(pieces, axis=0)


def gather_kernel(me_ref, rows_ref, grid_ref, *refs):
    near_refs, far_ref, total = refs[:5], refs[5], refs[6]
    cap = rows_ref.shape[1]
    step = pl.program_id(0)
    part = grid_ref.shape[0]
    found = dot(list_hots(me_ref[0], rows_ref, part, step * part), grid_ref[...])

    @pl.when(step == 0)
    def _():
        total[...] = found

    @pl.when(step == pl.num_programs(0) - 1)
    def _():
        rows = (total[...] + found).astype(BF16)
        lists = [rows[at : at + cap] for at in range(0, 8 * cap, cap)]
        write_near(near_refs, cap, lists)
        far_ref[...] = lists[7]


def scatter_kernel(skip, me_ref, rows_ref, *refs):
    near_refs, far_refs, out_ref = refs[:5], refs[5:-1], refs[-1]
    part = out_ref.shape[0]
    cap = rows_ref.shape[1]
    hots = list_hots(me_ref[0], rows_ref, part, pl.program_id(0) * part)
    far = far_refs[0][skip:, :].astype(F32)
    for ref in far_refs[1:]:
        far = far + ref[skip:, :].astype(F32)
    values = jnp.concatenate(read_back(near_refs, cap) + [far.astype(BF16)], axis=0)
    out_ref[...] = contract_rows(hots, values).astype(BF16)


def halves_of(ref):
    rows = ref.shape[-1] if len(ref.shape) == 3 else ref.shape[0]
    return [(start, slice(start, start + SUB)) for start in range(0, rows, SUB)]


def local_kernel(dst_ref, edge_ref, mesh_ref, w_edge_ref, w_receiver_ref, out_ref, weights):
    width = edge_ref.shape[1]

    @pl.when(pl.program_id(0) == 0)
    def _():
        weights[:width, :] = w_edge_ref[...]
        weights[width:, :] = dot(mesh_ref[...], w_receiver_ref[...]).astype(BF16)

    for start, part in halves_of(edge_ref):
        onehot = hot_rows(dst_ref[0, :, part], mesh_ref.shape[0])
        joined = jnp.concatenate([edge_ref[part, :], onehot], axis=1)
        out_ref[part, :] = dot(joined, weights[...]).astype(BF16)


def split_out(me, peers, first, send_ref, keep_ref, parts):
    for low in range(4):
        target = send_ref if low & first else keep_ref
        half = 1 if low & (3 - first) else 0
        at = 0
        for upper in range(peers // 4):
            owner = me ^ (4 * upper + low)
            for ref, share, far in parts:
                piece = ref[pl.ds(pl.multiple_of(owner * share, 16), share), :]
                if far:
                    ahead = lax.rem(owner - me + peers, peers)
                    apart = jnp.minimum(ahead, peers - ahead)
                    piece = jnp.where(apart > NEAR, piece.astype(F32), 0.0)
                target[half, at : at + share, :] = piece.astype(BF16)
                at += share


def forward_kernel(
    peers, me_ref, count_ref, src_ref, dst_ref, local_ref, edge_ref, *refs
):
    near_refs, far_refs = refs[:7], refs[7:11]
    (w_sender_ref, w_out_ref, w_node_in_ref, w_node_out_ref, mesh_ref, cotangent_ref) = refs[11:17]
    (received_ref, hidden_ref, slope_ref, norm_ref, inverse_ref) = refs[17:22]
    (send_ref, keep_ref, d_aggregate_ref, d_mesh_ref) = refs[22:26]
    (slot_proj, aggregate, grad_in, grad_out) = refs[26:]
    step = pl.program_id(0)
    me = me_ref[0]
    cap = near_refs[0].shape[0]
    width = edge_ref.shape[1]

    @pl.when(step == 0)
    def _():
        aggregate[...] = jnp.zeros_like(aggregate)
        w_sender = w_sender_ref[...]

        def place(owner, rows, projected):
            offset = pl.multiple_of(owner * cap, 16)
            received_ref[pl.ds(offset, cap), :] = rows
            slot_proj[pl.ds(offset, cap), :] = projected

        for low, ref in enumerate(far_refs):
            rows = ref[...]
            projected = dot(rows, w_sender).astype(BF16)
            for upper in range(peers // 4):
                span = slice(upper * cap, (upper + 1) * cap)
                place(me ^ (4 * upper + low), rows[span], projected[span])
        rows = jnp.concatenate(read_near(near_refs, cap), axis=0)
        projected = dot(rows, w_sender).astype(BF16)
        for spot, owner in enumerate(near_peers(me, peers)):
            place(owner, rows[spot * cap : (spot + 1) * cap], projected[spot * cap : (spot + 1) * cap])

    @pl.when(step * STEP < count_ref[0] * TILE)
    def _():
        parts = halves_of(edge_ref)
        pres = []
        for start, part in parts:
            onehot = hot_rows(src_ref[0, :, part], slot_proj.shape[0])
            pres.append(local_ref[part, :].astype(F32) + dot(onehot, slot_proj[...]))
        projs = []
        for (start, part), pre in zip(parts, pres):
            hidden, slope = silu_and_slope(pre)
            hidden = hidden.astype(BF16)
            hidden_ref[part, :] = hidden
            slope_ref[part, :] = slope.astype(BF16)
            projs.append(dot(hidden, w_out_ref[...]))
        for (start, part), proj in zip(parts, projs):
            normed, inverse = layer_norm(proj)
            norm_ref[part, :] = normed.astype(BF16)
            inverse_ref[0, :, part] = as_row(inverse)
            edge_new = (edge_ref[part, :].astype(F32) + normed).astype(BF16)
            receivers = live_only(dst_ref[0, :, part], step * STEP + start, count_ref[0] * TILE)
            aggregate[...] += dot(hot_columns(receivers, aggregate.shape[0]), edge_new)

    @pl.when(step == pl.num_programs(0) - 1)
    def _():
        mesh = mesh_ref[...]
        summed = aggregate[...].astype(BF16)
        node_pre = dot(mesh, w_node_in_ref[:width, :]) + dot(summed, w_node_in_ref[width:, :])
        hidden, slope = silu_and_slope(node_pre)
        hidden = hidden.astype(BF16)
        normed, inverse = layer_norm(dot(hidden, w_node_out_ref[...]))
        upstream = cotangent_ref[...].astype(F32)
        d_proj = norm_back(normed, inverse, upstream).astype(BF16)
        d_pre = (contract_cols(d_proj, w_node_out_ref[...]) * slope).astype(BF16)
        d_mesh_ref[...] = upstream + contract_cols(d_pre, w_node_in_ref[:width, :])
        d_aggregate_ref[...] = contract_cols(d_pre, w_node_in_ref[width:, :]).astype(BF16)
        grad_out[...] = contract_rows(hidden, d_proj)
        grad_in[:width, :] = contract_rows(mesh, d_pre)
        grad_in[width:, :] = contract_rows(summed, d_pre)
        split_out(
            me,
            peers,
            2,
            send_ref,
            keep_ref,
            ((grad_in, grad_in.shape[0] // peers, False), (grad_out, grad_out.shape[0] // peers, False)),
        )


def backward_kernel(peers, me_ref, count_ref, src_ref, dst_ref, inverse_ref, *refs):
    (hidden_ref, slope_ref, norm_ref, edge_ref) = refs[:4]
    (d_aggregate_ref, received_ref, mesh_ref, d_mesh_ref) = refs[4:8]
    (w_sender_ref, w_receiver_ref, w_edge_ref, w_out_ref) = refs[8:12]
    (edge_grad_ref, mesh_grad_ref, slot_send_ref, slot_keep_ref, edge_send_ref, edge_keep_ref) = refs[12:18]
    near_refs = refs[18:23]
    (end_sum, grad_in, grad_out, d_slots) = refs[23:]
    step = pl.program_id(0)
    me = me_ref[0]
    slots, width = received_ref.shape
    mesh_count = mesh_ref.shape[0]

    @pl.when(step == 0)
    def _():
        end_sum[...] = jnp.zeros_like(end_sum)
        grad_in[:width, :] = jnp.zeros((width, width), F32)
        grad_out[...] = jnp.zeros_like(grad_out)

    @pl.when(step * STEP < count_ref[0] * TILE)
    def _():
        parts = halves_of(hidden_ref)
        upstreams = []
        columns = []
        for start, part in parts:
            first = step * STEP + start
            live = count_ref[0] * TILE
            receivers = live_only(dst_ref[0, :, part], first, live)
            upstreams.append(dot(hot_rows(receivers, mesh_count), d_aggregate_ref[...]))
            senders = live_only(src_ref[0, :, part], first, live)
            columns.append(
                jnp.concatenate([hot_columns(senders, slots), hot_columns(receivers, mesh_count)], axis=0)
            )
        d_projs = []
        d_hiddens = []
        for (start, part), upstream in zip(parts, upstreams):
            inverse = as_column(inverse_ref[0, :, part])
            d_proj = norm_back(norm_ref[part, :].astype(F32), inverse, upstream).astype(BF16)
            d_projs.append(d_proj)
            d_hiddens.append(contract_cols(d_proj, w_out_ref[...]))
        for (start, part), d_proj, d_hidden, column, upstream in zip(
            parts, d_projs, d_hiddens, columns, upstreams
        ):
            grad_out[...] += contract_rows(hidden_ref[part, :], d_proj)
            d_pre = (d_hidden * slope_ref[part, :].astype(F32)).astype(BF16)
            edge_grad_ref[part, :] = (upstream + contract_cols(d_pre, w_edge_ref[...])).astype(BF16)
            end_sum[...] += dot(column, d_pre)
            grad_in[:width, :] += contract_rows(edge_ref[part, :], d_pre)

    @pl.when(step * STEP >= count_ref[0] * TILE)
    def _():
        edge_grad_ref[...] = jnp.zeros_like(edge_grad_ref)

    @pl.when(step == pl.num_programs(0) - 1)
    def _():
        summed = end_sum[:slots, :].astype(BF16)
        mesh_summed = end_sum[slots:, :].astype(BF16)
        d_slots[...] = contract_cols(summed, w_sender_ref[...]).astype(BF16)
        grad_in[width : 2 * width, :] = contract_rows(received_ref[...], summed)
        grad_in[2 * width :, :] = contract_rows(mesh_ref[...], mesh_summed)
        mesh_grad_ref[...] = (d_mesh_ref[...] + contract_cols(mesh_summed, w_receiver_ref[...])).astype(BF16)
        cap = near_refs[0].shape[0]
        owners = near_peers(me, peers)
        write_back(
            near_refs, cap, [d_slots[pl.ds(pl.multiple_of(owner * cap, 16), cap), :] for owner in owners]
        )
        out_share = grad_out.shape[0] // peers
        split_out(
            me, peers, 1, slot_send_ref, slot_keep_ref, ((grad_out, out_share, False), (d_slots, cap, True))
        )
        split_out(
            me, peers, 1, edge_send_ref, edge_keep_ref, ((grad_in, grad_in.shape[0] // peers, False),)
        )


def send(values, perm):
    return lax.ppermute(values, "lon", perm)


def by_xor(peers, bits):
    return [(peer, peer ^ bits) for peer in range(peers)]


def by_shift(peers, shift):
    return [(peer, (peer + shift) % peers) for peer in range(peers)]


def across_chips(peers):
    return [(peer, (peer + (3 if peer % 2 else -3)) % peers) for peer in range(peers)]


def exchange_near(peers, lists):
    mine, other, after, before, across = lists
    return [
        mine,
        other,
        send(after, by_shift(peers, 2)),
        send(before, by_shift(peers, -2)),
        send(across, across_chips(peers)),
    ]


def core_near(peers, near):
    mine, other, after, before, across = near
    swap = by_xor(peers, 1)
    return [mine, send(other, swap), after, before, across, send(after, swap), send(before, swap)]


def add(left, right):
    return (left.astype(F32) + right.astype(F32)).astype(BF16)


def first_sum(peers, bit, outgoing, kept):
    arrived = send(outgoing, by_xor(peers, bit))
    return add(kept[1], arrived[1]), add(kept[0], arrived[0])


def next_sum(peers, bit, outgoing, kept):
    return add(kept, send(outgoing, by_xor(peers, bit)))


def last_terms(peers, pieces):
    count = peers // 4
    share = pieces.shape[0] // count
    terms = [pieces[:share]]
    for place in range(1, count):
        piece = pieces[place * share : (place + 1) * share]
        terms.append(send(piece, by_xor(peers, 4 * place)))
    return terms


def halve_sum(peers, pieces):
    count = peers // 4
    blocks = pieces.reshape(count // 2, 2, -1, pieces.shape[1])
    kept, outgoing = [blocks[:, place].reshape(-1, pieces.shape[1]) for place in range(2)]
    return add(kept, send(outgoing, by_xor(peers, 4)))


def rest_terms(peers, pieces):
    count = peers // 8
    share = pieces.shape[0] // count
    terms = [pieces[:share]]
    for place in range(1, count):
        piece = pieces[place * share : (place + 1) * share]
        terms.append(send(piece, by_xor(peers, 8 * place)))
    return terms


def total_of(terms, start, stop):
    total = terms[0][start:stop].astype(F32)
    for term in terms[1:]:
        total = total + term[start:stop].astype(F32)
    return total


def whole(shape):
    return pl.BlockSpec(shape, lambda *_: (0,) * len(shape))


def on_device(
    grid_latent,
    mesh_latent,
    edge_latent,
    mesh_cotangent,
    edge_src,
    edge_dst,
    tile_count,
    send_rows,
    w_edge_in,
    w_edge_out,
    w_node_in,
    w_node_out,
):
    peers = lax.axis_size("lon")
    me = lax.axis_index("lon").astype(jnp.int32).reshape(1)
    upper = peers // 4
    rows = send_rows[0]
    cap = rows.shape[1]
    slots = peers * cap
    edges, width = edge_latent.shape
    mesh_count = mesh_latent.shape[0]
    grid_count = grid_latent.shape[0]
    tiles = edges // STEP
    src = edge_src.reshape(tiles, 1, STEP)
    dst = edge_dst.reshape(tiles, 1, STEP)
    smem = pl.BlockSpec(memory_space=pltpu.SMEM)
    params = pltpu.CompilerParams(vmem_limit_bytes=VMEM_BYTES)
    square = (width, width)

    def tile_of(last):
        return pl.BlockSpec((STEP, last), lambda step, *_: (step, 0))

    index_tile = pl.BlockSpec((1, 1, STEP), lambda step, *_: (step, 0, 0))

    def weight(place):
        return pl.BlockSpec(square, lambda *_: (place, 0))

    def halves(share):
        shape = (2, upper * share, width)
        return [jax.ShapeDtypeStruct(shape, BF16)] * 2, [whole(shape)] * 2

    grid_part = grid_count // 2
    near_rows = (cap, cap, 2 * cap, 2 * cap, cap)
    near_specs = [whole((count, width)) for count in near_rows]
    near_shapes = [jax.ShapeDtypeStruct((count, width), BF16) for count in near_rows]
    core_specs = near_specs + [whole((2 * cap, width))] * 2
    back_rows = (cap, 3 * cap, cap, cap, cap)
    back_specs = [whole((count, width)) for count in back_rows]
    back_shapes = [jax.ShapeDtypeStruct((count, width), BF16) for count in back_rows]
    return_specs = [whole((count, width)) for count in (cap, 3 * cap, 2 * cap, 2 * cap, cap)]
    lists = pl.pallas_call(
        gather_kernel,
        grid=(2,),
        in_specs=[smem, whole(rows.shape), pl.BlockSpec((grid_part, width), lambda step: (step, 0))],
        out_specs=near_specs + [whole((cap, width))],
        out_shape=near_shapes + [jax.ShapeDtypeStruct((cap, width), BF16)],
        scratch_shapes=[pltpu.VMEM((8 * cap, width), F32)],
        compiler_params=params,
        name="gather_lists",
    )(me, rows, grid_latent)

    hops = [send(lists[5], by_xor(peers, 4 * place)) for place in range(1, upper)]
    near = exchange_near(peers, lists[:5])
    far_own = jnp.concatenate([lists[5]] + hops, axis=0)
    far_own, receivers = lax.optimization_barrier((far_own, dst))
    far_next = send(far_own, by_xor(peers, 2))
    far_core = send(far_own, by_xor(peers, 1))
    local = pl.pallas_call(
        local_kernel,
        grid=(tiles,),
        in_specs=[index_tile, tile_of(width), whole(mesh_latent.shape), weight(0), weight(2)],
        out_specs=tile_of(width),
        out_shape=jax.ShapeDtypeStruct((edges, width), BF16),
        scratch_shapes=[pltpu.VMEM((width + mesh_count, width), BF16)],
        compiler_params=params,
        cost_estimate=pl.CostEstimate(
            flops=2 * edges * width * (width + mesh_count),
            bytes_accessed=4 * edges * width,
            transcendentals=0,
        ),
        name="edge_local",
    )(receivers, edge_latent, mesh_latent, w_edge_in, w_edge_in)
    far_next, far_core, near, local = lax.optimization_barrier((far_next, far_core, near, local))
    near = core_near(peers, near)
    far_both = send(far_next, by_xor(peers, 1))

    node_shape, node_spec = halves(w_node_in.shape[0] // peers + w_node_out.shape[0] // peers)
    (received, hidden, slope, norm, inverse, node_send, node_keep, d_aggregate, d_mesh) = pl.pallas_call(
        functools.partial(forward_kernel, peers),
        grid=(tiles,),
        in_specs=[smem, smem, index_tile, index_tile, tile_of(width), tile_of(width)]
        + core_specs
        + [whole((upper * cap, width))] * 4
        + [weight(1)]
        + [whole(w.shape) for w in (w_edge_out, w_node_in, w_node_out, mesh_latent, mesh_cotangent)],
        out_specs=[whole((slots, width))]
        + [tile_of(width)] * 3
        + [index_tile]
        + node_spec
        + [whole((mesh_count, width))] * 2,
        out_shape=[jax.ShapeDtypeStruct((slots, width), BF16)]
        + [jax.ShapeDtypeStruct((edges, width), BF16)] * 3
        + [jax.ShapeDtypeStruct((tiles, 1, STEP), F32)]
        + node_shape
        + [jax.ShapeDtypeStruct((mesh_count, width), BF16), jax.ShapeDtypeStruct((mesh_count, width), F32)],
        scratch_shapes=[
            pltpu.VMEM((slots, width), BF16),
            pltpu.VMEM((mesh_count, width), F32),
            pltpu.VMEM(w_node_in.shape, F32),
            pltpu.VMEM(w_node_out.shape, F32),
        ],
        compiler_params=params,
        name="forward",
    )(
        me,
        tile_count,
        src,
        dst,
        local,
        edge_latent,
        *near,
        far_own,
        far_core,
        far_next,
        far_both,
        w_edge_in,
        w_edge_out,
        w_node_in,
        w_node_out,
        mesh_latent,
        mesh_cotangent,
    )

    node_next, node_kept = first_sum(peers, 2, node_send, node_keep)
    slot_shape, slot_spec = halves(w_edge_out.shape[0] // peers + cap)
    edge_shape, edge_spec = halves(w_edge_in.shape[0] // peers)
    results = pl.pallas_call(
        functools.partial(backward_kernel, peers),
        grid=(tiles,),
        in_specs=[smem, smem, index_tile, index_tile, index_tile]
        + [tile_of(width)] * 4
        + [whole((mesh_count, width)), whole((slots, width))]
        + [whole((mesh_count, width))] * 2
        + [weight(1), weight(2), weight(0), whole(square)],
        out_specs=[tile_of(width), whole((mesh_count, width))] + slot_spec + edge_spec + back_specs,
        out_shape=[
            jax.ShapeDtypeStruct((edges, width), BF16),
            jax.ShapeDtypeStruct((mesh_count, width), BF16),
        ]
        + slot_shape
        + edge_shape
        + back_shapes,
        scratch_shapes=[
            pltpu.VMEM((slots + mesh_count, width), F32),
            pltpu.VMEM(w_edge_in.shape, F32),
            pltpu.VMEM(square, F32),
            pltpu.VMEM((slots, width), BF16),
        ],
        compiler_params=params,
        cost_estimate=pl.CostEstimate(
            flops=2 * edges * width * (2 * mesh_count + 4 * width + slots),
            bytes_accessed=10 * edges * width,
            transcendentals=0,
        ),
        name="backward",
    )(
        me,
        tile_count,
        src,
        dst,
        inverse,
        hidden,
        slope,
        norm,
        edge_latent,
        d_aggregate,
        received,
        mesh_latent,
        d_mesh,
        w_edge_in,
        w_edge_in,
        w_edge_in,
        w_edge_out,
    )
    (edge_grad, mesh_grad, slot_send, slot_keep, edge_send, edge_keep), returns = results[:6], results[6:]
    (node_next, node_kept, slot_send, slot_keep, edge_send, edge_keep, returns) = lax.optimization_barrier(
        (node_next, node_kept, slot_send, slot_keep, edge_send, edge_keep, returns)
    )
    slot_next, slot_kept = first_sum(peers, 1, slot_send, slot_keep)
    edge_next, edge_kept = first_sum(peers, 1, edge_send, edge_keep)
    node_pieces = next_sum(peers, 1, node_next, node_kept)
    swapped = send(returns[1], by_xor(peers, 1))
    slot_pieces = next_sum(peers, 2, slot_next, slot_kept)
    node_pieces, edge_next, edge_kept, swapped, slot_next = lax.optimization_barrier(
        (node_pieces, edge_next, edge_kept, swapped, slot_next)
    )
    node_pieces = halve_sum(peers, node_pieces)
    to_after = jnp.concatenate([returns[2], swapped[cap : 2 * cap]], axis=0)
    to_before = jnp.concatenate([returns[3], swapped[2 * cap :]], axis=0)
    near = [
        send(to_after, by_shift(peers, 2)),
        send(to_before, by_shift(peers, -2)),
        send(returns[4], across_chips(peers)),
    ]
    (slot_pieces, edge_next, edge_kept, near, node_pieces) = lax.optimization_barrier(
        (slot_pieces, edge_next, edge_kept, near, node_pieces)
    )
    node_terms = rest_terms(peers, node_pieces)
    edge_pieces = next_sum(peers, 2, edge_next, edge_kept)
    slot_terms = last_terms(peers, slot_pieces)
    edge_terms = last_terms(peers, edge_pieces)
    node_terms, slot_terms = lax.optimization_barrier((node_terms, slot_terms))
    returned = [returns[0], swapped, *near]
    node_rows = w_node_in.shape[0] // peers
    out_rows = w_edge_out.shape[0] // peers
    grid_grad = pl.pallas_call(
        functools.partial(scatter_kernel, out_rows),
        grid=(2,),
        in_specs=[smem, whole(rows.shape)]
        + return_specs
        + [whole((out_rows + cap, width))] * upper,
        out_specs=pl.BlockSpec((grid_part, width), lambda step: (step, 0)),
        out_shape=jax.ShapeDtypeStruct((grid_count, width), BF16),
        compiler_params=params,
        name="scatter_lists",
    )(me, rows, *returned, *slot_terms)
    return (
        grid_grad,
        edge_grad,
        mesh_grad,
        total_of(edge_terms, 0, w_edge_in.shape[0] // peers),
        total_of(slot_terms, 0, out_rows),
        total_of(node_terms, 0, node_rows),
        total_of(node_terms, node_rows, node_rows + w_node_out.shape[0] // peers),
    )


def solution(mesh):
    rows = P(("grp", "lon"), None)
    flat = P(("grp", "lon"))
    return jax.shard_map(
        on_device,
        mesh=mesh,
        in_specs=(rows, rows, rows, rows, flat, flat, flat, P(("grp", "lon"), None, None)) + (P(),) * 4,
        out_specs=(rows,) * 7,
        check_vma=False,
    )
```

```python
import functools

import jax
import jax.numpy as jnp
from jax import lax
from jax.experimental import pallas as pl
from jax.experimental.pallas import tpu as pltpu
from jax.sharding import PartitionSpec as P

TILE = 256
STEP = 1024
SUB = 512
LANES = 128
GRID_PARTS = 4
NEAR = 3
BF16 = jnp.bfloat16
F32 = jnp.float32
VMEM_BYTES = 24 * 1024 * 1024
GATHER_BYTES = 56 * 1024 * 1024


def dot(left, right):
    return lax.dot_general(left, right, (((1,), (0,)), ((), ())), preferred_element_type=F32)


def contract_rows(left, right):
    return lax.dot_general(left, right, (((0,), (0,)), ((), ())), preferred_element_type=F32)


def contract_cols(left, right):
    return lax.dot_general(left, right, (((1,), (1,)), ((), ())), preferred_element_type=F32)


def layer_norm(values):
    centered = values - jnp.mean(values, axis=1, keepdims=True)
    inverse = lax.rsqrt(jnp.mean(centered * centered, axis=1, keepdims=True) + 1e-05)
    return (centered * inverse, inverse)


def norm_back(normed, inverse, upstream):
    first = jnp.mean(upstream, axis=1, keepdims=True)
    second = jnp.mean(upstream * normed, axis=1, keepdims=True)
    return inverse * (upstream - first - normed * second)


def silu_and_slope(values):
    sigma = 0.5 + 0.5 * jnp.tanh(0.5 * values)
    hidden = values * sigma
    return (hidden, sigma + hidden * (1.0 - sigma))


def as_column(row):
    count = row.shape[1]
    block = min(count, LANES)
    down = lax.broadcasted_iota(jnp.int32, (block, block), 0)
    along = lax.broadcasted_iota(jnp.int32, (block, block), 1)
    columns = []
    for start in range(0, count, block):
        piece = row[:, start : start + block].astype(F32)
        picked = jnp.where(down == along, piece, 0.0)
        columns.append(jnp.sum(picked, axis=1, keepdims=True))
    return jnp.concatenate(columns, axis=0)


def as_row(column):
    count = column.shape[0]
    block = min(count, LANES)
    down = lax.broadcasted_iota(jnp.int32, (block, block), 0)
    along = lax.broadcasted_iota(jnp.int32, (block, block), 1)
    rows = []
    for start in range(0, count, block):
        picked = jnp.where(down == along, column[start : start + block], 0.0)
        rows.append(jnp.sum(picked, axis=0, keepdims=True))
    return jnp.concatenate(rows, axis=1)


def hot_rows(row, width, first=0):
    column = as_column(row).astype(jnp.int32) - first
    along = lax.broadcasted_iota(jnp.int32, (row.shape[1], width), 1)
    return (column == along).astype(F32).astype(BF16)


def hot_columns(row, height):
    down = lax.broadcasted_iota(jnp.int32, (height, row.shape[1]), 0)
    return (row == down).astype(F32).astype(BF16)


def live_only(row, first, count):
    place = first + lax.broadcasted_iota(jnp.int32, row.shape, 1)
    return jnp.where(place < count, row, -1)


def near_peers(me, peers):
    after = lax.rem(me + 2, peers)
    before = lax.rem(me + peers - 2, peers)
    across = lax.rem(me + peers - 3 + 6 * (me & 1), peers)
    return (me, me ^ 1, after, after ^ 1, before, before ^ 1, across)


def write_near(refs, cap, lists):
    mine, other, after, before, across = refs
    mine[...] = lists[0]
    other[...] = lists[1]
    after[:cap, :] = lists[2]
    after[cap:, :] = lists[3]
    before[:cap, :] = lists[4]
    before[cap:, :] = lists[5]
    across[...] = lists[6]


def read_near(refs, cap):
    mine, other, from_before, from_after, across, core_before, core_after = refs
    return [
        mine[...],
        other[...],
        from_after[:cap, :],
        core_after[cap:, :],
        from_before[:cap, :],
        core_before[cap:, :],
        across[...],
    ]


def write_back(refs, cap, lists):
    mine, swapped, after, before, across = refs
    mine[...] = lists[0]
    for place, index in enumerate((1, 3, 5)):
        swapped[place * cap : (place + 1) * cap, :] = lists[index]
    after[...] = lists[2]
    before[...] = lists[4]
    across[...] = lists[6]


def read_back(refs, cap):
    mine, swapped, from_before, from_after, across = refs
    return [
        mine[...],
        swapped[:cap, :],
        from_after[:cap, :],
        from_after[cap:, :],
        from_before[:cap, :],
        from_before[cap:, :],
        across[...],
    ]


def list_hots(me, rows_ref, grid_count, first):
    peers, cap = rows_ref.shape
    pieces = []
    for target in near_peers(me, peers):
        pieces.append(hot_rows(rows_ref[pl.ds(target, 1), :], grid_count, first))
    peer = lax.broadcasted_iota(jnp.int32, (peers, cap), 0)
    ahead = lax.rem(peer - me + peers, peers)
    apart = jnp.minimum(ahead, peers - ahead)
    far = jnp.max(jnp.where(apart > NEAR, rows_ref[...].astype(F32), -1.0), axis=0, keepdims=True)
    pieces.append(hot_rows(far.astype(jnp.int32), grid_count, first))
    return jnp.concatenate(pieces, axis=0)


def gather_kernel(me_ref, rows_hbm, grid_hbm, *refs):
    near_refs, far_ref = refs[:5], refs[5]
    rows_ref, grid_ref, rows_done, grid_done = refs[6:]
    cap = rows_ref.shape[1]
    part = grid_ref.shape[0] // GRID_PARTS
    copies = [
        pltpu.make_async_copy(
            grid_hbm.at[pl.ds(at * part, part)], grid_ref.at[pl.ds(at * part, part)], grid_done.at[at]
        )
        for at in range(GRID_PARTS)
    ]
    rows_copy = pltpu.make_async_copy(rows_hbm, rows_ref, rows_done)
    rows_copy.start()
    for copy in copies:
        copy.start()
    rows_copy.wait()
    found = None
    for at, copy in enumerate(copies):
        hots = list_hots(me_ref[0], rows_ref, part, at * part)
        copy.wait()
        piece = dot(hots, grid_ref[at * part : (at + 1) * part, :])
        found = piece if found is None else found + piece
    rows = found.astype(BF16)
    lists = [rows[at : at + cap] for at in range(0, 8 * cap, cap)]
    write_near(near_refs, cap, lists)
    far_ref[...] = lists[7]


def scatter_kernel(skip, me_ref, rows_ref, *refs):
    near_refs, far_refs, out_ref = refs[:5], refs[5:-1], refs[-1]
    part = out_ref.shape[0]
    cap = rows_ref.shape[1]
    hots = list_hots(me_ref[0], rows_ref, part, pl.program_id(0) * part)
    far = far_refs[0][skip:, :].astype(F32)
    for ref in far_refs[1:]:
        far = far + ref[skip:, :].astype(F32)
    values = jnp.concatenate(read_back(near_refs, cap) + [far.astype(BF16)], axis=0)
    out_ref[...] = contract_rows(hots, values).astype(BF16)


def halves_of(ref):
    rows = ref.shape[-1] if len(ref.shape) == 3 else ref.shape[0]
    return [(start, slice(start, start + SUB)) for start in range(0, rows, SUB)]


def local_kernel(dst_ref, edge_ref, mesh_ref, w_edge_ref, w_receiver_ref, out_ref, weights):
    width = edge_ref.shape[1]

    @pl.when(pl.program_id(0) == 0)
    def _():
        weights[:width, :] = w_edge_ref[...]
        weights[width:, :] = dot(mesh_ref[...], w_receiver_ref[...]).astype(BF16)

    for start, part in halves_of(edge_ref):
        onehot = hot_rows(dst_ref[0, :, part], mesh_ref.shape[0])
        joined = jnp.concatenate([edge_ref[part, :], onehot], axis=1)
        out_ref[part, :] = dot(joined, weights[...]).astype(BF16)


def split_out(me, peers, first, send_ref, keep_ref, parts):
    for low in range(4):
        target = send_ref if low & first else keep_ref
        half = 1 if low & (3 - first) else 0
        at = 0
        for upper in range(peers // 4):
            owner = me ^ (4 * upper + low)
            for ref, share, far in parts:
                piece = ref[pl.ds(pl.multiple_of(owner * share, 16), share), :]
                if far:
                    ahead = lax.rem(owner - me + peers, peers)
                    apart = jnp.minimum(ahead, peers - ahead)
                    piece = jnp.where(apart > NEAR, piece.astype(F32), 0.0)
                target[half, at : at + share, :] = piece.astype(BF16)
                at += share


def forward_kernel(
    peers, me_ref, count_ref, src_ref, dst_ref, local_ref, edge_ref, *refs
):
    near_refs, far_refs = refs[:7], refs[7:11]
    (w_sender_ref, w_out_ref, w_node_in_ref, w_node_out_ref, mesh_ref, cotangent_ref) = refs[11:17]
    (received_ref, hidden_ref, slope_ref, norm_ref, inverse_ref) = refs[17:22]
    (send_ref, keep_ref, d_aggregate_ref, d_mesh_ref) = refs[22:26]
    (slot_proj, aggregate, grad_in, grad_out) = refs[26:]
    step = pl.program_id(0)
    me = me_ref[0]
    cap = near_refs[0].shape[0]
    width = edge_ref.shape[1]

    @pl.when(step == 0)
    def _():
        aggregate[...] = jnp.zeros_like(aggregate)
        w_sender = w_sender_ref[...]

        def place(owner, rows, projected):
            offset = pl.multiple_of(owner * cap, 16)
            received_ref[pl.ds(offset, cap), :] = rows
            slot_proj[pl.ds(offset, cap), :] = projected

        for low, ref in enumerate(far_refs):
            rows = ref[...]
            projected = dot(rows, w_sender).astype(BF16)
            for upper in range(peers // 4):
                span = slice(upper * cap, (upper + 1) * cap)
                place(me ^ (4 * upper + low), rows[span], projected[span])
        rows = jnp.concatenate(read_near(near_refs, cap), axis=0)
        projected = dot(rows, w_sender).astype(BF16)
        for spot, owner in enumerate(near_peers(me, peers)):
            place(owner, rows[spot * cap : (spot + 1) * cap], projected[spot * cap : (spot + 1) * cap])

    @pl.when(step * STEP < count_ref[0] * TILE)
    def _():
        parts = halves_of(edge_ref)
        pres = []
        for start, part in parts:
            onehot = hot_rows(src_ref[0, :, part], slot_proj.shape[0])
            pres.append(local_ref[part, :].astype(F32) + dot(onehot, slot_proj[...]))
        projs = []
        for (start, part), pre in zip(parts, pres):
            hidden, slope = silu_and_slope(pre)
            hidden = hidden.astype(BF16)
            hidden_ref[part, :] = hidden
            slope_ref[part, :] = slope.astype(BF16)
            projs.append(dot(hidden, w_out_ref[...]))
        for (start, part), proj in zip(parts, projs):
            normed, inverse = layer_norm(proj)
            norm_ref[part, :] = normed.astype(BF16)
            inverse_ref[0, :, part] = as_row(inverse)
            edge_new = (edge_ref[part, :].astype(F32) + normed).astype(BF16)
            receivers = live_only(dst_ref[0, :, part], step * STEP + start, count_ref[0] * TILE)
            aggregate[...] += dot(hot_columns(receivers, aggregate.shape[0]), edge_new)

    @pl.when(step == pl.num_programs(0) - 1)
    def _():
        mesh = mesh_ref[...]
        summed = aggregate[...].astype(BF16)
        node_pre = dot(mesh, w_node_in_ref[:width, :]) + dot(summed, w_node_in_ref[width:, :])
        hidden, slope = silu_and_slope(node_pre)
        hidden = hidden.astype(BF16)
        normed, inverse = layer_norm(dot(hidden, w_node_out_ref[...]))
        upstream = cotangent_ref[...].astype(F32)
        d_proj = norm_back(normed, inverse, upstream).astype(BF16)
        d_pre = (contract_cols(d_proj, w_node_out_ref[...]) * slope).astype(BF16)
        d_mesh_ref[...] = upstream + contract_cols(d_pre, w_node_in_ref[:width, :])
        d_aggregate_ref[...] = contract_cols(d_pre, w_node_in_ref[width:, :]).astype(BF16)
        grad_out[...] = contract_rows(hidden, d_proj)
        grad_in[:width, :] = contract_rows(mesh, d_pre)
        grad_in[width:, :] = contract_rows(summed, d_pre)
        split_out(
            me,
            peers,
            2,
            send_ref,
            keep_ref,
            ((grad_in, grad_in.shape[0] // peers, False), (grad_out, grad_out.shape[0] // peers, False)),
        )


def backward_kernel(peers, me_ref, count_ref, src_ref, dst_ref, inverse_ref, *refs):
    (hidden_ref, slope_ref, norm_ref, edge_ref) = refs[:4]
    (d_aggregate_ref, received_ref, mesh_ref, d_mesh_ref) = refs[4:8]
    (w_sender_ref, w_receiver_ref, w_edge_ref, w_out_ref) = refs[8:12]
    (edge_grad_ref, mesh_grad_ref, slot_send_ref, slot_keep_ref, edge_send_ref, edge_keep_ref) = refs[12:18]
    near_refs = refs[18:23]
    (end_sum, grad_in, grad_out, d_slots) = refs[23:]
    step = pl.program_id(0)
    me = me_ref[0]
    slots, width = received_ref.shape
    mesh_count = mesh_ref.shape[0]

    @pl.when(step == 0)
    def _():
        end_sum[...] = jnp.zeros_like(end_sum)
        grad_in[:width, :] = jnp.zeros((width, width), F32)
        grad_out[...] = jnp.zeros_like(grad_out)

    @pl.when(step * STEP < count_ref[0] * TILE)
    def _():
        parts = halves_of(hidden_ref)
        upstreams = []
        columns = []
        for start, part in parts:
            first = step * STEP + start
            live = count_ref[0] * TILE
            receivers = live_only(dst_ref[0, :, part], first, live)
            upstreams.append(dot(hot_rows(receivers, mesh_count), d_aggregate_ref[...]))
            senders = live_only(src_ref[0, :, part], first, live)
            columns.append(
                jnp.concatenate([hot_columns(senders, slots), hot_columns(receivers, mesh_count)], axis=0)
            )
        d_projs = []
        d_hiddens = []
        for (start, part), upstream in zip(parts, upstreams):
            inverse = as_column(inverse_ref[0, :, part])
            d_proj = norm_back(norm_ref[part, :].astype(F32), inverse, upstream).astype(BF16)
            d_projs.append(d_proj)
            d_hiddens.append(contract_cols(d_proj, w_out_ref[...]))
        for (start, part), d_proj, d_hidden, column, upstream in zip(
            parts, d_projs, d_hiddens, columns, upstreams
        ):
            grad_out[...] += contract_rows(hidden_ref[part, :], d_proj)
            d_pre = (d_hidden * slope_ref[part, :].astype(F32)).astype(BF16)
            edge_grad_ref[part, :] = (upstream + contract_cols(d_pre, w_edge_ref[...])).astype(BF16)
            end_sum[...] += dot(column, d_pre)
            grad_in[:width, :] += contract_rows(edge_ref[part, :], d_pre)

    @pl.when(step * STEP >= count_ref[0] * TILE)
    def _():
        edge_grad_ref[...] = jnp.zeros_like(edge_grad_ref)

    @pl.when(step == pl.num_programs(0) - 1)
    def _():
        summed = end_sum[:slots, :].astype(BF16)
        mesh_summed = end_sum[slots:, :].astype(BF16)
        d_slots[...] = contract_cols(summed, w_sender_ref[...]).astype(BF16)
        grad_in[width : 2 * width, :] = contract_rows(received_ref[...], summed)
        grad_in[2 * width :, :] = contract_rows(mesh_ref[...], mesh_summed)
        mesh_grad_ref[...] = (d_mesh_ref[...] + contract_cols(mesh_summed, w_receiver_ref[...])).astype(BF16)
        cap = near_refs[0].shape[0]
        owners = near_peers(me, peers)
        write_back(
            near_refs, cap, [d_slots[pl.ds(pl.multiple_of(owner * cap, 16), cap), :] for owner in owners]
        )
        out_share = grad_out.shape[0] // peers
        split_out(
            me, peers, 1, slot_send_ref, slot_keep_ref, ((grad_out, out_share, False), (d_slots, cap, True))
        )
        split_out(
            me, peers, 1, edge_send_ref, edge_keep_ref, ((grad_in, grad_in.shape[0] // peers, False),)
        )


def send(values, perm):
    return lax.ppermute(values, "lon", perm)


def by_xor(peers, bits):
    return [(peer, peer ^ bits) for peer in range(peers)]


def by_shift(peers, shift):
    return [(peer, (peer + shift) % peers) for peer in range(peers)]


def across_chips(peers):
    return [(peer, (peer + (3 if peer % 2 else -3)) % peers) for peer in range(peers)]


def exchange_near(peers, lists):
    mine, other, after, before, across = lists
    return [
        mine,
        other,
        send(after, by_shift(peers, 2)),
        send(before, by_shift(peers, -2)),
        send(across, across_chips(peers)),
    ]


def core_near(peers, near):
    mine, other, after, before, across = near
    swap = by_xor(peers, 1)
    return [mine, send(other, swap), after, before, across, send(after, swap), send(before, swap)]


def add(left, right):
    return (left.astype(F32) + right.astype(F32)).astype(BF16)


def first_sum(peers, bit, outgoing, kept):
    arrived = send(outgoing, by_xor(peers, bit))
    return add(kept[1], arrived[1]), add(kept[0], arrived[0])


def next_sum(peers, bit, outgoing, kept):
    return add(kept, send(outgoing, by_xor(peers, bit)))


def last_terms(peers, pieces):
    count = peers // 4
    share = pieces.shape[0] // count
    terms = [pieces[:share]]
    for place in range(1, count):
        piece = pieces[place * share : (place + 1) * share]
        terms.append(send(piece, by_xor(peers, 4 * place)))
    return terms


def halve_sum(peers, pieces):
    count = peers // 4
    blocks = pieces.reshape(count // 2, 2, -1, pieces.shape[1])
    kept, outgoing = [blocks[:, place].reshape(-1, pieces.shape[1]) for place in range(2)]
    return add(kept, send(outgoing, by_xor(peers, 4)))


def rest_terms(peers, pieces):
    count = peers // 8
    share = pieces.shape[0] // count
    terms = [pieces[:share]]
    for place in range(1, count):
        piece = pieces[place * share : (place + 1) * share]
        terms.append(send(piece, by_xor(peers, 8 * place)))
    return terms


def total_of(terms, start, stop):
    total = terms[0][start:stop].astype(F32)
    for term in terms[1:]:
        total = total + term[start:stop].astype(F32)
    return total


def whole(shape):
    return pl.BlockSpec(shape, lambda *_: (0,) * len(shape))


def on_device(
    grid_latent,
    mesh_latent,
    edge_latent,
    mesh_cotangent,
    edge_src,
    edge_dst,
    tile_count,
    send_rows,
    w_edge_in,
    w_edge_out,
    w_node_in,
    w_node_out,
):
    peers = lax.axis_size("lon")
    me = lax.axis_index("lon").astype(jnp.int32).reshape(1)
    upper = peers // 4
    rows = send_rows[0]
    cap = rows.shape[1]
    slots = peers * cap
    edges, width = edge_latent.shape
    mesh_count = mesh_latent.shape[0]
    grid_count = grid_latent.shape[0]
    tiles = edges // STEP
    src = edge_src.reshape(tiles, 1, STEP)
    dst = edge_dst.reshape(tiles, 1, STEP)
    smem = pl.BlockSpec(memory_space=pltpu.SMEM)
    hbm = pl.BlockSpec(memory_space=pltpu.HBM)
    params = pltpu.CompilerParams(vmem_limit_bytes=VMEM_BYTES)
    square = (width, width)

    def tile_of(last):
        return pl.BlockSpec((STEP, last), lambda step, *_: (step, 0))

    index_tile = pl.BlockSpec((1, 1, STEP), lambda step, *_: (step, 0, 0))

    def weight(place):
        return pl.BlockSpec(square, lambda *_: (place, 0))

    def halves(share):
        shape = (2, upper * share, width)
        return [jax.ShapeDtypeStruct(shape, BF16)] * 2, [whole(shape)] * 2

    grid_part = grid_count // 2
    near_rows = (cap, cap, 2 * cap, 2 * cap, cap)
    near_specs = [whole((count, width)) for count in near_rows]
    near_shapes = [jax.ShapeDtypeStruct((count, width), BF16) for count in near_rows]
    core_specs = near_specs + [whole((2 * cap, width))] * 2
    back_rows = (cap, 3 * cap, cap, cap, cap)
    back_specs = [whole((count, width)) for count in back_rows]
    back_shapes = [jax.ShapeDtypeStruct((count, width), BF16) for count in back_rows]
    return_specs = [whole((count, width)) for count in (cap, 3 * cap, 2 * cap, 2 * cap, cap)]
    lists = pl.pallas_call(
        gather_kernel,
        in_specs=[smem, hbm, hbm],
        out_specs=near_specs + [whole((cap, width))],
        out_shape=near_shapes + [jax.ShapeDtypeStruct((cap, width), BF16)],
        scratch_shapes=[
            pltpu.VMEM(rows.shape, jnp.int32),
            pltpu.VMEM(grid_latent.shape, BF16),
            pltpu.SemaphoreType.DMA,
            pltpu.SemaphoreType.DMA((GRID_PARTS,)),
        ],
        compiler_params=pltpu.CompilerParams(vmem_limit_bytes=GATHER_BYTES),
        cost_estimate=pl.CostEstimate(
            flops=40 * 16 * cap * grid_count * width,
            bytes_accessed=2 * grid_count * width,
            transcendentals=0,
        ),
        name="gather_lists",
    )(me, rows, grid_latent)

    hops = [send(lists[5], by_xor(peers, 4 * place)) for place in range(1, upper)]
    near = exchange_near(peers, lists[:5])
    far_own = jnp.concatenate([lists[5]] + hops, axis=0)
    far_own, receivers = lax.optimization_barrier((far_own, dst))
    far_next = send(far_own, by_xor(peers, 2))
    far_core = send(far_own, by_xor(peers, 1))
    local = pl.pallas_call(
        local_kernel,
        grid=(tiles,),
        in_specs=[index_tile, tile_of(width), whole(mesh_latent.shape), weight(0), weight(2)],
        out_specs=tile_of(width),
        out_shape=jax.ShapeDtypeStruct((edges, width), BF16),
        scratch_shapes=[pltpu.VMEM((width + mesh_count, width), BF16)],
        compiler_params=params,
        cost_estimate=pl.CostEstimate(
            flops=2 * edges * width * (width + mesh_count),
            bytes_accessed=4 * edges * width,
            transcendentals=0,
        ),
        name="edge_local",
    )(receivers, edge_latent, mesh_latent, w_edge_in, w_edge_in)
    far_next, far_core, near, local = lax.optimization_barrier((far_next, far_core, near, local))
    near = core_near(peers, near)
    far_both = send(far_next, by_xor(peers, 1))

    node_shape, node_spec = halves(w_node_in.shape[0] // peers + w_node_out.shape[0] // peers)
    (received, hidden, slope, norm, inverse, node_send, node_keep, d_aggregate, d_mesh) = pl.pallas_call(
        functools.partial(forward_kernel, peers),
        grid=(tiles,),
        in_specs=[smem, smem, index_tile, index_tile, tile_of(width), tile_of(width)]
        + core_specs
        + [whole((upper * cap, width))] * 4
        + [weight(1)]
        + [whole(w.shape) for w in (w_edge_out, w_node_in, w_node_out, mesh_latent, mesh_cotangent)],
        out_specs=[whole((slots, width))]
        + [tile_of(width)] * 3
        + [index_tile]
        + node_spec
        + [whole((mesh_count, width))] * 2,
        out_shape=[jax.ShapeDtypeStruct((slots, width), BF16)]
        + [jax.ShapeDtypeStruct((edges, width), BF16)] * 3
        + [jax.ShapeDtypeStruct((tiles, 1, STEP), F32)]
        + node_shape
        + [jax.ShapeDtypeStruct((mesh_count, width), BF16), jax.ShapeDtypeStruct((mesh_count, width), F32)],
        scratch_shapes=[
            pltpu.VMEM((slots, width), BF16),
            pltpu.VMEM((mesh_count, width), F32),
            pltpu.VMEM(w_node_in.shape, F32),
            pltpu.VMEM(w_node_out.shape, F32),
        ],
        compiler_params=params,
        name="forward",
    )(
        me,
        tile_count,
        src,
        dst,
        local,
        edge_latent,
        *near,
        far_own,
        far_core,
        far_next,
        far_both,
        w_edge_in,
        w_edge_out,
        w_node_in,
        w_node_out,
        mesh_latent,
        mesh_cotangent,
    )

    node_next, node_kept = first_sum(peers, 2, node_send, node_keep)
    slot_shape, slot_spec = halves(w_edge_out.shape[0] // peers + cap)
    edge_shape, edge_spec = halves(w_edge_in.shape[0] // peers)
    results = pl.pallas_call(
        functools.partial(backward_kernel, peers),
        grid=(tiles,),
        in_specs=[smem, smem, index_tile, index_tile, index_tile]
        + [tile_of(width)] * 4
        + [whole((mesh_count, width)), whole((slots, width))]
        + [whole((mesh_count, width))] * 2
        + [weight(1), weight(2), weight(0), whole(square)],
        out_specs=[tile_of(width), whole((mesh_count, width))] + slot_spec + edge_spec + back_specs,
        out_shape=[
            jax.ShapeDtypeStruct((edges, width), BF16),
            jax.ShapeDtypeStruct((mesh_count, width), BF16),
        ]
        + slot_shape
        + edge_shape
        + back_shapes,
        scratch_shapes=[
            pltpu.VMEM((slots + mesh_count, width), F32),
            pltpu.VMEM(w_edge_in.shape, F32),
            pltpu.VMEM(square, F32),
            pltpu.VMEM((slots, width), BF16),
        ],
        compiler_params=params,
        cost_estimate=pl.CostEstimate(
            flops=2 * edges * width * (2 * mesh_count + 4 * width + slots),
            bytes_accessed=10 * edges * width,
            transcendentals=0,
        ),
        name="backward",
    )(
        me,
        tile_count,
        src,
        dst,
        inverse,
        hidden,
        slope,
        norm,
        edge_latent,
        d_aggregate,
        received,
        mesh_latent,
        d_mesh,
        w_edge_in,
        w_edge_in,
        w_edge_in,
        w_edge_out,
    )
    (edge_grad, mesh_grad, slot_send, slot_keep, edge_send, edge_keep), returns = results[:6], results[6:]
    (node_next, node_kept, slot_send, slot_keep, edge_send, edge_keep, returns) = lax.optimization_barrier(
        (node_next, node_kept, slot_send, slot_keep, edge_send, edge_keep, returns)
    )
    slot_next, slot_kept = first_sum(peers, 1, slot_send, slot_keep)
    edge_next, edge_kept = first_sum(peers, 1, edge_send, edge_keep)
    node_pieces = next_sum(peers, 1, node_next, node_kept)
    swapped = send(returns[1], by_xor(peers, 1))
    slot_pieces = next_sum(peers, 2, slot_next, slot_kept)
    node_pieces, edge_next, edge_kept, swapped, across = lax.optimization_barrier(
        (node_pieces, edge_next, edge_kept, swapped, returns[4])
    )
    node_pieces = halve_sum(peers, node_pieces)
    across = send(across, across_chips(peers))
    to_after = jnp.concatenate([returns[2], swapped[cap : 2 * cap]], axis=0)
    to_before = jnp.concatenate([returns[3], swapped[2 * cap :]], axis=0)
    (slot_pieces, edge_next, edge_kept, across, node_pieces, to_after, to_before) = lax.optimization_barrier(
        (slot_pieces, edge_next, edge_kept, across, node_pieces, to_after, to_before)
    )
    edge_pieces = next_sum(peers, 2, edge_next, edge_kept)
    slot_half = halve_sum(peers, slot_pieces)
    node_terms = rest_terms(peers, node_pieces)
    (slot_half, edge_pieces, node_terms, to_after, to_before) = lax.optimization_barrier(
        (slot_half, edge_pieces, node_terms, to_after, to_before)
    )
    slot_terms = rest_terms(peers, slot_half)
    edge_terms = last_terms(peers, edge_pieces)
    bundles = [send(to_after, by_shift(peers, 2)), send(to_before, by_shift(peers, -2))]
    node_terms, slot_terms = lax.optimization_barrier((node_terms, slot_terms))
    returned = [returns[0], swapped, *bundles, across]
    node_rows = w_node_in.shape[0] // peers
    out_rows = w_edge_out.shape[0] // peers
    grid_grad = pl.pallas_call(
        functools.partial(scatter_kernel, out_rows),
        grid=(2,),
        in_specs=[smem, whole(rows.shape)]
        + return_specs
        + [whole((out_rows + cap, width))] * (upper // 2),
        out_specs=pl.BlockSpec((grid_part, width), lambda step: (step, 0)),
        out_shape=jax.ShapeDtypeStruct((grid_count, width), BF16),
        compiler_params=params,
        name="scatter_lists",
    )(me, rows, *returned, *slot_terms)
    edge_terms, grid_grad = lax.optimization_barrier((edge_terms, grid_grad))
    return (
        grid_grad,
        edge_grad,
        mesh_grad,
        total_of(edge_terms, 0, w_edge_in.shape[0] // peers),
        total_of(slot_terms, 0, out_rows),
        total_of(node_terms, 0, node_rows),
        total_of(node_terms, node_rows, node_rows + w_node_out.shape[0] // peers),
    )


def solution(mesh):
    rows = P(("grp", "lon"), None)
    flat = P(("grp", "lon"))
    return jax.shard_map(
        on_device,
        mesh=mesh,
        in_specs=(rows, rows, rows, rows, flat, flat, flat, P(("grp", "lon"), None, None)) + (P(),) * 4,
        out_specs=(rows,) * 7,
        check_vma=False,
    )
```

```python
import functools

import jax
import jax.numpy as jnp
from jax import lax
from jax.experimental import pallas as pl
from jax.experimental.pallas import tpu as pltpu
from jax.sharding import PartitionSpec as P

TILE = 256
STEP = 1024
SUB = 512
LANES = 128
GRID_PARTS = 4
NEAR = 3
BF16 = jnp.bfloat16
F32 = jnp.float32
VMEM_BYTES = 24 * 1024 * 1024
GATHER_BYTES = 56 * 1024 * 1024


def dot(left, right):
    return lax.dot_general(left, right, (((1,), (0,)), ((), ())), preferred_element_type=F32)


def contract_rows(left, right):
    return lax.dot_general(left, right, (((0,), (0,)), ((), ())), preferred_element_type=F32)


def contract_cols(left, right):
    return lax.dot_general(left, right, (((1,), (1,)), ((), ())), preferred_element_type=F32)


def layer_norm(values):
    centered = values - jnp.mean(values, axis=1, keepdims=True)
    inverse = lax.rsqrt(jnp.mean(centered * centered, axis=1, keepdims=True) + 1e-05)
    return (centered * inverse, inverse)


def norm_back(normed, inverse, upstream):
    first = jnp.mean(upstream, axis=1, keepdims=True)
    second = jnp.mean(upstream * normed, axis=1, keepdims=True)
    return inverse * (upstream - first - normed * second)


def silu_and_slope(values):
    sigma = 0.5 + 0.5 * jnp.tanh(0.5 * values)
    hidden = values * sigma
    return (hidden, sigma + hidden * (1.0 - sigma))


def as_column(row):
    count = row.shape[1]
    block = min(count, LANES)
    down = lax.broadcasted_iota(jnp.int32, (block, block), 0)
    along = lax.broadcasted_iota(jnp.int32, (block, block), 1)
    columns = []
    for start in range(0, count, block):
        piece = row[:, start : start + block].astype(F32)
        picked = jnp.where(down == along, piece, 0.0)
        columns.append(jnp.sum(picked, axis=1, keepdims=True))
    return jnp.concatenate(columns, axis=0)


def as_row(column):
    count = column.shape[0]
    block = min(count, LANES)
    down = lax.broadcasted_iota(jnp.int32, (block, block), 0)
    along = lax.broadcasted_iota(jnp.int32, (block, block), 1)
    rows = []
    for start in range(0, count, block):
        picked = jnp.where(down == along, column[start : start + block], 0.0)
        rows.append(jnp.sum(picked, axis=0, keepdims=True))
    return jnp.concatenate(rows, axis=1)


def hot_rows(row, width, first=0):
    column = as_column(row).astype(jnp.int32) - first
    along = lax.broadcasted_iota(jnp.int32, (row.shape[1], width), 1)
    return (column == along).astype(F32).astype(BF16)


def hot_columns(row, height):
    down = lax.broadcasted_iota(jnp.int32, (height, row.shape[1]), 0)
    return (row == down).astype(F32).astype(BF16)


def live_only(row, first, count):
    place = first + lax.broadcasted_iota(jnp.int32, row.shape, 1)
    return jnp.where(place < count, row, -1)


def near_peers(me, peers):
    after = lax.rem(me + 2, peers)
    before = lax.rem(me + peers - 2, peers)
    across = lax.rem(me + peers - 3 + 6 * (me & 1), peers)
    return (me, me ^ 1, after, after ^ 1, before, before ^ 1, across)


def write_near(refs, cap, lists):
    mine, other, after, before, across = refs
    mine[...] = lists[0]
    other[...] = lists[1]
    after[:cap, :] = lists[2]
    after[cap:, :] = lists[3]
    before[:cap, :] = lists[4]
    before[cap:, :] = lists[5]
    across[...] = lists[6]


def read_near(refs, cap):
    mine, other, from_before, from_after, across, core_before, core_after = refs
    return [
        mine[...],
        other[...],
        from_after[:cap, :],
        core_after[cap:, :],
        from_before[:cap, :],
        core_before[cap:, :],
        across[...],
    ]


def list_hots(me, rows_ref, grid_count, first):
    peers, cap = rows_ref.shape
    pieces = []
    for target in near_peers(me, peers):
        pieces.append(hot_rows(rows_ref[pl.ds(target, 1), :], grid_count, first))
    peer = lax.broadcasted_iota(jnp.int32, (peers, cap), 0)
    ahead = lax.rem(peer - me + peers, peers)
    apart = jnp.minimum(ahead, peers - ahead)
    far = jnp.max(jnp.where(apart > NEAR, rows_ref[...].astype(F32), -1.0), axis=0, keepdims=True)
    pieces.append(hot_rows(far.astype(jnp.int32), grid_count, first))
    return jnp.concatenate(pieces, axis=0)


def gather_kernel(me_ref, rows_hbm, grid_hbm, *refs):
    near_refs, far_ref = refs[:5], refs[5]
    rows_ref, grid_ref, rows_done, grid_done = refs[6:]
    cap = rows_ref.shape[1]
    part = grid_ref.shape[0] // GRID_PARTS
    copies = [
        pltpu.make_async_copy(
            grid_hbm.at[pl.ds(at * part, part)], grid_ref.at[pl.ds(at * part, part)], grid_done.at[at]
        )
        for at in range(GRID_PARTS)
    ]
    rows_copy = pltpu.make_async_copy(rows_hbm, rows_ref, rows_done)
    rows_copy.start()
    for copy in copies:
        copy.start()
    rows_copy.wait()
    found = None
    for at, copy in enumerate(copies):
        hots = list_hots(me_ref[0], rows_ref, part, at * part)
        copy.wait()
        piece = dot(hots, grid_ref[at * part : (at + 1) * part, :])
        found = piece if found is None else found + piece
    rows = found.astype(BF16)
    lists = [rows[at : at + cap] for at in range(0, 8 * cap, cap)]
    write_near(near_refs, cap, lists)
    far_ref[...] = lists[7]


def scatter_kernel(skip, me_ref, rows_ref, *refs):
    near_refs, far_refs, out_ref = refs[:7], refs[7:-1], refs[-1]
    part = out_ref.shape[0]
    cap = rows_ref.shape[1]
    hots = list_hots(me_ref[0], rows_ref, part, pl.program_id(0) * part)
    far = far_refs[0][skip:, :].astype(F32)
    for ref in far_refs[1:]:
        far = far + ref[skip:, :].astype(F32)
    values = jnp.concatenate(read_near(near_refs, cap) + [far.astype(BF16)], axis=0)
    out_ref[...] = contract_rows(hots, values).astype(BF16)


def halves_of(ref):
    rows = ref.shape[-1] if len(ref.shape) == 3 else ref.shape[0]
    return [(start, slice(start, start + SUB)) for start in range(0, rows, SUB)]


def local_kernel(dst_ref, edge_ref, mesh_ref, w_edge_ref, w_receiver_ref, out_ref, weights):
    width = edge_ref.shape[1]

    @pl.when(pl.program_id(0) == 0)
    def _():
        weights[:width, :] = w_edge_ref[...]
        weights[width:, :] = dot(mesh_ref[...], w_receiver_ref[...]).astype(BF16)

    for start, part in halves_of(edge_ref):
        onehot = hot_rows(dst_ref[0, :, part], mesh_ref.shape[0])
        joined = jnp.concatenate([edge_ref[part, :], onehot], axis=1)
        out_ref[part, :] = dot(joined, weights[...]).astype(BF16)


def split_out(me, peers, first, send_ref, keep_ref, parts):
    for low in range(4):
        target = send_ref if low & first else keep_ref
        half = 1 if low & (3 - first) else 0
        at = 0
        for upper in range(peers // 4):
            owner = me ^ (4 * upper + low)
            for ref, share, far in parts:
                piece = ref[pl.ds(pl.multiple_of(owner * share, 16), share), :]
                if far:
                    ahead = lax.rem(owner - me + peers, peers)
                    apart = jnp.minimum(ahead, peers - ahead)
                    piece = jnp.where(apart > NEAR, piece.astype(F32), 0.0)
                target[half, at : at + share, :] = piece.astype(BF16)
                at += share


def forward_kernel(
    peers, me_ref, count_ref, src_ref, dst_ref, local_ref, edge_ref, *refs
):
    near_refs, far_refs = refs[:7], refs[7:11]
    (w_sender_ref, w_out_ref, w_node_in_ref, w_node_out_ref, mesh_ref, cotangent_ref) = refs[11:17]
    (received_ref, hidden_ref, slope_ref, norm_ref, inverse_ref) = refs[17:22]
    (send_ref, keep_ref, d_aggregate_ref, d_mesh_ref) = refs[22:26]
    (slot_proj, aggregate, grad_in, grad_out) = refs[26:]
    step = pl.program_id(0)
    me = me_ref[0]
    cap = near_refs[0].shape[0]
    width = edge_ref.shape[1]

    @pl.when(step == 0)
    def _():
        aggregate[...] = jnp.zeros_like(aggregate)
        w_sender = w_sender_ref[...]

        def place(owner, rows, projected):
            offset = pl.multiple_of(owner * cap, 16)
            received_ref[pl.ds(offset, cap), :] = rows
            slot_proj[pl.ds(offset, cap), :] = projected

        for low, ref in enumerate(far_refs):
            rows = ref[...]
            projected = dot(rows, w_sender).astype(BF16)
            for upper in range(peers // 4):
                span = slice(upper * cap, (upper + 1) * cap)
                place(me ^ (4 * upper + low), rows[span], projected[span])
        rows = jnp.concatenate(read_near(near_refs, cap), axis=0)
        projected = dot(rows, w_sender).astype(BF16)
        for spot, owner in enumerate(near_peers(me, peers)):
            place(owner, rows[spot * cap : (spot + 1) * cap], projected[spot * cap : (spot + 1) * cap])

    @pl.when(step * STEP < count_ref[0] * TILE)
    def _():
        parts = halves_of(edge_ref)
        pres = []
        for start, part in parts:
            onehot = hot_rows(src_ref[0, :, part], slot_proj.shape[0])
            pres.append(local_ref[part, :].astype(F32) + dot(onehot, slot_proj[...]))
        projs = []
        for (start, part), pre in zip(parts, pres):
            hidden, slope = silu_and_slope(pre)
            hidden = hidden.astype(BF16)
            hidden_ref[part, :] = hidden
            slope_ref[part, :] = slope.astype(BF16)
            projs.append(dot(hidden, w_out_ref[...]))
        for (start, part), proj in zip(parts, projs):
            normed, inverse = layer_norm(proj)
            norm_ref[part, :] = normed.astype(BF16)
            inverse_ref[0, :, part] = as_row(inverse)
            edge_new = (edge_ref[part, :].astype(F32) + normed).astype(BF16)
            receivers = live_only(dst_ref[0, :, part], step * STEP + start, count_ref[0] * TILE)
            aggregate[...] += dot(hot_columns(receivers, aggregate.shape[0]), edge_new)

    @pl.when(step == pl.num_programs(0) - 1)
    def _():
        mesh = mesh_ref[...]
        summed = aggregate[...].astype(BF16)
        node_pre = dot(mesh, w_node_in_ref[:width, :]) + dot(summed, w_node_in_ref[width:, :])
        hidden, slope = silu_and_slope(node_pre)
        hidden = hidden.astype(BF16)
        normed, inverse = layer_norm(dot(hidden, w_node_out_ref[...]))
        upstream = cotangent_ref[...].astype(F32)
        d_proj = norm_back(normed, inverse, upstream).astype(BF16)
        d_pre = (contract_cols(d_proj, w_node_out_ref[...]) * slope).astype(BF16)
        d_mesh_ref[...] = upstream + contract_cols(d_pre, w_node_in_ref[:width, :])
        d_aggregate_ref[...] = contract_cols(d_pre, w_node_in_ref[width:, :]).astype(BF16)
        grad_out[...] = contract_rows(hidden, d_proj)
        grad_in[:width, :] = contract_rows(mesh, d_pre)
        grad_in[width:, :] = contract_rows(summed, d_pre)
        split_out(
            me,
            peers,
            2,
            send_ref,
            keep_ref,
            ((grad_in, grad_in.shape[0] // peers, False), (grad_out, grad_out.shape[0] // peers, False)),
        )


def backward_kernel(peers, me_ref, count_ref, src_ref, dst_ref, inverse_ref, *refs):
    (hidden_ref, slope_ref, norm_ref, edge_ref) = refs[:4]
    (d_aggregate_ref, received_ref, mesh_ref, d_mesh_ref) = refs[4:8]
    (w_sender_ref, w_receiver_ref, w_out_ref) = refs[8:11]
    (d_pre_ref, mesh_grad_ref, slot_send_ref, slot_keep_ref, edge_send_ref, edge_keep_ref) = refs[11:17]
    near_refs = refs[17:22]
    (end_sum, grad_in, grad_out, d_slots) = refs[22:]
    step = pl.program_id(0)
    me = me_ref[0]
    slots, width = received_ref.shape
    mesh_count = mesh_ref.shape[0]

    @pl.when(step == 0)
    def _():
        end_sum[...] = jnp.zeros_like(end_sum)
        grad_in[:width, :] = jnp.zeros((width, width), F32)
        grad_out[...] = jnp.zeros_like(grad_out)

    @pl.when(step * STEP < count_ref[0] * TILE)
    def _():
        parts = halves_of(hidden_ref)
        upstreams = []
        columns = []
        for start, part in parts:
            first = step * STEP + start
            live = count_ref[0] * TILE
            receivers = live_only(dst_ref[0, :, part], first, live)
            upstreams.append(dot(hot_rows(receivers, mesh_count), d_aggregate_ref[...]))
            senders = live_only(src_ref[0, :, part], first, live)
            columns.append(
                jnp.concatenate([hot_columns(senders, slots), hot_columns(receivers, mesh_count)], axis=0)
            )
        d_projs = []
        d_hiddens = []
        for (start, part), upstream in zip(parts, upstreams):
            inverse = as_column(inverse_ref[0, :, part])
            d_proj = norm_back(norm_ref[part, :].astype(F32), inverse, upstream).astype(BF16)
            d_projs.append(d_proj)
            d_hiddens.append(contract_cols(d_proj, w_out_ref[...]))
        for (start, part), d_proj, d_hidden, column in zip(parts, d_projs, d_hiddens, columns):
            grad_out[...] += contract_rows(hidden_ref[part, :], d_proj)
            d_pre = (d_hidden * slope_ref[part, :].astype(F32)).astype(BF16)
            d_pre_ref[part, :] = d_pre
            end_sum[...] += dot(column, d_pre)
            grad_in[:width, :] += contract_rows(edge_ref[part, :], d_pre)

    @pl.when(step == pl.num_programs(0) - 1)
    def _():
        summed = end_sum[:slots, :].astype(BF16)
        mesh_summed = end_sum[slots:, :].astype(BF16)
        d_slots[...] = contract_cols(summed, w_sender_ref[...]).astype(BF16)
        grad_in[width : 2 * width, :] = contract_rows(received_ref[...], summed)
        grad_in[2 * width :, :] = contract_rows(mesh_ref[...], mesh_summed)
        mesh_grad_ref[...] = (d_mesh_ref[...] + contract_cols(mesh_summed, w_receiver_ref[...])).astype(BF16)
        cap = near_refs[0].shape[0]
        owners = near_peers(me, peers)
        write_near(
            near_refs, cap, [d_slots[pl.ds(pl.multiple_of(owner * cap, 16), cap), :] for owner in owners]
        )
        out_share = grad_out.shape[0] // peers
        split_out(
            me, peers, 1, slot_send_ref, slot_keep_ref, ((grad_out, out_share, False), (d_slots, cap, True))
        )
        split_out(
            me, peers, 1, edge_send_ref, edge_keep_ref, ((grad_in, grad_in.shape[0] // peers, False),)
        )


def edges_kernel(count_ref, dst_ref, d_pre_ref, d_aggregate_ref, w_edge_ref, edge_grad_ref):
    step = pl.program_id(0)

    @pl.when(step * STEP < count_ref[0] * TILE)
    def _():
        for start, part in halves_of(d_pre_ref):
            receivers = live_only(dst_ref[0, :, part], step * STEP + start, count_ref[0] * TILE)
            upstream = dot(hot_rows(receivers, d_aggregate_ref.shape[0]), d_aggregate_ref[...])
            edge_grad_ref[part, :] = (upstream + contract_cols(d_pre_ref[part, :], w_edge_ref[...])).astype(BF16)

    @pl.when(step * STEP >= count_ref[0] * TILE)
    def _():
        edge_grad_ref[...] = jnp.zeros_like(edge_grad_ref)


def send(values, perm):
    return lax.ppermute(values, "lon", perm)


def by_xor(peers, bits):
    return [(peer, peer ^ bits) for peer in range(peers)]


def by_shift(peers, shift):
    return [(peer, (peer + shift) % peers) for peer in range(peers)]


def across_chips(peers):
    return [(peer, (peer + (3 if peer % 2 else -3)) % peers) for peer in range(peers)]


def exchange_near(peers, lists):
    mine, other, after, before, across = lists
    return [
        mine,
        other,
        send(after, by_shift(peers, 2)),
        send(before, by_shift(peers, -2)),
        send(across, across_chips(peers)),
    ]


def core_bundles(peers, bundles):
    return [send(bundle, by_xor(peers, 1)) for bundle in bundles]


def add(left, right):
    return (left.astype(F32) + right.astype(F32)).astype(BF16)


def first_sum(peers, bit, outgoing, kept):
    arrived = send(outgoing, by_xor(peers, bit))
    return add(kept[1], arrived[1]), add(kept[0], arrived[0])


def next_sum(peers, bit, outgoing, kept):
    return add(kept, send(outgoing, by_xor(peers, bit)))


def last_terms(peers, pieces):
    count = peers // 4
    share = pieces.shape[0] // count
    terms = [pieces[:share]]
    for place in range(1, count):
        piece = pieces[place * share : (place + 1) * share]
        terms.append(send(piece, by_xor(peers, 4 * place)))
    return terms


def halve_sum(peers, pieces):
    count = peers // 4
    blocks = pieces.reshape(count // 2, 2, -1, pieces.shape[1])
    kept, outgoing = [blocks[:, place].reshape(-1, pieces.shape[1]) for place in range(2)]
    return add(kept, send(outgoing, by_xor(peers, 4)))


def rest_terms(peers, pieces):
    count = peers // 8
    share = pieces.shape[0] // count
    terms = [pieces[:share]]
    for place in range(1, count):
        piece = pieces[place * share : (place + 1) * share]
        terms.append(send(piece, by_xor(peers, 8 * place)))
    return terms


def total_of(terms, start, stop):
    total = terms[0][start:stop].astype(F32)
    for term in terms[1:]:
        total = total + term[start:stop].astype(F32)
    return total


def whole(shape):
    return pl.BlockSpec(shape, lambda *_: (0,) * len(shape))


def on_device(
    grid_latent,
    mesh_latent,
    edge_latent,
    mesh_cotangent,
    edge_src,
    edge_dst,
    tile_count,
    send_rows,
    w_edge_in,
    w_edge_out,
    w_node_in,
    w_node_out,
):
    peers = lax.axis_size("lon")
    me = lax.axis_index("lon").astype(jnp.int32).reshape(1)
    upper = peers // 4
    rows = send_rows[0]
    cap = rows.shape[1]
    slots = peers * cap
    edges, width = edge_latent.shape
    mesh_count = mesh_latent.shape[0]
    grid_count = grid_latent.shape[0]
    tiles = edges // STEP
    src = edge_src.reshape(tiles, 1, STEP)
    dst = edge_dst.reshape(tiles, 1, STEP)
    smem = pl.BlockSpec(memory_space=pltpu.SMEM)
    hbm = pl.BlockSpec(memory_space=pltpu.HBM)
    params = pltpu.CompilerParams(vmem_limit_bytes=VMEM_BYTES)
    square = (width, width)

    def tile_of(last):
        return pl.BlockSpec((STEP, last), lambda step, *_: (step, 0))

    index_tile = pl.BlockSpec((1, 1, STEP), lambda step, *_: (step, 0, 0))

    def weight(place):
        return pl.BlockSpec(square, lambda *_: (place, 0))

    def halves(share):
        shape = (2, upper * share, width)
        return [jax.ShapeDtypeStruct(shape, BF16)] * 2, [whole(shape)] * 2

    grid_part = grid_count // 2
    near_rows = (cap, cap, 2 * cap, 2 * cap, cap)
    near_specs = [whole((count, width)) for count in near_rows]
    near_shapes = [jax.ShapeDtypeStruct((count, width), BF16) for count in near_rows]
    core_specs = near_specs + [whole((2 * cap, width))] * 2
    lists = pl.pallas_call(
        gather_kernel,
        in_specs=[smem, hbm, hbm],
        out_specs=near_specs + [whole((cap, width))],
        out_shape=near_shapes + [jax.ShapeDtypeStruct((cap, width), BF16)],
        scratch_shapes=[
            pltpu.VMEM(rows.shape, jnp.int32),
            pltpu.VMEM(grid_latent.shape, BF16),
            pltpu.SemaphoreType.DMA,
            pltpu.SemaphoreType.DMA((GRID_PARTS,)),
        ],
        compiler_params=pltpu.CompilerParams(vmem_limit_bytes=GATHER_BYTES),
        cost_estimate=pl.CostEstimate(
            flops=40 * 16 * cap * grid_count * width,
            bytes_accessed=2 * grid_count * width,
            transcendentals=0,
        ),
        name="gather_lists",
    )(me, rows, grid_latent)

    hops = [send(lists[5], by_xor(peers, 4 * place)) for place in range(1, upper)]
    near = exchange_near(peers, lists[:5])
    far_own = jnp.concatenate([lists[5]] + hops, axis=0)
    far_own, receivers = lax.optimization_barrier((far_own, dst))
    far_next = send(far_own, by_xor(peers, 2))
    far_core = send(far_own, by_xor(peers, 1))
    local = pl.pallas_call(
        local_kernel,
        grid=(tiles,),
        in_specs=[index_tile, tile_of(width), whole(mesh_latent.shape), weight(0), weight(2)],
        out_specs=tile_of(width),
        out_shape=jax.ShapeDtypeStruct((edges, width), BF16),
        scratch_shapes=[pltpu.VMEM((width + mesh_count, width), BF16)],
        compiler_params=params,
        cost_estimate=pl.CostEstimate(
            flops=2 * edges * width * (width + mesh_count),
            bytes_accessed=4 * edges * width,
            transcendentals=0,
        ),
        name="edge_local",
    )(receivers, edge_latent, mesh_latent, w_edge_in, w_edge_in)
    far_next, far_core, near, local = lax.optimization_barrier((far_next, far_core, near, local))
    near = [near[0], send(near[1], by_xor(peers, 1)), *near[2:]] + core_bundles(peers, near[2:4])
    far_both = send(far_next, by_xor(peers, 1))

    node_shape, node_spec = halves(w_node_in.shape[0] // peers + w_node_out.shape[0] // peers)
    (received, hidden, slope, norm, inverse, node_send, node_keep, d_aggregate, d_mesh) = pl.pallas_call(
        functools.partial(forward_kernel, peers),
        grid=(tiles,),
        in_specs=[smem, smem, index_tile, index_tile, tile_of(width), tile_of(width)]
        + core_specs
        + [whole((upper * cap, width))] * 4
        + [weight(1)]
        + [whole(w.shape) for w in (w_edge_out, w_node_in, w_node_out, mesh_latent, mesh_cotangent)],
        out_specs=[whole((slots, width))]
        + [tile_of(width)] * 3
        + [index_tile]
        + node_spec
        + [whole((mesh_count, width))] * 2,
        out_shape=[jax.ShapeDtypeStruct((slots, width), BF16)]
        + [jax.ShapeDtypeStruct((edges, width), BF16)] * 3
        + [jax.ShapeDtypeStruct((tiles, 1, STEP), F32)]
        + node_shape
        + [jax.ShapeDtypeStruct((mesh_count, width), BF16), jax.ShapeDtypeStruct((mesh_count, width), F32)],
        scratch_shapes=[
            pltpu.VMEM((slots, width), BF16),
            pltpu.VMEM((mesh_count, width), F32),
            pltpu.VMEM(w_node_in.shape, F32),
            pltpu.VMEM(w_node_out.shape, F32),
        ],
        compiler_params=params,
        name="forward",
    )(
        me,
        tile_count,
        src,
        dst,
        local,
        edge_latent,
        *near,
        far_own,
        far_core,
        far_next,
        far_both,
        w_edge_in,
        w_edge_out,
        w_node_in,
        w_node_out,
        mesh_latent,
        mesh_cotangent,
    )

    node_next, node_kept = first_sum(peers, 2, node_send, node_keep)
    slot_shape, slot_spec = halves(w_edge_out.shape[0] // peers + cap)
    edge_shape, edge_spec = halves(w_edge_in.shape[0] // peers)
    results = pl.pallas_call(
        functools.partial(backward_kernel, peers),
        grid=(tiles,),
        in_specs=[smem, smem, index_tile, index_tile, index_tile]
        + [tile_of(width)] * 4
        + [whole((mesh_count, width)), whole((slots, width))]
        + [whole((mesh_count, width))] * 2
        + [weight(1), weight(2), whole(square)],
        out_specs=[tile_of(width), whole((mesh_count, width))] + slot_spec + edge_spec + near_specs,
        out_shape=[
            jax.ShapeDtypeStruct((edges, width), BF16),
            jax.ShapeDtypeStruct((mesh_count, width), BF16),
        ]
        + slot_shape
        + edge_shape
        + near_shapes,
        scratch_shapes=[
            pltpu.VMEM((slots + mesh_count, width), F32),
            pltpu.VMEM(w_edge_in.shape, F32),
            pltpu.VMEM(square, F32),
            pltpu.VMEM((slots, width), BF16),
        ],
        compiler_params=params,
        cost_estimate=pl.CostEstimate(
            flops=2 * edges * width * (2 * mesh_count + 3 * width + slots),
            bytes_accessed=10 * edges * width,
            transcendentals=0,
        ),
        name="backward",
    )(
        me,
        tile_count,
        src,
        dst,
        inverse,
        hidden,
        slope,
        norm,
        edge_latent,
        d_aggregate,
        received,
        mesh_latent,
        d_mesh,
        w_edge_in,
        w_edge_in,
        w_edge_out,
    )
    (d_pre, mesh_grad, slot_send, slot_keep, edge_send, edge_keep), returns = results[:6], results[6:]
    (node_next, node_kept, slot_send, slot_keep, edge_send, edge_keep, returns, d_pre) = lax.optimization_barrier(
        (node_next, node_kept, slot_send, slot_keep, edge_send, edge_keep, returns, d_pre)
    )
    slot_next, slot_kept = first_sum(peers, 1, slot_send, slot_keep)
    edge_next, edge_kept = first_sum(peers, 1, edge_send, edge_keep)
    node_pieces = next_sum(peers, 1, node_next, node_kept)
    bundles = [send(returns[2], by_shift(peers, 2)), send(returns[3], by_shift(peers, -2))]
    other = send(returns[1], by_xor(peers, 1))
    (slot_next, slot_kept, edge_next, edge_kept, node_pieces, bundles, other, d_pre) = lax.optimization_barrier(
        (slot_next, slot_kept, edge_next, edge_kept, node_pieces, bundles, other, d_pre)
    )
    slot_pieces = next_sum(peers, 2, slot_next, slot_kept)
    edge_pieces = next_sum(peers, 2, edge_next, edge_kept)
    node_terms = last_terms(peers, node_pieces)
    edge_grad = pl.pallas_call(
        edges_kernel,
        grid=(tiles,),
        in_specs=[smem, index_tile, tile_of(width), whole((mesh_count, width)), weight(0)],
        out_specs=tile_of(width),
        out_shape=jax.ShapeDtypeStruct((edges, width), BF16),
        compiler_params=params,
        cost_estimate=pl.CostEstimate(
            flops=2 * edges * width * (mesh_count + width), bytes_accessed=4 * edges * width, transcendentals=0
        ),
        name="edge_grad",
    )(tile_count, dst, d_pre, d_aggregate, w_edge_in)
    (slot_pieces, node_terms, across, bundles, edge_grad) = lax.optimization_barrier(
        (slot_pieces, node_terms, returns[4], bundles, edge_grad)
    )
    returned = [returns[0], other, *bundles, send(across, across_chips(peers))] + core_bundles(peers, bundles)
    slot_half = halve_sum(peers, slot_pieces)
    slot_half, edge_pieces, returned = lax.optimization_barrier((slot_half, edge_pieces, returned))
    slot_terms = rest_terms(peers, slot_half)
    edge_terms = last_terms(peers, edge_pieces)
    node_terms, slot_terms = lax.optimization_barrier((node_terms, slot_terms))
    node_rows = w_node_in.shape[0] // peers
    out_rows = w_edge_out.shape[0] // peers
    grid_grad = pl.pallas_call(
        functools.partial(scatter_kernel, out_rows),
        grid=(2,),
        in_specs=[smem, whole(rows.shape)]
        + core_specs
        + [whole((out_rows + cap, width))] * (upper // 2),
        out_specs=pl.BlockSpec((grid_part, width), lambda step: (step, 0)),
        out_shape=jax.ShapeDtypeStruct((grid_count, width), BF16),
        compiler_params=params,
        name="scatter_lists",
    )(me, rows, *returned, *slot_terms)
    edge_terms, grid_grad = lax.optimization_barrier((edge_terms, grid_grad))
    return (
        grid_grad,
        edge_grad,
        mesh_grad,
        total_of(edge_terms, 0, w_edge_in.shape[0] // peers),
        total_of(slot_terms, 0, out_rows),
        total_of(node_terms, 0, node_rows),
        total_of(node_terms, node_rows, node_rows + w_node_out.shape[0] // peers),
    )


def solution(mesh):
    rows = P(("grp", "lon"), None)
    flat = P(("grp", "lon"))
    return jax.shard_map(
        on_device,
        mesh=mesh,
        in_specs=(rows, rows, rows, rows, flat, flat, flat, P(("grp", "lon"), None, None)) + (P(),) * 4,
        out_specs=(rows,) * 7,
        check_vma=False,
    )
```

```python
import functools

import jax
import jax.numpy as jnp
from jax import lax
from jax.experimental import pallas as pl
from jax.experimental.pallas import tpu as pltpu
from jax.sharding import PartitionSpec as P

TILE = 256
STEP = 1024
SUB = 512
LANES = 128
GRID_PARTS = 4
NEAR = 3
BF16 = jnp.bfloat16
F32 = jnp.float32
VMEM_BYTES = 24 * 1024 * 1024
GATHER_BYTES = 56 * 1024 * 1024


def dot(left, right):
    return lax.dot_general(left, right, (((1,), (0,)), ((), ())), preferred_element_type=F32)


def contract_rows(left, right):
    return lax.dot_general(left, right, (((0,), (0,)), ((), ())), preferred_element_type=F32)


def contract_cols(left, right):
    return lax.dot_general(left, right, (((1,), (1,)), ((), ())), preferred_element_type=F32)


def layer_norm(values):
    centered = values - jnp.mean(values, axis=1, keepdims=True)
    inverse = lax.rsqrt(jnp.mean(centered * centered, axis=1, keepdims=True) + 1e-05)
    return (centered * inverse, inverse)


def norm_back(normed, inverse, upstream):
    first = jnp.mean(upstream, axis=1, keepdims=True)
    second = jnp.mean(upstream * normed, axis=1, keepdims=True)
    return inverse * (upstream - first - normed * second)


def silu_and_slope(values):
    sigma = 0.5 + 0.5 * jnp.tanh(0.5 * values)
    hidden = values * sigma
    return (hidden, sigma + hidden * (1.0 - sigma))


def as_column(row):
    count = row.shape[1]
    block = min(count, LANES)
    down = lax.broadcasted_iota(jnp.int32, (block, block), 0)
    along = lax.broadcasted_iota(jnp.int32, (block, block), 1)
    columns = []
    for start in range(0, count, block):
        piece = row[:, start : start + block].astype(F32)
        picked = jnp.where(down == along, piece, 0.0)
        columns.append(jnp.sum(picked, axis=1, keepdims=True))
    return jnp.concatenate(columns, axis=0)


def as_row(column):
    count = column.shape[0]
    block = min(count, LANES)
    down = lax.broadcasted_iota(jnp.int32, (block, block), 0)
    along = lax.broadcasted_iota(jnp.int32, (block, block), 1)
    rows = []
    for start in range(0, count, block):
        picked = jnp.where(down == along, column[start : start + block], 0.0)
        rows.append(jnp.sum(picked, axis=0, keepdims=True))
    return jnp.concatenate(rows, axis=1)


def hot_rows(row, width, first=0):
    column = as_column(row).astype(jnp.int32) - first
    along = lax.broadcasted_iota(jnp.int32, (row.shape[1], width), 1)
    return (column == along).astype(F32).astype(BF16)


def hot_columns(row, height):
    down = lax.broadcasted_iota(jnp.int32, (height, row.shape[1]), 0)
    return (row == down).astype(F32).astype(BF16)


def live_only(row, first, count):
    place = first + lax.broadcasted_iota(jnp.int32, row.shape, 1)
    return jnp.where(place < count, row, -1)


def near_peers(me, peers):
    after = lax.rem(me + 2, peers)
    before = lax.rem(me + peers - 2, peers)
    across = lax.rem(me + peers - 3 + 6 * (me & 1), peers)
    return (me, me ^ 1, after, after ^ 1, before, before ^ 1, across)


def write_near(refs, cap, lists):
    mine, other, after, before, across = refs
    mine[...] = lists[0]
    other[...] = lists[1]
    after[:cap, :] = lists[2]
    after[cap:, :] = lists[3]
    before[:cap, :] = lists[4]
    before[cap:, :] = lists[5]
    across[...] = lists[6]


def read_near(refs, cap):
    mine, other, from_before, from_after, across, core_before, core_after = refs
    return [
        mine[...],
        other[...],
        from_after[:cap, :],
        core_after[cap:, :],
        from_before[:cap, :],
        core_before[cap:, :],
        across[...],
    ]


def list_hots(me, rows_ref, grid_count, first):
    peers, cap = rows_ref.shape
    pieces = []
    for target in near_peers(me, peers):
        pieces.append(hot_rows(rows_ref[pl.ds(target, 1), :], grid_count, first))
    peer = lax.broadcasted_iota(jnp.int32, (peers, cap), 0)
    ahead = lax.rem(peer - me + peers, peers)
    apart = jnp.minimum(ahead, peers - ahead)
    far = jnp.max(jnp.where(apart > NEAR, rows_ref[...].astype(F32), -1.0), axis=0, keepdims=True)
    pieces.append(hot_rows(far.astype(jnp.int32), grid_count, first))
    return jnp.concatenate(pieces, axis=0)


def gather_kernel(me_ref, rows_hbm, grid_hbm, *refs):
    near_refs, far_ref = refs[:5], refs[5]
    rows_ref, grid_ref, rows_done, grid_done = refs[6:]
    cap = rows_ref.shape[1]
    part = grid_ref.shape[0] // GRID_PARTS
    copies = [
        pltpu.make_async_copy(
            grid_hbm.at[pl.ds(at * part, part)], grid_ref.at[pl.ds(at * part, part)], grid_done.at[at]
        )
        for at in range(GRID_PARTS)
    ]
    rows_copy = pltpu.make_async_copy(rows_hbm, rows_ref, rows_done)
    rows_copy.start()
    for copy in copies:
        copy.start()
    rows_copy.wait()
    found = None
    for at, copy in enumerate(copies):
        hots = list_hots(me_ref[0], rows_ref, part, at * part)
        copy.wait()
        piece = dot(hots, grid_ref[at * part : (at + 1) * part, :])
        found = piece if found is None else found + piece
    rows = found.astype(BF16)
    lists = [rows[at : at + cap] for at in range(0, 8 * cap, cap)]
    write_near(near_refs, cap, lists)
    far_ref[...] = lists[7]


def scatter_kernel(skip, me_ref, rows_ref, *refs):
    near_refs, far_refs, out_ref = refs[:7], refs[7:-1], refs[-1]
    part = out_ref.shape[0]
    cap = rows_ref.shape[1]
    hots = list_hots(me_ref[0], rows_ref, part, pl.program_id(0) * part)
    far = far_refs[0][skip:, :].astype(F32)
    for ref in far_refs[1:]:
        far = far + ref[skip:, :].astype(F32)
    values = jnp.concatenate(read_near(near_refs, cap) + [far.astype(BF16)], axis=0)
    out_ref[...] = contract_rows(hots, values).astype(BF16)


def halves_of(ref):
    rows = ref.shape[-1] if len(ref.shape) == 3 else ref.shape[0]
    return [(start, slice(start, start + SUB)) for start in range(0, rows, SUB)]


def local_kernel(dst_ref, edge_ref, mesh_ref, w_edge_ref, w_receiver_ref, out_ref, weights):
    width = edge_ref.shape[1]

    @pl.when(pl.program_id(0) == 0)
    def _():
        weights[:width, :] = w_edge_ref[...]
        weights[width:, :] = dot(mesh_ref[...], w_receiver_ref[...]).astype(BF16)

    for start, part in halves_of(edge_ref):
        onehot = hot_rows(dst_ref[0, :, part], mesh_ref.shape[0])
        joined = jnp.concatenate([edge_ref[part, :], onehot], axis=1)
        out_ref[part, :] = dot(joined, weights[...]).astype(BF16)


def split_out(me, peers, first, send_ref, keep_ref, parts):
    for low in range(4):
        target = send_ref if low & first else keep_ref
        half = 1 if low & (3 - first) else 0
        at = 0
        for upper in range(peers // 4):
            owner = me ^ (4 * upper + low)
            for ref, share, far in parts:
                piece = ref[pl.ds(pl.multiple_of(owner * share, 16), share), :]
                if far:
                    ahead = lax.rem(owner - me + peers, peers)
                    apart = jnp.minimum(ahead, peers - ahead)
                    piece = jnp.where(apart > NEAR, piece.astype(F32), 0.0)
                target[half, at : at + share, :] = piece.astype(BF16)
                at += share


def forward_kernel(
    peers, me_ref, count_ref, src_ref, dst_ref, local_ref, edge_ref, *refs
):
    near_refs, far_refs = refs[:7], refs[7:11]
    (w_sender_ref, w_out_ref, w_node_in_ref, w_node_out_ref, mesh_ref, cotangent_ref) = refs[11:17]
    (received_ref, hidden_ref, slope_ref, norm_ref, inverse_ref) = refs[17:22]
    (send_ref, keep_ref, d_aggregate_ref, d_mesh_ref) = refs[22:26]
    (slot_proj, aggregate, grad_in, grad_out) = refs[26:]
    step = pl.program_id(0)
    me = me_ref[0]
    cap = near_refs[0].shape[0]
    width = edge_ref.shape[1]

    @pl.when(step == 0)
    def _():
        aggregate[...] = jnp.zeros_like(aggregate)
        w_sender = w_sender_ref[...]

        def place(owner, rows, projected):
            offset = pl.multiple_of(owner * cap, 16)
            received_ref[pl.ds(offset, cap), :] = rows
            slot_proj[pl.ds(offset, cap), :] = projected

        for low, ref in enumerate(far_refs):
            rows = ref[...]
            projected = dot(rows, w_sender).astype(BF16)
            for upper in range(peers // 4):
                span = slice(upper * cap, (upper + 1) * cap)
                place(me ^ (4 * upper + low), rows[span], projected[span])
        rows = jnp.concatenate(read_near(near_refs, cap), axis=0)
        projected = dot(rows, w_sender).astype(BF16)
        for spot, owner in enumerate(near_peers(me, peers)):
            place(owner, rows[spot * cap : (spot + 1) * cap], projected[spot * cap : (spot + 1) * cap])

    @pl.when(step * STEP < count_ref[0] * TILE)
    def _():
        parts = halves_of(edge_ref)
        pres = []
        for start, part in parts:
            onehot = hot_rows(src_ref[0, :, part], slot_proj.shape[0])
            pres.append(local_ref[part, :].astype(F32) + dot(onehot, slot_proj[...]))
        projs = []
        for (start, part), pre in zip(parts, pres):
            hidden, slope = silu_and_slope(pre)
            hidden = hidden.astype(BF16)
            hidden_ref[part, :] = hidden
            slope_ref[part, :] = slope.astype(BF16)
            projs.append(dot(hidden, w_out_ref[...]))
        for (start, part), proj in zip(parts, projs):
            normed, inverse = layer_norm(proj)
            norm_ref[part, :] = normed.astype(BF16)
            inverse_ref[0, :, part] = as_row(inverse)
            edge_new = (edge_ref[part, :].astype(F32) + normed).astype(BF16)
            receivers = live_only(dst_ref[0, :, part], step * STEP + start, count_ref[0] * TILE)
            aggregate[...] += dot(hot_columns(receivers, aggregate.shape[0]), edge_new)

    @pl.when(step == pl.num_programs(0) - 1)
    def _():
        mesh = mesh_ref[...]
        summed = aggregate[...].astype(BF16)
        node_pre = dot(mesh, w_node_in_ref[:width, :]) + dot(summed, w_node_in_ref[width:, :])
        hidden, slope = silu_and_slope(node_pre)
        hidden = hidden.astype(BF16)
        normed, inverse = layer_norm(dot(hidden, w_node_out_ref[...]))
        upstream = cotangent_ref[...].astype(F32)
        d_proj = norm_back(normed, inverse, upstream).astype(BF16)
        d_pre = (contract_cols(d_proj, w_node_out_ref[...]) * slope).astype(BF16)
        d_mesh_ref[...] = upstream + contract_cols(d_pre, w_node_in_ref[:width, :])
        d_aggregate_ref[...] = contract_cols(d_pre, w_node_in_ref[width:, :]).astype(BF16)
        grad_out[...] = contract_rows(hidden, d_proj)
        grad_in[:width, :] = contract_rows(mesh, d_pre)
        grad_in[width:, :] = contract_rows(summed, d_pre)
        split_out(
            me,
            peers,
            2,
            send_ref,
            keep_ref,
            ((grad_in, grad_in.shape[0] // peers, False), (grad_out, grad_out.shape[0] // peers, False)),
        )


def backward_kernel(peers, me_ref, count_ref, src_ref, dst_ref, inverse_ref, *refs):
    (hidden_ref, slope_ref, norm_ref, edge_ref) = refs[:4]
    (d_aggregate_ref, received_ref, mesh_ref, d_mesh_ref) = refs[4:8]
    (w_sender_ref, w_receiver_ref, w_out_ref) = refs[8:11]
    (d_pre_ref, mesh_grad_ref, slot_send_ref, slot_keep_ref, edge_send_ref, edge_keep_ref) = refs[11:17]
    near_refs = refs[17:22]
    (end_sum, grad_in, grad_out, d_slots) = refs[22:]
    step = pl.program_id(0)
    me = me_ref[0]
    slots, width = received_ref.shape
    mesh_count = mesh_ref.shape[0]

    @pl.when(step == 0)
    def _():
        end_sum[...] = jnp.zeros_like(end_sum)
        grad_in[:width, :] = jnp.zeros((width, width), F32)
        grad_out[...] = jnp.zeros_like(grad_out)

    @pl.when(step * STEP < count_ref[0] * TILE)
    def _():
        parts = halves_of(hidden_ref)
        upstreams = []
        columns = []
        for start, part in parts:
            first = step * STEP + start
            live = count_ref[0] * TILE
            receivers = live_only(dst_ref[0, :, part], first, live)
            upstreams.append(dot(hot_rows(receivers, mesh_count), d_aggregate_ref[...]))
            senders = live_only(src_ref[0, :, part], first, live)
            columns.append(
                jnp.concatenate([hot_columns(senders, slots), hot_columns(receivers, mesh_count)], axis=0)
            )
        d_projs = []
        d_hiddens = []
        for (start, part), upstream in zip(parts, upstreams):
            inverse = as_column(inverse_ref[0, :, part])
            d_proj = norm_back(norm_ref[part, :].astype(F32), inverse, upstream).astype(BF16)
            d_projs.append(d_proj)
            d_hiddens.append(contract_cols(d_proj, w_out_ref[...]))
        for (start, part), d_proj, d_hidden, column in zip(parts, d_projs, d_hiddens, columns):
            grad_out[...] += contract_rows(hidden_ref[part, :], d_proj)
            d_pre = (d_hidden * slope_ref[part, :].astype(F32)).astype(BF16)
            d_pre_ref[part, :] = d_pre
            end_sum[...] += dot(column, d_pre)
            grad_in[:width, :] += contract_rows(edge_ref[part, :], d_pre)

    @pl.when(step == pl.num_programs(0) - 1)
    def _():
        summed = end_sum[:slots, :].astype(BF16)
        mesh_summed = end_sum[slots:, :].astype(BF16)
        d_slots[...] = contract_cols(summed, w_sender_ref[...]).astype(BF16)
        grad_in[width : 2 * width, :] = contract_rows(received_ref[...], summed)
        grad_in[2 * width :, :] = contract_rows(mesh_ref[...], mesh_summed)
        mesh_grad_ref[...] = (d_mesh_ref[...] + contract_cols(mesh_summed, w_receiver_ref[...])).astype(BF16)
        cap = near_refs[0].shape[0]
        owners = near_peers(me, peers)
        write_near(
            near_refs, cap, [d_slots[pl.ds(pl.multiple_of(owner * cap, 16), cap), :] for owner in owners]
        )
        out_share = grad_out.shape[0] // peers
        split_out(
            me, peers, 1, slot_send_ref, slot_keep_ref, ((grad_out, out_share, False), (d_slots, cap, True))
        )
        split_out(
            me, peers, 1, edge_send_ref, edge_keep_ref, ((grad_in, grad_in.shape[0] // peers, False),)
        )


def edges_kernel(count_ref, dst_ref, d_pre_ref, d_aggregate_ref, w_edge_ref, edge_grad_ref):
    step = pl.program_id(0)

    @pl.when(step * STEP < count_ref[0] * TILE)
    def _():
        for start, part in halves_of(d_pre_ref):
            receivers = live_only(dst_ref[0, :, part], step * STEP + start, count_ref[0] * TILE)
            upstream = dot(hot_rows(receivers, d_aggregate_ref.shape[0]), d_aggregate_ref[...])
            edge_grad_ref[part, :] = (upstream + contract_cols(d_pre_ref[part, :], w_edge_ref[...])).astype(BF16)

    @pl.when(step * STEP >= count_ref[0] * TILE)
    def _():
        edge_grad_ref[...] = jnp.zeros_like(edge_grad_ref)


def send(values, perm):
    return lax.ppermute(values, "lon", perm)


def by_xor(peers, bits):
    return [(peer, peer ^ bits) for peer in range(peers)]


def by_shift(peers, shift):
    return [(peer, (peer + shift) % peers) for peer in range(peers)]


def across_chips(peers):
    return [(peer, (peer + (3 if peer % 2 else -3)) % peers) for peer in range(peers)]


def exchange_near(peers, lists):
    mine, other, after, before, across = lists
    return [
        mine,
        other,
        send(after, by_shift(peers, 2)),
        send(before, by_shift(peers, -2)),
        send(across, across_chips(peers)),
    ]


def core_bundles(peers, bundles):
    return [send(bundle, by_xor(peers, 1)) for bundle in bundles]


def add(left, right):
    return (left.astype(F32) + right.astype(F32)).astype(BF16)


def first_sum(peers, bit, outgoing, kept):
    arrived = send(outgoing, by_xor(peers, bit))
    return add(kept[1], arrived[1]), add(kept[0], arrived[0])


def next_sum(peers, bit, outgoing, kept):
    return add(kept, send(outgoing, by_xor(peers, bit)))


def last_terms(peers, pieces):
    count = peers // 4
    share = pieces.shape[0] // count
    terms = [pieces[:share]]
    for place in range(1, count):
        piece = pieces[place * share : (place + 1) * share]
        terms.append(send(piece, by_xor(peers, 4 * place)))
    return terms


def halve_sum(peers, pieces):
    count = peers // 4
    blocks = pieces.reshape(count // 2, 2, -1, pieces.shape[1])
    kept, outgoing = [blocks[:, place].reshape(-1, pieces.shape[1]) for place in range(2)]
    return add(kept, send(outgoing, by_xor(peers, 4)))


def rest_terms(peers, pieces):
    count = peers // 8
    share = pieces.shape[0] // count
    terms = [pieces[:share]]
    for place in range(1, count):
        piece = pieces[place * share : (place + 1) * share]
        terms.append(send(piece, by_xor(peers, 8 * place)))
    return terms


def total_of(terms, start, stop):
    total = terms[0][start:stop].astype(F32)
    for term in terms[1:]:
        total = total + term[start:stop].astype(F32)
    return total


def whole(shape):
    return pl.BlockSpec(shape, lambda *_: (0,) * len(shape))


def on_device(
    grid_latent,
    mesh_latent,
    edge_latent,
    mesh_cotangent,
    edge_src,
    edge_dst,
    tile_count,
    send_rows,
    w_edge_in,
    w_edge_out,
    w_node_in,
    w_node_out,
):
    peers = lax.axis_size("lon")
    me = lax.axis_index("lon").astype(jnp.int32).reshape(1)
    upper = peers // 4
    rows = send_rows[0]
    cap = rows.shape[1]
    slots = peers * cap
    edges, width = edge_latent.shape
    mesh_count = mesh_latent.shape[0]
    grid_count = grid_latent.shape[0]
    tiles = edges // STEP
    src = edge_src.reshape(tiles, 1, STEP)
    dst = edge_dst.reshape(tiles, 1, STEP)
    smem = pl.BlockSpec(memory_space=pltpu.SMEM)
    hbm = pl.BlockSpec(memory_space=pltpu.HBM)
    params = pltpu.CompilerParams(vmem_limit_bytes=VMEM_BYTES)
    square = (width, width)

    def tile_of(last):
        return pl.BlockSpec((STEP, last), lambda step, *_: (step, 0))

    index_tile = pl.BlockSpec((1, 1, STEP), lambda step, *_: (step, 0, 0))

    def weight(place):
        return pl.BlockSpec(square, lambda *_: (place, 0))

    def halves(share):
        shape = (2, upper * share, width)
        return [jax.ShapeDtypeStruct(shape, BF16)] * 2, [whole(shape)] * 2

    grid_part = grid_count // 2
    near_rows = (cap, cap, 2 * cap, 2 * cap, cap)
    near_specs = [whole((count, width)) for count in near_rows]
    near_shapes = [jax.ShapeDtypeStruct((count, width), BF16) for count in near_rows]
    core_specs = near_specs + [whole((2 * cap, width))] * 2
    lists = pl.pallas_call(
        gather_kernel,
        in_specs=[smem, hbm, hbm],
        out_specs=near_specs + [whole((cap, width))],
        out_shape=near_shapes + [jax.ShapeDtypeStruct((cap, width), BF16)],
        scratch_shapes=[
            pltpu.VMEM(rows.shape, jnp.int32),
            pltpu.VMEM(grid_latent.shape, BF16),
            pltpu.SemaphoreType.DMA,
            pltpu.SemaphoreType.DMA((GRID_PARTS,)),
        ],
        compiler_params=pltpu.CompilerParams(vmem_limit_bytes=GATHER_BYTES),
        cost_estimate=pl.CostEstimate(
            flops=40 * 16 * cap * grid_count * width,
            bytes_accessed=2 * grid_count * width,
            transcendentals=0,
        ),
        name="gather_lists",
    )(me, rows, grid_latent)

    hops = [send(lists[5], by_xor(peers, 4 * place)) for place in range(1, upper)]
    near = exchange_near(peers, lists[:5])
    far_own = jnp.concatenate([lists[5]] + hops, axis=0)
    far_own, receivers = lax.optimization_barrier((far_own, dst))
    far_next = send(far_own, by_xor(peers, 2))
    far_core = send(far_own, by_xor(peers, 1))
    local = pl.pallas_call(
        local_kernel,
        grid=(tiles,),
        in_specs=[index_tile, tile_of(width), whole(mesh_latent.shape), weight(0), weight(2)],
        out_specs=tile_of(width),
        out_shape=jax.ShapeDtypeStruct((edges, width), BF16),
        scratch_shapes=[pltpu.VMEM((width + mesh_count, width), BF16)],
        compiler_params=params,
        cost_estimate=pl.CostEstimate(
            flops=2 * edges * width * (width + mesh_count),
            bytes_accessed=4 * edges * width,
            transcendentals=0,
        ),
        name="edge_local",
    )(receivers, edge_latent, mesh_latent, w_edge_in, w_edge_in)
    far_next, far_core, near, local = lax.optimization_barrier((far_next, far_core, near, local))
    near = [near[0], send(near[1], by_xor(peers, 1)), *near[2:]] + core_bundles(peers, near[2:4])
    far_both = send(far_next, by_xor(peers, 1))

    node_shape, node_spec = halves(w_node_in.shape[0] // peers + w_node_out.shape[0] // peers)
    (received, hidden, slope, norm, inverse, node_send, node_keep, d_aggregate, d_mesh) = pl.pallas_call(
        functools.partial(forward_kernel, peers),
        grid=(tiles,),
        in_specs=[smem, smem, index_tile, index_tile, tile_of(width), tile_of(width)]
        + core_specs
        + [whole((upper * cap, width))] * 4
        + [weight(1)]
        + [whole(w.shape) for w in (w_edge_out, w_node_in, w_node_out, mesh_latent, mesh_cotangent)],
        out_specs=[whole((slots, width))]
        + [tile_of(width)] * 3
        + [index_tile]
        + node_spec
        + [whole((mesh_count, width))] * 2,
        out_shape=[jax.ShapeDtypeStruct((slots, width), BF16)]
        + [jax.ShapeDtypeStruct((edges, width), BF16)] * 3
        + [jax.ShapeDtypeStruct((tiles, 1, STEP), F32)]
        + node_shape
        + [jax.ShapeDtypeStruct((mesh_count, width), BF16), jax.ShapeDtypeStruct((mesh_count, width), F32)],
        scratch_shapes=[
            pltpu.VMEM((slots, width), BF16),
            pltpu.VMEM((mesh_count, width), F32),
            pltpu.VMEM(w_node_in.shape, F32),
            pltpu.VMEM(w_node_out.shape, F32),
        ],
        compiler_params=params,
        name="forward",
    )(
        me,
        tile_count,
        src,
        dst,
        local,
        edge_latent,
        *near,
        far_own,
        far_core,
        far_next,
        far_both,
        w_edge_in,
        w_edge_out,
        w_node_in,
        w_node_out,
        mesh_latent,
        mesh_cotangent,
    )

    node_next, node_kept = first_sum(peers, 2, node_send, node_keep)
    slot_shape, slot_spec = halves(w_edge_out.shape[0] // peers + cap)
    edge_shape, edge_spec = halves(w_edge_in.shape[0] // peers)
    results = pl.pallas_call(
        functools.partial(backward_kernel, peers),
        grid=(tiles,),
        in_specs=[smem, smem, index_tile, index_tile, index_tile]
        + [tile_of(width)] * 4
        + [whole((mesh_count, width)), whole((slots, width))]
        + [whole((mesh_count, width))] * 2
        + [weight(1), weight(2), whole(square)],
        out_specs=[tile_of(width), whole((mesh_count, width))] + slot_spec + edge_spec + near_specs,
        out_shape=[
            jax.ShapeDtypeStruct((edges, width), BF16),
            jax.ShapeDtypeStruct((mesh_count, width), BF16),
        ]
        + slot_shape
        + edge_shape
        + near_shapes,
        scratch_shapes=[
            pltpu.VMEM((slots + mesh_count, width), F32),
            pltpu.VMEM(w_edge_in.shape, F32),
            pltpu.VMEM(square, F32),
            pltpu.VMEM((slots, width), BF16),
        ],
        compiler_params=params,
        cost_estimate=pl.CostEstimate(
            flops=2 * edges * width * (2 * mesh_count + 3 * width + slots),
            bytes_accessed=10 * edges * width,
            transcendentals=0,
        ),
        name="backward",
    )(
        me,
        tile_count,
        src,
        dst,
        inverse,
        hidden,
        slope,
        norm,
        edge_latent,
        d_aggregate,
        received,
        mesh_latent,
        d_mesh,
        w_edge_in,
        w_edge_in,
        w_edge_out,
    )
    (d_pre, mesh_grad, slot_send, slot_keep, edge_send, edge_keep), returns = results[:6], results[6:]
    (node_next, node_kept, slot_send, slot_keep, edge_send, edge_keep, returns, d_pre) = lax.optimization_barrier(
        (node_next, node_kept, slot_send, slot_keep, edge_send, edge_keep, returns, d_pre)
    )
    slot_next, slot_kept = first_sum(peers, 1, slot_send, slot_keep)
    edge_next, edge_kept = first_sum(peers, 1, edge_send, edge_keep)
    node_pieces = next_sum(peers, 1, node_next, node_kept)
    other = send(returns[1], by_xor(peers, 1))
    (slot_next, slot_kept, edge_next, edge_kept, node_pieces, other, d_pre, returns) = lax.optimization_barrier(
        (slot_next, slot_kept, edge_next, edge_kept, node_pieces, other, d_pre, returns)
    )
    slot_pieces = next_sum(peers, 2, slot_next, slot_kept)
    edge_pieces = next_sum(peers, 2, edge_next, edge_kept)
    node_pieces = halve_sum(peers, node_pieces)
    across = send(returns[4], across_chips(peers))
    edge_grad = pl.pallas_call(
        edges_kernel,
        grid=(tiles,),
        in_specs=[smem, index_tile, tile_of(width), whole((mesh_count, width)), weight(0)],
        out_specs=tile_of(width),
        out_shape=jax.ShapeDtypeStruct((edges, width), BF16),
        compiler_params=params,
        cost_estimate=pl.CostEstimate(
            flops=2 * edges * width * (mesh_count + width), bytes_accessed=4 * edges * width, transcendentals=0
        ),
        name="edge_grad",
    )(tile_count, dst, d_pre, d_aggregate, w_edge_in)
    (slot_pieces, node_pieces, across, edge_grad) = lax.optimization_barrier(
        (slot_pieces, node_pieces, across, edge_grad)
    )
    slot_half = halve_sum(peers, slot_pieces)
    node_terms = rest_terms(peers, node_pieces)
    (slot_half, edge_pieces, node_terms, to_after, to_before) = lax.optimization_barrier(
        (slot_half, edge_pieces, node_terms, returns[2], returns[3])
    )
    slot_terms = rest_terms(peers, slot_half)
    edge_terms = last_terms(peers, edge_pieces)
    bundles = [send(to_after, by_shift(peers, 2)), send(to_before, by_shift(peers, -2))]
    returned = [returns[0], other, *bundles, across] + core_bundles(peers, bundles)
    node_terms, slot_terms = lax.optimization_barrier((node_terms, slot_terms))
    node_rows = w_node_in.shape[0] // peers
    out_rows = w_edge_out.shape[0] // peers
    grid_grad = pl.pallas_call(
        functools.partial(scatter_kernel, out_rows),
        grid=(2,),
        in_specs=[smem, whole(rows.shape)]
        + core_specs
        + [whole((out_rows + cap, width))] * (upper // 2),
        out_specs=pl.BlockSpec((grid_part, width), lambda step: (step, 0)),
        out_shape=jax.ShapeDtypeStruct((grid_count, width), BF16),
        compiler_params=params,
        name="scatter_lists",
    )(me, rows, *returned, *slot_terms)
    edge_terms, grid_grad = lax.optimization_barrier((edge_terms, grid_grad))
    return (
        grid_grad,
        edge_grad,
        mesh_grad,
        total_of(edge_terms, 0, w_edge_in.shape[0] // peers),
        total_of(slot_terms, 0, out_rows),
        total_of(node_terms, 0, node_rows),
        total_of(node_terms, node_rows, node_rows + w_node_out.shape[0] // peers),
    )


def solution(mesh):
    rows = P(("grp", "lon"), None)
    flat = P(("grp", "lon"))
    return jax.shard_map(
        on_device,
        mesh=mesh,
        in_specs=(rows, rows, rows, rows, flat, flat, flat, P(("grp", "lon"), None, None)) + (P(),) * 4,
        out_specs=(rows,) * 7,
        check_vma=False,
    )
```

```python
import functools

import jax
import jax.numpy as jnp
from jax import lax
from jax.experimental import pallas as pl
from jax.experimental.pallas import tpu as pltpu
from jax.sharding import PartitionSpec as P

TILE = 256
STEP = 1024
SUB = 512
LANES = 128
BLOCK = 256
GRID_PARTS = 4
NEAR = 3
BF16 = jnp.bfloat16
F32 = jnp.float32
VMEM_BYTES = 24 * 1024 * 1024
GATHER_BYTES = 56 * 1024 * 1024


def dot(left, right):
    return lax.dot_general(left, right, (((1,), (0,)), ((), ())), preferred_element_type=F32)


def contract_rows(left, right):
    return lax.dot_general(left, right, (((0,), (0,)), ((), ())), preferred_element_type=F32)


def contract_cols(left, right):
    return lax.dot_general(left, right, (((1,), (1,)), ((), ())), preferred_element_type=F32)


def layer_norm(values):
    centered = values - jnp.mean(values, axis=1, keepdims=True)
    inverse = lax.rsqrt(jnp.mean(centered * centered, axis=1, keepdims=True) + 1e-05)
    return (centered * inverse, inverse)


def norm_back(normed, inverse, upstream):
    first = jnp.mean(upstream, axis=1, keepdims=True)
    second = jnp.mean(upstream * normed, axis=1, keepdims=True)
    return inverse * (upstream - first - normed * second)


def silu_and_slope(values):
    sigma = 0.5 + 0.5 * jnp.tanh(0.5 * values)
    hidden = values * sigma
    return (hidden, sigma + hidden * (1.0 - sigma))


def as_column(row):
    count = row.shape[1]
    block = min(count, LANES)
    down = lax.broadcasted_iota(jnp.int32, (block, block), 0)
    along = lax.broadcasted_iota(jnp.int32, (block, block), 1)
    columns = []
    for start in range(0, count, block):
        piece = row[:, start : start + block].astype(F32)
        picked = jnp.where(down == along, piece, 0.0)
        columns.append(jnp.sum(picked, axis=1, keepdims=True))
    return jnp.concatenate(columns, axis=0)


def as_row(column):
    count = column.shape[0]
    block = min(count, LANES)
    down = lax.broadcasted_iota(jnp.int32, (block, block), 0)
    along = lax.broadcasted_iota(jnp.int32, (block, block), 1)
    rows = []
    for start in range(0, count, block):
        picked = jnp.where(down == along, column[start : start + block], 0.0)
        rows.append(jnp.sum(picked, axis=0, keepdims=True))
    return jnp.concatenate(rows, axis=1)


def in_block(indices, first):
    place = indices - first
    return jnp.where((place >= 0) & (place < BLOCK), place, -1).astype(F32).astype(BF16)


def hot_rows(row, width, first=0):
    column = as_column(row).astype(jnp.int32)
    count = row.shape[1]
    one = jnp.ones((), BF16)
    zero = jnp.zeros((), BF16)
    blocks = []
    for start in range(0, width, BLOCK):
        size = min(BLOCK, width - start)
        along = lax.broadcasted_iota(jnp.int32, (count, size), 1).astype(F32).astype(BF16)
        blocks.append(jnp.where(in_block(column, first + start) == along, one, zero))
    return jnp.concatenate(blocks, axis=1)


def hot_columns(row, height):
    count = row.shape[1]
    one = jnp.ones((), BF16)
    zero = jnp.zeros((), BF16)
    blocks = []
    for start in range(0, height, BLOCK):
        size = min(BLOCK, height - start)
        down = lax.broadcasted_iota(jnp.int32, (size, count), 0).astype(F32).astype(BF16)
        blocks.append(jnp.where(in_block(row, start) == down, one, zero))
    return jnp.concatenate(blocks, axis=0)


def live_only(row, first, count):
    place = first + lax.broadcasted_iota(jnp.int32, row.shape, 1)
    return jnp.where(place < count, row, -1)


def near_peers(me, peers):
    after = lax.rem(me + 2, peers)
    before = lax.rem(me + peers - 2, peers)
    across = lax.rem(me + peers - 3 + 6 * (me & 1), peers)
    return (me, me ^ 1, after, after ^ 1, before, before ^ 1, across)


def write_near(refs, cap, lists):
    mine, other, after, before, across = refs
    mine[...] = lists[0]
    other[...] = lists[1]
    after[:cap, :] = lists[2]
    after[cap:, :] = lists[3]
    before[:cap, :] = lists[4]
    before[cap:, :] = lists[5]
    across[...] = lists[6]


def read_near(refs, cap):
    mine, other, from_before, from_after, across, core_before, core_after = refs
    return [
        mine[...],
        other[...],
        from_after[:cap, :],
        core_after[cap:, :],
        from_before[:cap, :],
        core_before[cap:, :],
        across[...],
    ]


def list_hots(me, rows_ref, grid_count, first):
    peers, cap = rows_ref.shape
    pieces = []
    for target in near_peers(me, peers):
        pieces.append(hot_rows(rows_ref[pl.ds(target, 1), :], grid_count, first))
    peer = lax.broadcasted_iota(jnp.int32, (peers, cap), 0)
    ahead = lax.rem(peer - me + peers, peers)
    apart = jnp.minimum(ahead, peers - ahead)
    far = jnp.max(jnp.where(apart > NEAR, rows_ref[...].astype(F32), -1.0), axis=0, keepdims=True)
    pieces.append(hot_rows(far.astype(jnp.int32), grid_count, first))
    return jnp.concatenate(pieces, axis=0)


def gather_kernel(me_ref, rows_hbm, grid_hbm, *refs):
    near_refs, far_ref = refs[:5], refs[5]
    rows_ref, grid_ref, rows_done, grid_done = refs[6:]
    cap = rows_ref.shape[1]
    part = grid_ref.shape[0] // GRID_PARTS
    copies = [
        pltpu.make_async_copy(
            grid_hbm.at[pl.ds(at * part, part)], grid_ref.at[pl.ds(at * part, part)], grid_done.at[at]
        )
        for at in range(GRID_PARTS)
    ]
    rows_copy = pltpu.make_async_copy(rows_hbm, rows_ref, rows_done)
    rows_copy.start()
    for copy in copies:
        copy.start()
    rows_copy.wait()
    found = None
    for at, copy in enumerate(copies):
        hots = list_hots(me_ref[0], rows_ref, part, at * part)
        copy.wait()
        piece = dot(hots, grid_ref[at * part : (at + 1) * part, :])
        found = piece if found is None else found + piece
    rows = found.astype(BF16)
    lists = [rows[at : at + cap] for at in range(0, 8 * cap, cap)]
    write_near(near_refs, cap, lists)
    far_ref[...] = lists[7]


def scatter_kernel(skip, me_ref, rows_ref, *refs):
    near_refs, far_refs, out_ref = refs[:7], refs[7:-1], refs[-1]
    part = out_ref.shape[0]
    cap = rows_ref.shape[1]
    hots = list_hots(me_ref[0], rows_ref, part, pl.program_id(0) * part)
    far = far_refs[0][skip:, :].astype(F32)
    for ref in far_refs[1:]:
        far = far + ref[skip:, :].astype(F32)
    values = jnp.concatenate(read_near(near_refs, cap) + [far.astype(BF16)], axis=0)
    out_ref[...] = contract_rows(hots, values).astype(BF16)


def halves_of(ref):
    rows = ref.shape[-1] if len(ref.shape) == 3 else ref.shape[0]
    return [(start, slice(start, start + SUB)) for start in range(0, rows, SUB)]


def local_kernel(dst_ref, edge_ref, mesh_ref, w_edge_ref, w_receiver_ref, out_ref, weights):
    width = edge_ref.shape[1]

    @pl.when(pl.program_id(0) == 0)
    def _():
        weights[:width, :] = w_edge_ref[...]
        weights[width:, :] = dot(mesh_ref[...], w_receiver_ref[...]).astype(BF16)

    for start, part in halves_of(edge_ref):
        onehot = hot_rows(dst_ref[0, :, part], mesh_ref.shape[0])
        joined = jnp.concatenate([edge_ref[part, :], onehot], axis=1)
        out_ref[part, :] = dot(joined, weights[...]).astype(BF16)


def split_out(me, peers, first, send_ref, keep_ref, parts):
    for low in range(4):
        target = send_ref if low & first else keep_ref
        half = 1 if low & (3 - first) else 0
        at = 0
        for upper in range(peers // 4):
            owner = me ^ (4 * upper + low)
            for ref, share, far in parts:
                piece = ref[pl.ds(pl.multiple_of(owner * share, 16), share), :]
                if far:
                    ahead = lax.rem(owner - me + peers, peers)
                    apart = jnp.minimum(ahead, peers - ahead)
                    piece = jnp.where(apart > NEAR, piece.astype(F32), 0.0)
                target[half, at : at + share, :] = piece.astype(BF16)
                at += share


def forward_kernel(
    peers, me_ref, count_ref, src_ref, dst_ref, local_ref, edge_ref, *refs
):
    near_refs, far_refs = refs[:7], refs[7:11]
    (w_sender_ref, w_out_ref, w_node_in_ref, w_node_out_ref, mesh_ref, cotangent_ref) = refs[11:17]
    (received_ref, hidden_ref, slope_ref, norm_ref, inverse_ref) = refs[17:22]
    (send_ref, keep_ref, d_aggregate_ref, d_centred_ref, d_mesh_ref) = refs[22:27]
    (slot_proj, aggregate, grad_in, grad_out, w_centred) = refs[27:]
    step = pl.program_id(0)
    me = me_ref[0]
    cap = near_refs[0].shape[0]
    width = edge_ref.shape[1]

    @pl.when(step == 0)
    def _():
        aggregate[...] = jnp.zeros_like(aggregate)
        w_out = w_out_ref[...].astype(F32)
        w_centred[...] = (w_out - jnp.mean(w_out, axis=1, keepdims=True)).astype(BF16)
        w_sender = w_sender_ref[...]

        def place(owner, rows, projected):
            offset = pl.multiple_of(owner * cap, 16)
            received_ref[pl.ds(offset, cap), :] = rows
            slot_proj[pl.ds(offset, cap), :] = projected

        for low, ref in enumerate(far_refs):
            rows = ref[...]
            projected = dot(rows, w_sender).astype(BF16)
            for upper in range(peers // 4):
                span = slice(upper * cap, (upper + 1) * cap)
                place(me ^ (4 * upper + low), rows[span], projected[span])
        rows = jnp.concatenate(read_near(near_refs, cap), axis=0)
        projected = dot(rows, w_sender).astype(BF16)
        for spot, owner in enumerate(near_peers(me, peers)):
            place(owner, rows[spot * cap : (spot + 1) * cap], projected[spot * cap : (spot + 1) * cap])

    @pl.when(step * STEP < count_ref[0] * TILE)
    def _():
        parts = halves_of(edge_ref)
        pres = []
        for start, part in parts:
            onehot = hot_rows(src_ref[0, :, part], slot_proj.shape[0])
            pres.append(local_ref[part, :].astype(F32) + dot(onehot, slot_proj[...]))
        projs = []
        for (start, part), pre in zip(parts, pres):
            hidden, slope = silu_and_slope(pre)
            hidden = hidden.astype(BF16)
            hidden_ref[part, :] = hidden
            slope_ref[part, :] = slope.astype(BF16)
            projs.append(dot(hidden, w_centred[...]))
        for (start, part), proj in zip(parts, projs):
            inverse = lax.rsqrt(jnp.mean(proj * proj, axis=1, keepdims=True) + 1e-05)
            normed = proj * inverse
            norm_ref[part, :] = normed.astype(BF16)
            inverse_ref[0, :, part] = as_row(inverse)
            edge_new = (edge_ref[part, :].astype(F32) + normed).astype(BF16)
            receivers = live_only(dst_ref[0, :, part], step * STEP + start, count_ref[0] * TILE)
            aggregate[...] += dot(hot_columns(receivers, aggregate.shape[0]), edge_new)

    @pl.when(step == pl.num_programs(0) - 1)
    def _():
        mesh = mesh_ref[...]
        summed = aggregate[...].astype(BF16)
        node_pre = dot(mesh, w_node_in_ref[:width, :]) + dot(summed, w_node_in_ref[width:, :])
        hidden, slope = silu_and_slope(node_pre)
        hidden = hidden.astype(BF16)
        normed, inverse = layer_norm(dot(hidden, w_node_out_ref[...]))
        upstream = cotangent_ref[...].astype(F32)
        d_proj = norm_back(normed, inverse, upstream).astype(BF16)
        d_pre = (contract_cols(d_proj, w_node_out_ref[...]) * slope).astype(BF16)
        d_mesh_ref[...] = upstream + contract_cols(d_pre, w_node_in_ref[:width, :])
        d_aggregate = contract_cols(d_pre, w_node_in_ref[width:, :]).astype(BF16)
        d_aggregate_ref[...] = d_aggregate
        d_aggregate = d_aggregate.astype(F32)
        d_centred_ref[...] = (d_aggregate - jnp.mean(d_aggregate, axis=1, keepdims=True)).astype(BF16)
        grad_out[...] = contract_rows(hidden, d_proj)
        grad_in[:width, :] = contract_rows(mesh, d_pre)
        grad_in[width:, :] = contract_rows(summed, d_pre)
        split_out(
            me,
            peers,
            2,
            send_ref,
            keep_ref,
            ((grad_in, grad_in.shape[0] // peers, False), (grad_out, grad_out.shape[0] // peers, False)),
        )


def backward_kernel(peers, me_ref, count_ref, src_ref, dst_ref, inverse_ref, *refs):
    (hidden_ref, slope_ref, norm_ref, edge_ref) = refs[:4]
    (d_centred_ref, received_ref, mesh_ref, d_mesh_ref) = refs[4:8]
    (w_sender_ref, w_receiver_ref, w_out_ref) = refs[8:11]
    (d_pre_ref, mesh_grad_ref, slot_send_ref, slot_keep_ref, edge_send_ref, edge_keep_ref) = refs[11:17]
    near_refs = refs[17:22]
    (end_sum, grad_in, grad_out, d_slots) = refs[22:]
    step = pl.program_id(0)
    me = me_ref[0]
    slots, width = received_ref.shape
    mesh_count = mesh_ref.shape[0]

    @pl.when(step == 0)
    def _():
        end_sum[...] = jnp.zeros_like(end_sum)
        grad_in[:width, :] = jnp.zeros((width, width), F32)
        grad_out[...] = jnp.zeros_like(grad_out)

    @pl.when(step * STEP < count_ref[0] * TILE)
    def _():
        parts = halves_of(hidden_ref)
        upstreams = []
        columns = []
        for start, part in parts:
            first = step * STEP + start
            live = count_ref[0] * TILE
            receivers = live_only(dst_ref[0, :, part], first, live)
            upstreams.append(dot(hot_rows(receivers, mesh_count), d_centred_ref[...]))
            senders = live_only(src_ref[0, :, part], first, live)
            columns.append(
                jnp.concatenate([hot_columns(senders, slots), hot_columns(receivers, mesh_count)], axis=0)
            )
        d_projs = []
        d_hiddens = []
        for (start, part), upstream in zip(parts, upstreams):
            inverse = as_column(inverse_ref[0, :, part])
            norm = norm_ref[part, :].astype(F32)
            second = jnp.mean(upstream * norm, axis=1, keepdims=True)
            d_proj = (inverse * (upstream - norm * second)).astype(BF16)
            d_projs.append(d_proj)
            d_hiddens.append(contract_cols(d_proj, w_out_ref[...]))
        for (start, part), d_proj, d_hidden, column in zip(parts, d_projs, d_hiddens, columns):
            grad_out[...] += contract_rows(hidden_ref[part, :], d_proj)
            d_pre = (d_hidden * slope_ref[part, :].astype(F32)).astype(BF16)
            d_pre_ref[part, :] = d_pre
            end_sum[...] += dot(column, d_pre)
            grad_in[:width, :] += contract_rows(edge_ref[part, :], d_pre)

    @pl.when(step == pl.num_programs(0) - 1)
    def _():
        summed = end_sum[:slots, :].astype(BF16)
        mesh_summed = end_sum[slots:, :].astype(BF16)
        d_slots[...] = contract_cols(summed, w_sender_ref[...]).astype(BF16)
        grad_in[width : 2 * width, :] = contract_rows(received_ref[...], summed)
        grad_in[2 * width :, :] = contract_rows(mesh_ref[...], mesh_summed)
        mesh_grad_ref[...] = (d_mesh_ref[...] + contract_cols(mesh_summed, w_receiver_ref[...])).astype(BF16)
        cap = near_refs[0].shape[0]
        owners = near_peers(me, peers)
        write_near(
            near_refs, cap, [d_slots[pl.ds(pl.multiple_of(owner * cap, 16), cap), :] for owner in owners]
        )
        out_share = grad_out.shape[0] // peers
        split_out(
            me, peers, 1, slot_send_ref, slot_keep_ref, ((grad_out, out_share, False), (d_slots, cap, True))
        )
        split_out(
            me, peers, 1, edge_send_ref, edge_keep_ref, ((grad_in, grad_in.shape[0] // peers, False),)
        )


def edges_kernel(count_ref, dst_ref, d_pre_ref, d_aggregate_ref, w_edge_ref, edge_grad_ref):
    step = pl.program_id(0)

    @pl.when(step * STEP < count_ref[0] * TILE)
    def _():
        for start, part in halves_of(d_pre_ref):
            receivers = live_only(dst_ref[0, :, part], step * STEP + start, count_ref[0] * TILE)
            upstream = dot(hot_rows(receivers, d_aggregate_ref.shape[0]), d_aggregate_ref[...])
            edge_grad_ref[part, :] = (upstream + contract_cols(d_pre_ref[part, :], w_edge_ref[...])).astype(BF16)

    @pl.when(step * STEP >= count_ref[0] * TILE)
    def _():
        edge_grad_ref[...] = jnp.zeros_like(edge_grad_ref)


def send(values, perm):
    return lax.ppermute(values, "lon", perm)


def by_xor(peers, bits):
    return [(peer, peer ^ bits) for peer in range(peers)]


def by_shift(peers, shift):
    return [(peer, (peer + shift) % peers) for peer in range(peers)]


def across_chips(peers):
    return [(peer, (peer + (3 if peer % 2 else -3)) % peers) for peer in range(peers)]


def exchange_near(peers, lists):
    mine, other, after, before, across = lists
    return [
        mine,
        other,
        send(after, by_shift(peers, 2)),
        send(before, by_shift(peers, -2)),
        send(across, across_chips(peers)),
    ]


def core_bundles(peers, bundles):
    return [send(bundle, by_xor(peers, 1)) for bundle in bundles]


def add(left, right):
    return (left.astype(F32) + right.astype(F32)).astype(BF16)


def first_sum(peers, bit, outgoing, kept):
    arrived = send(outgoing, by_xor(peers, bit))
    return add(kept[1], arrived[1]), add(kept[0], arrived[0])


def next_sum(peers, bit, outgoing, kept):
    return add(kept, send(outgoing, by_xor(peers, bit)))


def last_terms(peers, pieces):
    count = peers // 4
    share = pieces.shape[0] // count
    terms = [pieces[:share]]
    for place in range(1, count):
        piece = pieces[place * share : (place + 1) * share]
        terms.append(send(piece, by_xor(peers, 4 * place)))
    return terms


def halve_sum(peers, pieces):
    count = peers // 4
    blocks = pieces.reshape(count // 2, 2, -1, pieces.shape[1])
    kept, outgoing = [blocks[:, place].reshape(-1, pieces.shape[1]) for place in range(2)]
    return add(kept, send(outgoing, by_xor(peers, 4)))


def rest_terms(peers, pieces):
    count = peers // 8
    share = pieces.shape[0] // count
    terms = [pieces[:share]]
    for place in range(1, count):
        piece = pieces[place * share : (place + 1) * share]
        terms.append(send(piece, by_xor(peers, 8 * place)))
    return terms


def total_of(terms, start, stop):
    total = terms[0][start:stop].astype(F32)
    for term in terms[1:]:
        total = total + term[start:stop].astype(F32)
    return total


def whole(shape):
    return pl.BlockSpec(shape, lambda *_: (0,) * len(shape))


def on_device(
    grid_latent,
    mesh_latent,
    edge_latent,
    mesh_cotangent,
    edge_src,
    edge_dst,
    tile_count,
    send_rows,
    w_edge_in,
    w_edge_out,
    w_node_in,
    w_node_out,
):
    peers = lax.axis_size("lon")
    me = lax.axis_index("lon").astype(jnp.int32).reshape(1)
    upper = peers // 4
    rows = send_rows[0]
    cap = rows.shape[1]
    slots = peers * cap
    edges, width = edge_latent.shape
    mesh_count = mesh_latent.shape[0]
    grid_count = grid_latent.shape[0]
    tiles = edges // STEP
    src = edge_src.reshape(tiles, 1, STEP)
    dst = edge_dst.reshape(tiles, 1, STEP)
    smem = pl.BlockSpec(memory_space=pltpu.SMEM)
    hbm = pl.BlockSpec(memory_space=pltpu.HBM)
    params = pltpu.CompilerParams(vmem_limit_bytes=VMEM_BYTES)
    square = (width, width)

    def tile_of(last):
        return pl.BlockSpec((STEP, last), lambda step, *_: (step, 0))

    index_tile = pl.BlockSpec((1, 1, STEP), lambda step, *_: (step, 0, 0))

    def weight(place):
        return pl.BlockSpec(square, lambda *_: (place, 0))

    def halves(share):
        shape = (2, upper * share, width)
        return [jax.ShapeDtypeStruct(shape, BF16)] * 2, [whole(shape)] * 2

    grid_part = grid_count // 2
    near_rows = (cap, cap, 2 * cap, 2 * cap, cap)
    near_specs = [whole((count, width)) for count in near_rows]
    near_shapes = [jax.ShapeDtypeStruct((count, width), BF16) for count in near_rows]
    core_specs = near_specs + [whole((2 * cap, width))] * 2
    lists = pl.pallas_call(
        gather_kernel,
        in_specs=[smem, hbm, hbm],
        out_specs=near_specs + [whole((cap, width))],
        out_shape=near_shapes + [jax.ShapeDtypeStruct((cap, width), BF16)],
        scratch_shapes=[
            pltpu.VMEM(rows.shape, jnp.int32),
            pltpu.VMEM(grid_latent.shape, BF16),
            pltpu.SemaphoreType.DMA,
            pltpu.SemaphoreType.DMA((GRID_PARTS,)),
        ],
        compiler_params=pltpu.CompilerParams(vmem_limit_bytes=GATHER_BYTES),
        cost_estimate=pl.CostEstimate(
            flops=40 * 16 * cap * grid_count * width,
            bytes_accessed=2 * grid_count * width,
            transcendentals=0,
        ),
        name="gather_lists",
    )(me, rows, grid_latent)

    hops = [send(lists[5], by_xor(peers, 4 * place)) for place in range(1, upper)]
    near = exchange_near(peers, lists[:5])
    far_own = jnp.concatenate([lists[5]] + hops, axis=0)
    far_own, receivers = lax.optimization_barrier((far_own, dst))
    far_next = send(far_own, by_xor(peers, 2))
    far_core = send(far_own, by_xor(peers, 1))
    local = pl.pallas_call(
        local_kernel,
        grid=(tiles,),
        in_specs=[index_tile, tile_of(width), whole(mesh_latent.shape), weight(0), weight(2)],
        out_specs=tile_of(width),
        out_shape=jax.ShapeDtypeStruct((edges, width), BF16),
        scratch_shapes=[pltpu.VMEM((width + mesh_count, width), BF16)],
        compiler_params=params,
        cost_estimate=pl.CostEstimate(
            flops=2 * edges * width * (width + mesh_count),
            bytes_accessed=4 * edges * width,
            transcendentals=0,
        ),
        name="edge_local",
    )(receivers, edge_latent, mesh_latent, w_edge_in, w_edge_in)
    far_next, far_core, near, local = lax.optimization_barrier((far_next, far_core, near, local))
    near = [near[0], send(near[1], by_xor(peers, 1)), *near[2:]] + core_bundles(peers, near[2:4])
    far_both = send(far_next, by_xor(peers, 1))

    node_shape, node_spec = halves(w_node_in.shape[0] // peers + w_node_out.shape[0] // peers)
    (received, hidden, slope, norm, inverse, node_send, node_keep, d_aggregate, d_centred, d_mesh) = pl.pallas_call(
        functools.partial(forward_kernel, peers),
        grid=(tiles,),
        in_specs=[smem, smem, index_tile, index_tile, tile_of(width), tile_of(width)]
        + core_specs
        + [whole((upper * cap, width))] * 4
        + [weight(1)]
        + [whole(w.shape) for w in (w_edge_out, w_node_in, w_node_out, mesh_latent, mesh_cotangent)],
        out_specs=[whole((slots, width))]
        + [tile_of(width)] * 3
        + [index_tile]
        + node_spec
        + [whole((mesh_count, width))] * 3,
        out_shape=[jax.ShapeDtypeStruct((slots, width), BF16)]
        + [jax.ShapeDtypeStruct((edges, width), BF16)] * 3
        + [jax.ShapeDtypeStruct((tiles, 1, STEP), F32)]
        + node_shape
        + [jax.ShapeDtypeStruct((mesh_count, width), BF16)] * 2
        + [jax.ShapeDtypeStruct((mesh_count, width), F32)],
        scratch_shapes=[
            pltpu.VMEM((slots, width), BF16),
            pltpu.VMEM((mesh_count, width), F32),
            pltpu.VMEM(w_node_in.shape, F32),
            pltpu.VMEM(w_node_out.shape, F32),
            pltpu.VMEM(w_edge_out.shape, BF16),
        ],
        compiler_params=params,
        name="forward",
    )(
        me,
        tile_count,
        src,
        dst,
        local,
        edge_latent,
        *near,
        far_own,
        far_core,
        far_next,
        far_both,
        w_edge_in,
        w_edge_out,
        w_node_in,
        w_node_out,
        mesh_latent,
        mesh_cotangent,
    )

    node_next, node_kept = first_sum(peers, 2, node_send, node_keep)
    slot_shape, slot_spec = halves(w_edge_out.shape[0] // peers + cap)
    edge_shape, edge_spec = halves(w_edge_in.shape[0] // peers)
    results = pl.pallas_call(
        functools.partial(backward_kernel, peers),
        grid=(tiles,),
        in_specs=[smem, smem, index_tile, index_tile, index_tile]
        + [tile_of(width)] * 4
        + [whole((mesh_count, width)), whole((slots, width))]
        + [whole((mesh_count, width))] * 2
        + [weight(1), weight(2), whole(square)],
        out_specs=[tile_of(width), whole((mesh_count, width))] + slot_spec + edge_spec + near_specs,
        out_shape=[
            jax.ShapeDtypeStruct((edges, width), BF16),
            jax.ShapeDtypeStruct((mesh_count, width), BF16),
        ]
        + slot_shape
        + edge_shape
        + near_shapes,
        scratch_shapes=[
            pltpu.VMEM((slots + mesh_count, width), F32),
            pltpu.VMEM(w_edge_in.shape, F32),
            pltpu.VMEM(square, F32),
            pltpu.VMEM((slots, width), BF16),
        ],
        compiler_params=params,
        cost_estimate=pl.CostEstimate(
            flops=2 * edges * width * (2 * mesh_count + 3 * width + slots),
            bytes_accessed=10 * edges * width,
            transcendentals=0,
        ),
        name="backward",
    )(
        me,
        tile_count,
        src,
        dst,
        inverse,
        hidden,
        slope,
        norm,
        edge_latent,
        d_centred,
        received,
        mesh_latent,
        d_mesh,
        w_edge_in,
        w_edge_in,
        w_edge_out,
    )
    (d_pre, mesh_grad, slot_send, slot_keep, edge_send, edge_keep), returns = results[:6], results[6:]
    slot_next, slot_kept = first_sum(peers, 1, slot_send, slot_keep)
    edge_next, edge_kept = first_sum(peers, 1, edge_send, edge_keep)
    node_pieces = next_sum(peers, 1, node_next, node_kept)
    other = send(returns[1], by_xor(peers, 1))
    slot_pieces = next_sum(peers, 2, slot_next, slot_kept)
    (node_pieces, edge_next, edge_kept, other, across) = lax.optimization_barrier(
        (node_pieces, edge_next, edge_kept, other, returns[4])
    )
    node_pieces = halve_sum(peers, node_pieces)
    (slot_pieces, edge_next, edge_kept, across, node_pieces, d_pre) = lax.optimization_barrier(
        (slot_pieces, edge_next, edge_kept, across, node_pieces, d_pre)
    )
    edge_pieces = next_sum(peers, 2, edge_next, edge_kept)
    slot_half = halve_sum(peers, slot_pieces)
    edge_grad = pl.pallas_call(
        edges_kernel,
        grid=(tiles,),
        in_specs=[smem, index_tile, tile_of(width), whole((mesh_count, width)), weight(0)],
        out_specs=tile_of(width),
        out_shape=jax.ShapeDtypeStruct((edges, width), BF16),
        compiler_params=params,
        cost_estimate=pl.CostEstimate(
            flops=2 * edges * width * (mesh_count + width), bytes_accessed=4 * edges * width, transcendentals=0
        ),
        name="edge_grad",
    )(tile_count, dst, d_pre, d_aggregate, w_edge_in)
    slot_half, node_pieces, across, edge_grad, to_after, to_before = lax.optimization_barrier(
        (slot_half, node_pieces, across, edge_grad, returns[2], returns[3])
    )
    bundles = [send(to_after, by_shift(peers, 2)), send(to_before, by_shift(peers, -2))]
    across = send(across, across_chips(peers))
    node_terms = rest_terms(peers, node_pieces)
    slot_terms = rest_terms(peers, slot_half)
    returned = [returns[0], other, *bundles, across] + core_bundles(peers, bundles)
    edge_pieces, returned = lax.optimization_barrier((edge_pieces, returned))
    edge_terms = last_terms(peers, edge_pieces)
    node_terms, slot_terms = lax.optimization_barrier((node_terms, slot_terms))
    node_rows = w_node_in.shape[0] // peers
    out_rows = w_edge_out.shape[0] // peers
    grid_grad = pl.pallas_call(
        functools.partial(scatter_kernel, out_rows),
        grid=(2,),
        in_specs=[smem, whole(rows.shape)]
        + core_specs
        + [whole((out_rows + cap, width))] * (upper // 2),
        out_specs=pl.BlockSpec((grid_part, width), lambda step: (step, 0)),
        out_shape=jax.ShapeDtypeStruct((grid_count, width), BF16),
        compiler_params=params,
        name="scatter_lists",
    )(me, rows, *returned, *slot_terms)
    edge_terms, grid_grad = lax.optimization_barrier((edge_terms, grid_grad))
    return (
        grid_grad,
        edge_grad,
        mesh_grad,
        total_of(edge_terms, 0, w_edge_in.shape[0] // peers),
        total_of(slot_terms, 0, out_rows),
        total_of(node_terms, 0, node_rows),
        total_of(node_terms, node_rows, node_rows + w_node_out.shape[0] // peers),
    )


def solution(mesh):
    rows = P(("grp", "lon"), None)
    flat = P(("grp", "lon"))
    return jax.shard_map(
        on_device,
        mesh=mesh,
        in_specs=(rows, rows, rows, rows, flat, flat, flat, P(("grp", "lon"), None, None)) + (P(),) * 4,
        out_specs=(rows,) * 7,
        check_vma=False,
    )
```

```python
import functools

import jax
import jax.numpy as jnp
from jax import lax
from jax.experimental import pallas as pl
from jax.experimental.pallas import tpu as pltpu
from jax.sharding import PartitionSpec as P

TILE = 256
STEP = 1024
SUB = 512
LANES = 128
BLOCK = 256
GRID_PARTS = 4
NEAR = 3
BF16 = jnp.bfloat16
F32 = jnp.float32
VMEM_BYTES = 24 * 1024 * 1024
GATHER_BYTES = 56 * 1024 * 1024


def dot(left, right):
    return lax.dot_general(left, right, (((1,), (0,)), ((), ())), preferred_element_type=F32)


def contract_rows(left, right):
    return lax.dot_general(left, right, (((0,), (0,)), ((), ())), preferred_element_type=F32)


def contract_cols(left, right):
    return lax.dot_general(left, right, (((1,), (1,)), ((), ())), preferred_element_type=F32)


def layer_norm(values):
    centered = values - jnp.mean(values, axis=1, keepdims=True)
    inverse = lax.rsqrt(jnp.mean(centered * centered, axis=1, keepdims=True) + 1e-05)
    return (centered * inverse, inverse)


def norm_back(normed, inverse, upstream):
    first = jnp.mean(upstream, axis=1, keepdims=True)
    second = jnp.mean(upstream * normed, axis=1, keepdims=True)
    return inverse * (upstream - first - normed * second)


def silu_and_slope(values):
    sigma = 0.5 + 0.5 * jnp.tanh(0.5 * values)
    hidden = values * sigma
    return (hidden, sigma + hidden * (1.0 - sigma))


def as_column(row):
    count = row.shape[1]
    block = min(count, LANES)
    down = lax.broadcasted_iota(jnp.int32, (block, block), 0)
    along = lax.broadcasted_iota(jnp.int32, (block, block), 1)
    columns = []
    for start in range(0, count, block):
        piece = row[:, start : start + block].astype(F32)
        picked = jnp.where(down == along, piece, 0.0)
        columns.append(jnp.sum(picked, axis=1, keepdims=True))
    return jnp.concatenate(columns, axis=0)


def as_row(column):
    count = column.shape[0]
    block = min(count, LANES)
    down = lax.broadcasted_iota(jnp.int32, (block, block), 0)
    along = lax.broadcasted_iota(jnp.int32, (block, block), 1)
    rows = []
    for start in range(0, count, block):
        picked = jnp.where(down == along, column[start : start + block], 0.0)
        rows.append(jnp.sum(picked, axis=0, keepdims=True))
    return jnp.concatenate(rows, axis=1)


def in_block(indices, first):
    place = indices - first
    return jnp.where((place >= 0) & (place < BLOCK), place, -1).astype(F32).astype(BF16)


def hot_rows(row, width, first=0):
    column = as_column(row).astype(jnp.int32)
    count = row.shape[1]
    one = jnp.ones((), BF16)
    zero = jnp.zeros((), BF16)
    blocks = []
    for start in range(0, width, BLOCK):
        size = min(BLOCK, width - start)
        along = lax.broadcasted_iota(jnp.int32, (count, size), 1).astype(F32).astype(BF16)
        blocks.append(jnp.where(in_block(column, first + start) == along, one, zero))
    return jnp.concatenate(blocks, axis=1)


def hot_columns(row, height):
    count = row.shape[1]
    one = jnp.ones((), BF16)
    zero = jnp.zeros((), BF16)
    blocks = []
    for start in range(0, height, BLOCK):
        size = min(BLOCK, height - start)
        down = lax.broadcasted_iota(jnp.int32, (size, count), 0).astype(F32).astype(BF16)
        blocks.append(jnp.where(in_block(row, start) == down, one, zero))
    return jnp.concatenate(blocks, axis=0)


def live_only(row, first, count):
    place = first + lax.broadcasted_iota(jnp.int32, row.shape, 1)
    return jnp.where(place < count, row, -1)


def near_peers(me, peers):
    after = lax.rem(me + 2, peers)
    before = lax.rem(me + peers - 2, peers)
    across = lax.rem(me + peers - 3 + 6 * (me & 1), peers)
    return (me, me ^ 1, after, after ^ 1, before, before ^ 1, across)


def write_near(refs, cap, lists):
    mine, other, after, before, across = refs
    mine[...] = lists[0]
    other[...] = lists[1]
    after[:cap, :] = lists[2]
    after[cap:, :] = lists[3]
    before[:cap, :] = lists[4]
    before[cap:, :] = lists[5]
    across[...] = lists[6]


def read_near(refs, cap):
    mine, other, from_before, from_after, across, core_before, core_after = refs
    return [
        mine[...],
        other[...],
        from_after[:cap, :],
        core_after[cap:, :],
        from_before[:cap, :],
        core_before[cap:, :],
        across[...],
    ]


def list_hots(me, rows_ref, grid_count, first):
    peers, cap = rows_ref.shape
    pieces = []
    for target in near_peers(me, peers):
        pieces.append(hot_rows(rows_ref[pl.ds(target, 1), :], grid_count, first))
    peer = lax.broadcasted_iota(jnp.int32, (peers, cap), 0)
    ahead = lax.rem(peer - me + peers, peers)
    apart = jnp.minimum(ahead, peers - ahead)
    far = jnp.max(jnp.where(apart > NEAR, rows_ref[...].astype(F32), -1.0), axis=0, keepdims=True)
    pieces.append(hot_rows(far.astype(jnp.int32), grid_count, first))
    return jnp.concatenate(pieces, axis=0)


def gather_kernel(me_ref, rows_hbm, grid_hbm, *refs):
    near_refs, far_ref = refs[:5], refs[5]
    rows_ref, grid_ref, rows_done, grid_done = refs[6:]
    cap = rows_ref.shape[1]
    part = grid_ref.shape[0] // GRID_PARTS
    copies = [
        pltpu.make_async_copy(
            grid_hbm.at[pl.ds(at * part, part)], grid_ref.at[pl.ds(at * part, part)], grid_done.at[at]
        )
        for at in range(GRID_PARTS)
    ]
    rows_copy = pltpu.make_async_copy(rows_hbm, rows_ref, rows_done)
    rows_copy.start()
    for copy in copies:
        copy.start()
    rows_copy.wait()
    found = None
    for at, copy in enumerate(copies):
        hots = list_hots(me_ref[0], rows_ref, part, at * part)
        copy.wait()
        piece = dot(hots, grid_ref[at * part : (at + 1) * part, :])
        found = piece if found is None else found + piece
    rows = found.astype(BF16)
    lists = [rows[at : at + cap] for at in range(0, 8 * cap, cap)]
    write_near(near_refs, cap, lists)
    far_ref[...] = lists[7]


def scatter_kernel(skip, me_ref, rows_ref, *refs):
    near_refs, far_refs, out_ref = refs[:7], refs[7:-1], refs[-1]
    part = out_ref.shape[0]
    cap = rows_ref.shape[1]
    hots = list_hots(me_ref[0], rows_ref, part, pl.program_id(0) * part)
    far = far_refs[0][skip:, :].astype(F32)
    for ref in far_refs[1:]:
        far = far + ref[skip:, :].astype(F32)
    values = jnp.concatenate(read_near(near_refs, cap) + [far.astype(BF16)], axis=0)
    out_ref[...] = contract_rows(hots, values).astype(BF16)


def halves_of(ref):
    rows = ref.shape[-1] if len(ref.shape) == 3 else ref.shape[0]
    return [(start, slice(start, start + SUB)) for start in range(0, rows, SUB)]


def local_kernel(dst_ref, edge_ref, mesh_ref, w_edge_ref, w_receiver_ref, out_ref, weights):
    width = edge_ref.shape[1]

    @pl.when(pl.program_id(0) == 0)
    def _():
        weights[:width, :] = w_edge_ref[...]
        weights[width:, :] = dot(mesh_ref[...], w_receiver_ref[...]).astype(BF16)

    for start, part in halves_of(edge_ref):
        onehot = hot_rows(dst_ref[0, :, part], mesh_ref.shape[0])
        joined = jnp.concatenate([edge_ref[part, :], onehot], axis=1)
        out_ref[part, :] = dot(joined, weights[...]).astype(BF16)


def split_out(me, peers, first, send_ref, keep_ref, parts):
    for low in range(4):
        target = send_ref if low & first else keep_ref
        half = 1 if low & (3 - first) else 0
        at = 0
        for upper in range(peers // 4):
            owner = me ^ (4 * upper + low)
            for ref, share, far in parts:
                piece = ref[pl.ds(pl.multiple_of(owner * share, 16), share), :]
                if far:
                    ahead = lax.rem(owner - me + peers, peers)
                    apart = jnp.minimum(ahead, peers - ahead)
                    piece = jnp.where(apart > NEAR, piece.astype(F32), 0.0)
                target[half, at : at + share, :] = piece.astype(BF16)
                at += share


def forward_kernel(
    peers, me_ref, count_ref, src_ref, dst_ref, local_ref, edge_ref, *refs
):
    near_refs, far_refs = refs[:7], refs[7:11]
    (w_sender_ref, w_out_ref, w_node_in_ref, w_node_out_ref, mesh_ref, cotangent_ref) = refs[11:17]
    (received_ref, hidden_ref, slope_ref, norm_ref, inverse_ref) = refs[17:22]
    (send_ref, keep_ref, d_aggregate_ref, d_centred_ref, d_mesh_ref) = refs[22:27]
    (slot_proj, aggregate, grad_in, grad_out, w_centred) = refs[27:]
    step = pl.program_id(0)
    me = me_ref[0]
    cap = near_refs[0].shape[0]
    width = edge_ref.shape[1]

    @pl.when(step == 0)
    def _():
        aggregate[...] = jnp.zeros_like(aggregate)
        w_out = w_out_ref[...].astype(F32)
        w_centred[...] = (w_out - jnp.mean(w_out, axis=1, keepdims=True)).astype(BF16)
        w_sender = w_sender_ref[...]

        def place(owner, rows, projected):
            offset = pl.multiple_of(owner * cap, 16)
            received_ref[pl.ds(offset, cap), :] = rows
            slot_proj[pl.ds(offset, cap), :] = projected

        for low, ref in enumerate(far_refs):
            rows = ref[...]
            projected = dot(rows, w_sender).astype(BF16)
            for upper in range(peers // 4):
                span = slice(upper * cap, (upper + 1) * cap)
                place(me ^ (4 * upper + low), rows[span], projected[span])
        rows = jnp.concatenate(read_near(near_refs, cap), axis=0)
        projected = dot(rows, w_sender).astype(BF16)
        for spot, owner in enumerate(near_peers(me, peers)):
            place(owner, rows[spot * cap : (spot + 1) * cap], projected[spot * cap : (spot + 1) * cap])

    @pl.when(step * STEP < count_ref[0] * TILE)
    def _():
        parts = halves_of(edge_ref)
        pres = []
        for start, part in parts:
            onehot = hot_rows(src_ref[0, :, part], slot_proj.shape[0])
            pres.append(local_ref[part, :].astype(F32) + dot(onehot, slot_proj[...]))
        projs = []
        for (start, part), pre in zip(parts, pres):
            hidden, slope = silu_and_slope(pre)
            hidden = hidden.astype(BF16)
            hidden_ref[part, :] = hidden
            slope_ref[part, :] = slope.astype(BF16)
            projs.append(dot(hidden, w_centred[...]))
        for (start, part), proj in zip(parts, projs):
            inverse = lax.rsqrt(jnp.mean(proj * proj, axis=1, keepdims=True) + 1e-05)
            normed = proj * inverse
            norm_ref[part, :] = normed.astype(BF16)
            inverse_ref[0, :, part] = as_row(inverse)
            edge_new = (edge_ref[part, :].astype(F32) + normed).astype(BF16)
            receivers = live_only(dst_ref[0, :, part], step * STEP + start, count_ref[0] * TILE)
            aggregate[...] += dot(hot_columns(receivers, aggregate.shape[0]), edge_new)

    @pl.when(step == pl.num_programs(0) - 1)
    def _():
        mesh = mesh_ref[...]
        summed = aggregate[...].astype(BF16)
        node_pre = dot(mesh, w_node_in_ref[:width, :]) + dot(summed, w_node_in_ref[width:, :])
        hidden, slope = silu_and_slope(node_pre)
        hidden = hidden.astype(BF16)
        normed, inverse = layer_norm(dot(hidden, w_node_out_ref[...]))
        upstream = cotangent_ref[...].astype(F32)
        d_proj = norm_back(normed, inverse, upstream).astype(BF16)
        d_pre = (contract_cols(d_proj, w_node_out_ref[...]) * slope).astype(BF16)
        d_mesh_ref[...] = upstream + contract_cols(d_pre, w_node_in_ref[:width, :])
        d_aggregate = contract_cols(d_pre, w_node_in_ref[width:, :]).astype(BF16)
        d_aggregate_ref[...] = d_aggregate
        d_aggregate = d_aggregate.astype(F32)
        d_centred_ref[...] = (d_aggregate - jnp.mean(d_aggregate, axis=1, keepdims=True)).astype(BF16)
        grad_out[...] = contract_rows(hidden, d_proj)
        grad_in[:width, :] = contract_rows(mesh, d_pre)
        grad_in[width:, :] = contract_rows(summed, d_pre)
        split_out(
            me,
            peers,
            2,
            send_ref,
            keep_ref,
            ((grad_in, grad_in.shape[0] // peers, False), (grad_out, grad_out.shape[0] // peers, False)),
        )


def backward_kernel(peers, me_ref, count_ref, src_ref, dst_ref, inverse_ref, *refs):
    (hidden_ref, slope_ref, norm_ref, edge_ref) = refs[:4]
    (d_centred_ref, received_ref, mesh_ref, d_mesh_ref) = refs[4:8]
    (w_sender_ref, w_receiver_ref, w_out_ref) = refs[8:11]
    (d_pre_ref, mesh_grad_ref, slot_send_ref, slot_keep_ref, edge_send_ref, edge_keep_ref) = refs[11:17]
    near_refs = refs[17:22]
    (end_sum, grad_in, grad_out, d_slots) = refs[22:]
    step = pl.program_id(0)
    me = me_ref[0]
    slots, width = received_ref.shape
    mesh_count = mesh_ref.shape[0]

    @pl.when(step == 0)
    def _():
        end_sum[...] = jnp.zeros_like(end_sum)
        grad_in[:width, :] = jnp.zeros((width, width), F32)
        grad_out[...] = jnp.zeros_like(grad_out)

    @pl.when(step * STEP < count_ref[0] * TILE)
    def _():
        parts = halves_of(hidden_ref)
        upstreams = []
        columns = []
        for start, part in parts:
            first = step * STEP + start
            live = count_ref[0] * TILE
            receivers = live_only(dst_ref[0, :, part], first, live)
            upstreams.append(dot(hot_rows(receivers, mesh_count), d_centred_ref[...]))
            senders = live_only(src_ref[0, :, part], first, live)
            columns.append(
                jnp.concatenate([hot_columns(senders, slots), hot_columns(receivers, mesh_count)], axis=0)
            )
        d_projs = []
        d_hiddens = []
        for (start, part), upstream in zip(parts, upstreams):
            inverse = as_column(inverse_ref[0, :, part])
            norm = norm_ref[part, :].astype(F32)
            second = jnp.mean(upstream * norm, axis=1, keepdims=True)
            d_proj = (inverse * (upstream - norm * second)).astype(BF16)
            d_projs.append(d_proj)
            d_hiddens.append(contract_cols(d_proj, w_out_ref[...]))
        for (start, part), d_proj, d_hidden, column in zip(parts, d_projs, d_hiddens, columns):
            grad_out[...] += contract_rows(hidden_ref[part, :], d_proj)
            d_pre = (d_hidden * slope_ref[part, :].astype(F32)).astype(BF16)
            d_pre_ref[part, :] = d_pre
            end_sum[...] += dot(column, d_pre)
            grad_in[:width, :] += contract_rows(edge_ref[part, :], d_pre)

    @pl.when(step == pl.num_programs(0) - 1)
    def _():
        summed = end_sum[:slots, :].astype(BF16)
        mesh_summed = end_sum[slots:, :].astype(BF16)
        d_slots[...] = contract_cols(summed, w_sender_ref[...]).astype(BF16)
        grad_in[width : 2 * width, :] = contract_rows(received_ref[...], summed)
        grad_in[2 * width :, :] = contract_rows(mesh_ref[...], mesh_summed)
        mesh_grad_ref[...] = (d_mesh_ref[...] + contract_cols(mesh_summed, w_receiver_ref[...])).astype(BF16)
        cap = near_refs[0].shape[0]
        owners = near_peers(me, peers)
        write_near(
            near_refs, cap, [d_slots[pl.ds(pl.multiple_of(owner * cap, 16), cap), :] for owner in owners]
        )
        out_share = grad_out.shape[0] // peers
        split_out(
            me, peers, 1, slot_send_ref, slot_keep_ref, ((grad_out, out_share, False), (d_slots, cap, True))
        )
        split_out(
            me, peers, 1, edge_send_ref, edge_keep_ref, ((grad_in, grad_in.shape[0] // peers, False),)
        )


def edges_kernel(count_ref, dst_ref, d_pre_ref, d_aggregate_ref, w_edge_ref, edge_grad_ref):
    step = pl.program_id(0)

    @pl.when(step * STEP < count_ref[0] * TILE)
    def _():
        for start, part in halves_of(d_pre_ref):
            receivers = live_only(dst_ref[0, :, part], step * STEP + start, count_ref[0] * TILE)
            upstream = dot(hot_rows(receivers, d_aggregate_ref.shape[0]), d_aggregate_ref[...])
            edge_grad_ref[part, :] = (upstream + contract_cols(d_pre_ref[part, :], w_edge_ref[...])).astype(BF16)

    @pl.when(step * STEP >= count_ref[0] * TILE)
    def _():
        edge_grad_ref[...] = jnp.zeros_like(edge_grad_ref)


def send(values, perm):
    return lax.ppermute(values, "lon", perm)


def by_xor(peers, bits):
    return [(peer, peer ^ bits) for peer in range(peers)]


def by_shift(peers, shift):
    return [(peer, (peer + shift) % peers) for peer in range(peers)]


def across_chips(peers):
    return [(peer, (peer + (3 if peer % 2 else -3)) % peers) for peer in range(peers)]


def exchange_near(peers, lists):
    mine, other, after, before, across = lists
    return [
        mine,
        other,
        send(after, by_shift(peers, 2)),
        send(before, by_shift(peers, -2)),
        send(across, across_chips(peers)),
    ]


def core_bundles(peers, bundles):
    return [send(bundle, by_xor(peers, 1)) for bundle in bundles]


def add(left, right):
    return (left.astype(F32) + right.astype(F32)).astype(BF16)


def first_sum(peers, bit, outgoing, kept):
    arrived = send(outgoing, by_xor(peers, bit))
    return add(kept[1], arrived[1]), add(kept[0], arrived[0])


def next_sum(peers, bit, outgoing, kept):
    return add(kept, send(outgoing, by_xor(peers, bit)))


def last_terms(peers, pieces):
    count = peers // 4
    share = pieces.shape[0] // count
    terms = [pieces[:share]]
    for place in range(1, count):
        piece = pieces[place * share : (place + 1) * share]
        terms.append(send(piece, by_xor(peers, 4 * place)))
    return terms


def halve_sum(peers, pieces):
    count = peers // 4
    blocks = pieces.reshape(count // 2, 2, -1, pieces.shape[1])
    kept, outgoing = [blocks[:, place].reshape(-1, pieces.shape[1]) for place in range(2)]
    return add(kept, send(outgoing, by_xor(peers, 4)))


def rest_terms(peers, pieces):
    count = peers // 8
    share = pieces.shape[0] // count
    terms = [pieces[:share]]
    for place in range(1, count):
        piece = pieces[place * share : (place + 1) * share]
        terms.append(send(piece, by_xor(peers, 8 * place)))
    return terms


def total_of(terms, start, stop):
    total = terms[0][start:stop].astype(F32)
    for term in terms[1:]:
        total = total + term[start:stop].astype(F32)
    return total


def whole(shape):
    return pl.BlockSpec(shape, lambda *_: (0,) * len(shape))


def on_device(
    grid_latent,
    mesh_latent,
    edge_latent,
    mesh_cotangent,
    edge_src,
    edge_dst,
    tile_count,
    send_rows,
    w_edge_in,
    w_edge_out,
    w_node_in,
    w_node_out,
):
    peers = lax.axis_size("lon")
    me = lax.axis_index("lon").astype(jnp.int32).reshape(1)
    upper = peers // 4
    rows = send_rows[0]
    cap = rows.shape[1]
    slots = peers * cap
    edges, width = edge_latent.shape
    mesh_count = mesh_latent.shape[0]
    grid_count = grid_latent.shape[0]
    tiles = edges // STEP
    src = edge_src.reshape(tiles, 1, STEP)
    dst = edge_dst.reshape(tiles, 1, STEP)
    smem = pl.BlockSpec(memory_space=pltpu.SMEM)
    hbm = pl.BlockSpec(memory_space=pltpu.HBM)
    params = pltpu.CompilerParams(vmem_limit_bytes=VMEM_BYTES)
    square = (width, width)

    def tile_of(last):
        return pl.BlockSpec((STEP, last), lambda step, *_: (step, 0))

    index_tile = pl.BlockSpec((1, 1, STEP), lambda step, *_: (step, 0, 0))

    def weight(place):
        return pl.BlockSpec(square, lambda *_: (place, 0))

    def halves(share):
        shape = (2, upper * share, width)
        return [jax.ShapeDtypeStruct(shape, BF16)] * 2, [whole(shape)] * 2

    grid_part = grid_count // 2
    near_rows = (cap, cap, 2 * cap, 2 * cap, cap)
    near_specs = [whole((count, width)) for count in near_rows]
    near_shapes = [jax.ShapeDtypeStruct((count, width), BF16) for count in near_rows]
    core_specs = near_specs + [whole((2 * cap, width))] * 2
    lists = pl.pallas_call(
        gather_kernel,
        in_specs=[smem, hbm, hbm],
        out_specs=near_specs + [whole((cap, width))],
        out_shape=near_shapes + [jax.ShapeDtypeStruct((cap, width), BF16)],
        scratch_shapes=[
            pltpu.VMEM(rows.shape, jnp.int32),
            pltpu.VMEM(grid_latent.shape, BF16),
            pltpu.SemaphoreType.DMA,
            pltpu.SemaphoreType.DMA((GRID_PARTS,)),
        ],
        compiler_params=pltpu.CompilerParams(vmem_limit_bytes=GATHER_BYTES),
        cost_estimate=pl.CostEstimate(
            flops=40 * 16 * cap * grid_count * width,
            bytes_accessed=2 * grid_count * width,
            transcendentals=0,
        ),
        name="gather_lists",
    )(me, rows, grid_latent)

    hops = [send(lists[5], by_xor(peers, 4 * place)) for place in range(1, upper)]
    near = exchange_near(peers, lists[:5])
    far_own = jnp.concatenate([lists[5]] + hops, axis=0)
    far_own, receivers = lax.optimization_barrier((far_own, dst))
    far_next = send(far_own, by_xor(peers, 2))
    far_core = send(far_own, by_xor(peers, 1))
    local = pl.pallas_call(
        local_kernel,
        grid=(tiles,),
        in_specs=[index_tile, tile_of(width), whole(mesh_latent.shape), weight(0), weight(2)],
        out_specs=tile_of(width),
        out_shape=jax.ShapeDtypeStruct((edges, width), BF16),
        scratch_shapes=[pltpu.VMEM((width + mesh_count, width), BF16)],
        compiler_params=params,
        cost_estimate=pl.CostEstimate(
            flops=2 * edges * width * (width + mesh_count),
            bytes_accessed=4 * edges * width,
            transcendentals=0,
        ),
        name="edge_local",
    )(receivers, edge_latent, mesh_latent, w_edge_in, w_edge_in)
    far_next, far_core, near, local = lax.optimization_barrier((far_next, far_core, near, local))
    near = [near[0], send(near[1], by_xor(peers, 1)), *near[2:]] + core_bundles(peers, near[2:4])
    far_both = send(far_next, by_xor(peers, 1))

    node_shape, node_spec = halves(w_node_in.shape[0] // peers + w_node_out.shape[0] // peers)
    (received, hidden, slope, norm, inverse, node_send, node_keep, d_aggregate, d_centred, d_mesh) = pl.pallas_call(
        functools.partial(forward_kernel, peers),
        grid=(tiles,),
        in_specs=[smem, smem, index_tile, index_tile, tile_of(width), tile_of(width)]
        + core_specs
        + [whole((upper * cap, width))] * 4
        + [weight(1)]
        + [whole(w.shape) for w in (w_edge_out, w_node_in, w_node_out, mesh_latent, mesh_cotangent)],
        out_specs=[whole((slots, width))]
        + [tile_of(width)] * 3
        + [index_tile]
        + node_spec
        + [whole((mesh_count, width))] * 3,
        out_shape=[jax.ShapeDtypeStruct((slots, width), BF16)]
        + [jax.ShapeDtypeStruct((edges, width), BF16)] * 3
        + [jax.ShapeDtypeStruct((tiles, 1, STEP), F32)]
        + node_shape
        + [jax.ShapeDtypeStruct((mesh_count, width), BF16)] * 2
        + [jax.ShapeDtypeStruct((mesh_count, width), F32)],
        scratch_shapes=[
            pltpu.VMEM((slots, width), BF16),
            pltpu.VMEM((mesh_count, width), F32),
            pltpu.VMEM(w_node_in.shape, F32),
            pltpu.VMEM(w_node_out.shape, F32),
            pltpu.VMEM(w_edge_out.shape, BF16),
        ],
        compiler_params=params,
        name="forward",
    )(
        me,
        tile_count,
        src,
        dst,
        local,
        edge_latent,
        *near,
        far_own,
        far_core,
        far_next,
        far_both,
        w_edge_in,
        w_edge_out,
        w_node_in,
        w_node_out,
        mesh_latent,
        mesh_cotangent,
    )

    node_next, node_kept = first_sum(peers, 2, node_send, node_keep)
    slot_shape, slot_spec = halves(w_edge_out.shape[0] // peers + cap)
    edge_shape, edge_spec = halves(w_edge_in.shape[0] // peers)
    results = pl.pallas_call(
        functools.partial(backward_kernel, peers),
        grid=(tiles,),
        in_specs=[smem, smem, index_tile, index_tile, index_tile]
        + [tile_of(width)] * 4
        + [whole((mesh_count, width)), whole((slots, width))]
        + [whole((mesh_count, width))] * 2
        + [weight(1), weight(2), whole(square)],
        out_specs=[tile_of(width), whole((mesh_count, width))] + slot_spec + edge_spec + near_specs,
        out_shape=[
            jax.ShapeDtypeStruct((edges, width), BF16),
            jax.ShapeDtypeStruct((mesh_count, width), BF16),
        ]
        + slot_shape
        + edge_shape
        + near_shapes,
        scratch_shapes=[
            pltpu.VMEM((slots + mesh_count, width), F32),
            pltpu.VMEM(w_edge_in.shape, F32),
            pltpu.VMEM(square, F32),
            pltpu.VMEM((slots, width), BF16),
        ],
        compiler_params=params,
        cost_estimate=pl.CostEstimate(
            flops=2 * edges * width * (2 * mesh_count + 3 * width + slots),
            bytes_accessed=10 * edges * width,
            transcendentals=0,
        ),
        name="backward",
    )(
        me,
        tile_count,
        src,
        dst,
        inverse,
        hidden,
        slope,
        norm,
        edge_latent,
        d_centred,
        received,
        mesh_latent,
        d_mesh,
        w_edge_in,
        w_edge_in,
        w_edge_out,
    )
    (d_pre, mesh_grad, slot_send, slot_keep, edge_send, edge_keep), returns = results[:6], results[6:]
    slot_next, slot_kept = first_sum(peers, 1, slot_send, slot_keep)
    slot_pieces = next_sum(peers, 2, slot_next, slot_kept)
    (node_next, node_kept, edge_send, edge_keep, returns) = lax.optimization_barrier(
        (node_next, node_kept, edge_send, edge_keep, returns)
    )
    edge_next, edge_kept = first_sum(peers, 1, edge_send, edge_keep)
    other = send(returns[1], by_xor(peers, 1))
    node_pieces = next_sum(peers, 1, node_next, node_kept)
    bundles = [send(returns[2], by_shift(peers, 2)), send(returns[3], by_shift(peers, -2))]
    (node_pieces, edge_next, edge_kept, other, bundles) = lax.optimization_barrier(
        (node_pieces, edge_next, edge_kept, other, bundles)
    )
    node_pieces = halve_sum(peers, node_pieces)
    (slot_pieces, node_pieces, bundles, edge_next, edge_kept, d_pre) = lax.optimization_barrier(
        (slot_pieces, node_pieces, bundles, edge_next, edge_kept, d_pre)
    )
    edge_pieces = next_sum(peers, 2, edge_next, edge_kept)
    slot_half = halve_sum(peers, slot_pieces)
    edge_grad = pl.pallas_call(
        edges_kernel,
        grid=(tiles,),
        in_specs=[smem, index_tile, tile_of(width), whole((mesh_count, width)), weight(0)],
        out_specs=tile_of(width),
        out_shape=jax.ShapeDtypeStruct((edges, width), BF16),
        compiler_params=params,
        cost_estimate=pl.CostEstimate(
            flops=2 * edges * width * (mesh_count + width), bytes_accessed=4 * edges * width, transcendentals=0
        ),
        name="edge_grad",
    )(tile_count, dst, d_pre, d_aggregate, w_edge_in)
    slot_half, node_pieces, across, edge_grad = lax.optimization_barrier(
        (slot_half, node_pieces, returns[4], edge_grad)
    )
    slot_terms = rest_terms(peers, slot_half)
    node_terms = rest_terms(peers, node_pieces)
    across = send(across, across_chips(peers))
    edge_pieces, across, bundles = lax.optimization_barrier((edge_pieces, across, bundles))
    edge_terms = last_terms(peers, edge_pieces)
    returned = [returns[0], other, *bundles, across] + core_bundles(peers, bundles)
    node_terms, slot_terms = lax.optimization_barrier((node_terms, slot_terms))
    node_rows = w_node_in.shape[0] // peers
    out_rows = w_edge_out.shape[0] // peers
    grid_grad = pl.pallas_call(
        functools.partial(scatter_kernel, out_rows),
        grid=(2,),
        in_specs=[smem, whole(rows.shape)]
        + core_specs
        + [whole((out_rows + cap, width))] * (upper // 2),
        out_specs=pl.BlockSpec((grid_part, width), lambda step: (step, 0)),
        out_shape=jax.ShapeDtypeStruct((grid_count, width), BF16),
        compiler_params=params,
        name="scatter_lists",
    )(me, rows, *returned, *slot_terms)
    edge_terms, grid_grad = lax.optimization_barrier((edge_terms, grid_grad))
    return (
        grid_grad,
        edge_grad,
        mesh_grad,
        total_of(edge_terms, 0, w_edge_in.shape[0] // peers),
        total_of(slot_terms, 0, out_rows),
        total_of(node_terms, 0, node_rows),
        total_of(node_terms, node_rows, node_rows + w_node_out.shape[0] // peers),
    )


def solution(mesh):
    rows = P(("grp", "lon"), None)
    flat = P(("grp", "lon"))
    return jax.shard_map(
        on_device,
        mesh=mesh,
        in_specs=(rows, rows, rows, rows, flat, flat, flat, P(("grp", "lon"), None, None)) + (P(),) * 4,
        out_specs=(rows,) * 7,
        check_vma=False,
    )
```

```python
import functools

import jax
import jax.numpy as jnp
from jax import lax
from jax.experimental import pallas as pl
from jax.experimental.pallas import tpu as pltpu
from jax.sharding import PartitionSpec as P

TILE = 256
STEP = 1024
SUB = 512
LANES = 128
BLOCK = 256
GRID_PARTS = 4
NEAR = 3
BF16 = jnp.bfloat16
F32 = jnp.float32
VMEM_BYTES = 24 * 1024 * 1024
GATHER_BYTES = 56 * 1024 * 1024


def dot(left, right):
    return lax.dot_general(left, right, (((1,), (0,)), ((), ())), preferred_element_type=F32)


def contract_rows(left, right):
    return lax.dot_general(left, right, (((0,), (0,)), ((), ())), preferred_element_type=F32)


def contract_cols(left, right):
    return lax.dot_general(left, right, (((1,), (1,)), ((), ())), preferred_element_type=F32)


def layer_norm(values):
    centered = values - jnp.mean(values, axis=1, keepdims=True)
    inverse = lax.rsqrt(jnp.mean(centered * centered, axis=1, keepdims=True) + 1e-05)
    return (centered * inverse, inverse)


def norm_back(normed, inverse, upstream):
    first = jnp.mean(upstream, axis=1, keepdims=True)
    second = jnp.mean(upstream * normed, axis=1, keepdims=True)
    return inverse * (upstream - first - normed * second)


def silu_and_slope(values):
    sigma = 0.5 + 0.5 * jnp.tanh(0.5 * values)
    hidden = values * sigma
    return (hidden, sigma + hidden * (1.0 - sigma))


def as_column(row):
    count = row.shape[1]
    block = min(count, LANES)
    down = lax.broadcasted_iota(jnp.int32, (block, block), 0)
    along = lax.broadcasted_iota(jnp.int32, (block, block), 1)
    columns = []
    for start in range(0, count, block):
        piece = row[:, start : start + block].astype(F32)
        picked = jnp.where(down == along, piece, 0.0)
        columns.append(jnp.sum(picked, axis=1, keepdims=True))
    return jnp.concatenate(columns, axis=0)


def as_row(column):
    count = column.shape[0]
    block = min(count, LANES)
    down = lax.broadcasted_iota(jnp.int32, (block, block), 0)
    along = lax.broadcasted_iota(jnp.int32, (block, block), 1)
    rows = []
    for start in range(0, count, block):
        picked = jnp.where(down == along, column[start : start + block], 0.0)
        rows.append(jnp.sum(picked, axis=0, keepdims=True))
    return jnp.concatenate(rows, axis=1)


def in_block(indices, first):
    place = indices - first
    return jnp.where((place >= 0) & (place < BLOCK), place, -1).astype(F32).astype(BF16)


def hot_rows(row, width, first=0):
    column = as_column(row).astype(jnp.int32)
    count = row.shape[1]
    one = jnp.ones((), BF16)
    zero = jnp.zeros((), BF16)
    blocks = []
    for start in range(0, width, BLOCK):
        size = min(BLOCK, width - start)
        along = lax.broadcasted_iota(jnp.int32, (count, size), 1).astype(F32).astype(BF16)
        blocks.append(jnp.where(in_block(column, first + start) == along, one, zero))
    return jnp.concatenate(blocks, axis=1)


def hot_columns(row, height):
    count = row.shape[1]
    one = jnp.ones((), BF16)
    zero = jnp.zeros((), BF16)
    blocks = []
    for start in range(0, height, BLOCK):
        size = min(BLOCK, height - start)
        down = lax.broadcasted_iota(jnp.int32, (size, count), 0).astype(F32).astype(BF16)
        blocks.append(jnp.where(in_block(row, start) == down, one, zero))
    return jnp.concatenate(blocks, axis=0)


def live_only(row, first, count):
    place = first + lax.broadcasted_iota(jnp.int32, row.shape, 1)
    return jnp.where(place < count, row, -1)


def near_peers(me, peers):
    after = lax.rem(me + 2, peers)
    before = lax.rem(me + peers - 2, peers)
    across = lax.rem(me + peers - 3 + 6 * (me & 1), peers)
    return (me, me ^ 1, after, after ^ 1, before, before ^ 1, across)


def write_near(refs, cap, lists):
    mine, other, after, before, across = refs
    mine[...] = lists[0]
    other[...] = lists[1]
    after[:cap, :] = lists[2]
    after[cap:, :] = lists[3]
    before[:cap, :] = lists[4]
    before[cap:, :] = lists[5]
    across[...] = lists[6]


def read_near(refs, cap):
    mine, other, from_before, from_after, across, core_before, core_after = refs
    return [
        mine[...],
        other[...],
        from_after[:cap, :],
        core_after[cap:, :],
        from_before[:cap, :],
        core_before[cap:, :],
        across[...],
    ]


def write_back(refs, cap, lists):
    mine, swapped, after, before, across = refs
    mine[...] = lists[0]
    for place, index in enumerate((1, 3, 5)):
        swapped[place * cap : (place + 1) * cap, :] = lists[index]
    after[...] = lists[2]
    before[...] = lists[4]
    across[...] = lists[6]


def read_back(refs, cap):
    mine, swapped, from_before, from_after, across = refs
    return [
        mine[...],
        swapped[:cap, :],
        from_after[:cap, :],
        from_after[cap:, :],
        from_before[:cap, :],
        from_before[cap:, :],
        across[...],
    ]


def list_hots(me, rows_ref, grid_count, first):
    peers, cap = rows_ref.shape
    pieces = []
    for target in near_peers(me, peers):
        pieces.append(hot_rows(rows_ref[pl.ds(target, 1), :], grid_count, first))
    peer = lax.broadcasted_iota(jnp.int32, (peers, cap), 0)
    ahead = lax.rem(peer - me + peers, peers)
    apart = jnp.minimum(ahead, peers - ahead)
    far = jnp.max(jnp.where(apart > NEAR, rows_ref[...].astype(F32), -1.0), axis=0, keepdims=True)
    pieces.append(hot_rows(far.astype(jnp.int32), grid_count, first))
    return jnp.concatenate(pieces, axis=0)


def gather_kernel(me_ref, rows_hbm, grid_hbm, *refs):
    near_refs, far_ref = refs[:5], refs[5]
    rows_ref, grid_ref, rows_done, grid_done = refs[6:]
    cap = rows_ref.shape[1]
    part = grid_ref.shape[0] // GRID_PARTS
    copies = [
        pltpu.make_async_copy(
            grid_hbm.at[pl.ds(at * part, part)], grid_ref.at[pl.ds(at * part, part)], grid_done.at[at]
        )
        for at in range(GRID_PARTS)
    ]
    rows_copy = pltpu.make_async_copy(rows_hbm, rows_ref, rows_done)
    rows_copy.start()
    for copy in copies:
        copy.start()
    rows_copy.wait()
    found = None
    for at, copy in enumerate(copies):
        hots = list_hots(me_ref[0], rows_ref, part, at * part)
        copy.wait()
        piece = dot(hots, grid_ref[at * part : (at + 1) * part, :])
        found = piece if found is None else found + piece
    rows = found.astype(BF16)
    lists = [rows[at : at + cap] for at in range(0, 8 * cap, cap)]
    write_near(near_refs, cap, lists)
    far_ref[...] = lists[7]


def scatter_kernel(skip, me_ref, rows_ref, *refs):
    near_refs, far_refs, out_ref = refs[:5], refs[5:-1], refs[-1]
    part = out_ref.shape[0]
    cap = rows_ref.shape[1]
    hots = list_hots(me_ref[0], rows_ref, part, pl.program_id(0) * part)
    far = far_refs[0][skip:, :].astype(F32)
    for ref in far_refs[1:]:
        far = far + ref[skip:, :].astype(F32)
    values = jnp.concatenate(read_back(near_refs, cap) + [far.astype(BF16)], axis=0)
    out_ref[...] = contract_rows(hots, values).astype(BF16)


def halves_of(ref):
    rows = ref.shape[-1] if len(ref.shape) == 3 else ref.shape[0]
    return [(start, slice(start, start + SUB)) for start in range(0, rows, SUB)]


def local_kernel(dst_ref, edge_ref, mesh_ref, w_edge_ref, w_receiver_ref, out_ref, weights):
    width = edge_ref.shape[1]

    @pl.when(pl.program_id(0) == 0)
    def _():
        weights[:width, :] = w_edge_ref[...]
        weights[width:, :] = dot(mesh_ref[...], w_receiver_ref[...]).astype(BF16)

    for start, part in halves_of(edge_ref):
        onehot = hot_rows(dst_ref[0, :, part], mesh_ref.shape[0])
        joined = jnp.concatenate([edge_ref[part, :], onehot], axis=1)
        out_ref[part, :] = dot(joined, weights[...]).astype(BF16)


def split_out(me, peers, first, send_ref, keep_ref, parts):
    for low in range(4):
        target = send_ref if low & first else keep_ref
        half = 1 if low & (3 - first) else 0
        at = 0
        for upper in range(peers // 4):
            owner = me ^ (4 * upper + low)
            for ref, share, far in parts:
                piece = ref[pl.ds(pl.multiple_of(owner * share, 16), share), :]
                if far:
                    ahead = lax.rem(owner - me + peers, peers)
                    apart = jnp.minimum(ahead, peers - ahead)
                    piece = jnp.where(apart > NEAR, piece.astype(F32), 0.0)
                target[half, at : at + share, :] = piece.astype(BF16)
                at += share


def forward_kernel(
    peers, me_ref, count_ref, src_ref, dst_ref, local_ref, edge_ref, *refs
):
    near_refs, far_refs = refs[:7], refs[7:11]
    (w_sender_ref, w_out_ref, w_node_in_ref, w_node_out_ref, mesh_ref, cotangent_ref) = refs[11:17]
    (received_ref, hidden_ref, slope_ref, norm_ref, inverse_ref) = refs[17:22]
    (send_ref, keep_ref, d_aggregate_ref, d_mesh_ref) = refs[22:26]
    (slot_proj, aggregate, grad_in, grad_out, w_centred) = refs[26:]
    step = pl.program_id(0)
    me = me_ref[0]
    cap = near_refs[0].shape[0]
    width = edge_ref.shape[1]

    @pl.when(step == 0)
    def _():
        aggregate[...] = jnp.zeros_like(aggregate)
        w_out = w_out_ref[...].astype(F32)
        w_centred[...] = (w_out - jnp.mean(w_out, axis=1, keepdims=True)).astype(BF16)
        w_sender = w_sender_ref[...]

        def place(owner, rows, projected):
            offset = pl.multiple_of(owner * cap, 16)
            received_ref[pl.ds(offset, cap), :] = rows
            slot_proj[pl.ds(offset, cap), :] = projected

        for low, ref in enumerate(far_refs):
            rows = ref[...]
            projected = dot(rows, w_sender).astype(BF16)
            for upper in range(peers // 4):
                span = slice(upper * cap, (upper + 1) * cap)
                place(me ^ (4 * upper + low), rows[span], projected[span])
        rows = jnp.concatenate(read_near(near_refs, cap), axis=0)
        projected = dot(rows, w_sender).astype(BF16)
        for spot, owner in enumerate(near_peers(me, peers)):
            place(owner, rows[spot * cap : (spot + 1) * cap], projected[spot * cap : (spot + 1) * cap])

    @pl.when(step * STEP < count_ref[0] * TILE)
    def _():
        parts = halves_of(edge_ref)
        pres = []
        for start, part in parts:
            onehot = hot_rows(src_ref[0, :, part], slot_proj.shape[0])
            pres.append(local_ref[part, :].astype(F32) + dot(onehot, slot_proj[...]))
        projs = []
        for (start, part), pre in zip(parts, pres):
            hidden, slope = silu_and_slope(pre)
            hidden = hidden.astype(BF16)
            hidden_ref[part, :] = hidden
            slope_ref[part, :] = slope.astype(BF16)
            projs.append(dot(hidden, w_centred[...]))
        for (start, part), proj in zip(parts, projs):
            inverse = lax.rsqrt(jnp.mean(proj * proj, axis=1, keepdims=True) + 1e-05)
            normed = proj * inverse
            norm_ref[part, :] = normed.astype(BF16)
            inverse_ref[0, :, part] = as_row(inverse)
            edge_new = (edge_ref[part, :].astype(F32) + normed).astype(BF16)
            receivers = live_only(dst_ref[0, :, part], step * STEP + start, count_ref[0] * TILE)
            aggregate[...] += dot(hot_columns(receivers, aggregate.shape[0]), edge_new)

    @pl.when(step == pl.num_programs(0) - 1)
    def _():
        mesh = mesh_ref[...]
        summed = aggregate[...].astype(BF16)
        node_pre = dot(mesh, w_node_in_ref[:width, :]) + dot(summed, w_node_in_ref[width:, :])
        hidden, slope = silu_and_slope(node_pre)
        hidden = hidden.astype(BF16)
        normed, inverse = layer_norm(dot(hidden, w_node_out_ref[...]))
        upstream = cotangent_ref[...].astype(F32)
        d_proj = norm_back(normed, inverse, upstream).astype(BF16)
        d_pre = (contract_cols(d_proj, w_node_out_ref[...]) * slope).astype(BF16)
        d_mesh_ref[...] = upstream + contract_cols(d_pre, w_node_in_ref[:width, :])
        d_aggregate_ref[...] = contract_cols(d_pre, w_node_in_ref[width:, :]).astype(BF16)
        grad_out[...] = contract_rows(hidden, d_proj)
        grad_in[:width, :] = contract_rows(mesh, d_pre)
        grad_in[width:, :] = contract_rows(summed, d_pre)
        split_out(
            me,
            peers,
            2,
            send_ref,
            keep_ref,
            ((grad_in, grad_in.shape[0] // peers, False), (grad_out, grad_out.shape[0] // peers, False)),
        )


def backward_kernel(peers, me_ref, count_ref, src_ref, dst_ref, inverse_ref, *refs):
    (hidden_ref, slope_ref, norm_ref, edge_ref) = refs[:4]
    (d_aggregate_ref, received_ref, mesh_ref, d_mesh_ref) = refs[4:8]
    (w_sender_ref, w_receiver_ref, w_edge_ref, w_out_ref) = refs[8:12]
    (edge_grad_ref, mesh_grad_ref, slot_send_ref, slot_keep_ref, edge_send_ref, edge_keep_ref) = refs[12:18]
    near_refs = refs[18:23]
    (end_sum, grad_in, grad_out, d_slots) = refs[23:]
    step = pl.program_id(0)
    me = me_ref[0]
    slots, width = received_ref.shape
    mesh_count = mesh_ref.shape[0]

    @pl.when(step == 0)
    def _():
        end_sum[...] = jnp.zeros_like(end_sum)
        grad_in[:width, :] = jnp.zeros((width, width), F32)
        grad_out[...] = jnp.zeros_like(grad_out)

    @pl.when(step * STEP < count_ref[0] * TILE)
    def _():
        parts = halves_of(hidden_ref)
        upstreams = []
        columns = []
        for start, part in parts:
            first = step * STEP + start
            live = count_ref[0] * TILE
            receivers = live_only(dst_ref[0, :, part], first, live)
            upstreams.append(dot(hot_rows(receivers, mesh_count), d_aggregate_ref[...]))
            senders = live_only(src_ref[0, :, part], first, live)
            columns.append(
                jnp.concatenate([hot_columns(senders, slots), hot_columns(receivers, mesh_count)], axis=0)
            )
        d_projs = []
        d_hiddens = []
        for (start, part), upstream in zip(parts, upstreams):
            inverse = as_column(inverse_ref[0, :, part])
            d_proj = norm_back(norm_ref[part, :].astype(F32), inverse, upstream).astype(BF16)
            d_projs.append(d_proj)
            d_hiddens.append(contract_cols(d_proj, w_out_ref[...]))
        for (start, part), d_proj, d_hidden, column, upstream in zip(
            parts, d_projs, d_hiddens, columns, upstreams
        ):
            grad_out[...] += contract_rows(hidden_ref[part, :], d_proj)
            d_pre = (d_hidden * slope_ref[part, :].astype(F32)).astype(BF16)
            edge_grad_ref[part, :] = (upstream + contract_cols(d_pre, w_edge_ref[...])).astype(BF16)
            end_sum[...] += dot(column, d_pre)
            grad_in[:width, :] += contract_rows(edge_ref[part, :], d_pre)

    @pl.when(step * STEP >= count_ref[0] * TILE)
    def _():
        edge_grad_ref[...] = jnp.zeros_like(edge_grad_ref)

    @pl.when(step == pl.num_programs(0) - 1)
    def _():
        summed = end_sum[:slots, :].astype(BF16)
        mesh_summed = end_sum[slots:, :].astype(BF16)
        d_slots[...] = contract_cols(summed, w_sender_ref[...]).astype(BF16)
        grad_in[width : 2 * width, :] = contract_rows(received_ref[...], summed)
        grad_in[2 * width :, :] = contract_rows(mesh_ref[...], mesh_summed)
        mesh_grad_ref[...] = (d_mesh_ref[...] + contract_cols(mesh_summed, w_receiver_ref[...])).astype(BF16)
        cap = near_refs[0].shape[0]
        owners = near_peers(me, peers)
        write_back(
            near_refs, cap, [d_slots[pl.ds(pl.multiple_of(owner * cap, 16), cap), :] for owner in owners]
        )
        out_share = grad_out.shape[0] // peers
        split_out(
            me, peers, 1, slot_send_ref, slot_keep_ref, ((grad_out, out_share, False), (d_slots, cap, True))
        )
        split_out(
            me, peers, 1, edge_send_ref, edge_keep_ref, ((grad_in, grad_in.shape[0] // peers, False),)
        )


def send(values, perm):
    return lax.ppermute(values, "lon", perm)


def by_xor(peers, bits):
    return [(peer, peer ^ bits) for peer in range(peers)]


def by_shift(peers, shift):
    return [(peer, (peer + shift) % peers) for peer in range(peers)]


def across_chips(peers):
    return [(peer, (peer + (3 if peer % 2 else -3)) % peers) for peer in range(peers)]


def exchange_near(peers, lists):
    mine, other, after, before = lists
    return [mine, other, send(after, by_shift(peers, 2)), send(before, by_shift(peers, -2))]


def core_near(peers, near):
    mine, other, after, before, across = near
    swap = by_xor(peers, 1)
    return [mine, send(other, swap), after, before, across, send(after, swap), send(before, swap)]


def add(left, right):
    return (left.astype(F32) + right.astype(F32)).astype(BF16)


def first_sum(peers, bit, outgoing, kept):
    arrived = send(outgoing, by_xor(peers, bit))
    return add(kept[1], arrived[1]), add(kept[0], arrived[0])


def next_sum(peers, bit, outgoing, kept):
    return add(kept, send(outgoing, by_xor(peers, bit)))


def last_terms(peers, pieces):
    count = peers // 4
    share = pieces.shape[0] // count
    terms = [pieces[:share]]
    for place in range(1, count):
        piece = pieces[place * share : (place + 1) * share]
        terms.append(send(piece, by_xor(peers, 4 * place)))
    return terms


def total_of(terms, start, stop):
    total = terms[0][start:stop].astype(F32)
    for term in terms[1:]:
        total = total + term[start:stop].astype(F32)
    return total


def whole(shape):
    return pl.BlockSpec(shape, lambda *_: (0,) * len(shape))


def on_device(
    grid_latent,
    mesh_latent,
    edge_latent,
    mesh_cotangent,
    edge_src,
    edge_dst,
    tile_count,
    send_rows,
    w_edge_in,
    w_edge_out,
    w_node_in,
    w_node_out,
):
    peers = lax.axis_size("lon")
    me = lax.axis_index("lon").astype(jnp.int32).reshape(1)
    upper = peers // 4
    rows = send_rows[0]
    cap = rows.shape[1]
    slots = peers * cap
    edges, width = edge_latent.shape
    mesh_count = mesh_latent.shape[0]
    grid_count = grid_latent.shape[0]
    tiles = edges // STEP
    src = edge_src.reshape(tiles, 1, STEP)
    dst = edge_dst.reshape(tiles, 1, STEP)
    smem = pl.BlockSpec(memory_space=pltpu.SMEM)
    hbm = pl.BlockSpec(memory_space=pltpu.HBM)
    params = pltpu.CompilerParams(vmem_limit_bytes=VMEM_BYTES)
    square = (width, width)

    def tile_of(last):
        return pl.BlockSpec((STEP, last), lambda step, *_: (step, 0))

    index_tile = pl.BlockSpec((1, 1, STEP), lambda step, *_: (step, 0, 0))

    def weight(place):
        return pl.BlockSpec(square, lambda *_: (place, 0))

    def halves(share):
        shape = (2, upper * share, width)
        return [jax.ShapeDtypeStruct(shape, BF16)] * 2, [whole(shape)] * 2

    grid_part = grid_count // 2
    near_rows = (cap, cap, 2 * cap, 2 * cap, cap)
    near_specs = [whole((count, width)) for count in near_rows]
    near_shapes = [jax.ShapeDtypeStruct((count, width), BF16) for count in near_rows]
    core_specs = near_specs + [whole((2 * cap, width))] * 2
    back_rows = (cap, 3 * cap, cap, cap, cap)
    back_specs = [whole((count, width)) for count in back_rows]
    back_shapes = [jax.ShapeDtypeStruct((count, width), BF16) for count in back_rows]
    return_specs = [whole((count, width)) for count in (cap, 3 * cap, 2 * cap, 2 * cap, cap)]
    lists = pl.pallas_call(
        gather_kernel,
        in_specs=[smem, hbm, hbm],
        out_specs=near_specs + [whole((cap, width))],
        out_shape=near_shapes + [jax.ShapeDtypeStruct((cap, width), BF16)],
        scratch_shapes=[
            pltpu.VMEM(rows.shape, jnp.int32),
            pltpu.VMEM(grid_latent.shape, BF16),
            pltpu.SemaphoreType.DMA,
            pltpu.SemaphoreType.DMA((GRID_PARTS,)),
        ],
        compiler_params=pltpu.CompilerParams(vmem_limit_bytes=GATHER_BYTES),
        cost_estimate=pl.CostEstimate(
            flops=40 * 16 * cap * grid_count * width,
            bytes_accessed=2 * grid_count * width,
            transcendentals=0,
        ),
        name="gather_lists",
    )(me, rows, grid_latent)

    hops = [send(lists[5], by_xor(peers, 4 * place)) for place in range(1, upper)]
    near = exchange_near(peers, lists[:4])
    hops[0], across = lax.optimization_barrier((hops[0], lists[4]))
    near.append(send(across, across_chips(peers)))
    far_own = jnp.concatenate([lists[5]] + hops, axis=0)
    far_own, receivers = lax.optimization_barrier((far_own, dst))
    far_next = send(far_own, by_xor(peers, 2))
    far_core = send(far_own, by_xor(peers, 1))
    local = pl.pallas_call(
        local_kernel,
        grid=(tiles,),
        in_specs=[index_tile, tile_of(width), whole(mesh_latent.shape), weight(0), weight(2)],
        out_specs=tile_of(width),
        out_shape=jax.ShapeDtypeStruct((edges, width), BF16),
        scratch_shapes=[pltpu.VMEM((width + mesh_count, width), BF16)],
        compiler_params=params,
        cost_estimate=pl.CostEstimate(
            flops=2 * edges * width * (width + mesh_count),
            bytes_accessed=4 * edges * width,
            transcendentals=0,
        ),
        name="edge_local",
    )(receivers, edge_latent, mesh_latent, w_edge_in, w_edge_in)
    far_next, far_core, near, local = lax.optimization_barrier((far_next, far_core, near, local))
    near = core_near(peers, near)
    far_both = send(far_next, by_xor(peers, 1))

    node_shape, node_spec = halves(w_node_in.shape[0] // peers + w_node_out.shape[0] // peers)
    (received, hidden, slope, norm, inverse, node_send, node_keep, d_aggregate, d_mesh) = pl.pallas_call(
        functools.partial(forward_kernel, peers),
        grid=(tiles,),
        in_specs=[smem, smem, index_tile, index_tile, tile_of(width), tile_of(width)]
        + core_specs
        + [whole((upper * cap, width))] * 4
        + [weight(1)]
        + [whole(w.shape) for w in (w_edge_out, w_node_in, w_node_out, mesh_latent, mesh_cotangent)],
        out_specs=[whole((slots, width))]
        + [tile_of(width)] * 3
        + [index_tile]
        + node_spec
        + [whole((mesh_count, width))] * 2,
        out_shape=[jax.ShapeDtypeStruct((slots, width), BF16)]
        + [jax.ShapeDtypeStruct((edges, width), BF16)] * 3
        + [jax.ShapeDtypeStruct((tiles, 1, STEP), F32)]
        + node_shape
        + [jax.ShapeDtypeStruct((mesh_count, width), BF16), jax.ShapeDtypeStruct((mesh_count, width), F32)],
        scratch_shapes=[
            pltpu.VMEM((slots, width), BF16),
            pltpu.VMEM((mesh_count, width), F32),
            pltpu.VMEM(w_node_in.shape, F32),
            pltpu.VMEM(w_node_out.shape, F32),
            pltpu.VMEM(w_edge_out.shape, BF16),
        ],
        compiler_params=params,
        name="forward",
    )(
        me,
        tile_count,
        src,
        dst,
        local,
        edge_latent,
        *near,
        far_own,
        far_core,
        far_next,
        far_both,
        w_edge_in,
        w_edge_out,
        w_node_in,
        w_node_out,
        mesh_latent,
        mesh_cotangent,
    )

    node_next, node_kept = first_sum(peers, 2, node_send, node_keep)
    slot_shape, slot_spec = halves(w_edge_out.shape[0] // peers + cap)
    edge_shape, edge_spec = halves(w_edge_in.shape[0] // peers)
    results = pl.pallas_call(
        functools.partial(backward_kernel, peers),
        grid=(tiles,),
        in_specs=[smem, smem, index_tile, index_tile, index_tile]
        + [tile_of(width)] * 4
        + [whole((mesh_count, width)), whole((slots, width))]
        + [whole((mesh_count, width))] * 2
        + [weight(1), weight(2), weight(0), whole(square)],
        out_specs=[tile_of(width), whole((mesh_count, width))] + slot_spec + edge_spec + back_specs,
        out_shape=[
            jax.ShapeDtypeStruct((edges, width), BF16),
            jax.ShapeDtypeStruct((mesh_count, width), BF16),
        ]
        + slot_shape
        + edge_shape
        + back_shapes,
        scratch_shapes=[
            pltpu.VMEM((slots + mesh_count, width), F32),
            pltpu.VMEM(w_edge_in.shape, F32),
            pltpu.VMEM(square, F32),
            pltpu.VMEM((slots, width), BF16),
        ],
        compiler_params=params,
        cost_estimate=pl.CostEstimate(
            flops=2 * edges * width * (2 * mesh_count + 4 * width + slots),
            bytes_accessed=10 * edges * width,
            transcendentals=0,
        ),
        name="backward",
    )(
        me,
        tile_count,
        src,
        dst,
        inverse,
        hidden,
        slope,
        norm,
        edge_latent,
        d_aggregate,
        received,
        mesh_latent,
        d_mesh,
        w_edge_in,
        w_edge_in,
        w_edge_in,
        w_edge_out,
    )
    (edge_grad, mesh_grad, slot_send, slot_keep, edge_send, edge_keep), returns = results[:6], results[6:]
    (node_next, node_kept, slot_send, slot_keep, edge_send, edge_keep, returns) = lax.optimization_barrier(
        (node_next, node_kept, slot_send, slot_keep, edge_send, edge_keep, returns)
    )
    slot_next, slot_kept = first_sum(peers, 1, slot_send, slot_keep)
    edge_next, edge_kept = first_sum(peers, 1, edge_send, edge_keep)
    node_pieces = next_sum(peers, 1, node_next, node_kept)
    swapped = send(returns[1], by_xor(peers, 1))
    slot_pieces = next_sum(peers, 2, slot_next, slot_kept)
    node_pieces, edge_next, edge_kept, swapped, across = lax.optimization_barrier(
        (node_pieces, edge_next, edge_kept, swapped, returns[4])
    )
    node_terms = last_terms(peers, node_pieces)
    across = send(across, across_chips(peers))
    to_after = jnp.concatenate([returns[2], swapped[cap : 2 * cap]], axis=0)
    to_before = jnp.concatenate([returns[3], swapped[2 * cap :]], axis=0)
    (slot_pieces, edge_next, edge_kept, across, node_terms, to_after, to_before) = lax.optimization_barrier(
        (slot_pieces, edge_next, edge_kept, across, node_terms, to_after, to_before)
    )
    edge_pieces = next_sum(peers, 2, edge_next, edge_kept)
    slot_terms = last_terms(peers, slot_pieces)
    (slot_terms, edge_pieces, to_after, to_before) = lax.optimization_barrier(
        (slot_terms, edge_pieces, to_after, to_before)
    )
    edge_terms = last_terms(peers, edge_pieces)
    bundles = [send(to_after, by_shift(peers, 2)), send(to_before, by_shift(peers, -2))]
    node_terms, out_terms, bundles = lax.optimization_barrier((node_terms, slot_terms, bundles))
    returned = [returns[0], swapped, *bundles, across]
    node_rows = w_node_in.shape[0] // peers
    out_rows = w_edge_out.shape[0] // peers
    grid_grad = pl.pallas_call(
        functools.partial(scatter_kernel, out_rows),
        grid=(2,),
        in_specs=[smem, whole(rows.shape)]
        + return_specs
        + [whole((out_rows + cap, width))] * upper,
        out_specs=pl.BlockSpec((grid_part, width), lambda step: (step, 0)),
        out_shape=jax.ShapeDtypeStruct((grid_count, width), BF16),
        compiler_params=params,
        name="scatter_lists",
    )(me, rows, *returned, *slot_terms)
    edge_terms, grid_grad = lax.optimization_barrier((edge_terms, grid_grad))
    return (
        grid_grad,
        edge_grad,
        mesh_grad,
        total_of(edge_terms, 0, w_edge_in.shape[0] // peers),
        total_of(out_terms, 0, out_rows),
        total_of(node_terms, 0, node_rows),
        total_of(node_terms, node_rows, node_rows + w_node_out.shape[0] // peers),
    )


def solution(mesh):
    rows = P(("grp", "lon"), None)
    flat = P(("grp", "lon"))
    return jax.shard_map(
        on_device,
        mesh=mesh,
        in_specs=(rows, rows, rows, rows, flat, flat, flat, P(("grp", "lon"), None, None)) + (P(),) * 4,
        out_specs=(rows,) * 7,
        check_vma=False,
    )
```

```python
import functools

import jax
import jax.numpy as jnp
from jax import lax
from jax.experimental import pallas as pl
from jax.experimental.pallas import tpu as pltpu
from jax.sharding import PartitionSpec as P

TILE = 256
STEP = 1024
SUB = 512
LANES = 128
BLOCK = 256
GRID_PARTS = 4
NEAR = 3
BF16 = jnp.bfloat16
F32 = jnp.float32
VMEM_BYTES = 24 * 1024 * 1024
GATHER_BYTES = 56 * 1024 * 1024


def dot(left, right):
    return lax.dot_general(left, right, (((1,), (0,)), ((), ())), preferred_element_type=F32)


def contract_rows(left, right):
    return lax.dot_general(left, right, (((0,), (0,)), ((), ())), preferred_element_type=F32)


def contract_cols(left, right):
    return lax.dot_general(left, right, (((1,), (1,)), ((), ())), preferred_element_type=F32)


def layer_norm(values):
    centered = values - jnp.mean(values, axis=1, keepdims=True)
    inverse = lax.rsqrt(jnp.mean(centered * centered, axis=1, keepdims=True) + 1e-05)
    return (centered * inverse, inverse)


def norm_back(normed, inverse, upstream):
    first = jnp.mean(upstream, axis=1, keepdims=True)
    second = jnp.mean(upstream * normed, axis=1, keepdims=True)
    return inverse * (upstream - first - normed * second)


def silu_and_slope(values):
    sigma = 0.5 + 0.5 * jnp.tanh(0.5 * values)
    hidden = values * sigma
    return (hidden, sigma + hidden * (1.0 - sigma))


def as_column(row):
    count = row.shape[1]
    block = min(count, LANES)
    down = lax.broadcasted_iota(jnp.int32, (block, block), 0)
    along = lax.broadcasted_iota(jnp.int32, (block, block), 1)
    columns = []
    for start in range(0, count, block):
        piece = row[:, start : start + block].astype(F32)
        picked = jnp.where(down == along, piece, 0.0)
        columns.append(jnp.sum(picked, axis=1, keepdims=True))
    return jnp.concatenate(columns, axis=0)


def as_row(column):
    count = column.shape[0]
    block = min(count, LANES)
    down = lax.broadcasted_iota(jnp.int32, (block, block), 0)
    along = lax.broadcasted_iota(jnp.int32, (block, block), 1)
    rows = []
    for start in range(0, count, block):
        picked = jnp.where(down == along, column[start : start + block], 0.0)
        rows.append(jnp.sum(picked, axis=0, keepdims=True))
    return jnp.concatenate(rows, axis=1)


def in_block(indices, first):
    place = indices - first
    return jnp.where((place >= 0) & (place < BLOCK), place, -1).astype(F32).astype(BF16)


def hot_rows(row, width, first=0):
    column = as_column(row).astype(jnp.int32)
    count = row.shape[1]
    one = jnp.ones((), BF16)
    zero = jnp.zeros((), BF16)
    blocks = []
    for start in range(0, width, BLOCK):
        size = min(BLOCK, width - start)
        along = lax.broadcasted_iota(jnp.int32, (count, size), 1).astype(F32).astype(BF16)
        blocks.append(jnp.where(in_block(column, first + start) == along, one, zero))
    return jnp.concatenate(blocks, axis=1)


def hot_columns(row, height):
    count = row.shape[1]
    one = jnp.ones((), BF16)
    zero = jnp.zeros((), BF16)
    blocks = []
    for start in range(0, height, BLOCK):
        size = min(BLOCK, height - start)
        down = lax.broadcasted_iota(jnp.int32, (size, count), 0).astype(F32).astype(BF16)
        blocks.append(jnp.where(in_block(row, start) == down, one, zero))
    return jnp.concatenate(blocks, axis=0)


def live_only(row, first, count):
    place = first + lax.broadcasted_iota(jnp.int32, row.shape, 1)
    return jnp.where(place < count, row, -1)


def near_peers(me, peers):
    after = lax.rem(me + 2, peers)
    before = lax.rem(me + peers - 2, peers)
    across = lax.rem(me + peers - 3 + 6 * (me & 1), peers)
    return (me, me ^ 1, after, after ^ 1, before, before ^ 1, across)


def write_near(refs, cap, lists):
    mine, other, after, before, across = refs
    mine[...] = lists[0]
    other[...] = lists[1]
    after[:cap, :] = lists[2]
    after[cap:, :] = lists[3]
    before[:cap, :] = lists[4]
    before[cap:, :] = lists[5]
    across[...] = lists[6]


def read_near(refs, cap):
    mine, other, from_before, from_after, across, core_before, core_after = refs
    return [
        mine[...],
        other[...],
        from_after[:cap, :],
        core_after[cap:, :],
        from_before[:cap, :],
        core_before[cap:, :],
        across[...],
    ]


def write_back(refs, cap, lists):
    mine, swapped, after, before, across = refs
    mine[...] = lists[0]
    for place, index in enumerate((1, 3, 5)):
        swapped[place * cap : (place + 1) * cap, :] = lists[index]
    after[...] = lists[2]
    before[...] = lists[4]
    across[...] = lists[6]


def read_back(refs, cap):
    mine, swapped, from_before, from_after, across = refs
    return [
        mine[...],
        swapped[:cap, :],
        from_after[:cap, :],
        from_after[cap:, :],
        from_before[:cap, :],
        from_before[cap:, :],
        across[...],
    ]


def list_hots(me, rows_ref, grid_count, first):
    peers, cap = rows_ref.shape
    pieces = []
    for target in near_peers(me, peers):
        pieces.append(hot_rows(rows_ref[pl.ds(target, 1), :], grid_count, first))
    peer = lax.broadcasted_iota(jnp.int32, (peers, cap), 0)
    ahead = lax.rem(peer - me + peers, peers)
    apart = jnp.minimum(ahead, peers - ahead)
    far = jnp.max(jnp.where(apart > NEAR, rows_ref[...].astype(F32), -1.0), axis=0, keepdims=True)
    pieces.append(hot_rows(far.astype(jnp.int32), grid_count, first))
    return jnp.concatenate(pieces, axis=0)


def gather_kernel(me_ref, rows_hbm, grid_hbm, *refs):
    near_refs, far_ref = refs[:5], refs[5]
    rows_ref, grid_ref, rows_done, grid_done = refs[6:]
    cap = rows_ref.shape[1]
    part = grid_ref.shape[0] // GRID_PARTS
    copies = [
        pltpu.make_async_copy(
            grid_hbm.at[pl.ds(at * part, part)], grid_ref.at[pl.ds(at * part, part)], grid_done.at[at]
        )
        for at in range(GRID_PARTS)
    ]
    rows_copy = pltpu.make_async_copy(rows_hbm, rows_ref, rows_done)
    rows_copy.start()
    for copy in copies:
        copy.start()
    rows_copy.wait()
    found = None
    for at, copy in enumerate(copies):
        hots = list_hots(me_ref[0], rows_ref, part, at * part)
        copy.wait()
        piece = dot(hots, grid_ref[at * part : (at + 1) * part, :])
        found = piece if found is None else found + piece
    rows = found.astype(BF16)
    lists = [rows[at : at + cap] for at in range(0, 8 * cap, cap)]
    write_near(near_refs, cap, lists)
    far_ref[...] = lists[7]


def scatter_kernel(skip, me_ref, rows_ref, *refs):
    near_refs, far_refs, out_ref = refs[:5], refs[5:-1], refs[-1]
    part = out_ref.shape[0]
    cap = rows_ref.shape[1]
    hots = list_hots(me_ref[0], rows_ref, part, pl.program_id(0) * part)
    far = far_refs[0][skip:, :].astype(F32)
    for ref in far_refs[1:]:
        far = far + ref[skip:, :].astype(F32)
    values = jnp.concatenate(read_back(near_refs, cap) + [far.astype(BF16)], axis=0)
    out_ref[...] = contract_rows(hots, values).astype(BF16)


def halves_of(ref):
    rows = ref.shape[-1] if len(ref.shape) == 3 else ref.shape[0]
    return [(start, slice(start, start + SUB)) for start in range(0, rows, SUB)]


def local_kernel(dst_ref, edge_ref, mesh_ref, w_edge_ref, w_receiver_ref, out_ref, weights):
    width = edge_ref.shape[1]

    @pl.when(pl.program_id(0) == 0)
    def _():
        weights[:width, :] = w_edge_ref[...]
        weights[width:, :] = dot(mesh_ref[...], w_receiver_ref[...]).astype(BF16)

    for start, part in halves_of(edge_ref):
        onehot = hot_rows(dst_ref[0, :, part], mesh_ref.shape[0])
        joined = jnp.concatenate([edge_ref[part, :], onehot], axis=1)
        out_ref[part, :] = dot(joined, weights[...]).astype(BF16)


def split_out(me, peers, first, send_ref, keep_ref, parts):
    for low in range(4):
        target = send_ref if low & first else keep_ref
        half = 1 if low & (3 - first) else 0
        at = 0
        for upper in range(peers // 4):
            owner = me ^ (4 * upper + low)
            for ref, share, far in parts:
                piece = ref[pl.ds(pl.multiple_of(owner * share, 16), share), :]
                if far:
                    ahead = lax.rem(owner - me + peers, peers)
                    apart = jnp.minimum(ahead, peers - ahead)
                    piece = jnp.where(apart > NEAR, piece.astype(F32), 0.0)
                target[half, at : at + share, :] = piece.astype(BF16)
                at += share


def forward_kernel(
    peers, me_ref, count_ref, src_ref, dst_ref, local_ref, edge_ref, *refs
):
    near_refs, far_refs = refs[:7], refs[7:11]
    (w_sender_ref, w_out_ref, w_node_in_ref, w_node_out_ref, mesh_ref, cotangent_ref) = refs[11:17]
    (received_ref, hidden_ref, slope_ref, norm_ref, inverse_ref) = refs[17:22]
    (send_ref, keep_ref, d_aggregate_ref, d_mesh_ref) = refs[22:26]
    (slot_proj, aggregate, grad_in, grad_out, w_centred) = refs[26:]
    step = pl.program_id(0)
    me = me_ref[0]
    cap = near_refs[0].shape[0]
    width = edge_ref.shape[1]

    @pl.when(step == 0)
    def _():
        aggregate[...] = jnp.zeros_like(aggregate)
        w_out = w_out_ref[...].astype(F32)
        w_centred[...] = (w_out - jnp.mean(w_out, axis=1, keepdims=True)).astype(BF16)
        w_sender = w_sender_ref[...]

        def place(owner, rows, projected):
            offset = pl.multiple_of(owner * cap, 16)
            received_ref[pl.ds(offset, cap), :] = rows
            slot_proj[pl.ds(offset, cap), :] = projected

        for low, ref in enumerate(far_refs):
            rows = ref[...]
            projected = dot(rows, w_sender).astype(BF16)
            for upper in range(peers // 4):
                span = slice(upper * cap, (upper + 1) * cap)
                place(me ^ (4 * upper + low), rows[span], projected[span])
        rows = jnp.concatenate(read_near(near_refs, cap), axis=0)
        projected = dot(rows, w_sender).astype(BF16)
        for spot, owner in enumerate(near_peers(me, peers)):
            place(owner, rows[spot * cap : (spot + 1) * cap], projected[spot * cap : (spot + 1) * cap])

    @pl.when(step * STEP < count_ref[0] * TILE)
    def _():
        parts = halves_of(edge_ref)
        pres = []
        for start, part in parts:
            onehot = hot_rows(src_ref[0, :, part], slot_proj.shape[0])
            pres.append(local_ref[part, :].astype(F32) + dot(onehot, slot_proj[...]))
        projs = []
        for (start, part), pre in zip(parts, pres):
            hidden, slope = silu_and_slope(pre)
            hidden = hidden.astype(BF16)
            hidden_ref[part, :] = hidden
            slope_ref[part, :] = slope.astype(BF16)
            projs.append(dot(hidden, w_centred[...]))
        for (start, part), proj in zip(parts, projs):
            inverse = lax.rsqrt(jnp.mean(proj * proj, axis=1, keepdims=True) + 1e-05)
            normed = proj * inverse
            norm_ref[part, :] = normed.astype(BF16)
            inverse_ref[0, :, part] = as_row(inverse)
            edge_new = (edge_ref[part, :].astype(F32) + normed).astype(BF16)
            receivers = live_only(dst_ref[0, :, part], step * STEP + start, count_ref[0] * TILE)
            aggregate[...] += dot(hot_columns(receivers, aggregate.shape[0]), edge_new)

    @pl.when(step == pl.num_programs(0) - 1)
    def _():
        mesh = mesh_ref[...]
        summed = aggregate[...].astype(BF16)
        node_pre = dot(mesh, w_node_in_ref[:width, :]) + dot(summed, w_node_in_ref[width:, :])
        hidden, slope = silu_and_slope(node_pre)
        hidden = hidden.astype(BF16)
        normed, inverse = layer_norm(dot(hidden, w_node_out_ref[...]))
        upstream = cotangent_ref[...].astype(F32)
        d_proj = norm_back(normed, inverse, upstream).astype(BF16)
        d_pre = (contract_cols(d_proj, w_node_out_ref[...]) * slope).astype(BF16)
        d_mesh_ref[...] = upstream + contract_cols(d_pre, w_node_in_ref[:width, :])
        d_aggregate_ref[...] = contract_cols(d_pre, w_node_in_ref[width:, :]).astype(BF16)
        grad_out[...] = contract_rows(hidden, d_proj)
        grad_in[:width, :] = contract_rows(mesh, d_pre)
        grad_in[width:, :] = contract_rows(summed, d_pre)
        split_out(
            me,
            peers,
            2,
            send_ref,
            keep_ref,
            ((grad_in, grad_in.shape[0] // peers, False), (grad_out, grad_out.shape[0] // peers, False)),
        )


def backward_kernel(peers, me_ref, count_ref, src_ref, dst_ref, inverse_ref, *refs):
    (hidden_ref, slope_ref, norm_ref, edge_ref) = refs[:4]
    (d_aggregate_ref, received_ref, mesh_ref, d_mesh_ref) = refs[4:8]
    (w_sender_ref, w_receiver_ref, w_edge_ref, w_out_ref) = refs[8:12]
    (edge_grad_ref, mesh_grad_ref, slot_send_ref, slot_keep_ref, edge_send_ref, edge_keep_ref) = refs[12:18]
    near_refs = refs[18:23]
    (end_sum, grad_in, grad_out, d_slots) = refs[23:]
    step = pl.program_id(0)
    me = me_ref[0]
    slots, width = received_ref.shape
    mesh_count = mesh_ref.shape[0]

    @pl.when(step == 0)
    def _():
        end_sum[...] = jnp.zeros_like(end_sum)
        grad_in[:width, :] = jnp.zeros((width, width), F32)
        grad_out[...] = jnp.zeros_like(grad_out)

    @pl.when(step * STEP < count_ref[0] * TILE)
    def _():
        parts = halves_of(hidden_ref)
        upstreams = []
        columns = []
        for start, part in parts:
            first = step * STEP + start
            live = count_ref[0] * TILE
            receivers = live_only(dst_ref[0, :, part], first, live)
            upstreams.append(dot(hot_rows(receivers, mesh_count), d_aggregate_ref[...]))
            senders = live_only(src_ref[0, :, part], first, live)
            columns.append(
                jnp.concatenate([hot_columns(senders, slots), hot_columns(receivers, mesh_count)], axis=0)
            )
        d_projs = []
        d_hiddens = []
        for (start, part), upstream in zip(parts, upstreams):
            inverse = as_column(inverse_ref[0, :, part])
            d_proj = norm_back(norm_ref[part, :].astype(F32), inverse, upstream).astype(BF16)
            d_projs.append(d_proj)
            d_hiddens.append(contract_cols(d_proj, w_out_ref[...]))
        for (start, part), d_proj, d_hidden, column, upstream in zip(
            parts, d_projs, d_hiddens, columns, upstreams
        ):
            grad_out[...] += contract_rows(hidden_ref[part, :], d_proj)
            d_pre = (d_hidden * slope_ref[part, :].astype(F32)).astype(BF16)
            edge_grad_ref[part, :] = (upstream + contract_cols(d_pre, w_edge_ref[...])).astype(BF16)
            end_sum[...] += dot(column, d_pre)
            grad_in[:width, :] += contract_rows(edge_ref[part, :], d_pre)

    @pl.when(step * STEP >= count_ref[0] * TILE)
    def _():
        edge_grad_ref[...] = jnp.zeros_like(edge_grad_ref)

    @pl.when(step == pl.num_programs(0) - 1)
    def _():
        summed = end_sum[:slots, :].astype(BF16)
        mesh_summed = end_sum[slots:, :].astype(BF16)
        d_slots[...] = contract_cols(summed, w_sender_ref[...]).astype(BF16)
        grad_in[width : 2 * width, :] = contract_rows(received_ref[...], summed)
        grad_in[2 * width :, :] = contract_rows(mesh_ref[...], mesh_summed)
        mesh_grad_ref[...] = (d_mesh_ref[...] + contract_cols(mesh_summed, w_receiver_ref[...])).astype(BF16)
        cap = near_refs[0].shape[0]
        owners = near_peers(me, peers)
        write_back(
            near_refs, cap, [d_slots[pl.ds(pl.multiple_of(owner * cap, 16), cap), :] for owner in owners]
        )
        out_share = grad_out.shape[0] // peers
        split_out(
            me, peers, 1, slot_send_ref, slot_keep_ref, ((grad_out, out_share, False), (d_slots, cap, True))
        )
        split_out(
            me, peers, 1, edge_send_ref, edge_keep_ref, ((grad_in, grad_in.shape[0] // peers, False),)
        )


def send(values, perm):
    return lax.ppermute(values, "lon", perm)


def by_xor(peers, bits):
    return [(peer, peer ^ bits) for peer in range(peers)]


def by_shift(peers, shift):
    return [(peer, (peer + shift) % peers) for peer in range(peers)]


def across_chips(peers):
    return [(peer, (peer + (3 if peer % 2 else -3)) % peers) for peer in range(peers)]


def exchange_near(peers, lists):
    mine, other, after, before = lists
    return [mine, other, send(after, by_shift(peers, 2)), send(before, by_shift(peers, -2))]


def core_near(peers, near):
    mine, other, after, before, across = near
    swap = by_xor(peers, 1)
    return [mine, send(other, swap), after, before, across, send(after, swap), send(before, swap)]


def add(left, right):
    return (left.astype(F32) + right.astype(F32)).astype(BF16)


def first_sum(peers, bit, outgoing, kept):
    arrived = send(outgoing, by_xor(peers, bit))
    return add(kept[1], arrived[1]), add(kept[0], arrived[0])


def next_sum(peers, bit, outgoing, kept):
    return add(kept, send(outgoing, by_xor(peers, bit)))


def last_terms(peers, pieces):
    count = peers // 4
    share = pieces.shape[0] // count
    terms = [pieces[:share]]
    for place in range(1, count):
        piece = pieces[place * share : (place + 1) * share]
        terms.append(send(piece, by_xor(peers, 4 * place)))
    return terms


def halve_sum(peers, pieces):
    count = peers // 4
    blocks = pieces.reshape(count // 2, 2, -1, pieces.shape[1])
    kept, outgoing = [blocks[:, place].reshape(-1, pieces.shape[1]) for place in range(2)]
    return add(kept, send(outgoing, by_xor(peers, 4)))


def rest_terms(peers, pieces):
    count = peers // 8
    share = pieces.shape[0] // count
    terms = [pieces[:share]]
    for place in range(1, count):
        piece = pieces[place * share : (place + 1) * share]
        terms.append(send(piece, by_xor(peers, 8 * place)))
    return terms


def total_of(terms, start, stop):
    total = terms[0][start:stop].astype(F32)
    for term in terms[1:]:
        total = total + term[start:stop].astype(F32)
    return total


def whole(shape):
    return pl.BlockSpec(shape, lambda *_: (0,) * len(shape))


def on_device(
    grid_latent,
    mesh_latent,
    edge_latent,
    mesh_cotangent,
    edge_src,
    edge_dst,
    tile_count,
    send_rows,
    w_edge_in,
    w_edge_out,
    w_node_in,
    w_node_out,
):
    peers = lax.axis_size("lon")
    me = lax.axis_index("lon").astype(jnp.int32).reshape(1)
    upper = peers // 4
    rows = send_rows[0]
    cap = rows.shape[1]
    slots = peers * cap
    edges, width = edge_latent.shape
    mesh_count = mesh_latent.shape[0]
    grid_count = grid_latent.shape[0]
    tiles = edges // STEP
    src = edge_src.reshape(tiles, 1, STEP)
    dst = edge_dst.reshape(tiles, 1, STEP)
    smem = pl.BlockSpec(memory_space=pltpu.SMEM)
    hbm = pl.BlockSpec(memory_space=pltpu.HBM)
    params = pltpu.CompilerParams(vmem_limit_bytes=VMEM_BYTES)
    square = (width, width)

    def tile_of(last):
        return pl.BlockSpec((STEP, last), lambda step, *_: (step, 0))

    index_tile = pl.BlockSpec((1, 1, STEP), lambda step, *_: (step, 0, 0))

    def weight(place):
        return pl.BlockSpec(square, lambda *_: (place, 0))

    def halves(share):
        shape = (2, upper * share, width)
        return [jax.ShapeDtypeStruct(shape, BF16)] * 2, [whole(shape)] * 2

    grid_part = grid_count // 2
    near_rows = (cap, cap, 2 * cap, 2 * cap, cap)
    near_specs = [whole((count, width)) for count in near_rows]
    near_shapes = [jax.ShapeDtypeStruct((count, width), BF16) for count in near_rows]
    core_specs = near_specs + [whole((2 * cap, width))] * 2
    back_rows = (cap, 3 * cap, cap, cap, cap)
    back_specs = [whole((count, width)) for count in back_rows]
    back_shapes = [jax.ShapeDtypeStruct((count, width), BF16) for count in back_rows]
    return_specs = [whole((count, width)) for count in (cap, 3 * cap, 2 * cap, 2 * cap, cap)]
    lists = pl.pallas_call(
        gather_kernel,
        in_specs=[smem, hbm, hbm],
        out_specs=near_specs + [whole((cap, width))],
        out_shape=near_shapes + [jax.ShapeDtypeStruct((cap, width), BF16)],
        scratch_shapes=[
            pltpu.VMEM(rows.shape, jnp.int32),
            pltpu.VMEM(grid_latent.shape, BF16),
            pltpu.SemaphoreType.DMA,
            pltpu.SemaphoreType.DMA((GRID_PARTS,)),
        ],
        compiler_params=pltpu.CompilerParams(vmem_limit_bytes=GATHER_BYTES),
        cost_estimate=pl.CostEstimate(
            flops=40 * 16 * cap * grid_count * width,
            bytes_accessed=2 * grid_count * width,
            transcendentals=0,
        ),
        name="gather_lists",
    )(me, rows, grid_latent)

    hops = [send(lists[5], by_xor(peers, 4 * place)) for place in range(1, upper)]
    near = exchange_near(peers, lists[:4])
    hops[0], across = lax.optimization_barrier((hops[0], lists[4]))
    near.append(send(across, across_chips(peers)))
    far_own = jnp.concatenate([lists[5]] + hops, axis=0)
    far_own, receivers = lax.optimization_barrier((far_own, dst))
    far_next = send(far_own, by_xor(peers, 2))
    far_core = send(far_own, by_xor(peers, 1))
    local = pl.pallas_call(
        local_kernel,
        grid=(tiles,),
        in_specs=[index_tile, tile_of(width), whole(mesh_latent.shape), weight(0), weight(2)],
        out_specs=tile_of(width),
        out_shape=jax.ShapeDtypeStruct((edges, width), BF16),
        scratch_shapes=[pltpu.VMEM((width + mesh_count, width), BF16)],
        compiler_params=params,
        cost_estimate=pl.CostEstimate(
            flops=2 * edges * width * (width + mesh_count),
            bytes_accessed=4 * edges * width,
            transcendentals=0,
        ),
        name="edge_local",
    )(receivers, edge_latent, mesh_latent, w_edge_in, w_edge_in)
    far_next, far_core, near, local = lax.optimization_barrier((far_next, far_core, near, local))
    near = core_near(peers, near)
    far_both = send(far_next, by_xor(peers, 1))

    node_shape, node_spec = halves(w_node_in.shape[0] // peers + w_node_out.shape[0] // peers)
    (received, hidden, slope, norm, inverse, node_send, node_keep, d_aggregate, d_mesh) = pl.pallas_call(
        functools.partial(forward_kernel, peers),
        grid=(tiles,),
        in_specs=[smem, smem, index_tile, index_tile, tile_of(width), tile_of(width)]
        + core_specs
        + [whole((upper * cap, width))] * 4
        + [weight(1)]
        + [whole(w.shape) for w in (w_edge_out, w_node_in, w_node_out, mesh_latent, mesh_cotangent)],
        out_specs=[whole((slots, width))]
        + [tile_of(width)] * 3
        + [index_tile]
        + node_spec
        + [whole((mesh_count, width))] * 2,
        out_shape=[jax.ShapeDtypeStruct((slots, width), BF16)]
        + [jax.ShapeDtypeStruct((edges, width), BF16)] * 3
        + [jax.ShapeDtypeStruct((tiles, 1, STEP), F32)]
        + node_shape
        + [jax.ShapeDtypeStruct((mesh_count, width), BF16), jax.ShapeDtypeStruct((mesh_count, width), F32)],
        scratch_shapes=[
            pltpu.VMEM((slots, width), BF16),
            pltpu.VMEM((mesh_count, width), F32),
            pltpu.VMEM(w_node_in.shape, F32),
            pltpu.VMEM(w_node_out.shape, F32),
            pltpu.VMEM(w_edge_out.shape, BF16),
        ],
        compiler_params=params,
        name="forward",
    )(
        me,
        tile_count,
        src,
        dst,
        local,
        edge_latent,
        *near,
        far_own,
        far_core,
        far_next,
        far_both,
        w_edge_in,
        w_edge_out,
        w_node_in,
        w_node_out,
        mesh_latent,
        mesh_cotangent,
    )

    node_next, node_kept = first_sum(peers, 2, node_send, node_keep)
    slot_shape, slot_spec = halves(w_edge_out.shape[0] // peers + cap)
    edge_shape, edge_spec = halves(w_edge_in.shape[0] // peers)
    results = pl.pallas_call(
        functools.partial(backward_kernel, peers),
        grid=(tiles,),
        in_specs=[smem, smem, index_tile, index_tile, index_tile]
        + [tile_of(width)] * 4
        + [whole((mesh_count, width)), whole((slots, width))]
        + [whole((mesh_count, width))] * 2
        + [weight(1), weight(2), weight(0), whole(square)],
        out_specs=[tile_of(width), whole((mesh_count, width))] + slot_spec + edge_spec + back_specs,
        out_shape=[
            jax.ShapeDtypeStruct((edges, width), BF16),
            jax.ShapeDtypeStruct((mesh_count, width), BF16),
        ]
        + slot_shape
        + edge_shape
        + back_shapes,
        scratch_shapes=[
            pltpu.VMEM((slots + mesh_count, width), F32),
            pltpu.VMEM(w_edge_in.shape, F32),
            pltpu.VMEM(square, F32),
            pltpu.VMEM((slots, width), BF16),
        ],
        compiler_params=params,
        cost_estimate=pl.CostEstimate(
            flops=2 * edges * width * (2 * mesh_count + 4 * width + slots),
            bytes_accessed=10 * edges * width,
            transcendentals=0,
        ),
        name="backward",
    )(
        me,
        tile_count,
        src,
        dst,
        inverse,
        hidden,
        slope,
        norm,
        edge_latent,
        d_aggregate,
        received,
        mesh_latent,
        d_mesh,
        w_edge_in,
        w_edge_in,
        w_edge_in,
        w_edge_out,
    )
    (edge_grad, mesh_grad, slot_send, slot_keep, edge_send, edge_keep), returns = results[:6], results[6:]
    (node_next, node_kept, slot_send, slot_keep, edge_send, edge_keep, returns) = lax.optimization_barrier(
        (node_next, node_kept, slot_send, slot_keep, edge_send, edge_keep, returns)
    )
    slot_next, slot_kept = first_sum(peers, 1, slot_send, slot_keep)
    edge_next, edge_kept = first_sum(peers, 1, edge_send, edge_keep)
    node_pieces = next_sum(peers, 1, node_next, node_kept)
    swapped = send(returns[1], by_xor(peers, 1))
    slot_pieces = next_sum(peers, 2, slot_next, slot_kept)
    node_pieces, edge_next, edge_kept, swapped, across = lax.optimization_barrier(
        (node_pieces, edge_next, edge_kept, swapped, returns[4])
    )
    node_pieces = halve_sum(peers, node_pieces)
    across = send(across, across_chips(peers))
    to_after = jnp.concatenate([returns[2], swapped[cap : 2 * cap]], axis=0)
    to_before = jnp.concatenate([returns[3], swapped[2 * cap :]], axis=0)
    (slot_pieces, edge_next, edge_kept, across, node_pieces, to_after, to_before) = lax.optimization_barrier(
        (slot_pieces, edge_next, edge_kept, across, node_pieces, to_after, to_before)
    )
    edge_pieces = next_sum(peers, 2, edge_next, edge_kept)
    slot_terms = last_terms(peers, slot_pieces)
    node_terms = rest_terms(peers, node_pieces)
    (slot_terms, node_terms, edge_pieces, to_after, to_before) = lax.optimization_barrier(
        (slot_terms, node_terms, edge_pieces, to_after, to_before)
    )
    edge_terms = last_terms(peers, edge_pieces)
    bundles = [send(to_after, by_shift(peers, 2)), send(to_before, by_shift(peers, -2))]
    returned = [returns[0], swapped, *bundles, across]
    node_rows = w_node_in.shape[0] // peers
    out_rows = w_edge_out.shape[0] // peers
    grid_grad = pl.pallas_call(
        functools.partial(scatter_kernel, out_rows),
        grid=(2,),
        in_specs=[smem, whole(rows.shape)]
        + return_specs
        + [whole((out_rows + cap, width))] * upper,
        out_specs=pl.BlockSpec((grid_part, width), lambda step: (step, 0)),
        out_shape=jax.ShapeDtypeStruct((grid_count, width), BF16),
        compiler_params=params,
        name="scatter_lists",
    )(me, rows, *returned, *slot_terms)
    node_terms, out_terms, grid_grad = lax.optimization_barrier((node_terms, slot_terms, grid_grad))
    edge_terms, grid_grad = lax.optimization_barrier((edge_terms, grid_grad))
    return (
        grid_grad,
        edge_grad,
        mesh_grad,
        total_of(edge_terms, 0, w_edge_in.shape[0] // peers),
        total_of(out_terms, 0, out_rows),
        total_of(node_terms, 0, node_rows),
        total_of(node_terms, node_rows, node_rows + w_node_out.shape[0] // peers),
    )


def solution(mesh):
    rows = P(("grp", "lon"), None)
    flat = P(("grp", "lon"))
    return jax.shard_map(
        on_device,
        mesh=mesh,
        in_specs=(rows, rows, rows, rows, flat, flat, flat, P(("grp", "lon"), None, None)) + (P(),) * 4,
        out_specs=(rows,) * 7,
        check_vma=False,
    )
```

```python
import functools

import jax
import jax.numpy as jnp
from jax import lax
from jax.experimental import pallas as pl
from jax.experimental.pallas import tpu as pltpu
from jax.sharding import PartitionSpec as P

TILE = 256
STEP = 1024
SUB = 512
LANES = 128
BLOCK = 256
GRID_PARTS = 4
NEAR = 3
BF16 = jnp.bfloat16
F32 = jnp.float32
VMEM_BYTES = 24 * 1024 * 1024
GATHER_BYTES = 56 * 1024 * 1024


def dot(left, right):
    return lax.dot_general(left, right, (((1,), (0,)), ((), ())), preferred_element_type=F32)


def contract_rows(left, right):
    return lax.dot_general(left, right, (((0,), (0,)), ((), ())), preferred_element_type=F32)


def contract_cols(left, right):
    return lax.dot_general(left, right, (((1,), (1,)), ((), ())), preferred_element_type=F32)


def layer_norm(values):
    centered = values - jnp.mean(values, axis=1, keepdims=True)
    inverse = lax.rsqrt(jnp.mean(centered * centered, axis=1, keepdims=True) + 1e-05)
    return (centered * inverse, inverse)


def norm_back(normed, inverse, upstream):
    first = jnp.mean(upstream, axis=1, keepdims=True)
    second = jnp.mean(upstream * normed, axis=1, keepdims=True)
    return inverse * (upstream - first - normed * second)


def silu_and_slope(values):
    sigma = 0.5 + 0.5 * jnp.tanh(0.5 * values)
    hidden = values * sigma
    return (hidden, sigma + hidden * (1.0 - sigma))


def as_column(row):
    count = row.shape[1]
    block = min(count, LANES)
    down = lax.broadcasted_iota(jnp.int32, (block, block), 0)
    along = lax.broadcasted_iota(jnp.int32, (block, block), 1)
    columns = []
    for start in range(0, count, block):
        piece = row[:, start : start + block].astype(F32)
        picked = jnp.where(down == along, piece, 0.0)
        columns.append(jnp.sum(picked, axis=1, keepdims=True))
    return jnp.concatenate(columns, axis=0)


def as_row(column):
    count = column.shape[0]
    block = min(count, LANES)
    down = lax.broadcasted_iota(jnp.int32, (block, block), 0)
    along = lax.broadcasted_iota(jnp.int32, (block, block), 1)
    rows = []
    for start in range(0, count, block):
        picked = jnp.where(down == along, column[start : start + block], 0.0)
        rows.append(jnp.sum(picked, axis=0, keepdims=True))
    return jnp.concatenate(rows, axis=1)


def in_block(indices, first):
    place = indices - first
    return jnp.where((place >= 0) & (place < BLOCK), place, -1).astype(F32).astype(BF16)


def hot_rows(row, width, first=0):
    column = as_column(row).astype(jnp.int32)
    count = row.shape[1]
    one = jnp.ones((), BF16)
    zero = jnp.zeros((), BF16)
    blocks = []
    for start in range(0, width, BLOCK):
        size = min(BLOCK, width - start)
        along = lax.broadcasted_iota(jnp.int32, (count, size), 1).astype(F32).astype(BF16)
        blocks.append(jnp.where(in_block(column, first + start) == along, one, zero))
    return jnp.concatenate(blocks, axis=1)


def hot_columns(row, height):
    count = row.shape[1]
    one = jnp.ones((), BF16)
    zero = jnp.zeros((), BF16)
    blocks = []
    for start in range(0, height, BLOCK):
        size = min(BLOCK, height - start)
        down = lax.broadcasted_iota(jnp.int32, (size, count), 0).astype(F32).astype(BF16)
        blocks.append(jnp.where(in_block(row, start) == down, one, zero))
    return jnp.concatenate(blocks, axis=0)


def live_only(row, first, count):
    place = first + lax.broadcasted_iota(jnp.int32, row.shape, 1)
    return jnp.where(place < count, row, -1)


def near_peers(me, peers):
    after = lax.rem(me + 2, peers)
    before = lax.rem(me + peers - 2, peers)
    across = lax.rem(me + peers - 3 + 6 * (me & 1), peers)
    return (me, me ^ 1, after, after ^ 1, before, before ^ 1, across)


def write_near(refs, cap, lists):
    mine, other, after, before, across = refs
    mine[...] = lists[0]
    other[...] = lists[1]
    after[:cap, :] = lists[2]
    after[cap:, :] = lists[3]
    before[:cap, :] = lists[4]
    before[cap:, :] = lists[5]
    across[...] = lists[6]


def read_near(refs, cap):
    mine, other, from_before, from_after, across, core_before, core_after = refs
    return [
        mine[...],
        other[...],
        from_after[:cap, :],
        core_after[cap:, :],
        from_before[:cap, :],
        core_before[cap:, :],
        across[...],
    ]


def write_back(refs, cap, lists):
    mine, swapped, after, before, across = refs
    mine[...] = lists[0]
    for place, index in enumerate((1, 3, 5)):
        swapped[place * cap : (place + 1) * cap, :] = lists[index]
    after[...] = lists[2]
    before[...] = lists[4]
    across[...] = lists[6]


def read_back(refs, cap):
    mine, swapped, from_before, from_after, across = refs
    return [
        mine[...],
        swapped[:cap, :],
        from_after[:cap, :],
        from_after[cap:, :],
        from_before[:cap, :],
        from_before[cap:, :],
        across[...],
    ]


def list_hots(me, rows_ref, grid_count, first):
    peers, cap = rows_ref.shape
    pieces = []
    for target in near_peers(me, peers):
        pieces.append(hot_rows(rows_ref[pl.ds(target, 1), :], grid_count, first))
    peer = lax.broadcasted_iota(jnp.int32, (peers, cap), 0)
    ahead = lax.rem(peer - me + peers, peers)
    apart = jnp.minimum(ahead, peers - ahead)
    far = jnp.max(jnp.where(apart > NEAR, rows_ref[...].astype(F32), -1.0), axis=0, keepdims=True)
    pieces.append(hot_rows(far.astype(jnp.int32), grid_count, first))
    return jnp.concatenate(pieces, axis=0)


def gather_kernel(me_ref, rows_hbm, grid_hbm, *refs):
    near_refs, far_ref = refs[:5], refs[5]
    rows_ref, grid_ref, rows_done, grid_done = refs[6:]
    cap = rows_ref.shape[1]
    part = grid_ref.shape[0] // GRID_PARTS
    copies = [
        pltpu.make_async_copy(
            grid_hbm.at[pl.ds(at * part, part)], grid_ref.at[pl.ds(at * part, part)], grid_done.at[at]
        )
        for at in range(GRID_PARTS)
    ]
    rows_copy = pltpu.make_async_copy(rows_hbm, rows_ref, rows_done)
    rows_copy.start()
    for copy in copies:
        copy.start()
    rows_copy.wait()
    found = None
    for at, copy in enumerate(copies):
        hots = list_hots(me_ref[0], rows_ref, part, at * part)
        copy.wait()
        piece = dot(hots, grid_ref[at * part : (at + 1) * part, :])
        found = piece if found is None else found + piece
    rows = found.astype(BF16)
    lists = [rows[at : at + cap] for at in range(0, 8 * cap, cap)]
    write_near(near_refs, cap, lists)
    far_ref[...] = lists[7]


def scatter_kernel(skip, slot_count, me_ref, rows_ref, *refs):
    near_refs, refs = refs[:5], refs[5:]
    out_ref, grad_out_ref, node_in_ref, node_out_ref = refs[-4:]
    terms = refs[:-4]
    part = out_ref.shape[0]
    cap = rows_ref.shape[1]
    far_refs, node_refs = terms[:slot_count], terms[slot_count:]
    node_rows = node_in_ref.shape[0]

    def total(term_refs, start, stop):
        result = term_refs[0][start:stop, :].astype(F32)
        for ref in term_refs[1:]:
            result = result + ref[start:stop, :].astype(F32)
        return result

    hots = list_hots(me_ref[0], rows_ref, part, pl.program_id(0) * part)
    far = total(far_refs, skip, skip + cap)
    values = jnp.concatenate(read_back(near_refs, cap) + [far.astype(BF16)], axis=0)
    out_ref[...] = contract_rows(hots, values).astype(BF16)

    @pl.when(pl.program_id(0) == 0)
    def _():
        grad_out_ref[...] = total(far_refs, 0, skip)
        node_in_ref[...] = total(node_refs, 0, node_rows)
        node_out_ref[...] = total(node_refs, node_rows, node_rows + node_out_ref.shape[0])


def halves_of(ref):
    rows = ref.shape[-1] if len(ref.shape) == 3 else ref.shape[0]
    return [(start, slice(start, start + SUB)) for start in range(0, rows, SUB)]


def local_kernel(dst_ref, edge_ref, mesh_ref, w_edge_ref, w_receiver_ref, out_ref, weights):
    width = edge_ref.shape[1]

    @pl.when(pl.program_id(0) == 0)
    def _():
        weights[:width, :] = w_edge_ref[...]
        weights[width:, :] = dot(mesh_ref[...], w_receiver_ref[...]).astype(BF16)

    for start, part in halves_of(edge_ref):
        onehot = hot_rows(dst_ref[0, :, part], mesh_ref.shape[0])
        joined = jnp.concatenate([edge_ref[part, :], onehot], axis=1)
        out_ref[part, :] = dot(joined, weights[...]).astype(BF16)


def split_out(me, peers, first, send_ref, keep_ref, parts):
    for low in range(4):
        target = send_ref if low & first else keep_ref
        half = 1 if low & (3 - first) else 0
        at = 0
        for upper in range(peers // 4):
            owner = me ^ (4 * upper + low)
            for ref, share, far in parts:
                piece = ref[pl.ds(pl.multiple_of(owner * share, 16), share), :]
                if far:
                    ahead = lax.rem(owner - me + peers, peers)
                    apart = jnp.minimum(ahead, peers - ahead)
                    piece = jnp.where(apart > NEAR, piece.astype(F32), 0.0)
                target[half, at : at + share, :] = piece.astype(BF16)
                at += share


def forward_kernel(
    peers, me_ref, count_ref, src_ref, dst_ref, local_ref, edge_ref, *refs
):
    near_refs, far_refs = refs[:7], refs[7:11]
    (w_sender_ref, w_out_ref, w_node_in_ref, w_node_out_ref, mesh_ref, cotangent_ref) = refs[11:17]
    (received_ref, hidden_ref, slope_ref, norm_ref, inverse_ref) = refs[17:22]
    (send_ref, keep_ref, d_aggregate_ref, d_mesh_ref) = refs[22:26]
    (slot_proj, aggregate, grad_in, grad_out, w_centred) = refs[26:]
    step = pl.program_id(0)
    me = me_ref[0]
    cap = near_refs[0].shape[0]
    width = edge_ref.shape[1]

    @pl.when(step == 0)
    def _():
        aggregate[...] = jnp.zeros_like(aggregate)
        w_out = w_out_ref[...].astype(F32)
        w_centred[...] = (w_out - jnp.mean(w_out, axis=1, keepdims=True)).astype(BF16)
        w_sender = w_sender_ref[...]

        def place(owner, rows, projected):
            offset = pl.multiple_of(owner * cap, 16)
            received_ref[pl.ds(offset, cap), :] = rows
            slot_proj[pl.ds(offset, cap), :] = projected

        for low, ref in enumerate(far_refs):
            rows = ref[...]
            projected = dot(rows, w_sender).astype(BF16)
            for upper in range(peers // 4):
                span = slice(upper * cap, (upper + 1) * cap)
                place(me ^ (4 * upper + low), rows[span], projected[span])
        rows = jnp.concatenate(read_near(near_refs, cap), axis=0)
        projected = dot(rows, w_sender).astype(BF16)
        for spot, owner in enumerate(near_peers(me, peers)):
            place(owner, rows[spot * cap : (spot + 1) * cap], projected[spot * cap : (spot + 1) * cap])

    @pl.when(step * STEP < count_ref[0] * TILE)
    def _():
        parts = halves_of(edge_ref)
        pres = []
        for start, part in parts:
            onehot = hot_rows(src_ref[0, :, part], slot_proj.shape[0])
            pres.append(local_ref[part, :].astype(F32) + dot(onehot, slot_proj[...]))
        projs = []
        for (start, part), pre in zip(parts, pres):
            hidden, slope = silu_and_slope(pre)
            hidden = hidden.astype(BF16)
            hidden_ref[part, :] = hidden
            slope_ref[part, :] = slope.astype(BF16)
            projs.append(dot(hidden, w_centred[...]))
        for (start, part), proj in zip(parts, projs):
            inverse = lax.rsqrt(jnp.mean(proj * proj, axis=1, keepdims=True) + 1e-05)
            normed = proj * inverse
            norm_ref[part, :] = normed.astype(BF16)
            inverse_ref[0, :, part] = as_row(inverse)
            edge_new = (edge_ref[part, :].astype(F32) + normed).astype(BF16)
            receivers = live_only(dst_ref[0, :, part], step * STEP + start, count_ref[0] * TILE)
            aggregate[...] += dot(hot_columns(receivers, aggregate.shape[0]), edge_new)

    @pl.when(step == pl.num_programs(0) - 1)
    def _():
        mesh = mesh_ref[...]
        summed = aggregate[...].astype(BF16)
        node_pre = dot(mesh, w_node_in_ref[:width, :]) + dot(summed, w_node_in_ref[width:, :])
        hidden, slope = silu_and_slope(node_pre)
        hidden = hidden.astype(BF16)
        normed, inverse = layer_norm(dot(hidden, w_node_out_ref[...]))
        upstream = cotangent_ref[...].astype(F32)
        d_proj = norm_back(normed, inverse, upstream).astype(BF16)
        d_pre = (contract_cols(d_proj, w_node_out_ref[...]) * slope).astype(BF16)
        d_mesh_ref[...] = upstream + contract_cols(d_pre, w_node_in_ref[:width, :])
        d_aggregate_ref[...] = contract_cols(d_pre, w_node_in_ref[width:, :]).astype(BF16)
        grad_out[...] = contract_rows(hidden, d_proj)
        grad_in[:width, :] = contract_rows(mesh, d_pre)
        grad_in[width:, :] = contract_rows(summed, d_pre)
        split_out(
            me,
            peers,
            2,
            send_ref,
            keep_ref,
            ((grad_in, grad_in.shape[0] // peers, False), (grad_out, grad_out.shape[0] // peers, False)),
        )


def backward_kernel(peers, me_ref, count_ref, src_ref, dst_ref, inverse_ref, *refs):
    (hidden_ref, slope_ref, norm_ref, edge_ref) = refs[:4]
    (d_aggregate_ref, received_ref, mesh_ref, d_mesh_ref) = refs[4:8]
    (w_sender_ref, w_receiver_ref, w_edge_ref, w_out_ref) = refs[8:12]
    (edge_grad_ref, mesh_grad_ref, slot_send_ref, slot_keep_ref, edge_send_ref, edge_keep_ref) = refs[12:18]
    near_refs = refs[18:23]
    (end_sum, grad_in, grad_out, d_slots) = refs[23:]
    step = pl.program_id(0)
    me = me_ref[0]
    slots, width = received_ref.shape
    mesh_count = mesh_ref.shape[0]

    @pl.when(step == 0)
    def _():
        end_sum[...] = jnp.zeros_like(end_sum)
        grad_in[:width, :] = jnp.zeros((width, width), F32)
        grad_out[...] = jnp.zeros_like(grad_out)

    @pl.when(step * STEP < count_ref[0] * TILE)
    def _():
        parts = halves_of(hidden_ref)
        upstreams = []
        columns = []
        for start, part in parts:
            first = step * STEP + start
            live = count_ref[0] * TILE
            receivers = live_only(dst_ref[0, :, part], first, live)
            upstreams.append(dot(hot_rows(receivers, mesh_count), d_aggregate_ref[...]))
            senders = live_only(src_ref[0, :, part], first, live)
            columns.append(
                jnp.concatenate([hot_columns(senders, slots), hot_columns(receivers, mesh_count)], axis=0)
            )
        d_projs = []
        d_hiddens = []
        for (start, part), upstream in zip(parts, upstreams):
            inverse = as_column(inverse_ref[0, :, part])
            d_proj = norm_back(norm_ref[part, :].astype(F32), inverse, upstream).astype(BF16)
            d_projs.append(d_proj)
            d_hiddens.append(contract_cols(d_proj, w_out_ref[...]))
        for (start, part), d_proj, d_hidden, column, upstream in zip(
            parts, d_projs, d_hiddens, columns, upstreams
        ):
            grad_out[...] += contract_rows(hidden_ref[part, :], d_proj)
            d_pre = (d_hidden * slope_ref[part, :].astype(F32)).astype(BF16)
            edge_grad_ref[part, :] = (upstream + contract_cols(d_pre, w_edge_ref[...])).astype(BF16)
            end_sum[...] += dot(column, d_pre)
            grad_in[:width, :] += contract_rows(edge_ref[part, :], d_pre)

    @pl.when(step * STEP >= count_ref[0] * TILE)
    def _():
        edge_grad_ref[...] = jnp.zeros_like(edge_grad_ref)

    @pl.when(step == pl.num_programs(0) - 1)
    def _():
        summed = end_sum[:slots, :].astype(BF16)
        mesh_summed = end_sum[slots:, :].astype(BF16)
        d_slots[...] = contract_cols(summed, w_sender_ref[...]).astype(BF16)
        grad_in[width : 2 * width, :] = contract_rows(received_ref[...], summed)
        grad_in[2 * width :, :] = contract_rows(mesh_ref[...], mesh_summed)
        mesh_grad_ref[...] = (d_mesh_ref[...] + contract_cols(mesh_summed, w_receiver_ref[...])).astype(BF16)
        cap = near_refs[0].shape[0]
        owners = near_peers(me, peers)
        write_back(
            near_refs, cap, [d_slots[pl.ds(pl.multiple_of(owner * cap, 16), cap), :] for owner in owners]
        )
        out_share = grad_out.shape[0] // peers
        split_out(
            me, peers, 1, slot_send_ref, slot_keep_ref, ((grad_out, out_share, False), (d_slots, cap, True))
        )
        split_out(
            me, peers, 1, edge_send_ref, edge_keep_ref, ((grad_in, grad_in.shape[0] // peers, False),)
        )


def send(values, perm):
    return lax.ppermute(values, "lon", perm)


def by_xor(peers, bits):
    return [(peer, peer ^ bits) for peer in range(peers)]


def by_shift(peers, shift):
    return [(peer, (peer + shift) % peers) for peer in range(peers)]


def across_chips(peers):
    return [(peer, (peer + (3 if peer % 2 else -3)) % peers) for peer in range(peers)]


def exchange_near(peers, lists):
    mine, other, after, before = lists
    return [mine, other, send(after, by_shift(peers, 2)), send(before, by_shift(peers, -2))]


def core_near(peers, near):
    mine, other, after, before, across = near
    swap = by_xor(peers, 1)
    return [mine, send(other, swap), after, before, across, send(after, swap), send(before, swap)]


def add(left, right):
    return (left.astype(F32) + right.astype(F32)).astype(BF16)


def first_sum(peers, bit, outgoing, kept):
    arrived = send(outgoing, by_xor(peers, bit))
    return add(kept[1], arrived[1]), add(kept[0], arrived[0])


def next_sum(peers, bit, outgoing, kept):
    return add(kept, send(outgoing, by_xor(peers, bit)))


def last_terms(peers, pieces):
    count = peers // 4
    share = pieces.shape[0] // count
    terms = [pieces[:share]]
    for place in range(1, count):
        piece = pieces[place * share : (place + 1) * share]
        terms.append(send(piece, by_xor(peers, 4 * place)))
    return terms


def halve_sum(peers, pieces):
    count = peers // 4
    blocks = pieces.reshape(count // 2, 2, -1, pieces.shape[1])
    kept, outgoing = [blocks[:, place].reshape(-1, pieces.shape[1]) for place in range(2)]
    return add(kept, send(outgoing, by_xor(peers, 4)))


def rest_terms(peers, pieces):
    count = peers // 8
    share = pieces.shape[0] // count
    terms = [pieces[:share]]
    for place in range(1, count):
        piece = pieces[place * share : (place + 1) * share]
        terms.append(send(piece, by_xor(peers, 8 * place)))
    return terms


def total_of(terms, start, stop):
    total = terms[0][start:stop].astype(F32)
    for term in terms[1:]:
        total = total + term[start:stop].astype(F32)
    return total


def whole(shape):
    return pl.BlockSpec(shape, lambda *_: (0,) * len(shape))


def on_device(
    grid_latent,
    mesh_latent,
    edge_latent,
    mesh_cotangent,
    edge_src,
    edge_dst,
    tile_count,
    send_rows,
    w_edge_in,
    w_edge_out,
    w_node_in,
    w_node_out,
):
    peers = lax.axis_size("lon")
    me = lax.axis_index("lon").astype(jnp.int32).reshape(1)
    upper = peers // 4
    rows = send_rows[0]
    cap = rows.shape[1]
    slots = peers * cap
    edges, width = edge_latent.shape
    mesh_count = mesh_latent.shape[0]
    grid_count = grid_latent.shape[0]
    tiles = edges // STEP
    src = edge_src.reshape(tiles, 1, STEP)
    dst = edge_dst.reshape(tiles, 1, STEP)
    smem = pl.BlockSpec(memory_space=pltpu.SMEM)
    hbm = pl.BlockSpec(memory_space=pltpu.HBM)
    params = pltpu.CompilerParams(vmem_limit_bytes=VMEM_BYTES)
    square = (width, width)

    def tile_of(last):
        return pl.BlockSpec((STEP, last), lambda step, *_: (step, 0))

    index_tile = pl.BlockSpec((1, 1, STEP), lambda step, *_: (step, 0, 0))

    def weight(place):
        return pl.BlockSpec(square, lambda *_: (place, 0))

    def halves(share):
        shape = (2, upper * share, width)
        return [jax.ShapeDtypeStruct(shape, BF16)] * 2, [whole(shape)] * 2

    grid_part = grid_count // 2
    near_rows = (cap, cap, 2 * cap, 2 * cap, cap)
    near_specs = [whole((count, width)) for count in near_rows]
    near_shapes = [jax.ShapeDtypeStruct((count, width), BF16) for count in near_rows]
    core_specs = near_specs + [whole((2 * cap, width))] * 2
    back_rows = (cap, 3 * cap, cap, cap, cap)
    back_specs = [whole((count, width)) for count in back_rows]
    back_shapes = [jax.ShapeDtypeStruct((count, width), BF16) for count in back_rows]
    return_specs = [whole((count, width)) for count in (cap, 3 * cap, 2 * cap, 2 * cap, cap)]
    lists = pl.pallas_call(
        gather_kernel,
        in_specs=[smem, hbm, hbm],
        out_specs=near_specs + [whole((cap, width))],
        out_shape=near_shapes + [jax.ShapeDtypeStruct((cap, width), BF16)],
        scratch_shapes=[
            pltpu.VMEM(rows.shape, jnp.int32),
            pltpu.VMEM(grid_latent.shape, BF16),
            pltpu.SemaphoreType.DMA,
            pltpu.SemaphoreType.DMA((GRID_PARTS,)),
        ],
        compiler_params=pltpu.CompilerParams(vmem_limit_bytes=GATHER_BYTES),
        cost_estimate=pl.CostEstimate(
            flops=40 * 16 * cap * grid_count * width,
            bytes_accessed=2 * grid_count * width,
            transcendentals=0,
        ),
        name="gather_lists",
    )(me, rows, grid_latent)

    hops = [send(lists[5], by_xor(peers, 4 * place)) for place in range(1, upper)]
    near = exchange_near(peers, lists[:4])
    hops[0], across = lax.optimization_barrier((hops[0], lists[4]))
    near.append(send(across, across_chips(peers)))
    far_own = jnp.concatenate([lists[5]] + hops, axis=0)
    far_own, receivers = lax.optimization_barrier((far_own, dst))
    far_next = send(far_own, by_xor(peers, 2))
    far_core = send(far_own, by_xor(peers, 1))
    local = pl.pallas_call(
        local_kernel,
        grid=(tiles,),
        in_specs=[index_tile, tile_of(width), whole(mesh_latent.shape), weight(0), weight(2)],
        out_specs=tile_of(width),
        out_shape=jax.ShapeDtypeStruct((edges, width), BF16),
        scratch_shapes=[pltpu.VMEM((width + mesh_count, width), BF16)],
        compiler_params=params,
        cost_estimate=pl.CostEstimate(
            flops=2 * edges * width * (width + mesh_count),
            bytes_accessed=4 * edges * width,
            transcendentals=0,
        ),
        name="edge_local",
    )(receivers, edge_latent, mesh_latent, w_edge_in, w_edge_in)
    far_next, far_core, near, local = lax.optimization_barrier((far_next, far_core, near, local))
    near = core_near(peers, near)
    far_both = send(far_next, by_xor(peers, 1))

    node_shape, node_spec = halves(w_node_in.shape[0] // peers + w_node_out.shape[0] // peers)
    (received, hidden, slope, norm, inverse, node_send, node_keep, d_aggregate, d_mesh) = pl.pallas_call(
        functools.partial(forward_kernel, peers),
        grid=(tiles,),
        in_specs=[smem, smem, index_tile, index_tile, tile_of(width), tile_of(width)]
        + core_specs
        + [whole((upper * cap, width))] * 4
        + [weight(1)]
        + [whole(w.shape) for w in (w_edge_out, w_node_in, w_node_out, mesh_latent, mesh_cotangent)],
        out_specs=[whole((slots, width))]
        + [tile_of(width)] * 3
        + [index_tile]
        + node_spec
        + [whole((mesh_count, width))] * 2,
        out_shape=[jax.ShapeDtypeStruct((slots, width), BF16)]
        + [jax.ShapeDtypeStruct((edges, width), BF16)] * 3
        + [jax.ShapeDtypeStruct((tiles, 1, STEP), F32)]
        + node_shape
        + [jax.ShapeDtypeStruct((mesh_count, width), BF16), jax.ShapeDtypeStruct((mesh_count, width), F32)],
        scratch_shapes=[
            pltpu.VMEM((slots, width), BF16),
            pltpu.VMEM((mesh_count, width), F32),
            pltpu.VMEM(w_node_in.shape, F32),
            pltpu.VMEM(w_node_out.shape, F32),
            pltpu.VMEM(w_edge_out.shape, BF16),
        ],
        compiler_params=params,
        name="forward",
    )(
        me,
        tile_count,
        src,
        dst,
        local,
        edge_latent,
        *near,
        far_own,
        far_core,
        far_next,
        far_both,
        w_edge_in,
        w_edge_out,
        w_node_in,
        w_node_out,
        mesh_latent,
        mesh_cotangent,
    )

    node_next, node_kept = first_sum(peers, 2, node_send, node_keep)
    slot_shape, slot_spec = halves(w_edge_out.shape[0] // peers + cap)
    edge_shape, edge_spec = halves(w_edge_in.shape[0] // peers)
    results = pl.pallas_call(
        functools.partial(backward_kernel, peers),
        grid=(tiles,),
        in_specs=[smem, smem, index_tile, index_tile, index_tile]
        + [tile_of(width)] * 4
        + [whole((mesh_count, width)), whole((slots, width))]
        + [whole((mesh_count, width))] * 2
        + [weight(1), weight(2), weight(0), whole(square)],
        out_specs=[tile_of(width), whole((mesh_count, width))] + slot_spec + edge_spec + back_specs,
        out_shape=[
            jax.ShapeDtypeStruct((edges, width), BF16),
            jax.ShapeDtypeStruct((mesh_count, width), BF16),
        ]
        + slot_shape
        + edge_shape
        + back_shapes,
        scratch_shapes=[
            pltpu.VMEM((slots + mesh_count, width), F32),
            pltpu.VMEM(w_edge_in.shape, F32),
            pltpu.VMEM(square, F32),
            pltpu.VMEM((slots, width), BF16),
        ],
        compiler_params=params,
        cost_estimate=pl.CostEstimate(
            flops=2 * edges * width * (2 * mesh_count + 4 * width + slots),
            bytes_accessed=10 * edges * width,
            transcendentals=0,
        ),
        name="backward",
    )(
        me,
        tile_count,
        src,
        dst,
        inverse,
        hidden,
        slope,
        norm,
        edge_latent,
        d_aggregate,
        received,
        mesh_latent,
        d_mesh,
        w_edge_in,
        w_edge_in,
        w_edge_in,
        w_edge_out,
    )
    (edge_grad, mesh_grad, slot_send, slot_keep, edge_send, edge_keep), returns = results[:6], results[6:]
    (node_next, node_kept, slot_send, slot_keep, edge_send, edge_keep, returns) = lax.optimization_barrier(
        (node_next, node_kept, slot_send, slot_keep, edge_send, edge_keep, returns)
    )
    slot_next, slot_kept = first_sum(peers, 1, slot_send, slot_keep)
    slot_pieces = next_sum(peers, 2, slot_next, slot_kept)
    edge_next, edge_kept = first_sum(peers, 1, edge_send, edge_keep)
    node_pieces = next_sum(peers, 1, node_next, node_kept)
    swapped = send(returns[1], by_xor(peers, 1))
    node_pieces, edge_next, edge_kept, swapped, across = lax.optimization_barrier(
        (node_pieces, edge_next, edge_kept, swapped, returns[4])
    )
    node_pieces = halve_sum(peers, node_pieces)
    across = send(across, across_chips(peers))
    to_after = jnp.concatenate([returns[2], swapped[cap : 2 * cap]], axis=0)
    to_before = jnp.concatenate([returns[3], swapped[2 * cap :]], axis=0)
    (slot_pieces, edge_next, edge_kept, across, node_pieces, to_after, to_before) = lax.optimization_barrier(
        (slot_pieces, edge_next, edge_kept, across, node_pieces, to_after, to_before)
    )
    edge_pieces = next_sum(peers, 2, edge_next, edge_kept)
    slot_terms = last_terms(peers, slot_pieces)
    node_terms = rest_terms(peers, node_pieces)
    (slot_terms, node_terms, edge_pieces, to_after, to_before) = lax.optimization_barrier(
        (slot_terms, node_terms, edge_pieces, to_after, to_before)
    )
    edge_terms = last_terms(peers, edge_pieces)
    bundles = [send(to_after, by_shift(peers, 2)), send(to_before, by_shift(peers, -2))]
    returned = [returns[0], swapped, *bundles, across]
    node_rows = w_node_in.shape[0] // peers
    node_out_rows = w_node_out.shape[0] // peers
    out_rows = w_edge_out.shape[0] // peers
    grid_grad, grad_edge_out, grad_node_in, grad_node_out = pl.pallas_call(
        functools.partial(scatter_kernel, out_rows, len(slot_terms)),
        grid=(2,),
        in_specs=[smem, whole(rows.shape)]
        + return_specs
        + [whole((out_rows + cap, width))] * len(slot_terms)
        + [whole((node_rows + node_out_rows, width))] * len(node_terms),
        out_specs=[pl.BlockSpec((grid_count // 2, width), lambda step: (step, 0))]
        + [whole((count, width)) for count in (out_rows, node_rows, node_out_rows)],
        out_shape=[jax.ShapeDtypeStruct((grid_count, width), BF16)]
        + [jax.ShapeDtypeStruct((count, width), F32) for count in (out_rows, node_rows, node_out_rows)],
        compiler_params=params,
        name="scatter_lists",
    )(me, rows, *returned, *slot_terms, *node_terms)
    edge_terms, grid_grad = lax.optimization_barrier((edge_terms, grid_grad))
    return (
        grid_grad,
        edge_grad,
        mesh_grad,
        total_of(edge_terms, 0, w_edge_in.shape[0] // peers),
        grad_edge_out,
        grad_node_in,
        grad_node_out,
    )


def solution(mesh):
    rows = P(("grp", "lon"), None)
    flat = P(("grp", "lon"))
    return jax.shard_map(
        on_device,
        mesh=mesh,
        in_specs=(rows, rows, rows, rows, flat, flat, flat, P(("grp", "lon"), None, None)) + (P(),) * 4,
        out_specs=(rows,) * 7,
        check_vma=False,
    )
```

```python
import functools

import jax
import jax.numpy as jnp
from jax import lax
from jax.experimental import pallas as pl
from jax.experimental.pallas import tpu as pltpu
from jax.sharding import PartitionSpec as P

TILE = 256
STEP = 1024
SUB = 512
LANES = 128
BLOCK = 256
GRID_PARTS = 4
NEAR = 3
BF16 = jnp.bfloat16
F32 = jnp.float32
VMEM_BYTES = 24 * 1024 * 1024
GATHER_BYTES = 56 * 1024 * 1024


def dot(left, right):
    return lax.dot_general(left, right, (((1,), (0,)), ((), ())), preferred_element_type=F32)


def contract_rows(left, right):
    return lax.dot_general(left, right, (((0,), (0,)), ((), ())), preferred_element_type=F32)


def contract_cols(left, right):
    return lax.dot_general(left, right, (((1,), (1,)), ((), ())), preferred_element_type=F32)


def layer_norm(values):
    centered = values - jnp.mean(values, axis=1, keepdims=True)
    inverse = lax.rsqrt(jnp.mean(centered * centered, axis=1, keepdims=True) + 1e-05)
    return (centered * inverse, inverse)


def norm_back(normed, inverse, upstream):
    first = jnp.mean(upstream, axis=1, keepdims=True)
    second = jnp.mean(upstream * normed, axis=1, keepdims=True)
    return inverse * (upstream - first - normed * second)


def silu_and_slope(values):
    sigma = 0.5 + 0.5 * jnp.tanh(0.5 * values)
    hidden = values * sigma
    return (hidden, sigma + hidden * (1.0 - sigma))


def as_column(row):
    count = row.shape[1]
    block = min(count, LANES)
    down = lax.broadcasted_iota(jnp.int32, (block, block), 0)
    along = lax.broadcasted_iota(jnp.int32, (block, block), 1)
    columns = []
    for start in range(0, count, block):
        piece = row[:, start : start + block].astype(F32)
        picked = jnp.where(down == along, piece, 0.0)
        columns.append(jnp.sum(picked, axis=1, keepdims=True))
    return jnp.concatenate(columns, axis=0)


def as_row(column):
    count = column.shape[0]
    block = min(count, LANES)
    down = lax.broadcasted_iota(jnp.int32, (block, block), 0)
    along = lax.broadcasted_iota(jnp.int32, (block, block), 1)
    rows = []
    for start in range(0, count, block):
        picked = jnp.where(down == along, column[start : start + block], 0.0)
        rows.append(jnp.sum(picked, axis=0, keepdims=True))
    return jnp.concatenate(rows, axis=1)


def in_block(indices, first):
    place = indices - first
    return jnp.where((place >= 0) & (place < BLOCK), place, -1).astype(F32).astype(BF16)


def hot_rows(row, width, first=0):
    column = as_column(row).astype(jnp.int32)
    count = row.shape[1]
    one = jnp.ones((), BF16)
    zero = jnp.zeros((), BF16)
    blocks = []
    for start in range(0, width, BLOCK):
        size = min(BLOCK, width - start)
        along = lax.broadcasted_iota(jnp.int32, (count, size), 1).astype(F32).astype(BF16)
        blocks.append(jnp.where(in_block(column, first + start) == along, one, zero))
    return jnp.concatenate(blocks, axis=1)


def hot_columns(row, height):
    count = row.shape[1]
    one = jnp.ones((), BF16)
    zero = jnp.zeros((), BF16)
    blocks = []
    for start in range(0, height, BLOCK):
        size = min(BLOCK, height - start)
        down = lax.broadcasted_iota(jnp.int32, (size, count), 0).astype(F32).astype(BF16)
        blocks.append(jnp.where(in_block(row, start) == down, one, zero))
    return jnp.concatenate(blocks, axis=0)


def live_only(row, first, count):
    place = first + lax.broadcasted_iota(jnp.int32, row.shape, 1)
    return jnp.where(place < count, row, -1)


def near_peers(me, peers):
    after = lax.rem(me + 2, peers)
    before = lax.rem(me + peers - 2, peers)
    across = lax.rem(me + peers - 3 + 6 * (me & 1), peers)
    return (me, me ^ 1, after, after ^ 1, before, before ^ 1, across)


def write_near(refs, cap, lists):
    mine, other, after, before, across = refs
    mine[...] = lists[0]
    other[...] = lists[1]
    after[:cap, :] = lists[2]
    after[cap:, :] = lists[3]
    before[:cap, :] = lists[4]
    before[cap:, :] = lists[5]
    across[...] = lists[6]


def read_near(refs, cap):
    mine, other, from_before, from_after, across, core_before, core_after = refs
    return [
        mine[...],
        other[...],
        from_after[:cap, :],
        core_after[cap:, :],
        from_before[:cap, :],
        core_before[cap:, :],
        across[...],
    ]


def write_back(refs, cap, lists):
    mine, swapped, after, before, across = refs
    mine[...] = lists[0]
    for place, index in enumerate((1, 3, 5)):
        swapped[place * cap : (place + 1) * cap, :] = lists[index]
    after[...] = lists[2]
    before[...] = lists[4]
    across[...] = lists[6]


def read_back(refs, cap):
    mine, swapped, from_before, from_after, across = refs
    return [
        mine[...],
        swapped[:cap, :],
        from_after[:cap, :],
        from_after[cap:, :],
        from_before[:cap, :],
        from_before[cap:, :],
        across[...],
    ]


def list_hots(me, rows_ref, grid_count, first):
    peers, cap = rows_ref.shape
    pieces = []
    for target in near_peers(me, peers):
        pieces.append(hot_rows(rows_ref[pl.ds(target, 1), :], grid_count, first))
    peer = lax.broadcasted_iota(jnp.int32, (peers, cap), 0)
    ahead = lax.rem(peer - me + peers, peers)
    apart = jnp.minimum(ahead, peers - ahead)
    far = jnp.max(jnp.where(apart > NEAR, rows_ref[...].astype(F32), -1.0), axis=0, keepdims=True)
    pieces.append(hot_rows(far.astype(jnp.int32), grid_count, first))
    return jnp.concatenate(pieces, axis=0)


def gather_kernel(me_ref, rows_hbm, grid_hbm, *refs):
    near_refs, far_ref = refs[:5], refs[5]
    rows_ref, grid_ref, rows_done, grid_done = refs[6:]
    cap = rows_ref.shape[1]
    part = grid_ref.shape[0] // GRID_PARTS
    copies = [
        pltpu.make_async_copy(
            grid_hbm.at[pl.ds(at * part, part)], grid_ref.at[pl.ds(at * part, part)], grid_done.at[at]
        )
        for at in range(GRID_PARTS)
    ]
    rows_copy = pltpu.make_async_copy(rows_hbm, rows_ref, rows_done)
    rows_copy.start()
    for copy in copies:
        copy.start()
    rows_copy.wait()
    found = None
    for at, copy in enumerate(copies):
        hots = list_hots(me_ref[0], rows_ref, part, at * part)
        copy.wait()
        piece = dot(hots, grid_ref[at * part : (at + 1) * part, :])
        found = piece if found is None else found + piece
    rows = found.astype(BF16)
    lists = [rows[at : at + cap] for at in range(0, 8 * cap, cap)]
    write_near(near_refs, cap, lists)
    far_ref[...] = lists[7]


def scatter_kernel(skip, slot_count, me_ref, rows_ref, *refs):
    near_refs, refs = refs[:5], refs[5:]
    out_ref, grad_out_ref, node_in_ref, node_out_ref = refs[-4:]
    terms = refs[:-4]
    part = out_ref.shape[0]
    cap = rows_ref.shape[1]
    far_refs, node_refs = terms[:slot_count], terms[slot_count:]
    node_rows = node_in_ref.shape[0]

    def total(term_refs, start, stop):
        result = term_refs[0][start:stop, :].astype(F32)
        for ref in term_refs[1:]:
            result = result + ref[start:stop, :].astype(F32)
        return result

    hots = list_hots(me_ref[0], rows_ref, part, pl.program_id(0) * part)
    far = total(far_refs, skip, skip + cap)
    values = jnp.concatenate(read_back(near_refs, cap) + [far.astype(BF16)], axis=0)
    out_ref[...] = contract_rows(hots, values).astype(BF16)

    @pl.when(pl.program_id(0) == 0)
    def _():
        grad_out_ref[...] = total(far_refs, 0, skip)
        node_in_ref[...] = total(node_refs, 0, node_rows)
        node_out_ref[...] = total(node_refs, node_rows, node_rows + node_out_ref.shape[0])


def halves_of(ref):
    rows = ref.shape[-1] if len(ref.shape) == 3 else ref.shape[0]
    return [(start, slice(start, start + SUB)) for start in range(0, rows, SUB)]


def local_kernel(dst_ref, edge_ref, mesh_ref, w_edge_ref, w_receiver_ref, out_ref, weights):
    width = edge_ref.shape[1]

    @pl.when(pl.program_id(0) == 0)
    def _():
        weights[:width, :] = w_edge_ref[...]
        weights[width:, :] = dot(mesh_ref[...], w_receiver_ref[...]).astype(BF16)

    for start, part in halves_of(edge_ref):
        onehot = hot_rows(dst_ref[0, :, part], mesh_ref.shape[0])
        joined = jnp.concatenate([edge_ref[part, :], onehot], axis=1)
        out_ref[part, :] = dot(joined, weights[...]).astype(BF16)


def split_out(me, peers, first, send_ref, keep_ref, parts):
    for low in range(4):
        target = send_ref if low & first else keep_ref
        half = 1 if low & (3 - first) else 0
        at = 0
        for upper in range(peers // 4):
            owner = me ^ (4 * upper + low)
            for ref, share, far in parts:
                piece = ref[pl.ds(pl.multiple_of(owner * share, 16), share), :]
                if far:
                    ahead = lax.rem(owner - me + peers, peers)
                    apart = jnp.minimum(ahead, peers - ahead)
                    piece = jnp.where(apart > NEAR, piece.astype(F32), 0.0)
                target[half, at : at + share, :] = piece.astype(BF16)
                at += share


def forward_kernel(
    peers, me_ref, count_ref, src_ref, dst_ref, local_ref, edge_ref, *refs
):
    near_refs, far_refs = refs[:7], refs[7:11]
    (w_sender_ref, w_out_ref, w_node_in_ref, w_node_out_ref, mesh_ref, cotangent_ref) = refs[11:17]
    (received_ref, hidden_ref, slope_ref, norm_ref, inverse_ref) = refs[17:22]
    (send_ref, keep_ref, d_aggregate_ref, d_mesh_ref) = refs[22:26]
    (slot_proj, aggregate, grad_in, grad_out, w_centred) = refs[26:]
    step = pl.program_id(0)
    me = me_ref[0]
    cap = near_refs[0].shape[0]
    width = edge_ref.shape[1]

    @pl.when(step == 0)
    def _():
        aggregate[...] = jnp.zeros_like(aggregate)
        w_out = w_out_ref[...].astype(F32)
        w_centred[...] = (w_out - jnp.mean(w_out, axis=1, keepdims=True)).astype(BF16)
        w_sender = w_sender_ref[...]

        def place(owner, rows, projected):
            offset = pl.multiple_of(owner * cap, 16)
            received_ref[pl.ds(offset, cap), :] = rows
            slot_proj[pl.ds(offset, cap), :] = projected

        for low, ref in enumerate(far_refs):
            rows = ref[...]
            projected = dot(rows, w_sender).astype(BF16)
            for upper in range(peers // 4):
                span = slice(upper * cap, (upper + 1) * cap)
                place(me ^ (4 * upper + low), rows[span], projected[span])
        rows = jnp.concatenate(read_near(near_refs, cap), axis=0)
        projected = dot(rows, w_sender).astype(BF16)
        for spot, owner in enumerate(near_peers(me, peers)):
            place(owner, rows[spot * cap : (spot + 1) * cap], projected[spot * cap : (spot + 1) * cap])

    @pl.when(step * STEP < count_ref[0] * TILE)
    def _():
        parts = halves_of(edge_ref)
        pres = []
        for start, part in parts:
            onehot = hot_rows(src_ref[0, :, part], slot_proj.shape[0])
            pres.append(local_ref[part, :].astype(F32) + dot(onehot, slot_proj[...]))
        projs = []
        for (start, part), pre in zip(parts, pres):
            hidden, slope = silu_and_slope(pre)
            hidden = hidden.astype(BF16)
            hidden_ref[part, :] = hidden
            slope_ref[part, :] = slope.astype(BF16)
            projs.append(dot(hidden, w_centred[...]))
        for (start, part), proj in zip(parts, projs):
            inverse = lax.rsqrt(jnp.mean(proj * proj, axis=1, keepdims=True) + 1e-05)
            normed = proj * inverse
            norm_ref[part, :] = normed.astype(BF16)
            inverse_ref[0, :, part] = as_row(inverse)
            edge_new = (edge_ref[part, :].astype(F32) + normed).astype(BF16)
            receivers = live_only(dst_ref[0, :, part], step * STEP + start, count_ref[0] * TILE)
            aggregate[...] += dot(hot_columns(receivers, aggregate.shape[0]), edge_new)

    @pl.when(step == pl.num_programs(0) - 1)
    def _():
        mesh = mesh_ref[...]
        summed = aggregate[...].astype(BF16)
        node_pre = dot(mesh, w_node_in_ref[:width, :]) + dot(summed, w_node_in_ref[width:, :])
        hidden, slope = silu_and_slope(node_pre)
        hidden = hidden.astype(BF16)
        normed, inverse = layer_norm(dot(hidden, w_node_out_ref[...]))
        upstream = cotangent_ref[...].astype(F32)
        d_proj = norm_back(normed, inverse, upstream).astype(BF16)
        d_pre = (contract_cols(d_proj, w_node_out_ref[...]) * slope).astype(BF16)
        d_mesh_ref[...] = upstream + contract_cols(d_pre, w_node_in_ref[:width, :])
        d_aggregate_ref[...] = contract_cols(d_pre, w_node_in_ref[width:, :]).astype(BF16)
        grad_out[...] = contract_rows(hidden, d_proj)
        grad_in[:width, :] = contract_rows(mesh, d_pre)
        grad_in[width:, :] = contract_rows(summed, d_pre)
        split_out(
            me,
            peers,
            2,
            send_ref,
            keep_ref,
            ((grad_in, grad_in.shape[0] // peers, False), (grad_out, grad_out.shape[0] // peers, False)),
        )


def backward_kernel(peers, me_ref, count_ref, src_ref, dst_ref, inverse_ref, *refs):
    (hidden_ref, slope_ref, norm_ref, edge_ref) = refs[:4]
    (d_aggregate_ref, received_ref, mesh_ref, d_mesh_ref) = refs[4:8]
    (w_sender_ref, w_receiver_ref, w_edge_ref, w_out_ref) = refs[8:12]
    (edge_grad_ref, mesh_grad_ref, slot_send_ref, slot_keep_ref, edge_send_ref, edge_keep_ref) = refs[12:18]
    near_refs = refs[18:23]
    (end_sum, grad_in, grad_out, d_slots) = refs[23:]
    step = pl.program_id(0)
    me = me_ref[0]
    slots, width = received_ref.shape
    mesh_count = mesh_ref.shape[0]

    @pl.when(step == 0)
    def _():
        end_sum[...] = jnp.zeros_like(end_sum)
        grad_in[:width, :] = jnp.zeros((width, width), F32)
        grad_out[...] = jnp.zeros_like(grad_out)

    @pl.when(step * STEP < count_ref[0] * TILE)
    def _():
        parts = halves_of(hidden_ref)
        upstreams = []
        columns = []
        for start, part in parts:
            first = step * STEP + start
            live = count_ref[0] * TILE
            receivers = live_only(dst_ref[0, :, part], first, live)
            upstreams.append(dot(hot_rows(receivers, mesh_count), d_aggregate_ref[...]))
            senders = live_only(src_ref[0, :, part], first, live)
            columns.append(
                jnp.concatenate([hot_columns(senders, slots), hot_columns(receivers, mesh_count)], axis=0)
            )
        d_projs = []
        d_hiddens = []
        for (start, part), upstream in zip(parts, upstreams):
            inverse = as_column(inverse_ref[0, :, part])
            d_proj = norm_back(norm_ref[part, :].astype(F32), inverse, upstream).astype(BF16)
            d_projs.append(d_proj)
            d_hiddens.append(contract_cols(d_proj, w_out_ref[...]))
        for (start, part), d_proj, d_hidden, column, upstream in zip(
            parts, d_projs, d_hiddens, columns, upstreams
        ):
            grad_out[...] += contract_rows(hidden_ref[part, :], d_proj)
            d_pre = (d_hidden * slope_ref[part, :].astype(F32)).astype(BF16)
            edge_grad_ref[part, :] = (upstream + contract_cols(d_pre, w_edge_ref[...])).astype(BF16)
            end_sum[...] += dot(column, d_pre)
            grad_in[:width, :] += contract_rows(edge_ref[part, :], d_pre)

    @pl.when(step * STEP >= count_ref[0] * TILE)
    def _():
        edge_grad_ref[...] = jnp.zeros_like(edge_grad_ref)

    @pl.when(step == pl.num_programs(0) - 1)
    def _():
        summed = end_sum[:slots, :].astype(BF16)
        mesh_summed = end_sum[slots:, :].astype(BF16)
        d_slots[...] = contract_cols(summed, w_sender_ref[...]).astype(BF16)
        grad_in[width : 2 * width, :] = contract_rows(received_ref[...], summed)
        grad_in[2 * width :, :] = contract_rows(mesh_ref[...], mesh_summed)
        mesh_grad_ref[...] = (d_mesh_ref[...] + contract_cols(mesh_summed, w_receiver_ref[...])).astype(BF16)
        cap = near_refs[0].shape[0]
        owners = near_peers(me, peers)
        write_back(
            near_refs, cap, [d_slots[pl.ds(pl.multiple_of(owner * cap, 16), cap), :] for owner in owners]
        )
        out_share = grad_out.shape[0] // peers
        split_out(
            me, peers, 1, slot_send_ref, slot_keep_ref, ((grad_out, out_share, False), (d_slots, cap, True))
        )
        split_out(
            me, peers, 1, edge_send_ref, edge_keep_ref, ((grad_in, grad_in.shape[0] // peers, False),)
        )


def send(values, perm):
    return lax.ppermute(values, "lon", perm)


def by_xor(peers, bits):
    return [(peer, peer ^ bits) for peer in range(peers)]


def by_shift(peers, shift):
    return [(peer, (peer + shift) % peers) for peer in range(peers)]


def across_chips(peers):
    return [(peer, (peer + (3 if peer % 2 else -3)) % peers) for peer in range(peers)]


def exchange_near(peers, lists):
    mine, other, after, before, across = lists
    return [
        mine,
        other,
        send(after, by_shift(peers, 2)),
        send(before, by_shift(peers, -2)),
        send(across, across_chips(peers)),
    ]


def core_near(peers, near):
    mine, other, after, before, across = near
    swap = by_xor(peers, 1)
    return [mine, send(other, swap), after, before, across, send(after, swap), send(before, swap)]


def add(left, right):
    return (left.astype(F32) + right.astype(F32)).astype(BF16)


def first_sum(peers, bit, outgoing, kept):
    arrived = send(outgoing, by_xor(peers, bit))
    return add(kept[1], arrived[1]), add(kept[0], arrived[0])


def next_sum(peers, bit, outgoing, kept):
    return add(kept, send(outgoing, by_xor(peers, bit)))


def last_terms(peers, pieces):
    count = peers // 4
    share = pieces.shape[0] // count
    terms = [pieces[:share]]
    for place in range(1, count):
        piece = pieces[place * share : (place + 1) * share]
        terms.append(send(piece, by_xor(peers, 4 * place)))
    return terms


def halve_sum(peers, pieces):
    count = peers // 4
    blocks = pieces.reshape(count // 2, 2, -1, pieces.shape[1])
    kept, outgoing = [blocks[:, place].reshape(-1, pieces.shape[1]) for place in range(2)]
    return add(kept, send(outgoing, by_xor(peers, 4)))


def rest_terms(peers, pieces):
    count = peers // 8
    share = pieces.shape[0] // count
    terms = [pieces[:share]]
    for place in range(1, count):
        piece = pieces[place * share : (place + 1) * share]
        terms.append(send(piece, by_xor(peers, 8 * place)))
    return terms


def total_of(terms, start, stop):
    total = terms[0][start:stop].astype(F32)
    for term in terms[1:]:
        total = total + term[start:stop].astype(F32)
    return total


def whole(shape):
    return pl.BlockSpec(shape, lambda *_: (0,) * len(shape))


def on_device(
    grid_latent,
    mesh_latent,
    edge_latent,
    mesh_cotangent,
    edge_src,
    edge_dst,
    tile_count,
    send_rows,
    w_edge_in,
    w_edge_out,
    w_node_in,
    w_node_out,
):
    peers = lax.axis_size("lon")
    me = lax.axis_index("lon").astype(jnp.int32).reshape(1)
    upper = peers // 4
    rows = send_rows[0]
    cap = rows.shape[1]
    slots = peers * cap
    edges, width = edge_latent.shape
    mesh_count = mesh_latent.shape[0]
    grid_count = grid_latent.shape[0]
    tiles = edges // STEP
    src = edge_src.reshape(tiles, 1, STEP)
    dst = edge_dst.reshape(tiles, 1, STEP)
    smem = pl.BlockSpec(memory_space=pltpu.SMEM)
    hbm = pl.BlockSpec(memory_space=pltpu.HBM)
    params = pltpu.CompilerParams(vmem_limit_bytes=VMEM_BYTES)
    square = (width, width)

    def tile_of(last):
        return pl.BlockSpec((STEP, last), lambda step, *_: (step, 0))

    index_tile = pl.BlockSpec((1, 1, STEP), lambda step, *_: (step, 0, 0))

    def weight(place):
        return pl.BlockSpec(square, lambda *_: (place, 0))

    def halves(share):
        shape = (2, upper * share, width)
        return [jax.ShapeDtypeStruct(shape, BF16)] * 2, [whole(shape)] * 2

    grid_part = grid_count // 2
    near_rows = (cap, cap, 2 * cap, 2 * cap, cap)
    near_specs = [whole((count, width)) for count in near_rows]
    near_shapes = [jax.ShapeDtypeStruct((count, width), BF16) for count in near_rows]
    core_specs = near_specs + [whole((2 * cap, width))] * 2
    back_rows = (cap, 3 * cap, cap, cap, cap)
    back_specs = [whole((count, width)) for count in back_rows]
    back_shapes = [jax.ShapeDtypeStruct((count, width), BF16) for count in back_rows]
    return_specs = [whole((count, width)) for count in (cap, 3 * cap, 2 * cap, 2 * cap, cap)]
    lists = pl.pallas_call(
        gather_kernel,
        in_specs=[smem, hbm, hbm],
        out_specs=near_specs + [whole((cap, width))],
        out_shape=near_shapes + [jax.ShapeDtypeStruct((cap, width), BF16)],
        scratch_shapes=[
            pltpu.VMEM(rows.shape, jnp.int32),
            pltpu.VMEM(grid_latent.shape, BF16),
            pltpu.SemaphoreType.DMA,
            pltpu.SemaphoreType.DMA((GRID_PARTS,)),
        ],
        compiler_params=pltpu.CompilerParams(vmem_limit_bytes=GATHER_BYTES),
        cost_estimate=pl.CostEstimate(
            flops=40 * 16 * cap * grid_count * width,
            bytes_accessed=2 * grid_count * width,
            transcendentals=0,
        ),
        name="gather_lists",
    )(me, rows, grid_latent)

    hops = [send(lists[5], by_xor(peers, 4 * place)) for place in range(1, upper)]
    near = exchange_near(peers, lists[:5])
    far_own = jnp.concatenate([lists[5]] + hops, axis=0)
    far_own, receivers = lax.optimization_barrier((far_own, dst))
    far_next = send(far_own, by_xor(peers, 2))
    far_core = send(far_own, by_xor(peers, 1))
    local = pl.pallas_call(
        local_kernel,
        grid=(tiles,),
        in_specs=[index_tile, tile_of(width), whole(mesh_latent.shape), weight(0), weight(2)],
        out_specs=tile_of(width),
        out_shape=jax.ShapeDtypeStruct((edges, width), BF16),
        scratch_shapes=[pltpu.VMEM((width + mesh_count, width), BF16)],
        compiler_params=params,
        cost_estimate=pl.CostEstimate(
            flops=2 * edges * width * (width + mesh_count),
            bytes_accessed=4 * edges * width,
            transcendentals=0,
        ),
        name="edge_local",
    )(receivers, edge_latent, mesh_latent, w_edge_in, w_edge_in)
    far_next, far_core, near, local = lax.optimization_barrier((far_next, far_core, near, local))
    near = core_near(peers, near)
    far_both = send(far_next, by_xor(peers, 1))

    node_shape, node_spec = halves(w_node_in.shape[0] // peers + w_node_out.shape[0] // peers)
    (received, hidden, slope, norm, inverse, node_send, node_keep, d_aggregate, d_mesh) = pl.pallas_call(
        functools.partial(forward_kernel, peers),
        grid=(tiles,),
        in_specs=[smem, smem, index_tile, index_tile, tile_of(width), tile_of(width)]
        + core_specs
        + [whole((upper * cap, width))] * 4
        + [weight(1)]
        + [whole(w.shape) for w in (w_edge_out, w_node_in, w_node_out, mesh_latent, mesh_cotangent)],
        out_specs=[whole((slots, width))]
        + [tile_of(width)] * 3
        + [index_tile]
        + node_spec
        + [whole((mesh_count, width))] * 2,
        out_shape=[jax.ShapeDtypeStruct((slots, width), BF16)]
        + [jax.ShapeDtypeStruct((edges, width), BF16)] * 3
        + [jax.ShapeDtypeStruct((tiles, 1, STEP), F32)]
        + node_shape
        + [jax.ShapeDtypeStruct((mesh_count, width), BF16), jax.ShapeDtypeStruct((mesh_count, width), F32)],
        scratch_shapes=[
            pltpu.VMEM((slots, width), BF16),
            pltpu.VMEM((mesh_count, width), F32),
            pltpu.VMEM(w_node_in.shape, F32),
            pltpu.VMEM(w_node_out.shape, F32),
            pltpu.VMEM(w_edge_out.shape, BF16),
        ],
        compiler_params=params,
        name="forward",
    )(
        me,
        tile_count,
        src,
        dst,
        local,
        edge_latent,
        *near,
        far_own,
        far_core,
        far_next,
        far_both,
        w_edge_in,
        w_edge_out,
        w_node_in,
        w_node_out,
        mesh_latent,
        mesh_cotangent,
    )

    node_next, node_kept = first_sum(peers, 2, node_send, node_keep)
    slot_shape, slot_spec = halves(w_edge_out.shape[0] // peers + cap)
    edge_shape, edge_spec = halves(w_edge_in.shape[0] // peers)
    results = pl.pallas_call(
        functools.partial(backward_kernel, peers),
        grid=(tiles,),
        in_specs=[smem, smem, index_tile, index_tile, index_tile]
        + [tile_of(width)] * 4
        + [whole((mesh_count, width)), whole((slots, width))]
        + [whole((mesh_count, width))] * 2
        + [weight(1), weight(2), weight(0), whole(square)],
        out_specs=[tile_of(width), whole((mesh_count, width))] + slot_spec + edge_spec + back_specs,
        out_shape=[
            jax.ShapeDtypeStruct((edges, width), BF16),
            jax.ShapeDtypeStruct((mesh_count, width), BF16),
        ]
        + slot_shape
        + edge_shape
        + back_shapes,
        scratch_shapes=[
            pltpu.VMEM((slots + mesh_count, width), F32),
            pltpu.VMEM(w_edge_in.shape, F32),
            pltpu.VMEM(square, F32),
            pltpu.VMEM((slots, width), BF16),
        ],
        compiler_params=params,
        cost_estimate=pl.CostEstimate(
            flops=2 * edges * width * (2 * mesh_count + 4 * width + slots),
            bytes_accessed=10 * edges * width,
            transcendentals=0,
        ),
        name="backward",
    )(
        me,
        tile_count,
        src,
        dst,
        inverse,
        hidden,
        slope,
        norm,
        edge_latent,
        d_aggregate,
        received,
        mesh_latent,
        d_mesh,
        w_edge_in,
        w_edge_in,
        w_edge_in,
        w_edge_out,
    )
    (edge_grad, mesh_grad, slot_send, slot_keep, edge_send, edge_keep), returns = results[:6], results[6:]
    (node_next, node_kept, slot_send, slot_keep, edge_send, edge_keep, returns) = lax.optimization_barrier(
        (node_next, node_kept, slot_send, slot_keep, edge_send, edge_keep, returns)
    )
    slot_next, slot_kept = first_sum(peers, 1, slot_send, slot_keep)
    slot_pieces = next_sum(peers, 2, slot_next, slot_kept)
    edge_next, edge_kept = first_sum(peers, 1, edge_send, edge_keep)
    node_pieces = next_sum(peers, 1, node_next, node_kept)
    swapped = send(returns[1], by_xor(peers, 1))
    node_pieces, edge_next, edge_kept, swapped, across = lax.optimization_barrier(
        (node_pieces, edge_next, edge_kept, swapped, returns[4])
    )
    node_pieces = halve_sum(peers, node_pieces)
    across = send(across, across_chips(peers))
    to_after = jnp.concatenate([returns[2], swapped[cap : 2 * cap]], axis=0)
    to_before = jnp.concatenate([returns[3], swapped[2 * cap :]], axis=0)
    (slot_pieces, edge_next, edge_kept, across, node_pieces, to_after, to_before) = lax.optimization_barrier(
        (slot_pieces, edge_next, edge_kept, across, node_pieces, to_after, to_before)
    )
    edge_pieces = next_sum(peers, 2, edge_next, edge_kept)
    slot_terms = last_terms(peers, slot_pieces)
    node_terms = rest_terms(peers, node_pieces)
    (slot_terms, node_terms, edge_pieces, to_after, to_before) = lax.optimization_barrier(
        (slot_terms, node_terms, edge_pieces, to_after, to_before)
    )
    edge_terms = last_terms(peers, edge_pieces)
    bundles = [send(to_after, by_shift(peers, 2)), send(to_before, by_shift(peers, -2))]
    returned = [returns[0], swapped, *bundles, across]
    node_rows = w_node_in.shape[0] // peers
    node_out_rows = w_node_out.shape[0] // peers
    out_rows = w_edge_out.shape[0] // peers
    grid_grad, grad_edge_out, grad_node_in, grad_node_out = pl.pallas_call(
        functools.partial(scatter_kernel, out_rows, len(slot_terms)),
        grid=(2,),
        in_specs=[smem, whole(rows.shape)]
        + return_specs
        + [whole((out_rows + cap, width))] * len(slot_terms)
        + [whole((node_rows + node_out_rows, width))] * len(node_terms),
        out_specs=[pl.BlockSpec((grid_count // 2, width), lambda step: (step, 0))]
        + [whole((count, width)) for count in (out_rows, node_rows, node_out_rows)],
        out_shape=[jax.ShapeDtypeStruct((grid_count, width), BF16)]
        + [jax.ShapeDtypeStruct((count, width), F32) for count in (out_rows, node_rows, node_out_rows)],
        compiler_params=params,
        name="scatter_lists",
    )(me, rows, *returned, *slot_terms, *node_terms)
    edge_terms, grid_grad = lax.optimization_barrier((edge_terms, grid_grad))
    return (
        grid_grad,
        edge_grad,
        mesh_grad,
        total_of(edge_terms, 0, w_edge_in.shape[0] // peers),
        grad_edge_out,
        grad_node_in,
        grad_node_out,
    )


def solution(mesh):
    rows = P(("grp", "lon"), None)
    flat = P(("grp", "lon"))
    return jax.shard_map(
        on_device,
        mesh=mesh,
        in_specs=(rows, rows, rows, rows, flat, flat, flat, P(("grp", "lon"), None, None)) + (P(),) * 4,
        out_specs=(rows,) * 7,
        check_vma=False,
    )
```
